32 devices in a mesh: gx: 2 (over y), gy: 16 (over z, x, core).
Axes of the slice: x: 2, y: 2, z: 4, core: 2. Of those that a mesh axis runs over, the one named last changes fastest.
Arguments:
- tokens: bfloat16 [4096, 768], P(('gx', 'gy')), may hold values from -6 to 6
- timesteps: int32 [64], P(('gx', 'gy')), may hold values from 0 to 999
- lengths: int32 [32, 2], P(('gx', 'gy')), may hold values from 1 to 96, 128 in all within a row
- routes: int32 [4096, 2], P(('gx', 'gy')), may hold values from 0 to 7, all different within a row; in each aligned block of 128 rows (0 to 127, 128 to 255, ...) at most 64 rows name the same one
- cotangent: bfloat16 [4096, 768], P(('gx', 'gy')), may hold values from -6 to 6
- w_ada: bfloat16 [768, 4608], P(('gx', 'gy')), may hold values from -0.625 to 0.625
- w_qkv: bfloat16 [768, 2304], P(('gx', 'gy')), may hold values from -0.21875 to 0.21875
- w_out: bfloat16 [768, 768], P(('gx', 'gy')), may hold values from -0.875 to 0.875
- w_fc1: bfloat16 [768, 3072], P(('gx', 'gy')), may hold values from -0.21875 to 0.21875
- w_fc2: bfloat16 [3072, 768], P(('gx', 'gy')), may hold values from -0.109375 to 0.109375
- w_router: bfloat16 [768, 8], P(('gx', 'gy')), may hold values from -0.15625 to 0.15625
- e_fc1: bfloat16 [8, 768, 3072], P('gx', 'gy'), may hold values from -0.21875 to 0.21875
- e_fc2: bfloat16 [8, 3072, 768], P('gx', 'gy'), may hold values from -0.4375 to 0.4375
Outputs:
- output: bfloat16 [4096, 768], P(('gx', 'gy'))
- d_tokens: float32 [4096, 768], P(('gx', 'gy'))
- d_w_ada: float32 [768, 4608], P(('gx', 'gy'))
- d_w_qkv: float32 [768, 2304], P(('gx', 'gy'))
- d_w_out: float32 [768, 768], P(('gx', 'gy'))
- d_w_fc1: float32 [768, 3072], P(('gx', 'gy'))
- d_w_fc2: float32 [3072, 768], P(('gx', 'gy'))
- d_w_router: float32 [768, 8], P(('gx', 'gy'))
- d_e_fc1: float32 [8, 768, 3072], P('gx', 'gy')
- d_e_fc2: float32 [8, 3072, 768], P('gx', 'gy')
The draws below stay inside these ranges and needn't reach their ends.
Inputs may be any that keep to these rules, and one draw needn't show every extreme that they name: `lengths`: each device's row sums to 128; no item has more than 96 patches. `routes`: each row names two different experts. Among the rows of one device no expert is named more than 64 times; some device's rows name some expert exactly 64 times.
All inputs are finite; a program needn't handle non-finite values.
Results may differ from the reference program's by a relative error of at most 0.028.
Values may be sent and summed in bfloat16 or wider, within the bound.
A program may use at most 192 MiB of HBM per device.

```python
import math
import jax
import jax.numpy as jnp
import numpy as np
from jax import lax

D = 768
HEADS = 12
HD = 64
FF = 3072
E = 8
TOP = 2
ITEMS_DEV = 2
TOK_DEV = 128
CAP = 64
TOKENS = 4096
ITEMS = 64
N_GX = 2
N_GY = 16


def plant(result, own_key, low, largest):
    longest = result.shape.index(max(result.shape))
    spots = []
    for shift in (0, 1):
        where = [jax.random.randint(jax.random.fold_in(own_key, axis), (), 0, length) for axis, length in enumerate(result.shape)]
        where[longest] = (where[longest] + shift) % result.shape[longest]
        spots.append(tuple(where))
    return result.at[spots[0]].set(low).at[spots[1]].set(largest)


def level_of(own_key, dims, pieces, least, top_value):
    loudness, own = 1.0, jax.random.fold_in(own_key, 6)
    for dim, parts in pieces:
        heights = jnp.exp(jax.random.uniform(jax.random.fold_in(own, dim), (parts,), jnp.float32, least / len(pieces), top_value / len(pieces)))
        loudness = loudness * jnp.repeat(heights, dims[dim] // parts).reshape([-1 if axis == dim else 1 for axis in range(len(dims))])
    return loudness


def cumulative_ranks(count, slope):
    weights = [(1 << 20) // math.isqrt(standing ** slope) + 1 for standing in range(1, count + 1)]
    spread = 1 + sum(weights) // (1 << 30)
    return np.cumsum(np.array([max(1, weight // spread) for weight in weights]))


def ranked_ids(key, extent, amount, lean):
    table = cumulative_ranks(amount, lean)
    pick = jax.random.randint(jax.random.fold_in(key, 1), extent, 0, int(table[amount - 1]))
    rank = jnp.searchsorted(jnp.asarray(table, jnp.int32), pick, side="right")
    return jax.random.permutation(jax.random.fold_in(key, 2), amount)[rank].astype(jnp.int32)


def profile(amount, total, limit, slope):
    portions = [(1 << 20) // math.isqrt(grade ** slope) + 1 for grade in range(2, amount + 1)]
    surplus, given = total - limit - (amount - 1), [1] * (amount - 1)
    while surplus > 0:
        movable = [i for i in range(amount - 1) if given[i] < limit]
        pool, remaining = sum([portions[i] for i in movable]), surplus
        for i in movable:
            more = min(limit - given[i], max(1, remaining * portions[i] // pool), surplus)
            given[i] = given[i] + more
            surplus = surplus - more
    return np.array([limit] + given)


def ragged(stream_key, amount, total, reach, skew):
    if amount == 2:
        one = jax.random.randint(stream_key, (), max(1, total - reach), min(reach, total - 1) + 1)
        return jnp.stack([one, total - one])
    sizes = jnp.asarray(profile(amount, total, reach, skew), jnp.int32)
    pairs = (amount - 1) // 2
    giver, taker = sizes[1:1 + 2 * pairs:2], sizes[2:2 + 2 * pairs:2]
    margin = jnp.minimum(giver - 1, reach - taker)
    passed = jax.random.randint(jax.random.fold_in(stream_key, 1), (pairs,), 0, 1 << 20) % (margin + 1)
    sizes = sizes.at[1:1 + 2 * pairs:2].set(giver - passed).at[2:2 + 2 * pairs:2].set(taker + passed)
    return sizes[jax.random.permutation(jax.random.fold_in(stream_key, 2), amount)]


def deal_out(stream_key, own, number, rows, amount, top, limit, slope):
    order = jax.random.permutation(stream_key, amount)
    packed, ordinary = portions_of(amount, rows * top, limit, slope, True), portions_of(amount, rows * top, limit, slope, False)
    places = jnp.arange(amount)

    def named(sizes, rotation):
        used = int((sizes > 0).sum())
        fixed = max(1, used // 4)
        shifted = fixed + (places - fixed + rotation * (used - fixed)) % max(1, amount - fixed)
        return jnp.zeros((amount,), jnp.int32).at[order[jnp.where(places < fixed, places, shifted)]].set(jnp.asarray(sizes, jnp.int32))

    sizes = jnp.where(number % 4 == 0, named(packed, number // 4), named(ordinary, number - number // 4 - 1))
    mixed = jax.random.permutation(jax.random.fold_in(own, 3), amount)
    donor, receiver = mixed[0:amount // 2 * 2:2], mixed[1:amount // 2 * 2:2]
    room = jnp.minimum(sizes[donor] - 1, limit - sizes[receiver]) // 2
    room = jnp.where((donor == order[0]) | (receiver == order[0]) | (sizes[receiver] == 0), 0, jnp.maximum(room, 0))
    shifted = jax.random.randint(jax.random.fold_in(own, 4), (amount // 2,), 0, 1 << 20) % (room + 1)
    sizes = sizes.at[donor].add(-shifted).at[receiver].add(shifted)
    items = jnp.searchsorted(jnp.cumsum(sizes), jnp.arange(rows * top), side="right").astype(jnp.int32)
    listing = items.reshape(top, rows).T
    listing = listing[jax.random.permutation(jax.random.fold_in(own, 1), rows)]
    rotation = jax.random.randint(jax.random.fold_in(own, 2), (rows, 1), 0, top)
    return jnp.take_along_axis(listing, (jnp.arange(top)[None, :] + rotation) % top, axis=1)


def portions_of(count, total, bound, slope, full):
    weights = [(1 << 20) // math.isqrt(rank ** slope) + 1 for rank in range(1, count + 1)]
    largest = bound if full else min(bound, max(-(-total // count), total * weights[0] // sum(weights)))
    least = 1 if total - largest >= count - 1 else 0
    counts, rest = [largest] + [least] * (count - 1), total - largest - least * (count - 1)
    while rest > 0:
        candidates = [i for i in range(1, count) if counts[i] < largest] or [i for i in range(1, count) if counts[i] < bound]
        mass, remaining = sum([weights[i] for i in candidates]), rest
        for i in candidates:
            addition = min(bound - counts[i], max(1, remaining * weights[i] // mass), rest)
            counts[i] = counts[i] + addition
            rest = rest - addition
    return np.array(counts)


def scatter_about(rng, shape, scale, reach, shards=(), kind=jnp.bfloat16):
    drawn = scale * jax.random.normal(rng, shape, jnp.float32)
    if shards:
        drawn = drawn * level_of(rng, shape, shards, -0.22, 0.18)
    return jnp.clip(drawn, -reach, reach).astype(kind)


def setup_inputs(seed: int = 0) -> dict:
    keys = jax.random.split(jax.random.key(seed), 14)
    tokens = scatter_about(keys[0], (TOKENS, D), 1.0, 6.0, ((0, 32),))
    timesteps = plant(ranked_ids(keys[1], (ITEMS,), 1000, 2), jax.random.fold_in(keys[1], 3), 0, 999).astype(jnp.int32)
    lengths = jax.vmap(lambda own: ragged(own, ITEMS_DEV, TOK_DEV, 3 * TOK_DEV // 4, 2))(jax.random.split(keys[2], (N_GX * N_GY))).reshape((N_GX * N_GY, ITEMS_DEV)).astype(jnp.int32)
    routes_keys = jax.random.split(jax.random.fold_in(keys[3], 1), TOKENS // TOK_DEV)
    routes_turns = jax.random.permutation(jax.random.fold_in(keys[3], 3), TOKENS // TOK_DEV)
    routes = jax.vmap(lambda own, number: deal_out(jax.random.fold_in(keys[3], 2), own, number, TOK_DEV, E, TOP, CAP, 2))(routes_keys, routes_turns).reshape((TOKENS, TOP))
    cotangent = scatter_about(keys[4], (TOKENS, D), 1.0, 6.0, ((0, 32),))
    w_ada = scatter_about(keys[5], (D, 6 * D), (D // 8) ** -0.5, 0.625, ((0, 32),))
    w_qkv = scatter_about(keys[6], (D, 3 * D), D ** -0.5, 0.21875, ((0, 32),))
    w_out = scatter_about(keys[7], (D, D), (D // 16) ** -0.5, 0.875, ((0, 32),))
    w_fc1 = scatter_about(keys[8], (D, FF), D ** -0.5, 0.21875, ((0, 32),))
    w_fc2 = scatter_about(keys[9], (FF, D), FF ** -0.5, 0.109375, ((0, 32),))
    w_router = scatter_about(keys[10], (D, E), (2 * D) ** -0.5, 0.15625, ((0, 32),))
    e_fc1 = scatter_about(keys[11], (E, D, FF), D ** -0.5, 0.21875, ((0, 2), (1, 16)))
    e_fc2 = scatter_about(keys[12], (E, FF, D), (FF // 16) ** -0.5, 0.4375, ((0, 2), (1, 16)))
    return {"tokens": tokens, "timesteps": timesteps, "lengths": lengths, "routes": routes, "cotangent": cotangent, "w_ada": w_ada, "w_qkv": w_qkv, "w_out": w_out, "w_fc1": w_fc1, "w_fc2": w_fc2, "w_router": w_router, "e_fc1": e_fc1, "e_fc2": e_fc2}


@jax.custom_vjp
def low(v):
    return lax.optimization_barrier(v.astype(jnp.bfloat16)).astype(jnp.float32)

@jax.custom_vjp
def low_back(v):
    return v

def low_keep(v):
    return (low(v), None)

def low_pass(kept, grad):
    return (grad,)

def back_keep(v):
    return (v, None)

def back_low(kept, grad):
    return (low(grad),)
low.defvjp(low_keep, low_pass)
low_back.defvjp(back_keep, back_low)
precise = lax.Precision.HIGHEST
layer_epsilon = 1e-06

def product(left_side, right_side):
    return jnp.dot(left_side, right_side, precision=precise)

def layer_norm(values):
    average = lax.optimization_barrier(jnp.mean(values, axis=-1, keepdims=True))
    centred = values - average
    return centred * lax.rsqrt(lax.optimization_barrier(jnp.mean(centred * centred, axis=-1, keepdims=True)) + layer_epsilon)

def modulate(values, shift_by, scale_by):
    return layer_norm(values) * (1.0 + scale_by) + shift_by

def sinusoid(timesteps, model_width):
    half_width = model_width // 2
    frequency = jnp.exp(-math.log(10000.0) * jnp.arange(half_width, dtype=jnp.float32) / half_width)
    angles = timesteps.astype(jnp.float32)[:, None] * frequency[None, :]
    return jnp.concatenate([jnp.cos(angles), jnp.sin(angles)], axis=1)

def membership(lengths, tok_count):
    bounds = jnp.cumsum(lengths)[:-1]
    position = jnp.arange(tok_count, dtype=jnp.int32)
    item_of = lax.optimization_barrier(jnp.sum((position[:, None] >= bounds[None, :]).astype(jnp.int32), axis=1))
    item_ids = jnp.arange(lengths.shape[0], dtype=jnp.int32)
    return ((item_of[:, None] == item_ids[None, :]).astype(jnp.float32), item_of)

def slot_index(routes, expert_count, capacity):
    flat_routes = routes.reshape(-1)
    expert_hot = (flat_routes[:, None] == jnp.arange(expert_count, dtype=jnp.int32)[None, :]).astype(jnp.int32)
    before = jnp.cumsum(expert_hot, axis=0) - expert_hot
    rank_in = lax.optimization_barrier(jnp.sum(before * expert_hot, axis=1))
    return (flat_routes * capacity + rank_in).reshape(routes.shape)

def block_forward(weights, block_tokens, block_steps, block_lengths, block_routes):
    w_ada, w_qkv, w_out, w_fc1, w_fc2, w_router, e_fc1, e_fc2 = weights
    tok_count = block_tokens.shape[0]
    member, item_of = membership(block_lengths, tok_count)
    condition = low(jax.nn.silu(sinusoid(block_steps, D)))
    modulation = low_back(product(condition, w_ada))
    token_mod = product(member, modulation)
    shift_attn, scale_attn, gate_attn, shift_mlp, scale_mlp, gate_mlp = jnp.split(token_mod, 6, axis=1)
    attn_in = low(modulate(block_tokens, shift_attn, scale_attn))
    qkv_low = low(low_back(product(attn_in, w_qkv)))
    queries, key_rows, value_rows = [portion.reshape(tok_count, HEADS, HD) for portion in jnp.split(qkv_low, 3, axis=1)]
    same_item = item_of[:, None] == item_of[None, :]
    scores = low_back(jnp.einsum('qhd,khd->hqk', queries, key_rows, precision=precise) * HD ** (-0.5))
    scores = jnp.where(same_item[None], scores, -1e+30)
    probs_low = low(jax.nn.softmax(scores, axis=-1))
    attn_low = low(low_back(jnp.einsum('hqk,khd->qhd', probs_low, value_rows, precision=precise).reshape(tok_count, D)))
    middle = block_tokens + gate_attn * low_back(product(attn_low, w_out))
    mixed_in = low(modulate(middle, shift_mlp, scale_mlp))
    hidden = low(jax.nn.gelu(low_back(product(mixed_in, w_fc1))))
    shared = low_back(product(hidden, w_fc2))
    chance = jax.nn.softmax(low_back(product(mixed_in, w_router)), axis=-1)
    expert_ids = jnp.arange(E, dtype=jnp.int32)
    chosen = (block_routes[:, :, None] == expert_ids[None, None, :]).astype(jnp.float32)
    gate_values = lax.optimization_barrier(jnp.sum(chosen * chance[:, None, :], axis=2))
    slot_of = slot_index(block_routes, E, CAP)
    slot_ids = jnp.arange(E * CAP, dtype=jnp.int32)
    selector = (slot_of[:, :, None] == slot_ids[None, None, :]).astype(jnp.float32)
    slot_rows = jnp.einsum('tks,td->sd', selector, mixed_in, precision=precise).reshape(E, CAP, D)
    inner_act = low(jax.nn.gelu(low_back(jnp.einsum('ecd,edf->ecf', slot_rows, e_fc1, precision=precise))))
    expert_out = low(low_back(jnp.einsum('ecf,efd->ecd', inner_act, e_fc2, precision=precise))).reshape(E * CAP, D)
    picked = jnp.take(expert_out, slot_of, axis=0)
    expert_sum = lax.optimization_barrier(jnp.sum(gate_values[:, :, None] * picked, axis=1))
    return middle + gate_mlp * (shared + expert_sum)

def reference(tokens, timesteps, lengths, routes, cotangent, w_ada, w_qkv, w_out, w_fc1, w_fc2, w_router, e_fc1, e_fc2):
    blocks = lengths.shape[0]
    tok_count = tokens.shape[0] // blocks
    model_width = tokens.shape[1]
    block_tokens = tokens.astype(jnp.float32).reshape(blocks, tok_count, model_width)
    block_steps = timesteps.reshape(blocks, -1)
    block_routes = routes.reshape(blocks, tok_count, routes.shape[1])
    weights = tuple((weight.astype(jnp.float32) for weight in (w_ada, w_qkv, w_out, w_fc1, w_fc2, w_router, e_fc1, e_fc2)))
    checked = jax.checkpoint(block_forward)

    def forward(all_tokens, all_weights):

        def scan_body(carried, sliced):
            return (carried, checked(all_weights, sliced[0], sliced[1], sliced[2], sliced[3]))
        unused, outputs = lax.scan(scan_body, jnp.zeros((), jnp.float32), (all_tokens, block_steps, lengths, block_routes))
        return outputs
    output, pullback = jax.vjp(forward, block_tokens, weights)
    grad_tokens, grad_weights = pullback(cotangent.astype(jnp.float32).reshape(blocks, tok_count, model_width))
    return (output.reshape(-1, model_width).astype(jnp.bfloat16), grad_tokens.reshape(-1, model_width), grad_weights[0], grad_weights[1], grad_weights[2], grad_weights[3], grad_weights[4], grad_weights[5], grad_weights[6], grad_weights[7])
```

```python
import functools
import math

import jax
import jax.numpy as jnp
from jax import lax
from jax.experimental import pallas as pl
from jax.experimental.pallas import tpu as pltpu
from jax.sharding import PartitionSpec as P

HEADS = 12
CAP = 64
MESH = pl.DeviceIdType.MESH
ANY = pl.ANY
VMEM = pltpu.VMEM
DMA = pltpu.SemaphoreType.DMA
LINE = (1, 3, 2)

precise = lax.Precision.HIGHEST
layer_epsilon = 1e-06


def place():
    gy = lax.axis_index("gy")
    return lax.axis_index("gx"), gy // 4, (gy // 2) % 2, gy % 2


def device(y, z, x, c):
    return (y, 4 * z + 2 * x + c)


def chip(y, z, x):
    return 8 * y + 2 * z + x


def meet(partners):
    barrier = pltpu.get_barrier_semaphore()
    for partner in partners:
        pl.semaphore_signal(barrier, inc=1, device_id=partner, device_id_type=MESH)
    pl.semaphore_wait(barrier, len(partners))


def cross_partners(here):
    y, z, x, c = here
    return [device(y, (z + step) % 4, x, c) for step in LINE] + [
        device(1 - y, z, x, c),
        device(y, z, 1 - x, c),
    ]


def remote(source, target, send, recv, to):
    return pltpu.make_async_remote_copy(
        src_ref=source, dst_ref=target, send_sem=send, recv_sem=recv, device_id=to, device_id_type=MESH
    )


class Gather:
    def __init__(self, here, y_first, own, slot, send, recv, pair=None):
        self.here, self.y_first, self.own, self.slot = here, y_first, own, slot
        self.send, self.recv, self.pair, self.started = send, recv, pair, []

    def copy(self, source, number, recv, to):
        sent = remote(source, self.slot(number), self.send.at[len(self.started)], recv.at[number], to)
        sent.start()
        self.started.append(sent)

    def forward(self, source, number, to_y, to_x):
        y, z, x, c = self.here
        if to_y:
            self.copy(source, number, self.recv, device(1 - y, z, x, c))
        if to_x:
            self.copy(source, number, self.recv, device(y, z, 1 - x, c))
        if self.pair is not None:
            self.copy(source, number, self.pair, device(y, z, x, 1 - c))

    def arrive(self, number, recv=None):
        recv = self.recv if recv is None else recv
        block = self.slot(number)
        remote(block, block, self.send.at[0], recv.at[number], device(*self.here)).wait_recv()
        return block

    def start(self):
        y, z, x, c = self.here
        number = chip(y, z, x)
        for step in LINE:
            self.copy(self.own, number, self.recv, device(y, (z + step) % 4, x, c))
        self.forward(self.own, number, True, True)

    def line(self, step):
        y, z, x, c = self.here
        number = chip(y, (z + step) % 4, x)
        self.forward(self.arrive(number), number, True, True)

    def second(self, step):
        y, z, x, c = self.here
        if self.y_first:
            number = chip(1 - y, (z + step) % 4, x)
        else:
            number = chip(y, (z + step) % 4, 1 - x)
        self.forward(self.arrive(number), number, not self.y_first, self.y_first)

    def third(self, step):
        y, z, x, c = self.here
        for other in (0, 1):
            if self.y_first:
                number = chip(y if other == 0 else 1 - y, (z + step) % 4, 1 - x)
            else:
                number = chip(1 - y, (z + step) % 4, x if other == 0 else 1 - x)
            self.forward(self.arrive(number), number, False, False)

    def finish(self):
        for sent in self.started:
            sent.wait_send()
        if self.pair is not None:
            for number in range(16):
                self.arrive(number, self.pair)


def gather_all(gathers, between=None):
    for gather in gathers:
        gather.start()
    for gather in gathers:
        gather.second(0)
    for step in LINE:
        for gather in gathers:
            gather.line(step)
        for gather in gathers:
            gather.second(step)
    if between is not None:
        between()
    for step in (0,) + LINE:
        for gather in gathers:
            gather.third(step)
    for gather in gathers:
        gather.finish()


class Scatter:
    def __init__(self, here, y_first, part, got, send, recv):
        self.here, self.y_first, self.part, self.got = here, y_first, part, got
        self.send, self.recv, self.started = send, recv, []

    def number(self, a, b, step):
        y, z, x, c = self.here
        flip_y, flip_x = (a, b) if self.y_first else (b, a)
        return chip(1 - y if flip_y else y, (z + step) % 4, 1 - x if flip_x else x)

    def toward(self, second):
        y, z, x, c = self.here
        return device(1 - y, z, x, c) if self.y_first != second else device(y, z, 1 - x, c)

    def copy(self, source, index, to):
        sent = remote(source, self.got(index), self.send.at[len(self.started)], self.recv.at[index], to)
        sent.start()
        self.started.append(sent)

    def arrive(self, index):
        block = self.got(index)
        remote(block, block, self.send.at[0], self.recv.at[index], device(*self.here)).wait_recv()
        return block

    def first(self, step):
        for b in (1, 0):
            self.copy(self.part(self.number(1, b, step)), 4 * b + step, self.toward(False))

    def add(self, number, index):
        block, mine = self.arrive(index), self.part(number)
        total = mine[...].astype(jnp.float32) + block[...].astype(jnp.float32)
        mine[...] = total.astype(mine.dtype)

    def one(self, b, step):
        number = self.number(0, b, step)
        self.add(number, 4 * b + step)
        if b == 1:
            self.copy(self.part(number), 8 + step, self.toward(True))

    def two(self, step):
        y, z, x, c = self.here
        number = self.number(0, 0, step)
        self.add(number, 8 + step)
        if step:
            self.copy(self.part(number), 11 + step, device(y, (z + step) % 4, x, c))

    def total(self):
        result = self.part(self.number(0, 0, 0))[...].astype(jnp.float32)
        for step in (1, 2, 3):
            result = result + self.arrive(11 + step)[...].astype(jnp.float32)
        return result

    def finish(self):
        for sent in self.started:
            sent.wait_send()


def scatter_all(scatters):
    order = (2, 1, 3, 0)
    for scatter in scatters:
        scatter.first(order[0])
    for scatter in scatters:
        scatter.first(order[1])
    for turn, step in enumerate(order):
        for scatter in scatters:
            scatter.one(1, step)
        for scatter in scatters:
            scatter.one(0, step)
        if turn + 2 < 4:
            for scatter in scatters:
                scatter.first(order[turn + 2])
        for scatter in scatters:
            scatter.two(step)


def weights_kernel(
    fold, e1, e2, f1, f2, ada, qkv, out, w1, w1s, w2, w2s, stage, block_a, block_q, block_o,
    pre_send, pre_recv, g_send, g_recv, g_pair, a_send, a_recv, a_pair_send, a_pair, b_send, b_recv, b_pair, l_sem, d_send, d_recv,
):
    here = y, z, x, c = place()
    me, k, gy = chip(y, z, x), 2 * z + x, 4 * z + 2 * x + c
    rows = fold.shape[1]
    others = [(dy, dz, dx) for dy in (0, 1) for dz in (0, 1, 2, 3) for dx in (0, 1) if (dy, dz, dx) != (0, 0, 0)]
    spot = lambda dy, dz, dx: (1 - y if dy else y, (z + dz) % 4, 1 - x if dx else x)
    sibling = device(y, z, x, 1 - c)
    meet([device(*spot(*o), c) for o in others] + [sibling])

    pre = remote(fold.at[1 - c], stage.at[pl.ds(pl.multiple_of(rows * c, 8), rows)], pre_send, pre_recv, sibling)
    pre.start()
    stage[pl.ds(pl.multiple_of(rows * c, 8), rows), :] = fold[c]

    depth = e1.shape[1]
    width = w1.shape[2]
    cols = lambda n: pl.ds(pl.multiple_of(width * n, 128), width)
    strip = lambda n: pl.ds(pl.multiple_of(depth * n, 16), depth)
    started = []
    plane = [o for o in others if o[0] == 0]
    local = [
        pltpu.make_async_copy(e1.at[:, :, cols(k)], w1.at[:, strip(gy), :], l_sem.at[0]),
        pltpu.make_async_copy(e2, w2.at[:, pl.ds(pl.multiple_of(e2.shape[1] * c, 16), e2.shape[1]), :], l_sem.at[1]),
        pltpu.make_async_copy(f2, w2s.at[pl.ds(pl.multiple_of(f2.shape[0] * c, 16), f2.shape[0]), :], l_sem.at[2]),
        pltpu.make_async_copy(f1.at[me], w1s.at[c, me], l_sem.at[3]),
    ]
    for copy in local:
        copy.start()
    for i, o in enumerate(plane):
        ty, tz, tx = spot(*o)
        copy = remote(
            e1.at[:, :, cols(2 * tz + tx)], w1.at[:, strip(gy), :], a_send.at[i], a_recv.at[k], device(ty, tz, tx, c)
        )
        copy.start()
        started.append(copy)
    for i, o in enumerate(others):
        ty, tz, tx = spot(*o)
        copy = remote(f1.at[chip(ty, tz, tx)], w1s.at[c, me], b_send.at[i], b_recv.at[me], device(ty, tz, tx, c))
        copy.start()
        started.append(copy)
    twin = [
        remote(e2, w2.at[:, pl.ds(pl.multiple_of(e2.shape[1] * c, 16), e2.shape[1]), :], d_send.at[0], d_recv.at[0], sibling),
        remote(f2, w2s.at[pl.ds(pl.multiple_of(f2.shape[0] * c, 16), f2.shape[0]), :], d_send.at[1], d_recv.at[1], sibling),
    ]
    for copy in twin:
        copy.start()

    pre.wait()
    at = 0
    for block in (block_a, block_q, block_o):
        block[...] = stage[:, at : at + block.shape[1]].astype(jnp.bfloat16)
        at += block.shape[1]
    gathers, own = [], []
    for i, (block, full, y_first) in enumerate(((block_a, ada, True), (block_q, qkv, False), (block_o, out, False))):
        slot = functools.partial(lambda full, n: full.at[c, pl.ds(pl.multiple_of(2 * rows * n, 16), 2 * rows), :], full)
        gathers.append(Gather(here, y_first, block, slot, g_send.at[i], g_recv.at[i], g_pair.at[i]))
        copy = pltpu.make_async_copy(block, slot(me), l_sem.at[4 + i])
        copy.start()
        own.append(copy)

    def pass_on():
        for copy in local:
            copy.wait()
        for i, (dz, dx) in enumerate([(0, 0)] + [(o[1], o[2]) for o in plane]):
            sy, sz, sx = spot(0, dz, dx)
            source = 2 * sz + sx
            block = w1.at[:, strip(2 * source + c), :]
            if i:
                remote(block, block, a_send.at[0], a_recv.at[source], sibling).wait_recv()
            copy = remote(block, block, a_pair_send.at[i], a_pair.at[source], sibling)
            copy.start()
            started.append(copy)
        for o in others:
            number = chip(*spot(*o))
            remote(w1s.at[c, number], w1s.at[c, number], b_send.at[0], b_recv.at[number], sibling).wait_recv()
        copy = remote(w1s.at[c], w1s.at[c], b_pair.at[0], b_pair.at[1], sibling)
        copy.start()
        started.append(copy)

    gather_all(gathers, pass_on)
    for copy in own:
        copy.wait()
    for copy in started:
        copy.wait_send()
    for source in range(8):
        block = w1.at[:, strip(2 * source + 1 - c), :]
        remote(block, block, a_send.at[0], a_pair.at[source], sibling).wait_recv()
    remote(w1s.at[1 - c], w1s.at[1 - c], b_pair.at[0], b_pair.at[1], sibling).wait_recv()
    for copy in twin:
        copy.wait_send()
    other = pl.ds(pl.multiple_of(e2.shape[1] * (1 - c), 16), e2.shape[1])
    remote(w2.at[:, other, :], w2.at[:, other, :], d_send.at[0], d_recv.at[0], sibling).wait_recv()
    other = pl.ds(pl.multiple_of(f2.shape[0] * (1 - c), 16), f2.shape[0])
    remote(w2s.at[other, :], w2s.at[other, :], d_send.at[1], d_recv.at[1], sibling).wait_recv()


def gather_weights(w_ada, w_qkv, w_out, w_fc1, w_fc2, e_fc1, e_fc2):
    rows, model = w_out.shape
    half = lambda w, c: w[:, c * (w.shape[1] // 2) : (c + 1) * (w.shape[1] // 2)]
    fold = jnp.stack([jnp.concatenate([half(w, c) for w in (w_ada, w_qkv, w_out)], axis=1) for c in (0, 1)])
    fold = fold.astype(jnp.float32)
    ff = w_fc1.shape[1]
    slim = ff // 16
    f1 = w_fc1.reshape(rows, 16, slim).transpose(1, 0, 2).reshape(16, rows // 2, 2 * slim)
    f1 = jnp.pad(f1, ((0, 0), (0, 16 - rows // 2), (0, 0)))
    experts, depth, _ = e_fc1.shape
    wide = ff // 8
    bf = jnp.bfloat16
    shape = jax.ShapeDtypeStruct
    out_shape = (
        shape((2, model, w_ada.shape[1] // 2), bf),
        shape((2, model, w_qkv.shape[1] // 2), bf),
        shape((2, model, w_out.shape[1] // 2), bf),
        shape((experts, model, wide), bf),
        shape((2, 16, 16, 2 * slim), bf),
        shape((experts, 2 * e_fc2.shape[1], model), bf),
        shape((2 * w_fc2.shape[0], model), bf),
    )
    ada, qkv, out, w1, w1s, w2, w2s = pl.pallas_call(
        weights_kernel,
        out_shape=out_shape,
        in_specs=[pl.BlockSpec(memory_space=VMEM)] + [pl.BlockSpec(memory_space=ANY)] * 4,
        out_specs=[pl.BlockSpec(memory_space=ANY)] * 7,
        scratch_shapes=[
            VMEM((2 * rows, fold.shape[2]), jnp.float32),
            VMEM((2 * rows, w_ada.shape[1] // 2), bf),
            VMEM((2 * rows, w_qkv.shape[1] // 2), bf),
            VMEM((2 * rows, w_out.shape[1] // 2), bf),
            DMA, DMA, DMA((3, 31)), DMA((3, 16)), DMA((3, 16)),
            DMA((7,)), DMA((8,)), DMA((8,)), DMA((8,)), DMA((15,)), DMA((16,)), DMA((2,)), DMA((7,)), DMA((2,)), DMA((2,)),
        ],
        compiler_params=pltpu.CompilerParams(collective_id=1, has_side_effects=True, vmem_limit_bytes=32 << 20),
        name="weights",
    )(fold, e_fc1, e_fc2, f1, w_fc2)
    w1s = w1s[:, :, : rows // 2].reshape(2, 16, rows, slim).transpose(1, 0, 2, 3).reshape(model, slim)
    return ada, qkv, out, w1, w1s, w2, w2s


def tokens_kernel(mixed, grad, gates, all_mixed, all_grad, all_gates, send, recv, l_sem):
    here = y, z, x, c = place()
    meet(cross_partners(here))
    own, gathers = [], []
    for i, (block, full, y_first) in enumerate(((mixed, all_mixed, True), (grad, all_grad, False), (gates, all_gates, True))):
        slot = functools.partial(lambda full, n: full.at[n], full)
        gathers.append(Gather(here, y_first, block, slot, send.at[i], recv.at[i]))
        copy = pltpu.make_async_copy(block, slot(chip(y, z, x)), l_sem.at[i])
        copy.start()
        own.append(copy)
    gather_all(gathers)
    for copy in own:
        copy.wait()


def gather_tokens(mixed, grad, gates):
    return pl.pallas_call(
        tokens_kernel,
        out_shape=[jax.ShapeDtypeStruct((16,) + a.shape, a.dtype) for a in (mixed, grad, gates)],
        in_specs=[pl.BlockSpec(memory_space=VMEM)] * 3,
        out_specs=[pl.BlockSpec(memory_space=ANY)] * 3,
        scratch_shapes=[DMA((3, 15)), DMA((3, 16)), DMA((3,))],
        compiler_params=pltpu.CompilerParams(collective_id=2, has_side_effects=True, vmem_limit_bytes=16 << 20),
        name="tokens",
    )(mixed, grad, gates)


def nt(a, b):
    return lax.dot_general(a, b, (((1,), (1,)), ((), ())), preferred_element_type=jnp.float32)


def tn(a, b):
    return lax.dot_general(a, b, (((0,), (0,)), ((), ())), preferred_element_type=jnp.float32)


def nn(a, b):
    return jnp.dot(a, b, preferred_element_type=jnp.float32)


def gelu_both(h):
    root = math.sqrt(2.0 / math.pi)
    square = h * h
    t = jnp.tanh(h * (root + (root * 0.044715) * square))
    half = 0.5 * (1.0 + t)
    slope = half + (0.5 * h) * (1.0 - t * t) * (root + (3.0 * root * 0.044715) * square)
    return h * half, slope


def ffn_tile(lo, shards, X, G, gates, w1, w1s, w2, w2s, act, pre, act_s, pre_s, branch, back, gc):
    rows = pl.ds(pl.multiple_of(lo * 128, 128), shards * 128)
    experts = w1.shape[0]
    xt, gt = X[rows, :], G[rows, :]
    first = lax.axis_index("gx") * experts
    kind = lax.broadcasted_iota(jnp.int32, (16, experts * 128), 0)
    lane = lax.broadcasted_iota(jnp.int32, (16, experts * 128), 1) // 128 + first
    spread = ((kind == lane) | (kind == lane + 8)).astype(jnp.bfloat16)
    gate = jnp.concatenate([tn(gates[lo + s], spread) for s in range(shards)], axis=0)
    h = nn(xt, w1s[...])
    a, d = gelu_both(h)
    gi = nt(gt, w2s[...])
    a = a.astype(jnp.bfloat16)
    p = (gi * d).astype(jnp.bfloat16)
    act_s[rows, :] = a
    pre_s[rows, :] = p
    total = nn(a, w2s[...])
    total_back = nt(p, w1s[...])
    sums = [jnp.zeros((8, 128), jnp.float32) for _ in range(shards)]
    for e in range(experts):
        h = nn(xt, w1[e])
        a, d = gelu_both(h)
        gi = nt(gt, w2[e])
        g = gate[:, e * 128 : (e + 1) * 128]
        g = jnp.concatenate([g] * (w1.shape[2] // 128), axis=1)
        product = (a * gi).astype(jnp.bfloat16)
        row = (lax.broadcasted_iota(jnp.int32, (8, w1.shape[2]), 0) == first + e).astype(jnp.bfloat16)
        sums = [s + nt(row, product[i * 128 : (i + 1) * 128]) for i, s in enumerate(sums)]
        a = (a * g).astype(jnp.bfloat16)
        p = (gi * d * g).astype(jnp.bfloat16)
        act[e, rows, :] = a
        pre[e, rows, :] = p
        total += nn(a, w2[e])
        total_back += nt(p, w1[e])
    branch[rows, :] = total.astype(jnp.bfloat16)
    back[rows, :] = total_back.astype(jnp.bfloat16)
    for s in range(shards):
        gc[lo + s] = sums[s]


def ffn_kernel(X, G, gates, w1, w1s, w2, w2s, branch, back, gc, d1, d1s, d2, d2s, act, pre, act_s, pre_s):
    def body(i, carry):
        ffn_tile(2 * i, 2, X, G, gates, w1, w1s, w2, w2s, act, pre, act_s, pre_s, branch, back, gc)
        return carry

    lax.fori_loop(0, X.shape[0] // 256, body, 0)

    def grads(e, carry):
        d1[e] = tn(X[...], pre[e]).astype(jnp.bfloat16)
        d2[e] = tn(act[e], G[...]).astype(jnp.bfloat16)
        return carry

    lax.fori_loop(0, w1.shape[0], grads, 0)
    d1s[...] = tn(X[...], pre_s[...])
    d2s[...] = tn(act_s[...], G[...]).astype(jnp.bfloat16)


def ffn(X, G, gates, w1, w1s, w2, w2s):
    toks, model = X.shape
    experts, _, wide = w1.shape
    slim = w1s.shape[1]
    bf = jnp.bfloat16
    shape = jax.ShapeDtypeStruct
    return pl.pallas_call(
        ffn_kernel,
        out_shape=[
            shape((toks, model), bf),
            shape((toks, model), bf),
            shape((toks // 128, 8, 128), jnp.float32),
            shape((experts, model, wide), bf),
            shape((model, slim), jnp.float32),
            shape((experts, wide, model), bf),
            shape((slim, model), bf),
        ],
        in_specs=[pl.BlockSpec(memory_space=VMEM)] * 7,
        out_specs=[pl.BlockSpec(memory_space=VMEM)] * 7,
        scratch_shapes=[VMEM((experts, toks, wide), bf), VMEM((experts, toks, wide), bf), VMEM((toks, slim), bf), VMEM((toks, slim), bf)],
        compiler_params=pltpu.CompilerParams(vmem_limit_bytes=56 << 20),
        name="ffn",
    )(X, G, gates, w1, w1s, w2, w2s)


def sums_kernel(
    branch, back, gc, d1, d1s, d2, d2s, sum_branch, sum_back, sum_gc, own1, own1s, own2, own2s,
    p_branch, p_back, p_gc, r_branch, r_back, r_gc, from1, from1s, from2, from2s, out1,out1s,
    l_sem, send, recv, t_send, t_recv, a_send, a_recv, b_send, b_recv,
):
    here = y, z, x, c = place()
    me, k = chip(y, z, x), 2 * z + x
    others = [(dy, dz, dx) for dy in (0, 1) for dz in (0, 1, 2, 3) for dx in (0, 1) if (dy, dz, dx) != (0, 0, 0)]
    plane = [o for o in others if o[0] == 0]
    spot = lambda dy, dz, dx: (1 - y if dy else y, (z + dz) % 4, 1 - x if dx else x)
    sibling = device(y, z, x, 1 - c)
    local = [
        pltpu.make_async_copy(branch, p_branch, l_sem.at[0]),
        pltpu.make_async_copy(back, p_back, l_sem.at[1]),
        pltpu.make_async_copy(gc, p_gc, l_sem.at[2]),
    ]
    for copy in local:
        copy.start()
    meet([device(*spot(*o), c) for o in others] + [sibling])
    rows1, rows1s, rows2, rows2s = from1.shape[2], from1s.shape[1], own2.shape[1], own2s.shape[0]
    started = []
    for n in range(8):
        copy = remote(
            d1.at[:, pl.ds(pl.multiple_of(rows1 * (2 * n + 1 - c), 16), rows1), :], from1.at[:, n], t_send.at[n], t_recv.at[n], sibling
        )
        copy.start()
        started.append(copy)
    for n in range(16):
        copy = remote(
            d1s.at[pl.ds(pl.multiple_of(rows1s * (2 * n + 1 - c), 8), rows1s), :], from1s.at[n], t_send.at[8 + n], t_recv.at[8 + n], sibling
        )
        copy.start()
        started.append(copy)
    copy = remote(d2.at[:, pl.ds(pl.multiple_of(rows2 * (1 - c), 16), rows2), :], from2, t_send.at[24], t_recv.at[24], sibling)
    copy.start()
    started.append(copy)
    copy = remote(d2s.at[pl.ds(pl.multiple_of(rows2s * (1 - c), 16), rows2s), :], from2s, t_send.at[25], t_recv.at[25], sibling)
    copy.start()
    started.append(copy)

    for copy in local:
        copy.wait()
    scatters = []
    for i, (part, got, y_first) in enumerate(((p_branch, r_branch, False), (p_back, r_back, True), (p_gc, r_gc, False))):
        take = functools.partial(lambda ref, n: ref.at[n], part)
        land = functools.partial(lambda ref, n: ref.at[n], got)
        scatters.append(Scatter(here, y_first, take, land, send.at[i], recv.at[i]))

    order = [(0, 0, 0)] + plane
    wide = d1.shape[2]
    for i, o in enumerate(order):
        ty, tz, tx = spot(*o)
        n = 2 * tz + tx
        remote(from1.at[:, n], from1.at[:, n], t_send.at[0], t_recv.at[n], sibling).wait_recv()
        mine = d1[:, pl.ds(pl.multiple_of(rows1 * (2 * n + c), 16), rows1), :]
        out1[:, n] = (mine.astype(jnp.float32) + from1[:, n].astype(jnp.float32)).astype(jnp.bfloat16)
        target = own1.at[:, :, pl.ds(pl.multiple_of(wide * k, 128), wide)]
        if i:
            copy = remote(out1.at[:, n], target, a_send.at[i], a_recv.at[k], device(ty, tz, tx, c))
            copy.start()
            started.append(copy)
        else:
            keep = pltpu.make_async_copy(out1.at[:, n], target, l_sem.at[3])
            keep.start()
    for i, o in enumerate([(0, 0, 0)] + others):
        spot_o = spot(*o)
        n = chip(*spot_o)
        remote(from1s.at[n], from1s.at[n], t_send.at[0], t_recv.at[8 + n], sibling).wait_recv()
        out1s[n] = d1s[pl.ds(pl.multiple_of(rows1s * (2 * n + c), 8), rows1s), :] + from1s[n]
        if i:
            copy = remote(out1s.at[n], own1s.at[me], b_send.at[i], b_recv.at[me], device(*spot_o, c))
            copy.start()
            started.append(copy)
        else:
            keep_s = pltpu.make_async_copy(out1s.at[n], own1s.at[me], l_sem.at[4])
            keep_s.start()
    scatter_all(scatters)
    remote(from2, from2, t_send.at[0], t_recv.at[24], sibling).wait_recv()
    remote(from2s, from2s, t_send.at[0], t_recv.at[25], sibling).wait_recv()
    own2[...] = d2[:, pl.ds(pl.multiple_of(rows2 * c, 16), rows2), :].astype(jnp.float32) + from2[...].astype(jnp.float32)
    own2s[...] = d2s[pl.ds(pl.multiple_of(rows2s * c, 16), rows2s), :].astype(jnp.float32) + from2s[...].astype(jnp.float32)
    sum_branch[...] = scatters[0].total()
    sum_back[...] = scatters[1].total()
    sum_gc[...] = scatters[2].total()
    for scatter in scatters:
        scatter.finish()
    for o in plane:
        ty, tz, tx = spot(*o)
        n = 2 * tz + tx
        block = own1.at[:, :, pl.ds(pl.multiple_of(wide * n, 128), wide)]
        remote(block, block, a_send.at[0], a_recv.at[n], sibling).wait_recv()
    for o in others:
        n = chip(*spot(*o))
        remote(own1s.at[n], own1s.at[n], b_send.at[0], b_recv.at[n], sibling).wait_recv()
    keep.wait()
    keep_s.wait()
    for copy in started:
        copy.wait_send()


def scatter_sums(branch, back, gc, d1, d1s, d2, d2s):
    bf, f32 = jnp.bfloat16, jnp.float32
    model = branch.shape[1]
    slim = d1s.shape[1]
    d1s = jnp.pad(d1s, ((0, 0), (0, -slim % 128)))
    branch, back = branch.reshape(16, -1, model), back.reshape(16, -1, model)
    toks = branch.shape[1]
    experts, _, wide = d1.shape
    rows = model // 32
    rows2, rows2s = d2.shape[1] // 2, d2s.shape[0] // 2
    shape = jax.ShapeDtypeStruct
    return pl.pallas_call(
        sums_kernel,
        out_shape=[
            shape((toks, model), f32),
            shape((toks, model), f32),
            shape((8, 128), f32),
            shape((experts, 2 * rows, 8 * wide), bf),
            shape((16, rows, d1s.shape[1]), f32),
            shape((experts, rows2, model), f32),
            shape((rows2s, model), f32),
        ],
        in_specs=[pl.BlockSpec(memory_space=ANY)] * 3 + [pl.BlockSpec(memory_space=VMEM)] * 4,
        out_specs=[pl.BlockSpec(memory_space=VMEM)] * 3
        + [pl.BlockSpec(memory_space=ANY)] * 2
        + [pl.BlockSpec(memory_space=VMEM)] * 2,
        scratch_shapes=[
            VMEM(branch.shape, bf), VMEM(branch.shape, bf), VMEM(gc.shape, f32),
            VMEM((15, toks, model), bf), VMEM((15, toks, model), bf), VMEM((15, 8, 128), f32),
            VMEM((experts, 8, 2 * rows, wide), bf), VMEM((16, rows, d1s.shape[1]), f32),
            VMEM((experts, rows2, model), bf), VMEM((rows2s, model), bf),
            VMEM((experts, 8, 2 * rows, wide), bf), VMEM((16, rows, d1s.shape[1]), f32),
            DMA((5,)), DMA((3, 15)), DMA((3, 15)), DMA((26,)), DMA((26,)), DMA((8,)), DMA((8,)), DMA((16,)), DMA((16,)),
        ],
        compiler_params=pltpu.CompilerParams(collective_id=3, has_side_effects=True, vmem_limit_bytes=56 << 20),
        name="sums",
    )(branch, back, gc, d1, d1s, d2, d2s)


def owners_kernel(
    qkv, out, mod, total, all_mod, got_q, got_o, part, got, fin, block_sem_s, block_sem_r, send, recv, g_send, g_recv, g_pair, f_send, f_recv, l_sem,
):
    here = y, z, x, c = place()
    me = chip(y, z, x)
    sibling = device(y, z, x, 1 - c)
    meet(cross_partners(here) + [sibling])
    swaps = [
        remote(qkv.at[1 - c], got_q, block_sem_s.at[0], block_sem_r.at[0], sibling),
        remote(out.at[1 - c], got_o, block_sem_s.at[1], block_sem_r.at[1], sibling),
    ]
    for copy in swaps:
        copy.start()
    slot = lambda n: all_mod.at[n, c]
    spread = Gather(here, True, mod, slot, g_send, g_recv, g_pair)
    keep = pltpu.make_async_copy(mod, slot(me), l_sem.at[0])
    keep.start()
    spread.start()
    for copy in swaps:
        copy.wait()
    rows = part.shape[2]
    cut = part.shape[3]
    wide = got_q.shape[1]
    for n in range(16):
        at = slice(n * rows, (n + 1) * rows)
        q = (qkv[c, at, :].astype(jnp.float32) + got_q[at, :].astype(jnp.float32)).astype(jnp.bfloat16)
        o = (out[c, at, :].astype(jnp.float32) + got_o[at, :].astype(jnp.float32)).astype(jnp.bfloat16)
        part[0, n] = q[:, :cut]
        part[1, n] = jnp.concatenate([q[:, cut:], o], axis=1)
    scatters = []
    for i, y_first in enumerate((False, True)):
        take = functools.partial(lambda i, n: part.at[i, n], i)
        land = functools.partial(lambda i, n: got.at[i, n], i)
        scatters.append(Scatter(here, y_first, take, land, send.at[i], recv.at[i]))
    scatter_all(scatters)
    spread.second(0)
    for step in LINE:
        spread.line(step)
        spread.second(step)
    for step in (0,) + LINE:
        spread.third(step)
    fin[c] = jnp.concatenate([scatters[0].total(), scatters[1].total()], axis=1)
    half = rows // 2
    mine = pl.ds(pl.multiple_of(half * c, 8), half)
    theirs = pl.ds(pl.multiple_of(half * (1 - c), 8), half)
    swap = remote(fin.at[c, theirs, :], fin.at[c, theirs, :], f_send, f_recv, sibling)
    swap.start()
    for scatter in scatters:
        scatter.finish()
    spread.finish()
    keep.wait()
    swap.wait_send()
    remote(fin.at[1 - c, mine, :], fin.at[1 - c, mine, :], f_send, f_recv, sibling).wait_recv()
    total[0] = fin[0, mine, :]
    total[1] = fin[1, mine, :]


def to_owners(qkv, out, mod):
    bf, f32 = jnp.bfloat16, jnp.float32
    model = qkv.shape[1]
    rows = model // 16
    wide = qkv.shape[2] + out.shape[2]
    cut = wide // 2
    shape = jax.ShapeDtypeStruct
    return pl.pallas_call(
        owners_kernel,
        out_shape=[shape((2, rows // 2, wide), f32), shape((16, 2) + mod.shape, bf)],
        in_specs=[pl.BlockSpec(memory_space=VMEM)] * 3,
        out_specs=[pl.BlockSpec(memory_space=VMEM), pl.BlockSpec(memory_space=ANY)],
        scratch_shapes=[
            VMEM(qkv.shape[1:], bf), VMEM(out.shape[1:], bf), VMEM((2, 16, rows, cut), bf), VMEM((2, 15, rows, cut), bf),
            VMEM((2, rows, wide), f32),
            DMA((2,)), DMA((2,)), DMA((2, 15)), DMA((2, 15)), DMA((31,)), DMA((16,)), DMA((16,)), DMA, DMA, DMA((1,)),
        ],
        compiler_params=pltpu.CompilerParams(collective_id=4, has_side_effects=True, vmem_limit_bytes=40 << 20),
        name="owners",
    )(qkv, out, mod)


def layer_norm(values):
    average = jnp.mean(values, axis=-1, keepdims=True)
    centred = values - average
    return centred * lax.rsqrt(jnp.mean(centred * centred, axis=-1, keepdims=True) + layer_epsilon)


def modulate(values, shift_by, scale_by):
    return layer_norm(values) * (1.0 + scale_by) + shift_by


def sinusoid(timesteps, model_width):
    half_width = model_width // 2
    frequency = jnp.exp(-math.log(10000.0) * jnp.arange(half_width, dtype=jnp.float32) / half_width)
    angles = timesteps.astype(jnp.float32)[:, None] * frequency[None, :]
    return jnp.concatenate([jnp.cos(angles), jnp.sin(angles)], axis=1)


def membership(lengths, tok_count):
    bounds = jnp.cumsum(lengths)[:-1]
    position = jnp.arange(tok_count, dtype=jnp.int32)
    item_of = jnp.sum((position[:, None] >= bounds[None, :]).astype(jnp.int32), axis=1)
    item_ids = jnp.arange(lengths.shape[0], dtype=jnp.int32)
    return ((item_of[:, None] == item_ids[None, :]).astype(jnp.float32), item_of)


def slot_index(routes, expert_count, capacity):
    flat_routes = routes.reshape(-1)
    expert_hot = (
        flat_routes[:, None] == jnp.arange(expert_count, dtype=jnp.int32)[None, :]
    ).astype(jnp.int32)
    before = jnp.cumsum(expert_hot, axis=0) - expert_hot
    rank_in = jnp.sum(before * expert_hot, axis=1)
    return (flat_routes * capacity + rank_in).reshape(routes.shape)


def dot_float(left_side, right_side):
    return jnp.dot(left_side, right_side, preferred_element_type=jnp.float32)


def dot_rows(left_side, right_side):
    return jnp.einsum("td,tf->df", left_side, right_side, preferred_element_type=jnp.float32)


def dot_cols(left_side, right_side):
    return jnp.einsum("tf,df->td", left_side, right_side, preferred_element_type=jnp.float32)


def dot_halves(left_side, halves):
    return jnp.concatenate([dot_float(left_side, halves[0]), dot_float(left_side, halves[1])], axis=1)


def by_slices(
    tokens, timesteps, lengths, routes, cotangent, w_ada, w_qkv, w_out, w_fc1, w_fc2, w_router, e_fc1, e_fc2
):
    tok_count, model_width = tokens.shape
    head_count = HEADS
    head_size = model_width // head_count
    expert_count = w_router.shape[1]
    score_scale = head_size ** (-0.5)
    residual = tokens.astype(jnp.float32)
    member, item_of = membership(lengths[0], tok_count)
    ada, qkv_w, out_w, w1, w1s, w2, w2s = gather_weights(w_ada, w_qkv, w_out, w_fc1, w_fc2, e_fc1, e_fc2)
    router_full = lax.all_gather(w_router, ("gx", "gy"), axis=0, tiled=True)
    condition = jax.nn.silu(sinusoid(timesteps, model_width)).astype(jnp.bfloat16)
    modulation = dot_halves(condition, ada)
    token_mod = jnp.dot(member, modulation, precision=precise)
    shift_attn, scale_attn, gate_attn, shift_mlp, scale_mlp, gate_mlp = jnp.split(token_mod, 6, axis=1)
    attn_in = modulate(residual, shift_attn, scale_attn).astype(jnp.bfloat16)
    qkv_low = dot_halves(attn_in, qkv_w).astype(jnp.bfloat16)
    queries, key_rows, value_rows = [
        portion.reshape(tok_count, head_count, head_size) for portion in jnp.split(qkv_low, 3, axis=1)
    ]
    same_item = item_of[:, None] == item_of[None, :]
    scores = (
        jnp.einsum("qhd,khd->hqk", queries, key_rows, preferred_element_type=jnp.float32) * score_scale
    )
    scores = jnp.where(same_item[None], scores, -1e30)
    attn_probs = jax.nn.softmax(scores, axis=-1)
    probs_low = attn_probs.astype(jnp.bfloat16)
    attn_low = jnp.einsum("hqk,khd->qhd", probs_low, value_rows, preferred_element_type=jnp.float32)
    attn_low = attn_low.reshape(tok_count, model_width).astype(jnp.bfloat16)
    attn_proj = dot_halves(attn_low, out_w)
    middle = residual + gate_attn * attn_proj
    mixed_in = modulate(middle, shift_mlp, scale_mlp).astype(jnp.bfloat16)
    out_grad = cotangent.astype(jnp.float32)
    grad_branch = out_grad * gate_mlp
    chance = jax.nn.softmax(dot_float(mixed_in, router_full), axis=-1)
    expert_ids = jnp.arange(expert_count, dtype=jnp.int32)
    chosen = jnp.sum((routes[:, :, None] == expert_ids[None, None, :]).astype(jnp.float32), axis=1)
    gates = (chosen * chance).T
    gates_high = gates.astype(jnp.bfloat16)
    gates_low = (gates - gates_high.astype(jnp.float32)).astype(jnp.bfloat16)
    all_mixed, all_grad, all_gates = gather_tokens(
        mixed_in, grad_branch.astype(jnp.bfloat16), jnp.concatenate([gates_high, gates_low], axis=0)
    )
    flat = lambda a: a.reshape(-1, model_width)
    parts = ffn(flat(all_mixed), flat(all_grad), all_gates, w1, w1s, w2, w2s)
    branch, grad_mixed, grad_chance, own1, own1s, sum_e_out, sum_fc2 = scatter_sums(*parts)
    sum_e_in = own1.astype(jnp.float32)
    slim = w1s.shape[1]
    sum_fc1 = own1s[:, :, :slim].transpose(1, 0, 2).reshape(w_fc1.shape)
    output = (middle + gate_mlp * branch).astype(jnp.bfloat16)
    grad_gate_mlp = out_grad * branch
    grad_chance = grad_chance.T * chosen
    grad_logits = chance * (grad_chance - jnp.sum(grad_chance * chance, axis=-1, keepdims=True))
    grad_logits = grad_logits.astype(jnp.bfloat16)
    term_router = dot_rows(mixed_in, grad_logits)
    sum_router = lax.psum_scatter(term_router, ("gx", "gy"), scatter_dimension=0, tiled=True)
    grad_mixed = grad_mixed + dot_cols(grad_logits, router_full)
    unused_mix, mix_back = jax.vjp(modulate, middle, shift_mlp, scale_mlp)
    grad_mid_norm, grad_shift_mlp, grad_scale_mlp = mix_back(grad_mixed)
    grad_middle = out_grad + grad_mid_norm
    grad_gate_attn = grad_middle * attn_proj
    grad_proj = (grad_middle * gate_attn).astype(jnp.bfloat16)
    half = model_width // 2
    term_out = jnp.stack([dot_rows(attn_low, grad_proj[:, c * half : (c + 1) * half]) for c in (0, 1)])
    grad_attn = sum(dot_cols(grad_proj[:, c * half : (c + 1) * half], out_w[c]) for c in (0, 1))
    grad_attn = grad_attn.astype(jnp.bfloat16).reshape(tok_count, head_count, head_size)
    grad_probs = jnp.einsum("qhd,khd->hqk", grad_attn, value_rows, preferred_element_type=jnp.float32)
    grad_values = jnp.einsum("hqk,qhd->khd", probs_low, grad_attn, preferred_element_type=jnp.float32)
    grad_scores = attn_probs * (grad_probs - jnp.sum(grad_probs * attn_probs, axis=-1, keepdims=True))
    grad_scores = grad_scores.astype(jnp.bfloat16)
    grad_queries = (
        jnp.einsum("hqk,khd->qhd", grad_scores, key_rows, preferred_element_type=jnp.float32) * score_scale
    )
    grad_keys = (
        jnp.einsum("hqk,qhd->khd", grad_scores, queries, preferred_element_type=jnp.float32) * score_scale
    )
    grad_qkv = jnp.concatenate(
        [g.reshape(tok_count, model_width) for g in (grad_queries, grad_keys, grad_values)], axis=1
    ).astype(jnp.bfloat16)
    half = grad_qkv.shape[1] // 2
    term_qkv = jnp.stack([dot_rows(attn_in, grad_qkv[:, c * half : (c + 1) * half]) for c in (0, 1)])
    grad_attn_in = sum(dot_cols(grad_qkv[:, c * half : (c + 1) * half], qkv_w[c]) for c in (0, 1))
    unused_pre, pre_back = jax.vjp(modulate, residual, shift_attn, scale_attn)
    grad_input_norm, grad_shift_attn, grad_scale_attn = pre_back(grad_attn_in)
    d_tokens = grad_middle + grad_input_norm
    grad_token_mod = jnp.concatenate(
        [grad_shift_attn, grad_scale_attn, grad_gate_attn, grad_shift_mlp, grad_scale_mlp, grad_gate_mlp], axis=1
    )
    grad_modulation = jnp.einsum("ti,tc->ic", member, grad_token_mod, precision=precise).astype(jnp.bfloat16)
    items = grad_modulation.shape[0]
    both = jnp.concatenate([grad_modulation, condition], axis=1)
    width = both.shape[1]
    tile = jnp.pad(both.reshape(items * 8, width // 8), ((0, 0), (0, -(width // 8) % 128)))
    total, all_tile = to_owners(term_qkv.astype(jnp.bfloat16), term_out.astype(jnp.bfloat16), tile)
    all_both = all_tile[..., : width // 8].reshape(-1, width)
    all_modgrad, all_condition = all_both[:, : grad_modulation.shape[1]], all_both[:, grad_modulation.shape[1] :]
    own_share = w_ada.shape[0]
    own_start = lax.axis_index(("gx", "gy")) * own_share
    own_condition = lax.dynamic_slice_in_dim(all_condition, own_start, own_share, 1)
    owned_ada = dot_rows(own_condition, all_modgrad)
    sum_qkv = jnp.concatenate([total[0, :, :half], total[1, :, :half]], axis=1)
    sum_out = jnp.concatenate([total[0, :, half:], total[1, :, half:]], axis=1)
    return (output, d_tokens, owned_ada, sum_qkv, sum_out, sum_fc1, sum_fc2, sum_router, sum_e_in, sum_e_out)


def by_weights(
    tokens,
    timesteps,
    lengths,
    routes,
    cotangent,
    w_ada,
    w_qkv,
    w_out,
    w_fc1,
    w_fc2,
    w_router,
    e_fc1,
    e_fc2,
):
    tok_count, model_width = tokens.shape
    head_count = HEADS
    head_size = model_width // head_count
    expert_count = w_router.shape[1]
    capacity = CAP
    score_scale = head_size ** (-0.5)
    residual = tokens.astype(jnp.float32)
    member, item_of = membership(lengths[0], tok_count)
    ada_full, qkv_full, out_full = (
        lax.all_gather(w_ada, ("gx", "gy"), axis=0, tiled=True),
        lax.all_gather(w_qkv, ("gx", "gy"), axis=0, tiled=True),
        lax.all_gather(w_out, ("gx", "gy"), axis=0, tiled=True),
    )
    condition = jax.nn.silu(sinusoid(timesteps, model_width)).astype(jnp.bfloat16)
    modulation = dot_float(condition, ada_full)
    token_mod = jnp.dot(member, modulation, precision=precise)
    shift_attn, scale_attn, gate_attn, shift_mlp, scale_mlp, gate_mlp = jnp.split(
        token_mod, 6, axis=1
    )
    attn_in = modulate(residual, shift_attn, scale_attn).astype(jnp.bfloat16)
    qkv_low = dot_float(attn_in, qkv_full).astype(jnp.bfloat16)
    queries, key_rows, value_rows = [
        portion.reshape(tok_count, head_count, head_size)
        for portion in jnp.split(qkv_low, 3, axis=1)
    ]
    same_item = item_of[:, None] == item_of[None, :]
    scores = (
        jnp.einsum("qhd,khd->hqk", queries, key_rows, preferred_element_type=jnp.float32)
        * score_scale
    )
    scores = jnp.where(same_item[None], scores, -1e30)
    attn_probs = jax.nn.softmax(scores, axis=-1)
    probs_low = attn_probs.astype(jnp.bfloat16)
    attn_low = jnp.einsum("hqk,khd->qhd", probs_low, value_rows, preferred_element_type=jnp.float32)
    attn_low = attn_low.reshape(tok_count, model_width).astype(jnp.bfloat16)
    attn_proj = dot_float(attn_low, out_full)
    middle = residual + gate_attn * attn_proj
    mixed_in = modulate(middle, shift_mlp, scale_mlp).astype(jnp.bfloat16)
    fc1_full, fc2_full, router_full = (
        lax.all_gather(w_fc1, ("gx", "gy"), axis=0, tiled=True),
        lax.all_gather(w_fc2, ("gx", "gy"), axis=0, tiled=True),
        lax.all_gather(w_router, ("gx", "gy"), axis=0, tiled=True),
    )
    hidden_pre = dot_float(mixed_in, fc1_full)
    hidden = jax.nn.gelu(hidden_pre).astype(jnp.bfloat16)
    shared = dot_float(hidden, fc2_full)
    chance = jax.nn.softmax(dot_float(mixed_in, router_full), axis=-1)
    expert_ids = jnp.arange(expert_count, dtype=jnp.int32)
    chosen = (routes[:, :, None] == expert_ids[None, None, :]).astype(jnp.float32)
    gate_values = jnp.sum(chosen * chance[:, None, :], axis=2)
    slot_of = slot_index(routes, expert_count, capacity)
    slot_ids = jnp.arange(expert_count * capacity, dtype=jnp.int32)
    selector = (slot_of[:, :, None] == slot_ids[None, None, :]).astype(jnp.bfloat16)
    slot_rows = jnp.einsum("tks,td->sd", selector, mixed_in, preferred_element_type=jnp.float32)
    slot_rows = slot_rows.astype(jnp.bfloat16).reshape(expert_count, capacity, model_width)
    owned_rows = lax.all_to_all(slot_rows, "gx", split_axis=0, concat_axis=1, tiled=True)
    expert_in, expert_back = (
        lax.all_gather(e_fc1, "gy", axis=1, tiled=True),
        lax.all_gather(e_fc2, "gy", axis=1, tiled=True),
    )
    inner_pre = jnp.einsum(
        "ecd,edf->ecf", owned_rows, expert_in, preferred_element_type=jnp.float32
    )
    inner_act = jax.nn.gelu(inner_pre).astype(jnp.bfloat16)
    result = jnp.einsum(
        "ecf,efd->ecd", inner_act, expert_back, preferred_element_type=jnp.float32
    ).astype(jnp.bfloat16)
    returned = lax.all_to_all(result, "gx", split_axis=1, concat_axis=0, tiled=True).reshape(
        expert_count * capacity, model_width
    )
    picked = jnp.take(returned, slot_of, axis=0).astype(jnp.float32)
    branch = shared + jnp.sum(gate_values[:, :, None] * picked, axis=1)
    output = (middle + gate_mlp * branch).astype(jnp.bfloat16)
    out_grad = cotangent.astype(jnp.float32)
    grad_gate_mlp = out_grad * branch
    grad_branch = out_grad * gate_mlp
    grad_shared = grad_branch.astype(jnp.bfloat16)
    grad_picked = (gate_values[:, :, None] * grad_branch[:, None, :]).astype(jnp.bfloat16)
    grad_gates = jnp.sum(grad_branch[:, None, :] * picked, axis=2)
    grad_slots = jnp.einsum(
        "tks,tkd->sd", selector, grad_picked, preferred_element_type=jnp.float32
    )
    grad_slots = grad_slots.astype(jnp.bfloat16).reshape(expert_count, capacity, model_width)
    grad_owned = lax.all_to_all(grad_slots, "gx", split_axis=0, concat_axis=1, tiled=True)
    grad_inner = jnp.einsum(
        "ecd,efd->ecf", grad_owned, expert_back, preferred_element_type=jnp.float32
    )
    unused_inner, gelu_expert = jax.vjp(jax.nn.gelu, inner_pre)
    grad_inner_pre = gelu_expert(grad_inner)[0].astype(jnp.bfloat16)
    term_e_out = jnp.einsum(
        "ecf,ecd->efd", inner_act, grad_owned, preferred_element_type=jnp.float32
    )
    term_e_in = jnp.einsum(
        "ecd,ecf->edf", owned_rows, grad_inner_pre, preferred_element_type=jnp.float32
    )
    grad_rows = jnp.einsum(
        "ecf,edf->ecd", grad_inner_pre, expert_in, preferred_element_type=jnp.float32
    )
    grad_returned = (
        lax.all_to_all(
            grad_rows.astype(jnp.bfloat16), "gx", split_axis=1, concat_axis=0, tiled=True
        )
        .astype(grad_rows.dtype)
        .reshape(expert_count * capacity, model_width)
    )
    sum_e_in, sum_e_out = (
        lax.psum_scatter(
            term_e_in.astype(jnp.bfloat16), "gy", scatter_dimension=1, tiled=True
        ).astype(jnp.float32),
        lax.psum_scatter(
            term_e_out.astype(jnp.bfloat16), "gy", scatter_dimension=1, tiled=True
        ).astype(jnp.float32),
    )
    grad_chance = jnp.sum(chosen * grad_gates[:, :, None], axis=1)
    grad_logits = chance * (grad_chance - jnp.sum(grad_chance * chance, axis=-1, keepdims=True))
    grad_logits = grad_logits.astype(jnp.bfloat16)
    grad_hidden = dot_cols(grad_shared, fc2_full)
    unused_shared, gelu_shared = jax.vjp(jax.nn.gelu, hidden_pre)
    grad_hidden_pre = gelu_shared(grad_hidden)[0].astype(jnp.bfloat16)
    term_fc2 = dot_rows(hidden, grad_shared)
    term_fc1 = dot_rows(mixed_in, grad_hidden_pre)
    term_router = dot_rows(mixed_in, grad_logits)
    part_fc1, part_fc2, part_router = (
        lax.psum_scatter(
            term_fc1.astype(jnp.bfloat16), "gx", scatter_dimension=0, tiled=True
        ).astype(jnp.float32),
        lax.psum_scatter(
            term_fc2.astype(jnp.bfloat16), "gx", scatter_dimension=0, tiled=True
        ).astype(jnp.float32),
        lax.psum_scatter(
            term_router.astype(jnp.bfloat16), "gx", scatter_dimension=0, tiled=True
        ).astype(jnp.float32),
    )
    sum_fc1, sum_fc2, sum_router = (
        lax.psum_scatter(
            part_fc1.astype(jnp.bfloat16), "gy", scatter_dimension=0, tiled=True
        ).astype(jnp.float32),
        lax.psum_scatter(
            part_fc2.astype(jnp.bfloat16), "gy", scatter_dimension=0, tiled=True
        ).astype(jnp.float32),
        lax.psum_scatter(
            part_router.astype(jnp.bfloat16), "gy", scatter_dimension=0, tiled=True
        ).astype(jnp.float32),
    )
    grad_mixed = dot_cols(grad_hidden_pre, fc1_full) + dot_cols(grad_logits, router_full)
    grad_mixed = grad_mixed + jnp.sum(jnp.take(grad_returned, slot_of, axis=0), axis=1)
    unused_mix, mix_back = jax.vjp(modulate, middle, shift_mlp, scale_mlp)
    grad_mid_norm, grad_shift_mlp, grad_scale_mlp = mix_back(grad_mixed)
    grad_middle = out_grad + grad_mid_norm
    grad_gate_attn = grad_middle * attn_proj
    grad_proj = (grad_middle * gate_attn).astype(jnp.bfloat16)
    term_out = dot_rows(attn_low, grad_proj)
    grad_attn = (
        dot_cols(grad_proj, out_full).astype(jnp.bfloat16).reshape(tok_count, head_count, head_size)
    )
    grad_probs = jnp.einsum(
        "qhd,khd->hqk", grad_attn, value_rows, preferred_element_type=jnp.float32
    )
    grad_values = jnp.einsum(
        "hqk,qhd->khd", probs_low, grad_attn, preferred_element_type=jnp.float32
    )
    grad_scores = attn_probs * (
        grad_probs - jnp.sum(grad_probs * attn_probs, axis=-1, keepdims=True)
    )
    grad_scores = grad_scores.astype(jnp.bfloat16)
    grad_queries = (
        jnp.einsum("hqk,khd->qhd", grad_scores, key_rows, preferred_element_type=jnp.float32)
        * score_scale
    )
    grad_keys = (
        jnp.einsum("hqk,qhd->khd", grad_scores, queries, preferred_element_type=jnp.float32)
        * score_scale
    )
    grad_qkv = jnp.concatenate(
        [
            grad_queries.reshape(tok_count, model_width),
            grad_keys.reshape(tok_count, model_width),
            grad_values.reshape(tok_count, model_width),
        ],
        axis=1,
    ).astype(jnp.bfloat16)
    term_qkv = dot_rows(attn_in, grad_qkv)
    grad_attn_in = dot_cols(grad_qkv, qkv_full)
    unused_pre, pre_back = jax.vjp(modulate, residual, shift_attn, scale_attn)
    grad_input_norm, grad_shift_attn, grad_scale_attn = pre_back(grad_attn_in)
    d_tokens = grad_middle + grad_input_norm
    grad_token_mod = jnp.concatenate(
        [
            grad_shift_attn,
            grad_scale_attn,
            grad_gate_attn,
            grad_shift_mlp,
            grad_scale_mlp,
            grad_gate_mlp,
        ],
        axis=1,
    )
    grad_modulation = jnp.einsum("ti,tc->ic", member, grad_token_mod, precision=precise).astype(
        jnp.bfloat16
    )
    all_condition, all_modgrad = (
        lax.all_gather(condition, ("gx", "gy"), axis=0, tiled=True),
        lax.all_gather(grad_modulation, ("gx", "gy"), axis=0, tiled=True),
    )
    own_share = model_width // lax.axis_size(("gx", "gy"))
    own_start = lax.axis_index(("gx", "gy")) * own_share
    own_condition = lax.dynamic_slice_in_dim(all_condition, own_start, own_share, 1)
    owned_ada = dot_rows(own_condition, all_modgrad)
    attn_terms = (term_qkv, term_out)
    attn_parts = (
        lax.psum_scatter(
            attn_terms[0].astype(jnp.bfloat16), "gx", scatter_dimension=0, tiled=True
        ).astype(jnp.float32),
        lax.psum_scatter(
            attn_terms[1].astype(jnp.bfloat16), "gx", scatter_dimension=0, tiled=True
        ).astype(jnp.float32),
    )
    attn_sums = (
        lax.psum_scatter(
            attn_parts[0].astype(jnp.bfloat16), "gy", scatter_dimension=0, tiled=True
        ).astype(jnp.float32),
        lax.psum_scatter(
            attn_parts[1].astype(jnp.bfloat16), "gy", scatter_dimension=0, tiled=True
        ).astype(jnp.float32),
    )
    sum_qkv, sum_out = attn_sums
    return (
        output,
        d_tokens,
        owned_ada,
        sum_qkv,
        sum_out,
        sum_fc1,
        sum_fc2,
        sum_router,
        sum_e_in,
        sum_e_out,
    )


def solution(mesh):
    in_specs = (
        P(("gx", "gy"), None),
        P(("gx", "gy")),
        P(("gx", "gy"), None),
        P(("gx", "gy"), None),
        P(("gx", "gy"), None),
        P(("gx", "gy"), None),
        P(("gx", "gy"), None),
        P(("gx", "gy"), None),
        P(("gx", "gy"), None),
        P(("gx", "gy"), None),
        P(("gx", "gy"), None),
        P("gx", "gy", None),
        P("gx", "gy", None),
    )
    out_specs = (
        P(("gx", "gy"), None),
        P(("gx", "gy"), None),
        P(("gx", "gy"), None),
        P(("gx", "gy"), None),
        P(("gx", "gy"), None),
        P(("gx", "gy"), None),
        P(("gx", "gy"), None),
        P(("gx", "gy"), None),
        P("gx", "gy", None),
        P("gx", "gy", None),
    )
    step = by_slices if dict(mesh.shape) == {"gx": 2, "gy": 16} else by_weights
    return jax.shard_map(
        step, mesh=mesh, in_specs=in_specs, out_specs=out_specs, check_vma=False
    )
```

```python
import functools
import math

import jax
import jax.numpy as jnp
from jax import lax
from jax.experimental import pallas as pl
from jax.experimental.pallas import tpu as pltpu
from jax.sharding import PartitionSpec as P

HEADS = 12
CAP = 64
MESH = pl.DeviceIdType.MESH
ANY = pl.ANY
VMEM = pltpu.VMEM
DMA = pltpu.SemaphoreType.DMA
LINE = (1, 3, 2)

precise = lax.Precision.HIGHEST
layer_epsilon = 1e-06


def place():
    gy = lax.axis_index("gy")
    return lax.axis_index("gx"), gy // 4, (gy // 2) % 2, gy % 2


def device(y, z, x, c):
    return (y, 4 * z + 2 * x + c)


def chip(y, z, x):
    return 8 * y + 2 * z + x


def meet(partners):
    barrier = pltpu.get_barrier_semaphore()
    for partner in partners:
        pl.semaphore_signal(barrier, inc=1, device_id=partner, device_id_type=MESH)
    pl.semaphore_wait(barrier, len(partners))


def cross_partners(here):
    y, z, x, c = here
    return [device(y, (z + step) % 4, x, c) for step in LINE] + [
        device(1 - y, z, x, c),
        device(y, z, 1 - x, c),
    ]


def remote(source, target, send, recv, to):
    return pltpu.make_async_remote_copy(
        src_ref=source, dst_ref=target, send_sem=send, recv_sem=recv, device_id=to, device_id_type=MESH
    )


class Gather:
    def __init__(self, here, y_first, own, slot, send, recv, pair=None):
        self.here, self.y_first, self.own, self.slot = here, y_first, own, slot
        self.send, self.recv, self.pair, self.started = send, recv, pair, []

    def copy(self, source, number, recv, to):
        sent = remote(source, self.slot(number), self.send.at[len(self.started)], recv.at[number], to)
        sent.start()
        self.started.append(sent)

    def forward(self, source, number, to_y, to_x, to_pair=True):
        y, z, x, c = self.here
        if to_y:
            self.copy(source, number, self.recv, device(1 - y, z, x, c))
        if to_x:
            self.copy(source, number, self.recv, device(y, z, 1 - x, c))
        if to_pair and self.pair is not None:
            self.copy(source, number, self.pair, device(y, z, x, 1 - c))

    def arrive(self, number, recv=None):
        recv = self.recv if recv is None else recv
        block = self.slot(number)
        remote(block, block, self.send.at[0], recv.at[number], device(*self.here)).wait_recv()
        return block

    def start_line(self, step):
        y, z, x, c = self.here
        self.copy(self.own, chip(y, z, x), self.recv, device(y, (z + step) % 4, x, c))

    def start_first(self):
        y, z, x, c = self.here
        self.forward(self.own, chip(y, z, x), self.y_first, not self.y_first)

    def start_last(self):
        y, z, x, c = self.here
        self.forward(self.own, chip(y, z, x), not self.y_first, self.y_first, False)

    def line_first(self, step):
        y, z, x, c = self.here
        number = chip(y, (z + step) % 4, x)
        self.forward(self.arrive(number), number, self.y_first, not self.y_first)

    def line_last(self, step):
        y, z, x, c = self.here
        number = chip(y, (z + step) % 4, x)
        self.forward(self.slot(number), number, not self.y_first, self.y_first, False)

    def second(self, step):
        y, z, x, c = self.here
        if self.y_first:
            number = chip(1 - y, (z + step) % 4, x)
        else:
            number = chip(y, (z + step) % 4, 1 - x)
        self.forward(self.arrive(number), number, not self.y_first, self.y_first)

    def third(self, step):
        y, z, x, c = self.here
        for other in (0, 1):
            if self.y_first:
                number = chip(y if other == 0 else 1 - y, (z + step) % 4, 1 - x)
            else:
                number = chip(1 - y, (z + step) % 4, x if other == 0 else 1 - x)
            self.forward(self.arrive(number), number, False, False)

    def finish(self):
        for sent in self.started:
            sent.wait_send()
        if self.pair is not None:
            for number in range(16):
                self.arrive(number, self.pair)


def gather_start(gathers):
    for gather in gathers:
        gather.start_first()
    for gather in gathers:
        gather.start_line(1)
        gather.start_line(3)
    for gather in gathers:
        gather.start_last()
    for gather in gathers:
        gather.start_line(2)


def gather_line(gathers, step):
    for gather in gathers:
        gather.line_first(step)
    for gather in gathers:
        gather.line_last(step)


def gather_second(gathers, step):
    for gather in gathers:
        gather.second(step)


def gather_third(gathers, step):
    for gather in gathers:
        gather.third(step)


def gather_all(gathers, between=None):
    gather_start(gathers)
    gather_second(gathers, 0)
    for step in LINE:
        gather_line(gathers, step)
        gather_second(gathers, step)
    if between is not None:
        between()
    for step in (0,) + LINE:
        gather_third(gathers, step)
    for gather in gathers:
        gather.finish()


class Scatter:
    def __init__(self, here, y_first, part, got, send, recv):
        self.here, self.y_first, self.part, self.got = here, y_first, part, got
        self.send, self.recv, self.started = send, recv, []

    def number(self, a, b, step):
        y, z, x, c = self.here
        flip_y, flip_x = (a, b) if self.y_first else (b, a)
        return chip(1 - y if flip_y else y, (z + step) % 4, 1 - x if flip_x else x)

    def toward(self, second):
        y, z, x, c = self.here
        return device(1 - y, z, x, c) if self.y_first != second else device(y, z, 1 - x, c)

    def copy(self, source, index, to):
        sent = remote(source, self.got(index), self.send.at[len(self.started)], self.recv.at[index], to)
        sent.start()
        self.started.append(sent)

    def arrive(self, index):
        block = self.got(index)
        remote(block, block, self.send.at[0], self.recv.at[index], device(*self.here)).wait_recv()
        return block

    def first(self, step):
        for b in (1, 0):
            self.copy(self.part(self.number(1, b, step)), 4 * b + step, self.toward(False))

    def add(self, number, index):
        block, mine = self.arrive(index), self.part(number)
        total = mine[...].astype(jnp.float32) + block[...].astype(jnp.float32)
        mine[...] = total.astype(mine.dtype)

    def one(self, b, step):
        number = self.number(0, b, step)
        self.add(number, 4 * b + step)
        if b == 1:
            self.copy(self.part(number), 8 + step, self.toward(True))

    def two(self, step):
        y, z, x, c = self.here
        number = self.number(0, 0, step)
        self.add(number, 8 + step)
        if step:
            self.copy(self.part(number), 11 + step, device(y, (z + step) % 4, x, c))

    def total(self):
        result = self.part(self.number(0, 0, 0))[...].astype(jnp.float32)
        for step in (1, 2, 3):
            result = result + self.arrive(11 + step)[...].astype(jnp.float32)
        return result

    def finish(self):
        for sent in self.started:
            sent.wait_send()


def scatter_all(scatters, between):
    order = (2, 1, 3, 0)
    for scatter in scatters:
        scatter.first(order[0])
    for scatter in scatters:
        scatter.first(order[1])
    for turn, step in enumerate(order):
        for scatter in scatters:
            scatter.one(1, step)
        for scatter in scatters:
            scatter.one(0, step)
        if turn + 2 < 4:
            for scatter in scatters:
                scatter.first(order[turn + 2])
        for scatter in scatters:
            scatter.two(step)
        between(turn)


def weights_kernel(
    fold, e1, e2, f1, f2, ada, qkv, out, w1, w1s, w2, w2s, stage, block_a, block_q, block_o,
    pre_send, pre_recv, g_send, g_recv, g_pair, a_send, a_recv, a_pair_send, a_pair, b_send, b_recv, b_pair, l_sem, d_send, d_recv,
):
    here = y, z, x, c = place()
    me, k, gy = chip(y, z, x), 2 * z + x, 4 * z + 2 * x + c
    rows = fold.shape[1]
    others = [(dy, dz, dx) for dy in (0, 1) for dz in (0, 1, 2, 3) for dx in (0, 1) if (dy, dz, dx) != (0, 0, 0)]
    spot = lambda dy, dz, dx: (1 - y if dy else y, (z + dz) % 4, 1 - x if dx else x)
    sibling = device(y, z, x, 1 - c)
    meet([device(*spot(*o), c) for o in others] + [sibling])

    pre = remote(fold.at[1 - c], stage.at[pl.ds(pl.multiple_of(rows * c, 8), rows)], pre_send, pre_recv, sibling)
    pre.start()
    stage[pl.ds(pl.multiple_of(rows * c, 8), rows), :] = fold[c]

    depth = e1.shape[1]
    width = w1.shape[2]
    cols = lambda n: pl.ds(pl.multiple_of(width * n, 128), width)
    strip = lambda n: pl.ds(pl.multiple_of(depth * n, 16), depth)
    started = []
    plane = [o for o in others if o[0] == 0]
    local = [
        pltpu.make_async_copy(e1.at[:, :, cols(k)], w1.at[:, strip(gy), :], l_sem.at[0]),
        pltpu.make_async_copy(e2, w2.at[:, pl.ds(pl.multiple_of(e2.shape[1] * c, 16), e2.shape[1]), :], l_sem.at[1]),
        pltpu.make_async_copy(f2, w2s.at[pl.ds(pl.multiple_of(f2.shape[0] * c, 16), f2.shape[0]), :], l_sem.at[2]),
        pltpu.make_async_copy(f1.at[me], w1s.at[c, me], l_sem.at[3]),
    ]
    for copy in local:
        copy.start()
    for i, o in enumerate(plane):
        ty, tz, tx = spot(*o)
        copy = remote(
            e1.at[:, :, cols(2 * tz + tx)], w1.at[:, strip(gy), :], a_send.at[i], a_recv.at[k], device(ty, tz, tx, c)
        )
        copy.start()
        started.append(copy)
    for i, o in enumerate(others):
        ty, tz, tx = spot(*o)
        copy = remote(f1.at[chip(ty, tz, tx)], w1s.at[c, me], b_send.at[i], b_recv.at[me], device(ty, tz, tx, c))
        copy.start()
        started.append(copy)
    twin = [
        remote(e2, w2.at[:, pl.ds(pl.multiple_of(e2.shape[1] * c, 16), e2.shape[1]), :], d_send.at[0], d_recv.at[0], sibling),
        remote(f2, w2s.at[pl.ds(pl.multiple_of(f2.shape[0] * c, 16), f2.shape[0]), :], d_send.at[1], d_recv.at[1], sibling),
    ]
    for copy in twin:
        copy.start()

    pre.wait()
    at = 0
    for block in (block_a, block_q, block_o):
        block[...] = stage[:, at : at + block.shape[1]].astype(jnp.bfloat16)
        at += block.shape[1]
    gathers, own = [], []
    for i, (block, full, y_first) in enumerate(((block_a, ada, True), (block_q, qkv, False), (block_o, out, False))):
        slot = functools.partial(lambda full, n: full.at[c, pl.ds(pl.multiple_of(2 * rows * n, 16), 2 * rows), :], full)
        gathers.append(Gather(here, y_first, block, slot, g_send.at[i], g_recv.at[i], g_pair.at[i]))
        copy = pltpu.make_async_copy(block, slot(me), l_sem.at[4 + i])
        copy.start()
        own.append(copy)

    def pass_on():
        for copy in local:
            copy.wait()
        for i, (dz, dx) in enumerate([(0, 0)] + [(o[1], o[2]) for o in plane]):
            sy, sz, sx = spot(0, dz, dx)
            source = 2 * sz + sx
            block = w1.at[:, strip(2 * source + c), :]
            if i:
                remote(block, block, a_send.at[0], a_recv.at[source], sibling).wait_recv()
            copy = remote(block, block, a_pair_send.at[i], a_pair.at[source], sibling)
            copy.start()
            started.append(copy)
        for o in others:
            number = chip(*spot(*o))
            remote(w1s.at[c, number], w1s.at[c, number], b_send.at[0], b_recv.at[number], sibling).wait_recv()
        copy = remote(w1s.at[c], w1s.at[c], b_pair.at[0], b_pair.at[1], sibling)
        copy.start()
        started.append(copy)

    gather_all(gathers, pass_on)
    for copy in own:
        copy.wait()
    for copy in started:
        copy.wait_send()
    for source in range(8):
        block = w1.at[:, strip(2 * source + 1 - c), :]
        remote(block, block, a_send.at[0], a_pair.at[source], sibling).wait_recv()
    remote(w1s.at[1 - c], w1s.at[1 - c], b_pair.at[0], b_pair.at[1], sibling).wait_recv()
    for copy in twin:
        copy.wait_send()
    other = pl.ds(pl.multiple_of(e2.shape[1] * (1 - c), 16), e2.shape[1])
    remote(w2.at[:, other, :], w2.at[:, other, :], d_send.at[0], d_recv.at[0], sibling).wait_recv()
    other = pl.ds(pl.multiple_of(f2.shape[0] * (1 - c), 16), f2.shape[0])
    remote(w2s.at[other, :], w2s.at[other, :], d_send.at[1], d_recv.at[1], sibling).wait_recv()


def gather_weights(w_ada, w_qkv, w_out, w_router, w_fc1, w_fc2, e_fc1, e_fc2):
    rows, model = w_out.shape
    half = lambda w, c: w[:, c * (w.shape[1] // 2) : (c + 1) * (w.shape[1] // 2)]
    router = jnp.pad(w_router, ((0, 0), (0, -w_router.shape[1] % 128)))
    fold = jnp.stack([jnp.concatenate([half(w, c) for w in (w_ada, w_qkv, w_out)] + [router], axis=1) for c in (0, 1)])
    fold = fold.astype(jnp.float32)
    ff = w_fc1.shape[1]
    slim = ff // 16
    f1 = w_fc1.reshape(rows, 16, slim).transpose(1, 0, 2).reshape(16, rows // 2, 2 * slim)
    f1 = jnp.pad(f1, ((0, 0), (0, 16 - rows // 2), (0, 0)))
    experts, depth, _ = e_fc1.shape
    wide = ff // 8
    bf = jnp.bfloat16
    shape = jax.ShapeDtypeStruct
    out_shape = (
        shape((2, model, w_ada.shape[1] // 2), bf),
        shape((2, model, w_qkv.shape[1] // 2), bf),
        shape((2, model, w_out.shape[1] // 2 + router.shape[1]), bf),
        shape((experts, model, wide), bf),
        shape((2, 16, 16, 2 * slim), bf),
        shape((experts, 2 * e_fc2.shape[1], model), bf),
        shape((2 * w_fc2.shape[0], model), bf),
    )
    ada, qkv, out, w1, w1s, w2, w2s = pl.pallas_call(
        weights_kernel,
        out_shape=out_shape,
        in_specs=[pl.BlockSpec(memory_space=VMEM)] + [pl.BlockSpec(memory_space=ANY)] * 4,
        out_specs=[pl.BlockSpec(memory_space=ANY)] * 7,
        scratch_shapes=[
            VMEM((2 * rows, fold.shape[2]), jnp.float32),
            VMEM((2 * rows, w_ada.shape[1] // 2), bf),
            VMEM((2 * rows, w_qkv.shape[1] // 2), bf),
            VMEM((2 * rows, w_out.shape[1] // 2 + router.shape[1]), bf),
            DMA, DMA, DMA((3, 31)), DMA((3, 16)), DMA((3, 16)),
            DMA((7,)), DMA((8,)), DMA((8,)), DMA((8,)), DMA((15,)), DMA((16,)), DMA((2,)), DMA((7,)), DMA((2,)), DMA((2,)),
        ],
        compiler_params=pltpu.CompilerParams(collective_id=1, has_side_effects=True, vmem_limit_bytes=32 << 20),
        name="weights",
    )(fold, e_fc1, e_fc2, f1, w_fc2)
    w1s = w1s[:, :, : rows // 2].reshape(2, 16, rows, slim).transpose(1, 0, 2, 3).reshape(model, slim)
    return ada, qkv, out, w1, w1s, w2, w2s


def nt(a, b):
    return lax.dot_general(a, b, (((1,), (1,)), ((), ())), preferred_element_type=jnp.float32)


def tn(a, b):
    return lax.dot_general(a, b, (((0,), (0,)), ((), ())), preferred_element_type=jnp.float32)


def nn(a, b):
    return jnp.dot(a, b, preferred_element_type=jnp.float32)


def gelu_both(h):
    root = math.sqrt(2.0 / math.pi)
    square = h * h
    t = jnp.tanh(h * (root + (root * 0.044715) * square))
    half = 0.5 * (1.0 + t)
    slope = half + (0.5 * h) * (1.0 - t * t) * (root + (3.0 * root * 0.044715) * square)
    return h * half, slope


def ffn_chunk(xt, gt, w1, w2, gate, row):
    a, d = gelu_both(nn(xt, w1))
    gi = nt(gt, w2)
    product = None
    if gate is not None:
        product = nt(row, (a * gi).astype(jnp.bfloat16))
        a, d = a * gate, d * gate
    a = a.astype(jnp.bfloat16)
    p = (gi * d).astype(jnp.bfloat16)
    return a, p, nn(a, w2), nt(p, w1), product


def ffn_shared(slots, X, G, w1s, w2s, act_s, pre_s, sums, sums_back):
    toks = X.shape[1]
    xt = jnp.concatenate([X[n] for n in slots], axis=0)
    gt = jnp.concatenate([G[n] for n in slots], axis=0)
    a, p, total, total_back, _ = ffn_chunk(xt, gt, w1s[...], w2s[...], None, None)
    for i, n in enumerate(slots):
        act_s[n] = a[i * toks : (i + 1) * toks]
        pre_s[n] = p[i * toks : (i + 1) * toks]
    sums[...] = total
    sums_back[...] = total_back


def ffn_experts(low, high, slots, X, G, gates, w1, w2, act, pre, sums, sums_back, gc):
    experts, toks, wide = w1.shape[0], X.shape[1], w1.shape[2]
    first = lax.axis_index("gx") * experts
    xt = jnp.concatenate([X[n] for n in slots], axis=0)
    gt = jnp.concatenate([G[n] for n in slots], axis=0)

    def expert(e, product):
        kind = lax.broadcasted_iota(jnp.int32, (16, 128), 0)
        spread = ((kind == first + e) | (kind == first + e + 8)).astype(jnp.bfloat16)
        gate = jnp.concatenate([tn(gates[n], spread) for n in slots], axis=0)
        gate = jnp.concatenate([gate] * (wide // 128), axis=1)
        row = (lax.broadcasted_iota(jnp.int32, (8, wide), 0) == first + e).astype(jnp.bfloat16)
        a, p, total, total_back, more = ffn_chunk(xt, gt, w1[e], w2[e], gate, row)
        for i, n in enumerate(slots):
            act[e, n] = a[i * toks : (i + 1) * toks]
            pre[e, n] = p[i * toks : (i + 1) * toks]
        sums[...] += total
        sums_back[...] += total_back
        return product + more

    product = lax.fori_loop(low, high, expert, jnp.zeros((8, len(slots) * toks), jnp.float32))
    for i, n in enumerate(slots):
        part = product[:, i * toks : (i + 1) * toks]
        gc[n] = part if low == 0 else gc[n] + part


def block_kernel(
    mixed, grad, gates, w1_in, w1s_in, w2_in, w2s_in,
    sum_branch, sum_back, sum_gc, own1, own1s, own2, own2s,
    X, G, gt, w1, w1s, w2, w2s, act, pre, act_s, pre_s, tile_sum, tile_back,
    p_branch, p_back, p_gc, r_branch, r_back, r_gc, d1, d1s, d2, d2s, from1, from1s, from2, from2s,
    l_sem, g_send, g_recv, send, recv, t_send, t_recv,
):
    here = y, z, x, c = place()
    me = chip(y, z, x)
    spot = lambda dy, dz, dx: (1 - y if dy else y, (z + dz) % 4, 1 - x if dx else x)
    sibling = device(y, z, x, 1 - c)
    experts = w1.shape[0]
    meet(cross_partners(here) + [sibling])

    gathers, local = [], []
    for i, (block, full, y_first) in enumerate(((mixed, X, True), (grad, G, False), (gates, gt, True))):
        slot = functools.partial(lambda full, n: full.at[n], full)
        gathers.append(Gather(here, y_first, block, slot, g_send.at[i], g_recv.at[i]))
        local.append(pltpu.make_async_copy(block, slot(me), l_sem.at[i]))
    gather_start(gathers)
    for i, (source, target) in enumerate(((w1_in, w1), (w1s_in, w1s), (w2_in, w2), (w2s_in, w2s))):
        local.append(pltpu.make_async_copy(source, target, l_sem.at[3 + i]))
    for copy in local:
        copy.start()

    def tile(step, part):
        slots = [chip(*spot(dy, step, dx)) for dy in (0, 1) for dx in (0, 1)]
        if part == 0:
            ffn_shared(slots, X, G, w1s, w2s, act_s, pre_s, tile_sum, tile_back)
        low, high = (0, experts // 2) if part == 0 else (experts // 2, experts)
        ffn_experts(low, high, slots, X, G, gt, w1, w2, act, pre, tile_sum, tile_back, p_gc)
        if part == 1:
            toks = X.shape[1]
            for i, n in enumerate(slots):
                at = slice(i * toks, (i + 1) * toks)
                p_branch[n] = tile_sum[at, :].astype(jnp.bfloat16)
                p_back[n] = tile_back[at, :].astype(jnp.bfloat16)

    scatters = []
    for i, (part, got, y_first) in enumerate(((p_branch, r_branch, False), (p_back, r_back, True), (p_gc, r_gc, False))):
        take = functools.partial(lambda ref, n: ref.at[n], part)
        land = functools.partial(lambda ref, n: ref.at[n], got)
        scatters.append(Scatter(here, y_first, take, land, send.at[i], recv.at[i]))

    def back_first(step):
        for scatter in scatters:
            scatter.first(step)

    gather_second(gathers, 0)
    gather_line(gathers, 1)
    gather_second(gathers, 1)
    gather_third(gathers, 0)
    for copy in local:
        copy.wait()
    tile(0, 0)
    gather_line(gathers, 3)
    tile(0, 1)
    gather_third(gathers, 1)
    tile(1, 0)
    gather_second(gathers, 3)
    tile(1, 1)
    gather_line(gathers, 2)
    gather_third(gathers, 3)
    tile(3, 0)
    gather_second(gathers, 2)
    back_first(1)
    tile(3, 1)
    back_first(3)
    gather_third(gathers, 2)
    tile(2, 0)
    tile(2, 1)

    def back_one(step):
        for scatter in scatters:
            scatter.one(1, step)
        for scatter in scatters:
            scatter.one(0, step)

    def back_two(step):
        for scatter in scatters:
            scatter.two(step)

    flat = lambda value: value.reshape(value.shape[0] * value.shape[1], value.shape[2])
    twins = [None] * (2 * experts)

    def weight(e):
        d1[e] = tn(flat(X[...]), flat(pre[e])).astype(jnp.bfloat16).reshape(d1.shape[1:])
        d2[e] = tn(flat(act[e]), flat(G[...])).astype(jnp.bfloat16).reshape(d2.shape[1:])
        for i, (part, got) in enumerate(((d1.at[e, :, 1 - c], from1.at[e]), (d2.at[e, 1 - c], from2.at[e]))):
            twins[2 * e + i] = remote(part, got, t_send.at[2 * e + i], t_recv.at[2 * e + i], sibling)
            twins[2 * e + i].start()

    def home(e):
        twins[2 * e].wait()
        own1[e] = (d1[e, :, c].astype(jnp.float32) + from1[e].astype(jnp.float32)).astype(jnp.bfloat16)
        twins[2 * e + 1].wait()
        own2[e] = d2[e, c].astype(jnp.float32) + from2[e].astype(jnp.float32)

    back_one(1)
    back_first(2)
    back_two(1)
    weight(0)
    back_one(3)
    back_two(3)
    home(0)
    weight(1)
    back_one(2)
    back_first(0)
    back_two(2)
    home(1)
    weight(2)
    home(2)
    weight(3)
    d1s[...] = tn(flat(X[...]), flat(pre_s[...])).reshape(d1s.shape)
    d2s[...] = tn(flat(act_s[...]), flat(G[...])).astype(jnp.bfloat16).reshape(d2s.shape)
    twin1s = remote(d1s.at[:, 1 - c], from1s, t_send.at[2 * experts], t_recv.at[2 * experts], sibling)
    twin2s = remote(d2s.at[1 - c], from2s, t_send.at[2 * experts + 1], t_recv.at[2 * experts + 1], sibling)
    twin1s.start()
    twin2s.start()
    home(3)
    back_one(0)
    twin1s.wait()
    own1s[...] = d1s[:, c] + from1s[...]
    twin2s.wait()
    own2s[...] = d2s[c].astype(jnp.float32) + from2s[...].astype(jnp.float32)
    back_two(0)
    sum_branch[...] = scatters[0].total()
    sum_back[...] = scatters[1].total()
    sum_gc[...] = scatters[2].total()
    for gather in gathers:
        gather.finish()
    for scatter in scatters:
        scatter.finish()


def block(mixed, grad, gates, w1, w1s, w2, w2s):
    bf, f32 = jnp.bfloat16, jnp.float32
    toks, model = mixed.shape
    experts, _, wide = w1.shape
    slim = w1s.shape[1]
    rows = model // 32
    shape = jax.ShapeDtypeStruct
    blocks = lambda *dims: VMEM((16, toks) + dims, bf)
    return pl.pallas_call(
        block_kernel,
        out_shape=[
            shape((toks, model), f32),
            shape((toks, model), f32),
            shape((8, 128), f32),
            shape((experts, 8, 2 * rows, wide), bf),
            shape((16, rows, slim), f32),
            shape((experts, wide // 2, model), f32),
            shape((slim // 2, model), f32),
        ],
        in_specs=[pl.BlockSpec(memory_space=VMEM)] * 3 + [pl.BlockSpec(memory_space=ANY)] * 4,
        out_specs=[pl.BlockSpec(memory_space=VMEM)] * 7,
        scratch_shapes=[
            blocks(model), blocks(model), VMEM((16, 16, 128), bf),
            VMEM(w1.shape, bf), VMEM(w1s.shape, bf), VMEM(w2.shape, bf), VMEM(w2s.shape, bf),
            VMEM((experts, 16, toks, wide), bf), VMEM((experts, 16, toks, wide), bf), blocks(slim), blocks(slim),
            VMEM((4 * toks, model), f32), VMEM((4 * toks, model), f32),
            blocks(model), blocks(model), VMEM((16, 8, 128), f32),
            VMEM((15, toks, model), bf), VMEM((15, toks, model), bf), VMEM((15, 8, 128), f32),
            VMEM((experts, 8, 2, 2 * rows, wide), bf), VMEM((16, 2, rows, slim), f32),
            VMEM((experts, 2, wide // 2, model), bf), VMEM((2, slim // 2, model), bf),
            VMEM((experts, 8, 2 * rows, wide), bf), VMEM((16, rows, slim), f32),
            VMEM((experts, wide // 2, model), bf), VMEM((slim // 2, model), bf),
            DMA((7,)), DMA((3, 15)), DMA((3, 16)), DMA((3, 15)), DMA((3, 15)), DMA((2 * experts + 2,)), DMA((2 * experts + 2,)),
        ],
        compiler_params=pltpu.CompilerParams(collective_id=2, has_side_effects=True, vmem_limit_bytes=62 << 20),
        name="block",
    )(mixed, grad, gates, w1, w1s, w2, w2s)


def owners_kernel(
    qkv, out, mod, part1, part1s, total, all_mod, own1, own1s, got_q, got_o, part_a, part_b, got_a, got_b, fin, block_sem_s, block_sem_r, send, recv, g_send, g_recv, g_pair, f_send, f_recv, l_sem, a_send, a_recv, b_send, b_recv,
):
    here = y, z, x, c = place()
    me = chip(y, z, x)
    sibling = device(y, z, x, 1 - c)
    others = [(dy, dz, dx) for dy in (0, 1) for dz in (0, 1, 2, 3) for dx in (0, 1) if (dy, dz, dx) != (0, 0, 0)]
    plane = [o for o in others if o[0] == 0]
    spot = lambda dy, dz, dx: (1 - y if dy else y, (z + dz) % 4, 1 - x if dx else x)
    meet([device(*spot(*o), c) for o in others] + [sibling])
    swaps = [
        remote(qkv.at[1 - c], got_q, block_sem_s.at[0], block_sem_r.at[0], sibling),
        remote(out.at[1 - c], got_o, block_sem_s.at[1], block_sem_r.at[1], sibling),
    ]
    for copy in swaps:
        copy.start()
    slot = lambda n: all_mod.at[n, c]
    spread = Gather(here, True, mod, slot, g_send, g_recv, g_pair)
    keep = pltpu.make_async_copy(mod, slot(me), l_sem.at[0])
    keep.start()
    gather_start([spread])
    for copy in swaps:
        copy.wait()
    rows = got_q.shape[0] // 16
    cut = part_a.shape[2]
    for n in range(16):
        at = slice(n * rows, (n + 1) * rows)
        q = (qkv[c, at, :].astype(jnp.float32) + got_q[at, :].astype(jnp.float32)).astype(jnp.bfloat16)
        o = (out[c, at, :].astype(jnp.float32) + got_o[at, :].astype(jnp.float32)).astype(jnp.bfloat16)
        part_a[n] = q[:, :cut]
        part_b[n] = jnp.concatenate([q[:, cut:], o], axis=1)
    scatters = []
    for i, (part, got, y_first) in enumerate(((part_a, got_a, False), (part_b, got_b, True))):
        take = functools.partial(lambda ref, n: ref.at[n], part)
        land = functools.partial(lambda ref, n: ref.at[n], got)
        scatters.append(Scatter(here, y_first, take, land, send.at[i], recv.at[i]))

    def turn(at):
        if at == 0:
            spread.second(0)
            for step in LINE:
                gather_line([spread], step)
        elif at == 1:
            for step in LINE:
                spread.second(step)
        elif at == 2:
            for step in (0,) + LINE:
                spread.third(step)

    k, wide = 2 * z + x, part1.shape[3]
    columns = lambda n: own1.at[:, :, pl.ds(pl.multiple_of(wide * n, 128), wide)]
    home = [pltpu.make_async_copy(part1.at[:, k], columns(k), l_sem.at[1]), pltpu.make_async_copy(part1s.at[me], own1s.at[me], l_sem.at[2])]
    for copy in home:
        copy.start()
    started = []
    for i, o in enumerate(plane):
        ty, tz, tx = spot(*o)
        started.append(remote(part1.at[:, 2 * tz + tx], columns(k), a_send.at[i], a_recv.at[k], device(ty, tz, tx, c)))
    for i, o in enumerate(others):
        started.append(remote(part1s.at[chip(*spot(*o))], own1s.at[me], b_send.at[i], b_recv.at[me], device(*spot(*o), c)))
    for copy in started:
        copy.start()
    scatter_all(scatters, turn)
    for i, o in enumerate(plane):
        n = 2 * spot(*o)[1] + spot(*o)[2]
        block = columns(n)
        remote(block, block, a_send.at[i], a_recv.at[n], sibling).wait_recv()
    for i, o in enumerate(others):
        n = chip(*spot(*o))
        remote(own1s.at[n], own1s.at[n], b_send.at[i], b_recv.at[n], sibling).wait_recv()
    fin[c] = jnp.concatenate([scatters[0].total(), scatters[1].total()], axis=1)
    half = rows // 2
    mine = pl.ds(pl.multiple_of(half * c, 8), half)
    theirs = pl.ds(pl.multiple_of(half * (1 - c), 8), half)
    swap = remote(fin.at[c, theirs, :], fin.at[c, theirs, :], f_send, f_recv, sibling)
    swap.start()
    for scatter in scatters:
        scatter.finish()
    spread.finish()
    keep.wait()
    for copy in home:
        copy.wait()
    for copy in started:
        copy.wait_send()
    swap.wait_send()
    remote(fin.at[1 - c, mine, :], fin.at[1 - c, mine, :], f_send, f_recv, sibling).wait_recv()
    total[0] = fin[0, mine, :]
    total[1] = fin[1, mine, :]


def to_owners(qkv, out, mod, part1, part1s):
    bf, f32 = jnp.bfloat16, jnp.float32
    model = qkv.shape[1]
    rows = model // 16
    wide = qkv.shape[2] + out.shape[2]
    cut = wide // 256 * 128
    shape = jax.ShapeDtypeStruct
    return pl.pallas_call(
        owners_kernel,
        out_shape=[
            shape((2, rows // 2, wide), f32),
            shape((16, 2) + mod.shape, bf),
            shape((part1.shape[0], part1.shape[2], 8 * part1.shape[3]), bf),
            shape(part1s.shape, f32),
        ],
        in_specs=[pl.BlockSpec(memory_space=VMEM)] * 3 + [pl.BlockSpec(memory_space=ANY)] * 2,
        out_specs=[pl.BlockSpec(memory_space=VMEM)] + [pl.BlockSpec(memory_space=ANY)] * 3,
        scratch_shapes=[
            VMEM(qkv.shape[1:], bf), VMEM(out.shape[1:], bf), VMEM((16, rows, cut), bf), VMEM((16, rows, wide - cut), bf),
            VMEM((15, rows, cut), bf), VMEM((15, rows, wide - cut), bf),
            VMEM((2, rows, wide), f32),
            DMA((2,)), DMA((2,)), DMA((2, 15)), DMA((2, 15)), DMA((31,)), DMA((16,)), DMA((16,)), DMA, DMA, DMA((3,)),
            DMA((7,)), DMA((8,)), DMA((15,)), DMA((16,)),
        ],
        compiler_params=pltpu.CompilerParams(collective_id=4, has_side_effects=True, vmem_limit_bytes=40 << 20),
        name="owners",
    )(qkv, out, mod, part1, part1s)


def layer_norm(values):
    average = jnp.mean(values, axis=-1, keepdims=True)
    centred = values - average
    return centred * lax.rsqrt(jnp.mean(centred * centred, axis=-1, keepdims=True) + layer_epsilon)


def modulate(values, shift_by, scale_by):
    return layer_norm(values) * (1.0 + scale_by) + shift_by


def sinusoid(timesteps, model_width):
    half_width = model_width // 2
    frequency = jnp.exp(-math.log(10000.0) * jnp.arange(half_width, dtype=jnp.float32) / half_width)
    angles = timesteps.astype(jnp.float32)[:, None] * frequency[None, :]
    return jnp.concatenate([jnp.cos(angles), jnp.sin(angles)], axis=1)


def membership(lengths, tok_count):
    bounds = jnp.cumsum(lengths)[:-1]
    position = jnp.arange(tok_count, dtype=jnp.int32)
    item_of = jnp.sum((position[:, None] >= bounds[None, :]).astype(jnp.int32), axis=1)
    item_ids = jnp.arange(lengths.shape[0], dtype=jnp.int32)
    return ((item_of[:, None] == item_ids[None, :]).astype(jnp.float32), item_of)


def slot_index(routes, expert_count, capacity):
    flat_routes = routes.reshape(-1)
    expert_hot = (
        flat_routes[:, None] == jnp.arange(expert_count, dtype=jnp.int32)[None, :]
    ).astype(jnp.int32)
    before = jnp.cumsum(expert_hot, axis=0) - expert_hot
    rank_in = jnp.sum(before * expert_hot, axis=1)
    return (flat_routes * capacity + rank_in).reshape(routes.shape)


def dot_float(left_side, right_side):
    return jnp.dot(left_side, right_side, preferred_element_type=jnp.float32)


def dot_rows(left_side, right_side):
    return jnp.einsum("td,tf->df", left_side, right_side, preferred_element_type=jnp.float32)


def dot_cols(left_side, right_side):
    return jnp.einsum("tf,df->td", left_side, right_side, preferred_element_type=jnp.float32)


def dot_halves(left_side, halves):
    return jnp.concatenate([dot_float(left_side, halves[0]), dot_float(left_side, halves[1])], axis=1)


def by_slices(
    tokens, timesteps, lengths, routes, cotangent, w_ada, w_qkv, w_out, w_fc1, w_fc2, w_router, e_fc1, e_fc2
):
    tok_count, model_width = tokens.shape
    head_count = HEADS
    head_size = model_width // head_count
    expert_count = w_router.shape[1]
    score_scale = head_size ** (-0.5)
    residual = tokens.astype(jnp.float32)
    member, item_of = membership(lengths[0], tok_count)
    ada, qkv_w, out_w, w1, w1s, w2, w2s = gather_weights(w_ada, w_qkv, w_out, w_router, w_fc1, w_fc2, e_fc1, e_fc2)
    half = model_width // 2
    router_full = out_w[0, :, half : half + expert_count]
    out_w = out_w[:, :, :half]
    condition = jax.nn.silu(sinusoid(timesteps, model_width)).astype(jnp.bfloat16)
    modulation = dot_halves(condition, ada)
    token_mod = jnp.dot(member, modulation, precision=precise)
    shift_attn, scale_attn, gate_attn, shift_mlp, scale_mlp, gate_mlp = jnp.split(token_mod, 6, axis=1)
    attn_in = modulate(residual, shift_attn, scale_attn).astype(jnp.bfloat16)
    qkv_low = dot_halves(attn_in, qkv_w).astype(jnp.bfloat16)
    queries, key_rows, value_rows = [
        portion.reshape(tok_count, head_count, head_size) for portion in jnp.split(qkv_low, 3, axis=1)
    ]
    same_item = item_of[:, None] == item_of[None, :]
    scores = (
        jnp.einsum("qhd,khd->hqk", queries, key_rows, preferred_element_type=jnp.float32) * score_scale
    )
    scores = jnp.where(same_item[None], scores, -1e30)
    attn_probs = jax.nn.softmax(scores, axis=-1)
    probs_low = attn_probs.astype(jnp.bfloat16)
    attn_low = jnp.einsum("hqk,khd->qhd", probs_low, value_rows, preferred_element_type=jnp.float32)
    attn_low = attn_low.reshape(tok_count, model_width).astype(jnp.bfloat16)
    attn_proj = dot_halves(attn_low, out_w)
    middle = residual + gate_attn * attn_proj
    mixed_in = modulate(middle, shift_mlp, scale_mlp).astype(jnp.bfloat16)
    out_grad = cotangent.astype(jnp.float32)
    grad_branch = out_grad * gate_mlp
    chance = jax.nn.softmax(dot_float(mixed_in, router_full), axis=-1)
    expert_ids = jnp.arange(expert_count, dtype=jnp.int32)
    chosen = jnp.sum((routes[:, :, None] == expert_ids[None, None, :]).astype(jnp.float32), axis=1)
    gates = (chosen * chance).T
    gates_high = gates.astype(jnp.bfloat16)
    gates_low = (gates - gates_high.astype(jnp.float32)).astype(jnp.bfloat16)
    branch, grad_mixed, grad_chance, part1, part1s, sum_e_out, sum_fc2 = block(
        mixed_in, grad_branch.astype(jnp.bfloat16), jnp.concatenate([gates_high, gates_low], axis=0), w1, w1s, w2, w2s
    )
    output = (middle + gate_mlp * branch).astype(jnp.bfloat16)
    grad_gate_mlp = out_grad * branch
    grad_chance = grad_chance.T * chosen
    grad_logits = chance * (grad_chance - jnp.sum(grad_chance * chance, axis=-1, keepdims=True))
    grad_logits = grad_logits.astype(jnp.bfloat16)
    term_router = dot_rows(mixed_in, grad_logits)
    term_router = jnp.pad(term_router, ((0, 0), (0, -expert_count % 128)))
    grad_mixed = grad_mixed + dot_cols(grad_logits, router_full)
    unused_mix, mix_back = jax.vjp(modulate, middle, shift_mlp, scale_mlp)
    grad_mid_norm, grad_shift_mlp, grad_scale_mlp = mix_back(grad_mixed)
    grad_middle = out_grad + grad_mid_norm
    grad_gate_attn = grad_middle * attn_proj
    grad_proj = (grad_middle * gate_attn).astype(jnp.bfloat16)
    term_out = [dot_rows(attn_low, grad_proj[:, c * half : (c + 1) * half]) for c in (0, 1)]
    term_out = jnp.stack([jnp.concatenate([term, term_router], axis=1) for term in term_out])
    grad_attn = sum(dot_cols(grad_proj[:, c * half : (c + 1) * half], out_w[c]) for c in (0, 1))
    grad_attn = grad_attn.astype(jnp.bfloat16).reshape(tok_count, head_count, head_size)
    grad_probs = jnp.einsum("qhd,khd->hqk", grad_attn, value_rows, preferred_element_type=jnp.float32)
    grad_values = jnp.einsum("hqk,qhd->khd", probs_low, grad_attn, preferred_element_type=jnp.float32)
    grad_scores = attn_probs * (grad_probs - jnp.sum(grad_probs * attn_probs, axis=-1, keepdims=True))
    grad_scores = grad_scores.astype(jnp.bfloat16)
    grad_queries = (
        jnp.einsum("hqk,khd->qhd", grad_scores, key_rows, preferred_element_type=jnp.float32) * score_scale
    )
    grad_keys = (
        jnp.einsum("hqk,qhd->khd", grad_scores, queries, preferred_element_type=jnp.float32) * score_scale
    )
    grad_qkv = jnp.concatenate(
        [g.reshape(tok_count, model_width) for g in (grad_queries, grad_keys, grad_values)], axis=1
    ).astype(jnp.bfloat16)
    part = grad_qkv.shape[1] // 2
    term_qkv = jnp.stack([dot_rows(attn_in, grad_qkv[:, c * part : (c + 1) * part]) for c in (0, 1)])
    grad_attn_in = sum(dot_cols(grad_qkv[:, c * part : (c + 1) * part], qkv_w[c]) for c in (0, 1))
    unused_pre, pre_back = jax.vjp(modulate, residual, shift_attn, scale_attn)
    grad_input_norm, grad_shift_attn, grad_scale_attn = pre_back(grad_attn_in)
    d_tokens = grad_middle + grad_input_norm
    grad_token_mod = jnp.concatenate(
        [grad_shift_attn, grad_scale_attn, grad_gate_attn, grad_shift_mlp, grad_scale_mlp, grad_gate_mlp], axis=1
    )
    grad_modulation = jnp.einsum("ti,tc->ic", member, grad_token_mod, precision=precise).astype(jnp.bfloat16)
    items = grad_modulation.shape[0]
    both = jnp.concatenate([grad_modulation, condition], axis=1)
    width = both.shape[1]
    tile = jnp.pad(both.reshape(items * 8, width // 8), ((0, 0), (0, -(width // 8) % 128)))
    total, all_tile, own1, own1s = to_owners(
        term_qkv.astype(jnp.bfloat16), term_out.astype(jnp.bfloat16), tile, part1, part1s
    )
    sum_e_in = own1.astype(jnp.float32)
    sum_fc1 = own1s.transpose(1, 0, 2).reshape(w_fc1.shape)
    all_both = all_tile[..., : width // 8].reshape(-1, width)
    all_modgrad, all_condition = all_both[:, : grad_modulation.shape[1]], all_both[:, grad_modulation.shape[1] :]
    own_share = w_ada.shape[0]
    own_start = lax.axis_index(("gx", "gy")) * own_share
    own_condition = lax.dynamic_slice_in_dim(all_condition, own_start, own_share, 1)
    owned_ada = dot_rows(own_condition, all_modgrad)
    sum_qkv = jnp.concatenate([total[0, :, :part], total[1, :, :part]], axis=1)
    sum_out = jnp.concatenate([total[0, :, part : part + half], total[1, :, part : part + half]], axis=1)
    sum_router = total[0, :, part + half : part + half + expert_count]
    return (output, d_tokens, owned_ada, sum_qkv, sum_out, sum_fc1, sum_fc2, sum_router, sum_e_in, sum_e_out)


def by_weights(
    tokens,
    timesteps,
    lengths,
    routes,
    cotangent,
    w_ada,
    w_qkv,
    w_out,
    w_fc1,
    w_fc2,
    w_router,
    e_fc1,
    e_fc2,
):
    tok_count, model_width = tokens.shape
    head_count = HEADS
    head_size = model_width // head_count
    expert_count = w_router.shape[1]
    capacity = CAP
    score_scale = head_size ** (-0.5)
    residual = tokens.astype(jnp.float32)
    member, item_of = membership(lengths[0], tok_count)
    ada_full, qkv_full, out_full = (
        lax.all_gather(w_ada, ("gx", "gy"), axis=0, tiled=True),
        lax.all_gather(w_qkv, ("gx", "gy"), axis=0, tiled=True),
        lax.all_gather(w_out, ("gx", "gy"), axis=0, tiled=True),
    )
    condition = jax.nn.silu(sinusoid(timesteps, model_width)).astype(jnp.bfloat16)
    modulation = dot_float(condition, ada_full)
    token_mod = jnp.dot(member, modulation, precision=precise)
    shift_attn, scale_attn, gate_attn, shift_mlp, scale_mlp, gate_mlp = jnp.split(
        token_mod, 6, axis=1
    )
    attn_in = modulate(residual, shift_attn, scale_attn).astype(jnp.bfloat16)
    qkv_low = dot_float(attn_in, qkv_full).astype(jnp.bfloat16)
    queries, key_rows, value_rows = [
        portion.reshape(tok_count, head_count, head_size)
        for portion in jnp.split(qkv_low, 3, axis=1)
    ]
    same_item = item_of[:, None] == item_of[None, :]
    scores = (
        jnp.einsum("qhd,khd->hqk", queries, key_rows, preferred_element_type=jnp.float32)
        * score_scale
    )
    scores = jnp.where(same_item[None], scores, -1e30)
    attn_probs = jax.nn.softmax(scores, axis=-1)
    probs_low = attn_probs.astype(jnp.bfloat16)
    attn_low = jnp.einsum("hqk,khd->qhd", probs_low, value_rows, preferred_element_type=jnp.float32)
    attn_low = attn_low.reshape(tok_count, model_width).astype(jnp.bfloat16)
    attn_proj = dot_float(attn_low, out_full)
    middle = residual + gate_attn * attn_proj
    mixed_in = modulate(middle, shift_mlp, scale_mlp).astype(jnp.bfloat16)
    fc1_full, fc2_full, router_full = (
        lax.all_gather(w_fc1, ("gx", "gy"), axis=0, tiled=True),
        lax.all_gather(w_fc2, ("gx", "gy"), axis=0, tiled=True),
        lax.all_gather(w_router, ("gx", "gy"), axis=0, tiled=True),
    )
    hidden_pre = dot_float(mixed_in, fc1_full)
    hidden = jax.nn.gelu(hidden_pre).astype(jnp.bfloat16)
    shared = dot_float(hidden, fc2_full)
    chance = jax.nn.softmax(dot_float(mixed_in, router_full), axis=-1)
    expert_ids = jnp.arange(expert_count, dtype=jnp.int32)
    chosen = (routes[:, :, None] == expert_ids[None, None, :]).astype(jnp.float32)
    gate_values = jnp.sum(chosen * chance[:, None, :], axis=2)
    slot_of = slot_index(routes, expert_count, capacity)
    slot_ids = jnp.arange(expert_count * capacity, dtype=jnp.int32)
    selector = (slot_of[:, :, None] == slot_ids[None, None, :]).astype(jnp.bfloat16)
    slot_rows = jnp.einsum("tks,td->sd", selector, mixed_in, preferred_element_type=jnp.float32)
    slot_rows = slot_rows.astype(jnp.bfloat16).reshape(expert_count, capacity, model_width)
    owned_rows = lax.all_to_all(slot_rows, "gx", split_axis=0, concat_axis=1, tiled=True)
    expert_in, expert_back = (
        lax.all_gather(e_fc1, "gy", axis=1, tiled=True),
        lax.all_gather(e_fc2, "gy", axis=1, tiled=True),
    )
    inner_pre = jnp.einsum(
        "ecd,edf->ecf", owned_rows, expert_in, preferred_element_type=jnp.float32
    )
    inner_act = jax.nn.gelu(inner_pre).astype(jnp.bfloat16)
    result = jnp.einsum(
        "ecf,efd->ecd", inner_act, expert_back, preferred_element_type=jnp.float32
    ).astype(jnp.bfloat16)
    returned = lax.all_to_all(result, "gx", split_axis=1, concat_axis=0, tiled=True).reshape(
        expert_count * capacity, model_width
    )
    picked = jnp.take(returned, slot_of, axis=0).astype(jnp.float32)
    branch = shared + jnp.sum(gate_values[:, :, None] * picked, axis=1)
    output = (middle + gate_mlp * branch).astype(jnp.bfloat16)
    out_grad = cotangent.astype(jnp.float32)
    grad_gate_mlp = out_grad * branch
    grad_branch = out_grad * gate_mlp
    grad_shared = grad_branch.astype(jnp.bfloat16)
    grad_picked = (gate_values[:, :, None] * grad_branch[:, None, :]).astype(jnp.bfloat16)
    grad_gates = jnp.sum(grad_branch[:, None, :] * picked, axis=2)
    grad_slots = jnp.einsum(
        "tks,tkd->sd", selector, grad_picked, preferred_element_type=jnp.float32
    )
    grad_slots = grad_slots.astype(jnp.bfloat16).reshape(expert_count, capacity, model_width)
    grad_owned = lax.all_to_all(grad_slots, "gx", split_axis=0, concat_axis=1, tiled=True)
    grad_inner = jnp.einsum(
        "ecd,efd->ecf", grad_owned, expert_back, preferred_element_type=jnp.float32
    )
    unused_inner, gelu_expert = jax.vjp(jax.nn.gelu, inner_pre)
    grad_inner_pre = gelu_expert(grad_inner)[0].astype(jnp.bfloat16)
    term_e_out = jnp.einsum(
        "ecf,ecd->efd", inner_act, grad_owned, preferred_element_type=jnp.float32
    )
    term_e_in = jnp.einsum(
        "ecd,ecf->edf", owned_rows, grad_inner_pre, preferred_element_type=jnp.float32
    )
    grad_rows = jnp.einsum(
        "ecf,edf->ecd", grad_inner_pre, expert_in, preferred_element_type=jnp.float32
    )
    grad_returned = (
        lax.all_to_all(
            grad_rows.astype(jnp.bfloat16), "gx", split_axis=1, concat_axis=0, tiled=True
        )
        .astype(grad_rows.dtype)
        .reshape(expert_count * capacity, model_width)
    )
    sum_e_in, sum_e_out = (
        lax.psum_scatter(
            term_e_in.astype(jnp.bfloat16), "gy", scatter_dimension=1, tiled=True
        ).astype(jnp.float32),
        lax.psum_scatter(
            term_e_out.astype(jnp.bfloat16), "gy", scatter_dimension=1, tiled=True
        ).astype(jnp.float32),
    )
    grad_chance = jnp.sum(chosen * grad_gates[:, :, None], axis=1)
    grad_logits = chance * (grad_chance - jnp.sum(grad_chance * chance, axis=-1, keepdims=True))
    grad_logits = grad_logits.astype(jnp.bfloat16)
    grad_hidden = dot_cols(grad_shared, fc2_full)
    unused_shared, gelu_shared = jax.vjp(jax.nn.gelu, hidden_pre)
    grad_hidden_pre = gelu_shared(grad_hidden)[0].astype(jnp.bfloat16)
    term_fc2 = dot_rows(hidden, grad_shared)
    term_fc1 = dot_rows(mixed_in, grad_hidden_pre)
    term_router = dot_rows(mixed_in, grad_logits)
    part_fc1, part_fc2, part_router = (
        lax.psum_scatter(
            term_fc1.astype(jnp.bfloat16), "gx", scatter_dimension=0, tiled=True
        ).astype(jnp.float32),
        lax.psum_scatter(
            term_fc2.astype(jnp.bfloat16), "gx", scatter_dimension=0, tiled=True
        ).astype(jnp.float32),
        lax.psum_scatter(
            term_router.astype(jnp.bfloat16), "gx", scatter_dimension=0, tiled=True
        ).astype(jnp.float32),
    )
    sum_fc1, sum_fc2, sum_router = (
        lax.psum_scatter(
            part_fc1.astype(jnp.bfloat16), "gy", scatter_dimension=0, tiled=True
        ).astype(jnp.float32),
        lax.psum_scatter(
            part_fc2.astype(jnp.bfloat16), "gy", scatter_dimension=0, tiled=True
        ).astype(jnp.float32),
        lax.psum_scatter(
            part_router.astype(jnp.bfloat16), "gy", scatter_dimension=0, tiled=True
        ).astype(jnp.float32),
    )
    grad_mixed = dot_cols(grad_hidden_pre, fc1_full) + dot_cols(grad_logits, router_full)
    grad_mixed = grad_mixed + jnp.sum(jnp.take(grad_returned, slot_of, axis=0), axis=1)
    unused_mix, mix_back = jax.vjp(modulate, middle, shift_mlp, scale_mlp)
    grad_mid_norm, grad_shift_mlp, grad_scale_mlp = mix_back(grad_mixed)
    grad_middle = out_grad + grad_mid_norm
    grad_gate_attn = grad_middle * attn_proj
    grad_proj = (grad_middle * gate_attn).astype(jnp.bfloat16)
    term_out = dot_rows(attn_low, grad_proj)
    grad_attn = (
        dot_cols(grad_proj, out_full).astype(jnp.bfloat16).reshape(tok_count, head_count, head_size)
    )
    grad_probs = jnp.einsum(
        "qhd,khd->hqk", grad_attn, value_rows, preferred_element_type=jnp.float32
    )
    grad_values = jnp.einsum(
        "hqk,qhd->khd", probs_low, grad_attn, preferred_element_type=jnp.float32
    )
    grad_scores = attn_probs * (
        grad_probs - jnp.sum(grad_probs * attn_probs, axis=-1, keepdims=True)
    )
    grad_scores = grad_scores.astype(jnp.bfloat16)
    grad_queries = (
        jnp.einsum("hqk,khd->qhd", grad_scores, key_rows, preferred_element_type=jnp.float32)
        * score_scale
    )
    grad_keys = (
        jnp.einsum("hqk,qhd->khd", grad_scores, queries, preferred_element_type=jnp.float32)
        * score_scale
    )
    grad_qkv = jnp.concatenate(
        [
            grad_queries.reshape(tok_count, model_width),
            grad_keys.reshape(tok_count, model_width),
            grad_values.reshape(tok_count, model_width),
        ],
        axis=1,
    ).astype(jnp.bfloat16)
    term_qkv = dot_rows(attn_in, grad_qkv)
    grad_attn_in = dot_cols(grad_qkv, qkv_full)
    unused_pre, pre_back = jax.vjp(modulate, residual, shift_attn, scale_attn)
    grad_input_norm, grad_shift_attn, grad_scale_attn = pre_back(grad_attn_in)
    d_tokens = grad_middle + grad_input_norm
    grad_token_mod = jnp.concatenate(
        [
            grad_shift_attn,
            grad_scale_attn,
            grad_gate_attn,
            grad_shift_mlp,
            grad_scale_mlp,
            grad_gate_mlp,
        ],
        axis=1,
    )
    grad_modulation = jnp.einsum("ti,tc->ic", member, grad_token_mod, precision=precise).astype(
        jnp.bfloat16
    )
    all_condition, all_modgrad = (
        lax.all_gather(condition, ("gx", "gy"), axis=0, tiled=True),
        lax.all_gather(grad_modulation, ("gx", "gy"), axis=0, tiled=True),
    )
    own_share = model_width // lax.axis_size(("gx", "gy"))
    own_start = lax.axis_index(("gx", "gy")) * own_share
    own_condition = lax.dynamic_slice_in_dim(all_condition, own_start, own_share, 1)
    owned_ada = dot_rows(own_condition, all_modgrad)
    attn_terms = (term_qkv, term_out)
    attn_parts = (
        lax.psum_scatter(
            attn_terms[0].astype(jnp.bfloat16), "gx", scatter_dimension=0, tiled=True
        ).astype(jnp.float32),
        lax.psum_scatter(
            attn_terms[1].astype(jnp.bfloat16), "gx", scatter_dimension=0, tiled=True
        ).astype(jnp.float32),
    )
    attn_sums = (
        lax.psum_scatter(
            attn_parts[0].astype(jnp.bfloat16), "gy", scatter_dimension=0, tiled=True
        ).astype(jnp.float32),
        lax.psum_scatter(
            attn_parts[1].astype(jnp.bfloat16), "gy", scatter_dimension=0, tiled=True
        ).astype(jnp.float32),
    )
    sum_qkv, sum_out = attn_sums
    return (
        output,
        d_tokens,
        owned_ada,
        sum_qkv,
        sum_out,
        sum_fc1,
        sum_fc2,
        sum_router,
        sum_e_in,
        sum_e_out,
    )


def solution(mesh):
    in_specs = (
        P(("gx", "gy"), None),
        P(("gx", "gy")),
        P(("gx", "gy"), None),
        P(("gx", "gy"), None),
        P(("gx", "gy"), None),
        P(("gx", "gy"), None),
        P(("gx", "gy"), None),
        P(("gx", "gy"), None),
        P(("gx", "gy"), None),
        P(("gx", "gy"), None),
        P(("gx", "gy"), None),
        P("gx", "gy", None),
        P("gx", "gy", None),
    )
    out_specs = (
        P(("gx", "gy"), None),
        P(("gx", "gy"), None),
        P(("gx", "gy"), None),
        P(("gx", "gy"), None),
        P(("gx", "gy"), None),
        P(("gx", "gy"), None),
        P(("gx", "gy"), None),
        P(("gx", "gy"), None),
        P("gx", "gy", None),
        P("gx", "gy", None),
    )
    step = by_slices if dict(mesh.shape) == {"gx": 2, "gy": 16} else by_weights
    return jax.shard_map(
        step, mesh=mesh, in_specs=in_specs, out_specs=out_specs, check_vma=False
    )
```

```python
import functools
import math

import jax
import jax.numpy as jnp
from jax import lax
from jax.experimental import pallas as pl
from jax.experimental.pallas import tpu as pltpu
from jax.sharding import PartitionSpec as P

HEADS = 12
CAP = 64
MESH = pl.DeviceIdType.MESH
ANY = pl.ANY
VMEM = pltpu.VMEM
DMA = pltpu.SemaphoreType.DMA
LINE = (1, 3, 2)

precise = lax.Precision.HIGHEST
layer_epsilon = 1e-06


def place():
    gy = lax.axis_index("gy")
    return lax.axis_index("gx"), gy // 4, (gy // 2) % 2, gy % 2


def device(y, z, x, c):
    return (y, 4 * z + 2 * x + c)


def chip(y, z, x):
    return 8 * y + 2 * z + x


def meet(partners):
    barrier = pltpu.get_barrier_semaphore()
    for partner in partners:
        pl.semaphore_signal(barrier, inc=1, device_id=partner, device_id_type=MESH)
    pl.semaphore_wait(barrier, len(partners))


def cross_partners(here):
    y, z, x, c = here
    return [device(y, (z + step) % 4, x, c) for step in LINE] + [
        device(1 - y, z, x, c),
        device(y, z, 1 - x, c),
    ]


def remote(source, target, send, recv, to):
    return pltpu.make_async_remote_copy(
        src_ref=source, dst_ref=target, send_sem=send, recv_sem=recv, device_id=to, device_id_type=MESH
    )


class Gather:
    def __init__(self, here, y_first, own, slot, send, recv, pair=None):
        self.here, self.y_first, self.own, self.slot = here, y_first, own, slot
        self.send, self.recv, self.pair, self.started = send, recv, pair, []

    def copy(self, source, number, recv, to):
        sent = remote(source, self.slot(number), self.send.at[len(self.started)], recv.at[number], to)
        sent.start()
        self.started.append(sent)

    def forward(self, source, number, to_y, to_x, to_pair=True):
        y, z, x, c = self.here
        if to_y:
            self.copy(source, number, self.recv, device(1 - y, z, x, c))
        if to_x:
            self.copy(source, number, self.recv, device(y, z, 1 - x, c))
        if to_pair and self.pair is not None:
            self.copy(source, number, self.pair, device(y, z, x, 1 - c))

    def arrive(self, number, recv=None):
        recv = self.recv if recv is None else recv
        block = self.slot(number)
        remote(block, block, self.send.at[0], recv.at[number], device(*self.here)).wait_recv()
        return block

    def start_line(self, step):
        y, z, x, c = self.here
        self.copy(self.own, chip(y, z, x), self.recv, device(y, (z + step) % 4, x, c))

    def start_first(self):
        y, z, x, c = self.here
        self.forward(self.own, chip(y, z, x), self.y_first, not self.y_first)

    def start_last(self):
        y, z, x, c = self.here
        self.forward(self.own, chip(y, z, x), not self.y_first, self.y_first, False)

    def line_first(self, step):
        y, z, x, c = self.here
        number = chip(y, (z + step) % 4, x)
        self.forward(self.arrive(number), number, self.y_first, not self.y_first)

    def line_last(self, step):
        y, z, x, c = self.here
        number = chip(y, (z + step) % 4, x)
        self.forward(self.slot(number), number, not self.y_first, self.y_first, False)

    def second(self, step):
        y, z, x, c = self.here
        if self.y_first:
            number = chip(1 - y, (z + step) % 4, x)
        else:
            number = chip(y, (z + step) % 4, 1 - x)
        self.forward(self.arrive(number), number, not self.y_first, self.y_first)

    def third(self, step):
        y, z, x, c = self.here
        for other in (0, 1):
            if self.y_first:
                number = chip(y if other == 0 else 1 - y, (z + step) % 4, 1 - x)
            else:
                number = chip(1 - y, (z + step) % 4, x if other == 0 else 1 - x)
            self.forward(self.arrive(number), number, False, False)

    def finish(self):
        for sent in self.started:
            sent.wait_send()
        if self.pair is not None:
            for number in range(16):
                self.arrive(number, self.pair)


def gather_start(gathers):
    for gather in gathers:
        gather.start_first()
    for gather in gathers:
        gather.start_line(1)
        gather.start_line(3)
    for gather in gathers:
        gather.start_last()
    for gather in gathers:
        gather.start_line(2)


def gather_line(gathers, step):
    for gather in gathers:
        gather.line_first(step)
    for gather in gathers:
        gather.line_last(step)


def gather_second(gathers, step):
    for gather in gathers:
        gather.second(step)


def gather_third(gathers, step):
    for gather in gathers:
        gather.third(step)


def gather_all(gathers, between=None):
    gather_start(gathers)
    gather_second(gathers, 0)
    for step in LINE:
        gather_line(gathers, step)
        gather_second(gathers, step)
    if between is not None:
        between()
    for step in (0,) + LINE:
        gather_third(gathers, step)
    for gather in gathers:
        gather.finish()


class Scatter:
    def __init__(self, here, y_first, part, got, send, recv):
        self.here, self.y_first, self.part, self.got = here, y_first, part, got
        self.send, self.recv, self.started = send, recv, []

    def number(self, a, b, step):
        y, z, x, c = self.here
        flip_y, flip_x = (a, b) if self.y_first else (b, a)
        return chip(1 - y if flip_y else y, (z + step) % 4, 1 - x if flip_x else x)

    def toward(self, second):
        y, z, x, c = self.here
        return device(1 - y, z, x, c) if self.y_first != second else device(y, z, 1 - x, c)

    def copy(self, source, index, to):
        sent = remote(source, self.got(index), self.send.at[len(self.started)], self.recv.at[index], to)
        sent.start()
        self.started.append(sent)

    def arrive(self, index):
        block = self.got(index)
        remote(block, block, self.send.at[0], self.recv.at[index], device(*self.here)).wait_recv()
        return block

    def first(self, step):
        for b in (1, 0):
            self.copy(self.part(self.number(1, b, step)), 4 * b + step, self.toward(False))

    def add(self, number, index):
        block, mine = self.arrive(index), self.part(number)
        total = mine[...].astype(jnp.float32) + block[...].astype(jnp.float32)
        mine[...] = total.astype(mine.dtype)

    def one(self, b, step):
        number = self.number(0, b, step)
        self.add(number, 4 * b + step)
        if b == 1:
            self.copy(self.part(number), 8 + step, self.toward(True))

    def two(self, step):
        y, z, x, c = self.here
        number = self.number(0, 0, step)
        self.add(number, 8 + step)
        if step:
            self.copy(self.part(number), 11 + step, device(y, (z + step) % 4, x, c))

    def total(self):
        result = self.part(self.number(0, 0, 0))[...].astype(jnp.float32)
        for step in (1, 2, 3):
            result = result + self.arrive(11 + step)[...].astype(jnp.float32)
        return result

    def finish(self):
        for sent in self.started:
            sent.wait_send()


def scatter_all(scatters, between):
    order = (2, 1, 3, 0)
    for scatter in scatters:
        scatter.first(order[0])
    for scatter in scatters:
        scatter.first(order[1])
    for turn, step in enumerate(order):
        for scatter in scatters:
            scatter.one(1, step)
        for scatter in scatters:
            scatter.one(0, step)
        if turn + 2 < 4:
            for scatter in scatters:
                scatter.first(order[turn + 2])
        for scatter in scatters:
            scatter.two(step)
        between(turn)


def nt(a, b):
    return lax.dot_general(a, b, (((1,), (1,)), ((), ())), preferred_element_type=jnp.float32)


def tn(a, b):
    return lax.dot_general(a, b, (((0,), (0,)), ((), ())), preferred_element_type=jnp.float32)


def nn(a, b):
    return jnp.dot(a, b, preferred_element_type=jnp.float32)


def low(value):
    return value.astype(jnp.bfloat16)


def wide_float(value):
    return value.astype(jnp.float32)


def norm(values):
    centred = values - jnp.mean(values, axis=-1, keepdims=True)
    scale = lax.rsqrt(jnp.mean(centred * centred, axis=-1, keepdims=True) + layer_epsilon)
    return centred * scale, scale


def norm_back(grad, normed, scale):
    pulled = grad - jnp.mean(grad, axis=-1, keepdims=True) - normed * jnp.mean(grad * normed, axis=-1, keepdims=True)
    return scale * pulled


def item_mask(lengths, shape):
    return lax.broadcasted_iota(jnp.int32, shape, 0) >= lengths[0, 0]


def choices(routes, square):
    square[...] = jnp.zeros_like(square)
    square[0 : routes.shape[0], :] = wide_float(routes[...])
    named = square[...].T
    lane = wide_float(lax.broadcasted_iota(jnp.int32, (1, 128), 1))
    return (named[:, 0:1] == lane) | (named[:, 1:2] == lane)


def own_modulation(here, mod, item, half, part):
    y, z, x, c = here
    model = item.shape[1]
    first = 8 * y + 4 * x + 2 * c
    at = slice(part * model, (part + 1) * model)
    return jnp.where(item, mod[half, pl.ds(first + 1, 1), at], mod[half, pl.ds(first, 1), at])


def head_lanes():
    lane = lax.broadcasted_iota(jnp.int32, (1, 128), 1)
    return lane < 64, [low(wide_float(lane < 64)), low(wide_float(lane >= 64))]


def front_kernel(
    lengths, tokens, cotangent, routes, cond, w_ada, w_qkv, w_out, w_router, w_fc1, e1, e2, f2,
    w1, w1s, w2, w2s, qkv_w, out_w, conds, mod, mixed, grad, gates, attn_in, qkv, probs, attn_low, attn_proj, middle, chance,
    square, f1, s_got, s_rows, q_full, o_full, q_fold, o_fold, q_stage, o_stage, q_block, o_block, c_buf, part, sib, z_part, z_got, xy_part, xy_got,
    pre_send, pre_recv, g_send, g_recv, g_pair, a_send, a_recv, a_pair_send, a_pair, b_send, b_recv, b_pair, l_sem, d_send, d_recv,
    c_send, c_recv, m_send, m_recv,
):
    here = y, z, x, c = place()
    me, k, gy = chip(y, z, x), 2 * z + x, 4 * z + 2 * x + c
    rows, model = w_out.shape
    others = [(dy, dz, dx) for dy in (0, 1) for dz in (0, 1, 2, 3) for dx in (0, 1) if (dy, dz, dx) != (0, 0, 0)]
    spot = lambda dy, dz, dx: (1 - y if dy else y, (z + dz) % 4, 1 - x if dx else x)
    sibling = device(y, z, x, 1 - c)
    peers = [(*spot(dy, dz, dx), c if same else 1 - c) for same in (True, False) for dy, dz, dx in [(0, 0, 0)] + others]
    peers = peers[1:]
    meet([device(*peer) for peer in peers])

    started = []

    def go(copy):
        copy.start()
        started.append(copy)

    number = 2 * me + c
    for i, peer in enumerate(peers):
        go(remote(cond.at[2 * chip(*peer[:3]) + peer[3]], c_buf.at[number], c_send.at[i], c_recv.at[number], device(*peer)))

    mine = pl.ds(pl.multiple_of(rows * c, 8), rows)
    square[...] = jnp.zeros_like(square)
    square[0 : w_router.shape[0], 0:rows] = wide_float(w_router[...])
    router = square[...].T[:rows]
    for w, fold, stage, i in ((w_qkv, q_fold, q_stage, 0), (w_out, o_fold, o_stage, 1)):
        cut = w.shape[1] // 2
        for h in (0, 1):
            fold[h, :, :cut] = wide_float(w[:, h * cut : (h + 1) * cut])
            if i:
                fold[h, :, cut:] = router
        go(remote(fold.at[1 - c], stage.at[mine, :], pre_send.at[i], pre_recv.at[i], sibling))
        stage[mine, :] = fold[c]

    depth, width = e1.shape[1], w1.shape[2]
    cols = lambda n: pl.ds(pl.multiple_of(width * n, 128), width)
    strip = lambda n: pl.ds(pl.multiple_of(depth * n, 16), depth)
    half2, half2s = e2.shape[1], f2.shape[0]
    at2 = lambda core: pl.ds(pl.multiple_of(half2 * core, 16), half2)
    at2s = lambda core: pl.ds(pl.multiple_of(half2s * core, 16), half2s)
    local = [
        pltpu.make_async_copy(e1.at[:, :, cols(k)], w1.at[:, strip(gy), :], l_sem.at[0]),
        pltpu.make_async_copy(e2, w2.at[:, at2(c), :], l_sem.at[1]),
        pltpu.make_async_copy(f2, w2s.at[at2s(c), :], l_sem.at[2]),
    ]
    for copy in local:
        copy.start()
    plane = [o for o in others if o[0] == 0]

    def send_experts(steps):
        for i, o in enumerate(plane):
            if o[1] in steps:
                ty, tz, tx = spot(*o)
                go(remote(e1.at[:, :, cols(2 * tz + tx)], w1.at[:, strip(gy), :], a_send.at[i], a_recv.at[k], device(ty, tz, tx, c)))

    send_experts((0, 1))

    for i, (stage, block) in enumerate(((q_stage, q_block), (o_stage, o_block))):
        theirs = stage.at[pl.ds(pl.multiple_of(rows * (1 - c), 8), rows), :]
        remote(theirs, theirs, pre_send.at[i], pre_recv.at[i], sibling).wait_recv()
        block[...] = low(stage[...])
    gathers = []
    for i, (block, full, y_first) in enumerate(((q_block, q_full, False), (o_block, o_full, True))):
        slot = functools.partial(lambda full, n: full.at[c, pl.ds(pl.multiple_of(2 * rows * n, 16), 2 * rows), :], full)
        gathers.append(Gather(here, y_first, block, slot, g_send.at[i], g_recv.at[i], g_pair.at[i]))
        slot(me)[...] = block[...]
    gather_start(gathers)

    c_buf[number] = cond[number]
    for peer in peers:
        block = c_buf.at[2 * chip(*peer[:3]) + peer[3]]
        remote(block, block, c_send.at[0], c_recv.at[2 * chip(*peer[:3]) + peer[3]], sibling).wait_recv()
    for gz in range(4):
        for gy_ in range(2):
            group = [c_buf[2 * chip(gy_, gz, gx_) + core] for gx_ in (0, 1) for core in (0, 1)]
            conds[pl.ds(8 * (2 * gz + gy_), 8), :] = group[0] + group[1] + group[2] + group[3]
    lhs = low(conds[...])[:, :rows]
    for h in (0, 1):
        at = slice(h * part.shape[2], (h + 1) * part.shape[2])
        part[h] = nn(lhs, w_ada[:, at])
    go(remote(part.at[1 - c], sib, m_send.at[0], m_recv.at[0], sibling))

    gather_second(gathers, 0)
    remote(sib, sib, m_send.at[0], m_recv.at[0], sibling).wait_recv()
    for gz in range(4):
        at = slice(16 * gz, 16 * (gz + 1))
        z_part[gz] = part[c, at, :] + sib[at, :]
    for step in LINE:
        go(remote(z_part.at[(z + step) % 4], z_got.at[step - 1], m_send.at[step], m_recv.at[step], device(y, (z + step) % 4, x, c)))
    gather_line(gathers, 1)
    send_experts((3,))
    slim = w1s.shape[1]
    for n in range(16):
        block = wide_float(w_fc1[:, slim * n : slim * (n + 1)])
        f1[n] = low(jnp.concatenate([block, jnp.zeros((f1.shape[1] - rows, slim), jnp.float32)], axis=0))
    for i, o in enumerate(others):
        ty, tz, tx = spot(*o)
        go(remote(f1.at[chip(ty, tz, tx)], s_got.at[c, me], b_send.at[i], b_recv.at[me], device(ty, tz, tx, c)))
    s_got[c, me] = f1[me]
    gather_second(gathers, 1)
    gather_line(gathers, 3)
    send_experts((2,))
    total = wide_float(z_part[z])
    for step in LINE:
        remote(z_got.at[step - 1], z_got.at[step - 1], m_send.at[0], m_recv.at[step], sibling).wait_recv()
        total = total + wide_float(z_got[step - 1])
    xy_part[0] = total
    go(remote(xy_part.at[0], xy_got.at[0], m_send.at[4], m_recv.at[4], device(y, z, 1 - x, c)))
    gather_second(gathers, 3)
    remote(xy_got.at[0], xy_got.at[0], m_send.at[0], m_recv.at[4], sibling).wait_recv()
    xy_part[1] = xy_part[0] + xy_got[0]
    go(remote(xy_part.at[1], xy_got.at[1], m_send.at[5], m_recv.at[5], device(1 - y, z, x, c)))
    gather_line(gathers, 2)
    remote(xy_got.at[1], xy_got.at[1], m_send.at[0], m_recv.at[5], sibling).wait_recv()
    mod[c] = xy_part[1] + xy_got[1]
    go(remote(mod.at[c], mod.at[c], m_send.at[6], m_recv.at[6], sibling))
    gather_second(gathers, 2)
    twin = [
        remote(e2, w2.at[:, at2(c), :], d_send.at[0], d_recv.at[0], sibling),
        remote(f2, w2s.at[at2s(c), :], d_send.at[1], d_recv.at[1], sibling),
    ]
    for copy in twin:
        go(copy)
    remote(mod.at[1 - c], mod.at[1 - c], m_send.at[0], m_recv.at[6], sibling).wait_recv()

    item = item_mask(lengths, tokens.shape)
    residual = wide_float(tokens[...])
    normed, _ = norm(residual)
    attn_in[...] = low(normed * (1.0 + own_modulation(here, mod, item, 0, 1)) + own_modulation(here, mod, item, 0, 0))
    grad[...] = low(wide_float(cotangent[...]) * own_modulation(here, mod, item, 1, 2))
    for step in (0,) + LINE:
        gather_third(gathers, step)
    for gather in gathers:
        gather.finish()
    keep = [pltpu.make_async_copy(q_full, qkv_w, l_sem.at[4]), pltpu.make_async_copy(o_full, out_w, l_sem.at[5])]
    for copy in keep:
        copy.start()

    cut = q_full.shape[2]
    for h in (0, 1):
        qkv[:, h * cut : (h + 1) * cut] = low(nn(attn_in[...], q_full[h]))

    for copy in local:
        copy.wait()
    for i, o in enumerate([(0, 0, 0)] + [o for step in (0, 1, 3, 2) for o in plane if o[1] == step]):
        _, sz, sx = spot(*o)
        source = 2 * sz + sx
        block = w1.at[:, strip(2 * source + c), :]
        if i:
            remote(block, block, a_send.at[0], a_recv.at[source], sibling).wait_recv()
        go(remote(block, block, a_pair_send.at[i], a_pair.at[source], sibling))
    for o in others:
        n = chip(*spot(*o))
        remote(s_got.at[c, n], s_got.at[c, n], b_send.at[0], b_recv.at[n], sibling).wait_recv()
    go(remote(s_got.at[c], s_got.at[c], b_pair.at[0], b_pair.at[1], sibling))

    side = wide_float(item[:, :128])
    same = side == side.T
    left, sides = head_lanes()
    for pair in range(model // 128):
        q, key, value = [qkv[:, base + 128 * pair : base + 128 * (pair + 1)] for base in (0, model, 2 * model)]
        outs = []
        for j, side in enumerate(sides):
            scores = jnp.where(same, nt(q * side, key) * 0.125, -1e30)
            weight = jnp.exp(scores - jnp.max(scores, axis=-1, keepdims=True))
            prob = weight / jnp.sum(weight, axis=-1, keepdims=True)
            probs[2 * pair + j] = prob
            outs.append(nn(low(prob), value))
        attn_low[:, 128 * pair : 128 * (pair + 1)] = low(jnp.where(left, outs[0], outs[1]))
    cut = model // 2
    for h in (0, 1):
        attn_proj[:, h * cut : (h + 1) * cut] = nn(attn_low[...], o_full[h, :, :cut])
    middle[...] = residual + own_modulation(here, mod, item, 0, 2) * attn_proj[...]
    normed, _ = norm(middle[...])
    mixed[...] = low(normed * (1.0 + own_modulation(here, mod, item, 1, 1)) + own_modulation(here, mod, item, 1, 0))
    lane = lax.broadcasted_iota(jnp.int32, (1, 128), 1)
    logits = jnp.where(lane < 8, nn(mixed[...], o_full[0, :, cut:]), -1e30)
    weight = jnp.exp(logits - jnp.max(logits, axis=-1, keepdims=True))
    chance[...] = weight / jnp.sum(weight, axis=-1, keepdims=True)
    turned = jnp.where(choices(routes, square), chance[...], 0.0).T[:8]
    high = low(turned)
    gates[...] = jnp.concatenate([high, low(turned - wide_float(high))], axis=0)

    for copy in keep:
        copy.wait()
    for copy in started:
        copy.wait_send()
    for source in range(8):
        block = w1.at[:, strip(2 * source + 1 - c), :]
        remote(block, block, a_send.at[0], a_pair.at[source], sibling).wait_recv()
    remote(s_got.at[1 - c], s_got.at[1 - c], b_pair.at[0], b_pair.at[1], sibling).wait_recv()
    for n in range(32):
        s_rows[n * rows : (n + 1) * rows, :] = wide_float(s_got[n % 2, n // 2])[:rows]
    w1s[...] = low(s_rows[...])
    remote(w2.at[:, at2(1 - c), :], w2.at[:, at2(1 - c), :], d_send.at[0], d_recv.at[0], sibling).wait_recv()
    remote(w2s.at[at2s(1 - c), :], w2s.at[at2s(1 - c), :], d_send.at[1], d_recv.at[1], sibling).wait_recv()


def front(lengths, tokens, cotangent, routes, condition, w_ada, w_qkv, w_out, w_router, w_fc1, w_fc2, e_fc1, e_fc2):
    rows, model = w_out.shape
    toks = tokens.shape[0]
    y, z, x, c = place()
    cond = condition.astype(jnp.float32).reshape(-1, 32, rows).transpose(1, 0, 2)
    spot = jnp.arange(8) == (4 * x + 2 * c + jnp.arange(2))[:, None]
    cond = jnp.einsum("dir,is->dsr", cond, spot.astype(jnp.float32), precision=precise)
    cond = jnp.pad(cond, ((0, 0), (0, 0), (0, 128 - rows)))
    ff = w_fc1.shape[1]
    slim, wide = ff // 16, ff // 8
    experts = e_fc1.shape[0]
    bf, f32 = jnp.bfloat16, jnp.float32
    shape = jax.ShapeDtypeStruct
    q_half, o_half, a_half = w_qkv.shape[1] // 2, w_out.shape[1] // 2 + 128, w_ada.shape[1] // 2
    result = pl.pallas_call(
        front_kernel,
        out_shape=(
            shape((experts, model, wide), bf),
            shape((model, slim), bf),
            shape((experts, 2 * e_fc2.shape[1], model), bf),
            shape((2 * w_fc2.shape[0], model), bf),
            shape((2, model, q_half), bf),
            shape((2, model, o_half), bf),
            shape((64, 128), f32),
            shape((2, 16, a_half), f32),
            shape((toks, model), bf),
            shape((toks, model), bf),
            shape((16, toks), bf),
            shape((toks, model), bf),
            shape((toks, 3 * model), bf),
            shape((HEADS, toks, toks), f32),
            shape((toks, model), bf),
            shape((toks, model), f32),
            shape((toks, model), f32),
            shape((toks, 128), f32),
        ),
        in_specs=[pl.BlockSpec(memory_space=pltpu.SMEM)]
        + [pl.BlockSpec(memory_space=VMEM)] * 9
        + [pl.BlockSpec(memory_space=ANY)] * 3,
        out_specs=[pl.BlockSpec(memory_space=ANY), pl.BlockSpec(memory_space=VMEM)]
        + [pl.BlockSpec(memory_space=ANY)] * 4
        + [pl.BlockSpec(memory_space=VMEM)] * 12,
        scratch_shapes=[
            VMEM((128, 128), f32), VMEM((16, 32, slim), bf), VMEM((2, 16, 32, slim), bf), VMEM((model, slim), f32),
            VMEM((2, model, q_half), bf), VMEM((2, model, o_half), bf),
            VMEM((2, rows, q_half), f32), VMEM((2, rows, o_half), f32), VMEM((2 * rows, q_half), f32), VMEM((2 * rows, o_half), f32),
            VMEM((2 * rows, q_half), bf), VMEM((2 * rows, o_half), bf),
            VMEM((32, 8, 128), f32), VMEM((2, 64, a_half), f32), VMEM((64, a_half), f32),
            VMEM((4, 16, a_half), f32), VMEM((3, 16, a_half), f32), VMEM((2, 16, a_half), f32), VMEM((2, 16, a_half), f32),
            DMA((2,)), DMA((2,)), DMA((2, 31)), DMA((2, 16)), DMA((2, 16)), DMA((7,)), DMA((8,)), DMA((8,)), DMA((8,)),
            DMA((15,)), DMA((16,)), DMA((2,)), DMA((6,)), DMA((2,)), DMA((2,)), DMA((31,)), DMA((32,)), DMA((7,)), DMA((7,)),
        ],
        compiler_params=pltpu.CompilerParams(collective_id=1, has_side_effects=True, vmem_limit_bytes=62 << 20),
        name="front",
    )(lengths, tokens, cotangent, routes.T, cond, w_ada, w_qkv, w_out, w_router.T, w_fc1, e_fc1, e_fc2, w_fc2)
    return result


def gelu_both(h):
    root = math.sqrt(2.0 / math.pi)
    square = h * h
    t = jnp.tanh(h * (root + (root * 0.044715) * square))
    half = 0.5 * (1.0 + t)
    slope = half + (0.5 * h) * (1.0 - t * t) * (root + (3.0 * root * 0.044715) * square)
    return h * half, slope


def ffn_chunk(xt, gt, w1, w2, gate, row):
    a, d = gelu_both(nn(xt, w1))
    gi = nt(gt, w2)
    product = None
    if gate is not None:
        product = nt(row, (a * gi).astype(jnp.bfloat16))
        a, d = a * gate, d * gate
    a = a.astype(jnp.bfloat16)
    p = (gi * d).astype(jnp.bfloat16)
    return a, p, nn(a, w2), nt(p, w1), product


def ffn_shared(slots, X, G, w1s, w2s, act_s, pre_s, sums, sums_back):
    toks = X.shape[1]
    xt = jnp.concatenate([X[n] for n in slots], axis=0)
    gt = jnp.concatenate([G[n] for n in slots], axis=0)
    a, p, total, total_back, _ = ffn_chunk(xt, gt, w1s[...], w2s[...], None, None)
    for i, n in enumerate(slots):
        act_s[n] = a[i * toks : (i + 1) * toks]
        pre_s[n] = p[i * toks : (i + 1) * toks]
    sums[...] = total
    sums_back[...] = total_back


def ffn_experts(low, high, slots, X, G, gates, w1, w2, act, pre, sums, sums_back, gc):
    experts, toks, wide = w1.shape[0], X.shape[1], w1.shape[2]
    first = lax.axis_index("gx") * experts
    xt = jnp.concatenate([X[n] for n in slots], axis=0)
    gt = jnp.concatenate([G[n] for n in slots], axis=0)

    def expert(e, product):
        kind = lax.broadcasted_iota(jnp.int32, (16, 128), 0)
        spread = ((kind == first + e) | (kind == first + e + 8)).astype(jnp.bfloat16)
        gate = jnp.concatenate([tn(gates[n], spread) for n in slots], axis=0)
        gate = jnp.concatenate([gate] * (wide // 128), axis=1)
        row = (lax.broadcasted_iota(jnp.int32, (8, wide), 0) == first + e).astype(jnp.bfloat16)
        a, p, total, total_back, more = ffn_chunk(xt, gt, w1[e], w2[e], gate, row)
        for i, n in enumerate(slots):
            act[e, n] = a[i * toks : (i + 1) * toks]
            pre[e, n] = p[i * toks : (i + 1) * toks]
        sums[...] += total
        sums_back[...] += total_back
        return product + more

    product = lax.fori_loop(low, high, expert, jnp.zeros((8, len(slots) * toks), jnp.float32))
    for i, n in enumerate(slots):
        part = product[:, i * toks : (i + 1) * toks]
        gc[n] = part if low == 0 else gc[n] + part


def block_kernel(
    mixed, grad, gates, w1_in, w1s_in, w2_in, w2s_in,
    sum_branch, sum_back, sum_gc, own1, own1s, own2, own2s,
    X, G, gt, w1, w1s, w2, w2s, act, pre, act_s, pre_s, tile_sum, tile_back,
    p_branch, p_back, p_gc, r_branch, r_back, r_gc, d1, d1s, d2, d2s, from1, from1s, from2, from2s,
    l_sem, g_send, g_recv, send, recv, t_send, t_recv,
):
    here = y, z, x, c = place()
    me = chip(y, z, x)
    spot = lambda dy, dz, dx: (1 - y if dy else y, (z + dz) % 4, 1 - x if dx else x)
    sibling = device(y, z, x, 1 - c)
    experts = w1.shape[0]
    meet(cross_partners(here) + [sibling])

    gathers, local = [], []
    for i, (block, full, y_first) in enumerate(((mixed, X, True), (grad, G, False), (gates, gt, True))):
        slot = functools.partial(lambda full, n: full.at[n], full)
        gathers.append(Gather(here, y_first, block, slot, g_send.at[i], g_recv.at[i]))
        local.append(pltpu.make_async_copy(block, slot(me), l_sem.at[i]))
    gather_start(gathers)
    for i, (source, target) in enumerate(((w1_in, w1), (w1s_in, w1s), (w2_in, w2), (w2s_in, w2s))):
        local.append(pltpu.make_async_copy(source, target, l_sem.at[3 + i]))
    for copy in local:
        copy.start()

    def tile(step, part):
        slots = [chip(*spot(dy, step, dx)) for dy in (0, 1) for dx in (0, 1)]
        if part == 0:
            ffn_shared(slots, X, G, w1s, w2s, act_s, pre_s, tile_sum, tile_back)
        low, high = (0, experts // 2) if part == 0 else (experts // 2, experts)
        ffn_experts(low, high, slots, X, G, gt, w1, w2, act, pre, tile_sum, tile_back, p_gc)
        if part == 1:
            toks = X.shape[1]
            for i, n in enumerate(slots):
                at = slice(i * toks, (i + 1) * toks)
                p_branch[n] = tile_sum[at, :].astype(jnp.bfloat16)
                p_back[n] = tile_back[at, :].astype(jnp.bfloat16)

    scatters = []
    for i, (part, got, y_first) in enumerate(((p_branch, r_branch, False), (p_back, r_back, True), (p_gc, r_gc, False))):
        take = functools.partial(lambda ref, n: ref.at[n], part)
        land = functools.partial(lambda ref, n: ref.at[n], got)
        scatters.append(Scatter(here, y_first, take, land, send.at[i], recv.at[i]))

    def back_first(step):
        for scatter in scatters:
            scatter.first(step)

    gather_second(gathers, 0)
    gather_line(gathers, 1)
    gather_second(gathers, 1)
    gather_third(gathers, 0)
    for copy in local:
        copy.wait()
    tile(0, 0)
    gather_line(gathers, 3)
    tile(0, 1)
    gather_third(gathers, 1)
    tile(1, 0)
    gather_second(gathers, 3)
    tile(1, 1)
    gather_line(gathers, 2)
    gather_third(gathers, 3)
    tile(3, 0)
    gather_second(gathers, 2)
    back_first(1)
    tile(3, 1)
    back_first(3)
    gather_third(gathers, 2)
    tile(2, 0)
    tile(2, 1)

    def back_one(step):
        for scatter in scatters:
            scatter.one(1, step)
        for scatter in scatters:
            scatter.one(0, step)

    def back_two(step):
        for scatter in scatters:
            scatter.two(step)

    flat = lambda value: value.reshape(value.shape[0] * value.shape[1], value.shape[2])
    twins = [None] * (2 * experts)

    def weight(e):
        d1[e] = tn(flat(X[...]), flat(pre[e])).astype(jnp.bfloat16).reshape(d1.shape[1:])
        d2[e] = tn(flat(act[e]), flat(G[...])).astype(jnp.bfloat16).reshape(d2.shape[1:])
        for i, (part, got) in enumerate(((d1.at[e, :, 1 - c], from1.at[e]), (d2.at[e, 1 - c], from2.at[e]))):
            twins[2 * e + i] = remote(part, got, t_send.at[2 * e + i], t_recv.at[2 * e + i], sibling)
            twins[2 * e + i].start()

    def home(e):
        twins[2 * e].wait()
        own1[e] = (d1[e, :, c].astype(jnp.float32) + from1[e].astype(jnp.float32)).astype(jnp.bfloat16)
        twins[2 * e + 1].wait()
        own2[e] = d2[e, c].astype(jnp.float32) + from2[e].astype(jnp.float32)

    back_one(1)
    back_first(2)
    back_two(1)
    weight(0)
    back_one(3)
    back_two(3)
    home(0)
    weight(1)
    back_one(2)
    back_first(0)
    back_two(2)
    home(1)
    weight(2)
    home(2)
    weight(3)
    d1s[...] = tn(flat(X[...]), flat(pre_s[...])).reshape(d1s.shape)
    d2s[...] = tn(flat(act_s[...]), flat(G[...])).astype(jnp.bfloat16).reshape(d2s.shape)
    twin1s = remote(d1s.at[:, 1 - c], from1s, t_send.at[2 * experts], t_recv.at[2 * experts], sibling)
    twin2s = remote(d2s.at[1 - c], from2s, t_send.at[2 * experts + 1], t_recv.at[2 * experts + 1], sibling)
    twin1s.start()
    twin2s.start()
    home(3)
    back_one(0)
    twin1s.wait()
    own1s[...] = d1s[:, c] + from1s[...]
    twin2s.wait()
    own2s[...] = d2s[c].astype(jnp.float32) + from2s[...].astype(jnp.float32)
    back_two(0)
    sum_branch[...] = scatters[0].total()
    sum_back[...] = scatters[1].total()
    sum_gc[...] = scatters[2].total()
    for gather in gathers:
        gather.finish()
    for scatter in scatters:
        scatter.finish()


def block(mixed, grad, gates, w1, w1s, w2, w2s):
    bf, f32 = jnp.bfloat16, jnp.float32
    toks, model = mixed.shape
    experts, _, wide = w1.shape
    slim = w1s.shape[1]
    rows = model // 32
    shape = jax.ShapeDtypeStruct
    blocks = lambda *dims: VMEM((16, toks) + dims, bf)
    return pl.pallas_call(
        block_kernel,
        out_shape=[
            shape((toks, model), f32),
            shape((toks, model), f32),
            shape((8, 128), f32),
            shape((experts, 8, 2 * rows, wide), bf),
            shape((16, rows, slim), f32),
            shape((experts, wide // 2, model), f32),
            shape((slim // 2, model), f32),
        ],
        in_specs=[pl.BlockSpec(memory_space=VMEM)] * 3 + [pl.BlockSpec(memory_space=ANY)] * 4,
        out_specs=[pl.BlockSpec(memory_space=VMEM)] * 7,
        scratch_shapes=[
            blocks(model), blocks(model), VMEM((16, 16, 128), bf),
            VMEM(w1.shape, bf), VMEM(w1s.shape, bf), VMEM(w2.shape, bf), VMEM(w2s.shape, bf),
            VMEM((experts, 16, toks, wide), bf), VMEM((experts, 16, toks, wide), bf), blocks(slim), blocks(slim),
            VMEM((4 * toks, model), f32), VMEM((4 * toks, model), f32),
            blocks(model), blocks(model), VMEM((16, 8, 128), f32),
            VMEM((15, toks, model), bf), VMEM((15, toks, model), bf), VMEM((15, 8, 128), f32),
            VMEM((experts, 8, 2, 2 * rows, wide), bf), VMEM((16, 2, rows, slim), f32),
            VMEM((experts, 2, wide // 2, model), bf), VMEM((2, slim // 2, model), bf),
            VMEM((experts, 8, 2 * rows, wide), bf), VMEM((16, rows, slim), f32),
            VMEM((experts, wide // 2, model), bf), VMEM((slim // 2, model), bf),
            DMA((7,)), DMA((3, 15)), DMA((3, 16)), DMA((3, 15)), DMA((3, 15)), DMA((2 * experts + 2,)), DMA((2 * experts + 2,)),
        ],
        compiler_params=pltpu.CompilerParams(collective_id=2, has_side_effects=True, vmem_limit_bytes=62 << 20),
        name="block",
    )(mixed, grad, gates, w1, w1s, w2, w2s)


def rear_kernel(
    lengths, sum_branch, sum_back, sum_gc, tokens, cotangent, routes, mod, conds, mixed, attn_in, qkv, probs, attn_low, attn_proj, middle,
    chance, qkv_in, out_in, part1, part1s,
    output, d_tokens, d_ada, d_qkv, d_out, d_router, own1, own1s,
    square, q_w, o_w, grad_attn, grad_qkv, grad_mid, o_mine, o_got, q_mine, q_got, part_o, part_a, part_b,
    got_o, got_a, got_b, fin, mod_tile, all_mod,
    l_sem, s_send, s_recv, send, recv, g_send, g_recv, g_pair, f_send, f_recv, a_send, a_recv, b_send, b_recv,
):
    here = y, z, x, c = place()
    me, k = chip(y, z, x), 2 * z + x
    sibling = device(y, z, x, 1 - c)
    others = [(dy, dz, dx) for dy in (0, 1) for dz in (0, 1, 2, 3) for dx in (0, 1) if (dy, dz, dx) != (0, 0, 0)]
    plane = [o for o in others if o[0] == 0]
    spot = lambda dy, dz, dx: (1 - y if dy else y, (z + dz) % 4, 1 - x if dx else x)
    local = [pltpu.make_async_copy(qkv_in, q_w, l_sem.at[0]), pltpu.make_async_copy(out_in, o_w, l_sem.at[1])]
    for copy in local:
        copy.start()
    meet([device(*spot(*o), c) for o in others] + [sibling])
    started = []

    def go(copy):
        copy.start()
        started.append(copy)

    wide = part1.shape[3]
    columns = lambda n: own1.at[:, :, pl.ds(pl.multiple_of(wide * n, 128), wide)]
    home = [pltpu.make_async_copy(part1.at[:, k], columns(k), l_sem.at[2]), pltpu.make_async_copy(part1s.at[me], own1s.at[me], l_sem.at[3])]
    for copy in home:
        copy.start()
    for i, o in enumerate(plane):
        ty, tz, tx = spot(*o)
        go(remote(part1.at[:, 2 * tz + tx], columns(k), a_send.at[i], a_recv.at[k], device(ty, tz, tx, c)))
    for i, o in enumerate(others):
        go(remote(part1s.at[chip(*spot(*o))], own1s.at[me], b_send.at[i], b_recv.at[me], device(*spot(*o), c)))

    item = item_mask(lengths, tokens.shape)
    first = ~item
    model = item.shape[1]
    cut = model // 2
    modulation = functools.partial(own_modulation, here, mod, item)
    rows16 = {}

    def per_item(part, value):
        for i, mask in enumerate((first, ~first)):
            rows16[2 * part + i] = jnp.sum(jnp.where(mask, value, 0.0), axis=0, keepdims=True)

    out_grad = wide_float(cotangent[...])
    branch = sum_branch[...]
    output[...] = low(middle[...] + modulation(1, 2) * branch)
    per_item(5, out_grad * branch)
    chosen = choices(routes, square)
    turned = jnp.concatenate([sum_gc[...], jnp.zeros((120, 128), jnp.float32)], axis=0).T
    grad_chance = jnp.where(chosen, turned, 0.0)
    share = chance[...]
    grad_logits = low(share * (grad_chance - jnp.sum(grad_chance * share, axis=-1, keepdims=True)))
    term_router = tn(mixed[...], grad_logits)
    for copy in local:
        copy.wait()
    grad_mixed = sum_back[...] + nt(grad_logits, o_w[0, :, cut:])
    normed, scale = norm(middle[...])
    per_item(3, grad_mixed)
    per_item(4, grad_mixed * normed)
    grad_mid[...] = out_grad + norm_back(grad_mixed * (1.0 + modulation(1, 1)), normed, scale)
    per_item(2, grad_mid[...] * attn_proj[...])
    grad_proj = low(grad_mid[...] * modulation(0, 2))
    for h in (0, 1):
        term = jnp.concatenate([tn(attn_low[...], grad_proj[:, h * cut : (h + 1) * cut]), term_router], axis=1)
        o_mine[h] = low(term)
    swap_o = remote(o_mine.at[1 - c], o_got, s_send.at[0], s_recv.at[0], sibling)
    swap_o.start()
    grad_attn[...] = low(nt(grad_proj[:, :cut], o_w[0, :, :cut]) + nt(grad_proj[:, cut:], o_w[1, :, :cut]))

    rows = o_got.shape[0] // 16
    scatters = []
    for i, (part, got, y_first) in enumerate(((part_o, got_o, False), (part_a, got_a, True), (part_b, got_b, False))):
        take = functools.partial(lambda ref, n: ref.at[n], part)
        land = functools.partial(lambda ref, n: ref.at[n], got)
        scatters.append(Scatter(here, y_first, take, land, send.at[i], recv.at[i]))

    def out_stage(stage):
        tool = scatters[0]
        if stage == 0:
            swap_o.wait()
            for n in range(16):
                at = slice(n * rows, (n + 1) * rows)
                part_o[n] = low(wide_float(o_mine[c, at, :]) + wide_float(o_got[at, :]))
            for step in (2, 1, 3, 0):
                tool.first(step)
        else:
            for step in ((2,), (1, 3), (0,))[stage - 1]:
                tool.one(1, step)
                tool.one(0, step)
        if stage > 1:
            for step in ((2,), (1, 3))[stage - 2]:
                tool.two(step)

    left, sides = head_lanes()
    for pair in range(model // 128):
        at = slice(128 * pair, 128 * (pair + 1))
        q, key, value = [qkv[:, base + 128 * pair : base + 128 * (pair + 1)] for base in (0, model, 2 * model)]
        ga = grad_attn[:, at]
        outs = []
        for j, side in enumerate(sides):
            prob = probs[2 * pair + j]
            grad_probs = nt(ga * side, value)
            grad_scores = low(prob * (grad_probs - jnp.sum(grad_probs * prob, axis=-1, keepdims=True)))
            outs.append((nn(grad_scores, key) * 0.125, tn(grad_scores, q) * 0.125, tn(low(prob), ga)))
        for base, one, two in zip((0, model, 2 * model), *outs):
            grad_qkv[:, base + 128 * pair : base + 128 * (pair + 1)] = low(jnp.where(left, one, two))
        if pair in (1, 3, 5):
            out_stage(pair // 2)

    third = q_w.shape[2]
    for h in (0, 1):
        q_mine[h] = low(tn(attn_in[...], grad_qkv[:, h * third : (h + 1) * third]))
    swap_q = remote(q_mine.at[1 - c], q_got, s_send.at[1], s_recv.at[1], sibling)
    swap_q.start()
    out_stage(3)
    grad_in = nt(grad_qkv[:, :third], q_w[0]) + nt(grad_qkv[:, third:], q_w[1])
    normed, scale = norm(wide_float(tokens[...]))
    per_item(0, grad_in)
    per_item(1, grad_in * normed)
    d_tokens[...] = grad_mid[...] + norm_back(grad_in * (1.0 + modulation(0, 1)), normed, scale)
    rows16[12] = jnp.zeros((4, model), jnp.float32)
    mod_tile[...] = low(jnp.concatenate([rows16[i] for i in range(13)], axis=0))

    slot = lambda n: all_mod.at[n, c]
    spread = Gather(here, True, mod_tile, slot, g_send, g_recv, g_pair)
    all_mod[me, c] = mod_tile[...]
    gather_start([spread])
    swap_q.wait()
    edge = part_a.shape[2]
    for n in range(16):
        at = slice(n * rows, (n + 1) * rows)
        total = low(wide_float(q_mine[c, at, :]) + wide_float(q_got[at, :]))
        part_a[n] = total[:, :edge]
        part_b[n] = total[:, edge:]

    def turn(at):
        if at == 0:
            scatters[0].two(0)
            spread.second(0)
            for step in LINE:
                gather_line([spread], step)
        elif at == 1:
            for step in LINE:
                spread.second(step)
        elif at == 2:
            for step in (0,) + LINE:
                spread.third(step)
            spread.finish()

    scatter_all(scatters[1:], turn)
    fin[c] = jnp.concatenate([scatters[1].total(), scatters[2].total(), scatters[0].total()], axis=1)
    half = rows // 2
    mine = pl.ds(pl.multiple_of(half * c, 8), half)
    theirs = pl.ds(pl.multiple_of(half * (1 - c), 8), half)
    swap = remote(fin.at[c, theirs, :], fin.at[c, theirs, :], f_send, f_recv, sibling)
    swap.start()

    flat = all_mod[...].reshape(32 * 16, model)
    row = lax.broadcasted_iota(jnp.int32, (64, 512), 1)
    spot_of = row // 16
    place_of = 16 * ((spot_of // 4) % 4) + 8 * (spot_of // 16) + 4 * ((spot_of // 2) % 2) + 2 * (spot_of % 2) + row % 2
    meets = lax.broadcasted_iota(jnp.int32, (64, 512), 0) == place_of
    columns_in = low(conds[...])
    for part in range(6):
        pick = low(wide_float(meets & ((row % 16) // 2 == part)))
        lhs = low(tn(columns_in, pick))
        d_ada[:, part * model : (part + 1) * model] = nn(lhs, flat)[: d_ada.shape[0]]

    for i, o in enumerate(plane):
        n = 2 * spot(*o)[1] + spot(*o)[2]
        remote(columns(n), columns(n), a_send.at[i], a_recv.at[n], sibling).wait_recv()
    for copy in home:
        copy.wait()
    for i, o in enumerate(others):
        n = chip(*spot(*o))
        remote(own1s.at[n], own1s.at[n], b_send.at[i], b_recv.at[n], sibling).wait_recv()
    for scatter in scatters:
        scatter.finish()
    for copy in started:
        copy.wait_send()
    swap.wait_send()
    remote(fin.at[1 - c, mine, :], fin.at[1 - c, mine, :], f_send, f_recv, sibling).wait_recv()
    for h in (0, 1):
        d_qkv[:, h * third : (h + 1) * third] = fin[h, mine, :third]
        d_out[:, h * cut : (h + 1) * cut] = fin[h, mine, third : third + cut]
    d_router[0:half, :] = fin[0, mine, third + cut :]
    d_router[half:, :] = jnp.zeros((128 - half, 128), jnp.float32)


def rear(lengths, sums, tokens, cotangent, routes, saved, qkv_w, out_w, part1, part1s):
    bf, f32 = jnp.bfloat16, jnp.float32
    toks, model = tokens.shape
    rows = model // 16
    experts, _, depth, wide = part1.shape
    q_half, o_half = qkv_w.shape[2], out_w.shape[2]
    a_half = model
    shape = jax.ShapeDtypeStruct
    return pl.pallas_call(
        rear_kernel,
        out_shape=[
            shape((toks, model), bf),
            shape((toks, model), f32),
            shape((rows // 2, 6 * model), f32),
            shape((rows // 2, 2 * q_half), f32),
            shape((rows // 2, model), f32),
            shape((128, 128), f32),
            shape((experts, depth, 8 * wide), bf),
            shape(part1s.shape, f32),
        ],
        in_specs=[pl.BlockSpec(memory_space=pltpu.SMEM)]
        + [pl.BlockSpec(memory_space=VMEM)] * 16
        + [pl.BlockSpec(memory_space=ANY)] * 4,
        out_specs=[pl.BlockSpec(memory_space=VMEM)] * 6 + [pl.BlockSpec(memory_space=ANY)] * 2,
        scratch_shapes=[
            VMEM((128, 128), f32), VMEM(qkv_w.shape, bf), VMEM(out_w.shape, bf),
            VMEM((toks, model), bf), VMEM((toks, 3 * model), bf), VMEM((toks, model), f32),
            VMEM((2, model, o_half), bf), VMEM((model, o_half), bf),
            VMEM((2, model, q_half), bf), VMEM((model, q_half), bf),
            VMEM((16, rows, o_half), bf), VMEM((16, rows, a_half), bf), VMEM((16, rows, q_half - a_half), bf),
            VMEM((15, rows, o_half), bf), VMEM((15, rows, a_half), bf), VMEM((15, rows, q_half - a_half), bf),
            VMEM((2, rows, q_half + o_half), f32), VMEM((16, model), bf), VMEM((16, 2, 16, model), bf),
            DMA((4,)), DMA((2,)), DMA((2,)), DMA((3, 15)), DMA((3, 15)), DMA((31,)), DMA((16,)), DMA((16,)), DMA, DMA,
            DMA((7,)), DMA((8,)), DMA((15,)), DMA((16,)),
        ],
        compiler_params=pltpu.CompilerParams(collective_id=3, has_side_effects=True, vmem_limit_bytes=62 << 20),
        name="rear",
    )(lengths, *sums, tokens, cotangent, routes.T, *saved, qkv_w, out_w, part1, part1s)


def finish_kernel(*refs):
    count = (len(refs) - 4) // 3
    inputs, outputs, staged = refs[:count], refs[count : 2 * count], refs[2 * count : 3 * count]
    e1, fc1, sem_in, sem = refs[3 * count :]
    loads = [pltpu.make_async_copy(a, b, sem_in.at[i]) for i, (a, b) in enumerate(zip(inputs, staged))]
    stores = []

    def store(source, target):
        stores.append(pltpu.make_async_copy(source, target, sem.at[len(stores)]))
        stores[-1].start()

    for copy in loads:
        copy.start()
    low_e1, slices, router = staged[:3]
    loads[0].wait()
    for e in range(low_e1.shape[0]):
        e1[e] = wide_float(low_e1[e])
        store(e1.at[e], outputs[0].at[e])
    for load, source, target in zip(loads[3:], staged[3:], outputs[3:]):
        load.wait()
        store(source, target)
    loads[1].wait()
    loads[2].wait()
    slim = slices.shape[2]
    for n in range(slices.shape[0] // 2):
        fc1[:, 2 * n * slim : 2 * (n + 1) * slim] = jnp.concatenate([slices[2 * n], slices[2 * n + 1]], axis=1)
    store(fc1, outputs[1])
    outputs[2][...] = router[...].T[: outputs[2].shape[0]]
    for copy in stores:
        copy.wait()


def finish(own1, own1s, d_router, *others):
    f32 = jnp.float32
    rows = own1s.shape[1]
    wide = (rows, own1s.shape[0] * own1s.shape[2])
    shape = jax.ShapeDtypeStruct
    result = pl.pallas_call(
        finish_kernel,
        out_shape=[shape(own1.shape, f32), shape(wide, f32), shape((8, 128), f32)] + [shape(a.shape, a.dtype) for a in others],
        in_specs=[pl.BlockSpec(memory_space=ANY)] * (3 + len(others)),
        out_specs=[pl.BlockSpec(memory_space=ANY)] * 2
        + [pl.BlockSpec(memory_space=VMEM)]
        + [pl.BlockSpec(memory_space=ANY)] * len(others),
        scratch_shapes=[VMEM(a.shape, a.dtype) for a in (own1, own1s, d_router, *others)]
        + [VMEM(own1.shape, f32), VMEM(wide, f32), DMA((3 + len(others),)), DMA((8 + len(others),))],
        compiler_params=pltpu.CompilerParams(vmem_limit_bytes=62 << 20),
        name="finish",
    )(own1, own1s, d_router, *others)
    return result[0], result[1], result[2][:, :rows].T, *result[3:]


def layer_norm(values):
    average = jnp.mean(values, axis=-1, keepdims=True)
    centred = values - average
    return centred * lax.rsqrt(jnp.mean(centred * centred, axis=-1, keepdims=True) + layer_epsilon)


def modulate(values, shift_by, scale_by):
    return layer_norm(values) * (1.0 + scale_by) + shift_by


def sinusoid(timesteps, model_width):
    half_width = model_width // 2
    frequency = jnp.exp(-math.log(10000.0) * jnp.arange(half_width, dtype=jnp.float32) / half_width)
    angles = timesteps.astype(jnp.float32)[:, None] * frequency[None, :]
    return jnp.concatenate([jnp.cos(angles), jnp.sin(angles)], axis=1)


def membership(lengths, tok_count):
    bounds = jnp.cumsum(lengths)[:-1]
    position = jnp.arange(tok_count, dtype=jnp.int32)
    item_of = jnp.sum((position[:, None] >= bounds[None, :]).astype(jnp.int32), axis=1)
    item_ids = jnp.arange(lengths.shape[0], dtype=jnp.int32)
    return ((item_of[:, None] == item_ids[None, :]).astype(jnp.float32), item_of)


def slot_index(routes, expert_count, capacity):
    flat_routes = routes.reshape(-1)
    expert_hot = (
        flat_routes[:, None] == jnp.arange(expert_count, dtype=jnp.int32)[None, :]
    ).astype(jnp.int32)
    before = jnp.cumsum(expert_hot, axis=0) - expert_hot
    rank_in = jnp.sum(before * expert_hot, axis=1)
    return (flat_routes * capacity + rank_in).reshape(routes.shape)


def dot_float(left_side, right_side):
    return jnp.dot(left_side, right_side, preferred_element_type=jnp.float32)


def dot_rows(left_side, right_side):
    return jnp.einsum("td,tf->df", left_side, right_side, preferred_element_type=jnp.float32)


def dot_cols(left_side, right_side):
    return jnp.einsum("tf,df->td", left_side, right_side, preferred_element_type=jnp.float32)


def dot_halves(left_side, halves):
    return jnp.concatenate([dot_float(left_side, halves[0]), dot_float(left_side, halves[1])], axis=1)


def by_slices(
    tokens, timesteps, lengths, routes, cotangent, w_ada, w_qkv, w_out, w_fc1, w_fc2, w_router, e_fc1, e_fc2
):
    model_width = tokens.shape[1]
    condition = jax.nn.silu(sinusoid(timesteps, model_width)).astype(jnp.bfloat16)
    (w1, w1s, w2, w2s, qkv_w, out_w, conds, mod, mixed, grad, gates, attn_in, qkv, probs, attn_low, attn_proj, middle,
     chance) = front(
        lengths, tokens, cotangent, routes, condition, w_ada, w_qkv, w_out, w_router, w_fc1, w_fc2, e_fc1, e_fc2
    )
    *sums, part1, part1s, d_e2, d_fc2 = block(mixed, grad, gates, w1, w1s, w2, w2s)
    saved = (mod, conds, mixed, attn_in, qkv, probs, attn_low, attn_proj, middle, chance)
    output, d_tokens, d_ada, d_qkv, d_out, d_router, own1, own1s = rear(
        lengths, sums, tokens, cotangent, routes, saved, qkv_w, out_w, part1, part1s
    )
    d_e1, d_fc1, d_router, output, d_tokens, d_ada, d_qkv, d_out, d_fc2, d_e2 = finish(
        own1, own1s, d_router, output, d_tokens, d_ada, d_qkv, d_out, d_fc2, d_e2
    )
    return (output, d_tokens, d_ada, d_qkv, d_out, d_fc1, d_fc2, d_router, d_e1, d_e2)


def by_weights(
    tokens,
    timesteps,
    lengths,
    routes,
    cotangent,
    w_ada,
    w_qkv,
    w_out,
    w_fc1,
    w_fc2,
    w_router,
    e_fc1,
    e_fc2,
):
    tok_count, model_width = tokens.shape
    head_count = HEADS
    head_size = model_width // head_count
    expert_count = w_router.shape[1]
    capacity = CAP
    score_scale = head_size ** (-0.5)
    residual = tokens.astype(jnp.float32)
    member, item_of = membership(lengths[0], tok_count)
    ada_full, qkv_full, out_full = (
        lax.all_gather(w_ada, ("gx", "gy"), axis=0, tiled=True),
        lax.all_gather(w_qkv, ("gx", "gy"), axis=0, tiled=True),
        lax.all_gather(w_out, ("gx", "gy"), axis=0, tiled=True),
    )
    condition = jax.nn.silu(sinusoid(timesteps, model_width)).astype(jnp.bfloat16)
    modulation = dot_float(condition, ada_full)
    token_mod = jnp.dot(member, modulation, precision=precise)
    shift_attn, scale_attn, gate_attn, shift_mlp, scale_mlp, gate_mlp = jnp.split(
        token_mod, 6, axis=1
    )
    attn_in = modulate(residual, shift_attn, scale_attn).astype(jnp.bfloat16)
    qkv_low = dot_float(attn_in, qkv_full).astype(jnp.bfloat16)
    queries, key_rows, value_rows = [
        portion.reshape(tok_count, head_count, head_size)
        for portion in jnp.split(qkv_low, 3, axis=1)
    ]
    same_item = item_of[:, None] == item_of[None, :]
    scores = (
        jnp.einsum("qhd,khd->hqk", queries, key_rows, preferred_element_type=jnp.float32)
        * score_scale
    )
    scores = jnp.where(same_item[None], scores, -1e30)
    attn_probs = jax.nn.softmax(scores, axis=-1)
    probs_low = attn_probs.astype(jnp.bfloat16)
    attn_low = jnp.einsum("hqk,khd->qhd", probs_low, value_rows, preferred_element_type=jnp.float32)
    attn_low = attn_low.reshape(tok_count, model_width).astype(jnp.bfloat16)
    attn_proj = dot_float(attn_low, out_full)
    middle = residual + gate_attn * attn_proj
    mixed_in = modulate(middle, shift_mlp, scale_mlp).astype(jnp.bfloat16)
    fc1_full, fc2_full, router_full = (
        lax.all_gather(w_fc1, ("gx", "gy"), axis=0, tiled=True),
        lax.all_gather(w_fc2, ("gx", "gy"), axis=0, tiled=True),
        lax.all_gather(w_router, ("gx", "gy"), axis=0, tiled=True),
    )
    hidden_pre = dot_float(mixed_in, fc1_full)
    hidden = jax.nn.gelu(hidden_pre).astype(jnp.bfloat16)
    shared = dot_float(hidden, fc2_full)
    chance = jax.nn.softmax(dot_float(mixed_in, router_full), axis=-1)
    expert_ids = jnp.arange(expert_count, dtype=jnp.int32)
    chosen = (routes[:, :, None] == expert_ids[None, None, :]).astype(jnp.float32)
    gate_values = jnp.sum(chosen * chance[:, None, :], axis=2)
    slot_of = slot_index(routes, expert_count, capacity)
    slot_ids = jnp.arange(expert_count * capacity, dtype=jnp.int32)
    selector = (slot_of[:, :, None] == slot_ids[None, None, :]).astype(jnp.bfloat16)
    slot_rows = jnp.einsum("tks,td->sd", selector, mixed_in, preferred_element_type=jnp.float32)
    slot_rows = slot_rows.astype(jnp.bfloat16).reshape(expert_count, capacity, model_width)
    owned_rows = lax.all_to_all(slot_rows, "gx", split_axis=0, concat_axis=1, tiled=True)
    expert_in, expert_back = (
        lax.all_gather(e_fc1, "gy", axis=1, tiled=True),
        lax.all_gather(e_fc2, "gy", axis=1, tiled=True),
    )
    inner_pre = jnp.einsum(
        "ecd,edf->ecf", owned_rows, expert_in, preferred_element_type=jnp.float32
    )
    inner_act = jax.nn.gelu(inner_pre).astype(jnp.bfloat16)
    result = jnp.einsum(
        "ecf,efd->ecd", inner_act, expert_back, preferred_element_type=jnp.float32
    ).astype(jnp.bfloat16)
    returned = lax.all_to_all(result, "gx", split_axis=1, concat_axis=0, tiled=True).reshape(
        expert_count * capacity, model_width
    )
    picked = jnp.take(returned, slot_of, axis=0).astype(jnp.float32)
    branch = shared + jnp.sum(gate_values[:, :, None] * picked, axis=1)
    output = (middle + gate_mlp * branch).astype(jnp.bfloat16)
    out_grad = cotangent.astype(jnp.float32)
    grad_gate_mlp = out_grad * branch
    grad_branch = out_grad * gate_mlp
    grad_shared = grad_branch.astype(jnp.bfloat16)
    grad_picked = (gate_values[:, :, None] * grad_branch[:, None, :]).astype(jnp.bfloat16)
    grad_gates = jnp.sum(grad_branch[:, None, :] * picked, axis=2)
    grad_slots = jnp.einsum(
        "tks,tkd->sd", selector, grad_picked, preferred_element_type=jnp.float32
    )
    grad_slots = grad_slots.astype(jnp.bfloat16).reshape(expert_count, capacity, model_width)
    grad_owned = lax.all_to_all(grad_slots, "gx", split_axis=0, concat_axis=1, tiled=True)
    grad_inner = jnp.einsum(
        "ecd,efd->ecf", grad_owned, expert_back, preferred_element_type=jnp.float32
    )
    unused_inner, gelu_expert = jax.vjp(jax.nn.gelu, inner_pre)
    grad_inner_pre = gelu_expert(grad_inner)[0].astype(jnp.bfloat16)
    term_e_out = jnp.einsum(
        "ecf,ecd->efd", inner_act, grad_owned, preferred_element_type=jnp.float32
    )
    term_e_in = jnp.einsum(
        "ecd,ecf->edf", owned_rows, grad_inner_pre, preferred_element_type=jnp.float32
    )
    grad_rows = jnp.einsum(
        "ecf,edf->ecd", grad_inner_pre, expert_in, preferred_element_type=jnp.float32
    )
    grad_returned = (
        lax.all_to_all(
            grad_rows.astype(jnp.bfloat16), "gx", split_axis=1, concat_axis=0, tiled=True
        )
        .astype(grad_rows.dtype)
        .reshape(expert_count * capacity, model_width)
    )
    sum_e_in, sum_e_out = (
        lax.psum_scatter(
            term_e_in.astype(jnp.bfloat16), "gy", scatter_dimension=1, tiled=True
        ).astype(jnp.float32),
        lax.psum_scatter(
            term_e_out.astype(jnp.bfloat16), "gy", scatter_dimension=1, tiled=True
        ).astype(jnp.float32),
    )
    grad_chance = jnp.sum(chosen * grad_gates[:, :, None], axis=1)
    grad_logits = chance * (grad_chance - jnp.sum(grad_chance * chance, axis=-1, keepdims=True))
    grad_logits = grad_logits.astype(jnp.bfloat16)
    grad_hidden = dot_cols(grad_shared, fc2_full)
    unused_shared, gelu_shared = jax.vjp(jax.nn.gelu, hidden_pre)
    grad_hidden_pre = gelu_shared(grad_hidden)[0].astype(jnp.bfloat16)
    term_fc2 = dot_rows(hidden, grad_shared)
    term_fc1 = dot_rows(mixed_in, grad_hidden_pre)
    term_router = dot_rows(mixed_in, grad_logits)
    part_fc1, part_fc2, part_router = (
        lax.psum_scatter(
            term_fc1.astype(jnp.bfloat16), "gx", scatter_dimension=0, tiled=True
        ).astype(jnp.float32),
        lax.psum_scatter(
            term_fc2.astype(jnp.bfloat16), "gx", scatter_dimension=0, tiled=True
        ).astype(jnp.float32),
        lax.psum_scatter(
            term_router.astype(jnp.bfloat16), "gx", scatter_dimension=0, tiled=True
        ).astype(jnp.float32),
    )
    sum_fc1, sum_fc2, sum_router = (
        lax.psum_scatter(
            part_fc1.astype(jnp.bfloat16), "gy", scatter_dimension=0, tiled=True
        ).astype(jnp.float32),
        lax.psum_scatter(
            part_fc2.astype(jnp.bfloat16), "gy", scatter_dimension=0, tiled=True
        ).astype(jnp.float32),
        lax.psum_scatter(
            part_router.astype(jnp.bfloat16), "gy", scatter_dimension=0, tiled=True
        ).astype(jnp.float32),
    )
    grad_mixed = dot_cols(grad_hidden_pre, fc1_full) + dot_cols(grad_logits, router_full)
    grad_mixed = grad_mixed + jnp.sum(jnp.take(grad_returned, slot_of, axis=0), axis=1)
    unused_mix, mix_back = jax.vjp(modulate, middle, shift_mlp, scale_mlp)
    grad_mid_norm, grad_shift_mlp, grad_scale_mlp = mix_back(grad_mixed)
    grad_middle = out_grad + grad_mid_norm
    grad_gate_attn = grad_middle * attn_proj
    grad_proj = (grad_middle * gate_attn).astype(jnp.bfloat16)
    term_out = dot_rows(attn_low, grad_proj)
    grad_attn = (
        dot_cols(grad_proj, out_full).astype(jnp.bfloat16).reshape(tok_count, head_count, head_size)
    )
    grad_probs = jnp.einsum(
        "qhd,khd->hqk", grad_attn, value_rows, preferred_element_type=jnp.float32
    )
    grad_values = jnp.einsum(
        "hqk,qhd->khd", probs_low, grad_attn, preferred_element_type=jnp.float32
    )
    grad_scores = attn_probs * (
        grad_probs - jnp.sum(grad_probs * attn_probs, axis=-1, keepdims=True)
    )
    grad_scores = grad_scores.astype(jnp.bfloat16)
    grad_queries = (
        jnp.einsum("hqk,khd->qhd", grad_scores, key_rows, preferred_element_type=jnp.float32)
        * score_scale
    )
    grad_keys = (
        jnp.einsum("hqk,qhd->khd", grad_scores, queries, preferred_element_type=jnp.float32)
        * score_scale
    )
    grad_qkv = jnp.concatenate(
        [
            grad_queries.reshape(tok_count, model_width),
            grad_keys.reshape(tok_count, model_width),
            grad_values.reshape(tok_count, model_width),
        ],
        axis=1,
    ).astype(jnp.bfloat16)
    term_qkv = dot_rows(attn_in, grad_qkv)
    grad_attn_in = dot_cols(grad_qkv, qkv_full)
    unused_pre, pre_back = jax.vjp(modulate, residual, shift_attn, scale_attn)
    grad_input_norm, grad_shift_attn, grad_scale_attn = pre_back(grad_attn_in)
    d_tokens = grad_middle + grad_input_norm
    grad_token_mod = jnp.concatenate(
        [
            grad_shift_attn,
            grad_scale_attn,
            grad_gate_attn,
            grad_shift_mlp,
            grad_scale_mlp,
            grad_gate_mlp,
        ],
        axis=1,
    )
    grad_modulation = jnp.einsum("ti,tc->ic", member, grad_token_mod, precision=precise).astype(
        jnp.bfloat16
    )
    all_condition, all_modgrad = (
        lax.all_gather(condition, ("gx", "gy"), axis=0, tiled=True),
        lax.all_gather(grad_modulation, ("gx", "gy"), axis=0, tiled=True),
    )
    own_share = model_width // lax.axis_size(("gx", "gy"))
    own_start = lax.axis_index(("gx", "gy")) * own_share
    own_condition = lax.dynamic_slice_in_dim(all_condition, own_start, own_share, 1)
    owned_ada = dot_rows(own_condition, all_modgrad)
    attn_terms = (term_qkv, term_out)
    attn_parts = (
        lax.psum_scatter(
            attn_terms[0].astype(jnp.bfloat16), "gx", scatter_dimension=0, tiled=True
        ).astype(jnp.float32),
        lax.psum_scatter(
            attn_terms[1].astype(jnp.bfloat16), "gx", scatter_dimension=0, tiled=True
        ).astype(jnp.float32),
    )
    attn_sums = (
        lax.psum_scatter(
            attn_parts[0].astype(jnp.bfloat16), "gy", scatter_dimension=0, tiled=True
        ).astype(jnp.float32),
        lax.psum_scatter(
            attn_parts[1].astype(jnp.bfloat16), "gy", scatter_dimension=0, tiled=True
        ).astype(jnp.float32),
    )
    sum_qkv, sum_out = attn_sums
    return (
        output,
        d_tokens,
        owned_ada,
        sum_qkv,
        sum_out,
        sum_fc1,
        sum_fc2,
        sum_router,
        sum_e_in,
        sum_e_out,
    )


def solution(mesh):
    in_specs = (
        P(("gx", "gy"), None),
        P(("gx", "gy")),
        P(("gx", "gy"), None),
        P(("gx", "gy"), None),
        P(("gx", "gy"), None),
        P(("gx", "gy"), None),
        P(("gx", "gy"), None),
        P(("gx", "gy"), None),
        P(("gx", "gy"), None),
        P(("gx", "gy"), None),
        P(("gx", "gy"), None),
        P("gx", "gy", None),
        P("gx", "gy", None),
    )
    out_specs = (
        P(("gx", "gy"), None),
        P(("gx", "gy"), None),
        P(("gx", "gy"), None),
        P(("gx", "gy"), None),
        P(("gx", "gy"), None),
        P(("gx", "gy"), None),
        P(("gx", "gy"), None),
        P(("gx", "gy"), None),
        P("gx", "gy", None),
        P("gx", "gy", None),
    )
    step = by_slices if dict(mesh.shape) == {"gx": 2, "gy": 16} else by_weights
    return jax.shard_map(
        step, mesh=mesh, in_specs=in_specs, out_specs=out_specs, check_vma=False
    )
```

```python
import functools
import math

import jax
import jax.numpy as jnp
from jax import lax
from jax.experimental import pallas as pl
from jax.experimental.pallas import tpu as pltpu
from jax.sharding import PartitionSpec as P

HEADS = 12
CAP = 64
MESH = pl.DeviceIdType.MESH
ANY = pl.ANY
VMEM = pltpu.VMEM
DMA = pltpu.SemaphoreType.DMA
LINE = (1, 2, 3)

precise = lax.Precision.HIGHEST
layer_epsilon = 1e-06


def place():
    gy = lax.axis_index("gy")
    return lax.axis_index("gx"), gy // 4, (gy // 2) % 2, gy % 2


def device(y, z, x, c):
    return (y, 4 * z + 2 * x + c)


def chip(y, z, x):
    return 8 * y + 2 * z + x


def along(z, step):
    return z + step - 2 * (z % 2) * (step % 2) - 4 * (z // 2) * (step // 2)


def meet(partners):
    barrier = pltpu.get_barrier_semaphore()
    for partner in partners:
        pl.semaphore_signal(barrier, inc=1, device_id=partner, device_id_type=MESH)
    pl.semaphore_wait(barrier, len(partners))


def cross_partners(here):
    y, z, x, c = here
    return [device(y, along(z, step), x, c) for step in LINE] + [
        device(1 - y, z, x, c),
        device(y, z, 1 - x, c),
    ]


def remote(source, target, send, recv, to):
    return pltpu.make_async_remote_copy(
        src_ref=source, dst_ref=target, send_sem=send, recv_sem=recv, device_id=to, device_id_type=MESH
    )


class Gather:
    def __init__(self, here, y_first, own, slot, send, recv, pair=None):
        self.here, self.y_first, self.own, self.slot = here, y_first, own, slot
        self.send, self.recv, self.pair, self.started = send, recv, pair, []

    def number(self, a, step, b):
        y, z, x, c = self.here
        flip_y, flip_x = (a, b) if self.y_first else (b, a)
        return chip(1 - y if flip_y else y, along(z, step), 1 - x if flip_x else x)

    def copy(self, source, number, to, recv=None):
        recv = self.recv if recv is None else recv
        sent = remote(source, self.slot(number), self.send.at[len(self.started)], recv.at[number], to)
        sent.start()
        self.started.append(sent)

    def to_side(self, source, number, second):
        y, z, x, c = self.here
        self.copy(source, number, device(1 - y, z, x, c) if self.y_first != second else device(y, z, 1 - x, c))

    def to_line(self, source, number, step):
        y, z, x, c = self.here
        self.copy(source, number, device(y, along(z, step), x, c))

    def to_pair(self, source, number):
        y, z, x, c = self.here
        if self.pair is not None:
            self.copy(source, number, device(y, z, x, 1 - c), self.pair)

    def arrive(self, number, recv=None):
        recv = self.recv if recv is None else recv
        block = self.slot(number)
        remote(block, block, self.send.at[0], recv.at[number], device(*self.here)).wait_recv()
        return block

    def start_first(self):
        self.to_side(self.own, self.number(0, 0, 0), False)
        self.to_pair(self.own, self.number(0, 0, 0))

    def start_line(self, step):
        self.to_line(self.own, self.number(0, 0, 0), step)

    def start_last(self):
        self.to_side(self.own, self.number(0, 0, 0), True)

    def line_first(self, step):
        number = self.number(0, step, 0)
        block = self.arrive(number)
        if step == 2:
            self.to_line(block, number, 1)
        self.to_side(block, number, False)
        self.to_pair(block, number)

    def line_last(self, step):
        number = self.number(0, step, 0)
        self.to_side(self.slot(number), number, True)

    def second(self, step):
        number = self.number(1, step, 0)
        block = self.arrive(number)
        self.to_side(block, number, True)
        self.to_pair(block, number)

    def third(self, step):
        for a in (0, 1):
            number = self.number(a, step, 1)
            self.to_pair(self.arrive(number), number)

    def finish(self):
        for sent in self.started:
            sent.wait_send()
        if self.pair is not None:
            for number in range(16):
                self.arrive(number, self.pair)


def gather_start(gathers):
    for gather in gathers:
        gather.start_first()
    for step in (1, 2):
        for gather in gathers:
            gather.start_line(step)
    for gather in gathers:
        gather.start_last()


def gather_line(gathers, step):
    for gather in gathers:
        gather.line_first(step)
    for gather in gathers:
        gather.line_last(step)


def gather_second(gathers, step):
    for gather in gathers:
        gather.second(step)


def gather_third(gathers, step):
    for gather in gathers:
        gather.third(step)


def gather_all(gathers, between=None):
    gather_start(gathers)
    gather_second(gathers, 0)
    for step in LINE:
        gather_line(gathers, step)
        gather_second(gathers, step)
    if between is not None:
        between()
    for step in (0,) + LINE:
        gather_third(gathers, step)
    for gather in gathers:
        gather.finish()


class Scatter:
    def __init__(self, here, y_first, part, got, send, recv, relay=False):
        self.here, self.y_first, self.part, self.got, self.relay = here, y_first, part, got, relay
        self.send, self.recv, self.started = send, recv, []

    def number(self, a, b, step):
        y, z, x, c = self.here
        flip_y, flip_x = (a, b) if self.y_first else (b, a)
        return chip(1 - y if flip_y else y, along(z, step), 1 - x if flip_x else x)

    def toward(self, second):
        y, z, x, c = self.here
        return device(1 - y, z, x, c) if self.y_first != second else device(y, z, 1 - x, c)

    def copy(self, source, index, to):
        sent = remote(source, self.got(index), self.send.at[len(self.started)], self.recv.at[index], to)
        sent.start()
        self.started.append(sent)

    def arrive(self, index):
        block = self.got(index)
        remote(block, block, self.send.at[0], self.recv.at[index], device(*self.here)).wait_recv()
        return block

    def first(self, step):
        for b in (1, 0):
            self.copy(self.part(self.number(1, b, step)), 4 * b + step, self.toward(False))

    def add(self, number, index):
        block, mine = self.arrive(index), self.part(number)
        total = mine[...].astype(jnp.float32) + block[...].astype(jnp.float32)
        mine[...] = total.astype(mine.dtype)

    def one(self, b, step):
        number = self.number(0, b, step)
        self.add(number, 4 * b + step)
        if b == 1:
            self.copy(self.part(number), 8 + step, self.toward(True))

    def two(self, step):
        y, z, x, c = self.here
        number = self.number(0, 0, step)
        self.add(number, 8 + step)
        if self.relay and step == 2:
            self.add(number, 14)
        if step:
            self.copy(self.part(number), 11 + step, device(y, along(z, 1 if self.relay and step == 3 else step), x, c))

    def total(self):
        result = self.part(self.number(0, 0, 0))[...].astype(jnp.float32)
        for step in (1, 2) if self.relay else (1, 2, 3):
            result = result + self.arrive(11 + step)[...].astype(jnp.float32)
        return result

    def finish(self):
        for sent in self.started:
            sent.wait_send()


def scatter_all(scatters, more, between):
    order = (3, 2, 1, 0)
    for turn, step in enumerate(order):
        for b in (1, 0):
            for scatter in scatters:
                scatter.one(b, step)
        if turn + 2 < 4:
            more(order[turn + 2])
        if turn:
            for scatter in scatters:
                scatter.two(order[turn - 1])
        between(turn)
    for scatter in scatters:
        scatter.two(order[3])


def nt(a, b):
    return lax.dot_general(a, b, (((1,), (1,)), ((), ())), preferred_element_type=jnp.float32)


def tn(a, b):
    return lax.dot_general(a, b, (((0,), (0,)), ((), ())), preferred_element_type=jnp.float32)


def nn(a, b):
    return jnp.dot(a, b, preferred_element_type=jnp.float32)


def low(value):
    return value.astype(jnp.bfloat16)


def wide_float(value):
    return value.astype(jnp.float32)


def norm(values):
    centred = values - jnp.mean(values, axis=-1, keepdims=True)
    scale = lax.rsqrt(jnp.mean(centred * centred, axis=-1, keepdims=True) + layer_epsilon)
    return centred * scale, scale


def norm_back(grad, normed, scale):
    pulled = grad - jnp.mean(grad, axis=-1, keepdims=True) - normed * jnp.mean(grad * normed, axis=-1, keepdims=True)
    return scale * pulled


def item_mask(lengths, shape):
    return lax.broadcasted_iota(jnp.int32, shape, 0) >= lengths[0, 0]


def choices(routes, square):
    square[...] = jnp.zeros_like(square)
    square[0 : routes.shape[0], :] = wide_float(routes[...])
    named = square[...].T
    lane = wide_float(lax.broadcasted_iota(jnp.int32, (1, 128), 1))
    return (named[:, 0:1] == lane) | (named[:, 1:2] == lane)


def own_modulation(here, mod, item, half, part):
    first = 2 * here[3]
    model = item.shape[1]
    at = slice(part * model, (part + 1) * model)
    return jnp.where(item, mod[half, pl.ds(first + 1, 1), at], mod[half, pl.ds(first, 1), at])


def head_lanes():
    lane = lax.broadcasted_iota(jnp.int32, (1, 128), 1)
    return lane < 64, [low(wide_float(lane < 64)), low(wide_float(lane >= 64))]


def front_kernel(
    lengths, tokens, cotangent, routes, cond, w_ada, w_qkv, w_out, w_router, w_fc1, e1,
    w1, w1s_out, qkv_w, out_w, mod_out, mixed_out, grad_out, gates_out, attn_in_out, qkv_out, probs_out, attn_low_out, attn_proj_out, middle_out, chance_out,
    w1s, mod, mixed, grad, gates, attn_in, qkv, probs, attn_low, attn_proj, middle, chance,
    square, strip_own, f1, s_got, s_rows, q_full, o_full, a_full, q_fold, o_fold, a_fold, q_stage, o_stage, a_stage, q_block, o_block, c_buf, z_part, z_got,
    pre_send, pre_recv, g_send, g_recv, g_pair, a_send, a_recv, a_pair_send, a_pair, b_send, b_recv, b_pair, l_sem, o_sem,
    c_send, c_recv, m_send, m_recv, r_send, r_recv,
):
    here = y, z, x, c = place()
    me, k, gy = chip(y, z, x), 2 * z + x, 4 * z + 2 * x + c
    rows, model = w_out.shape
    others = [(dy, dz, dx) for dy in (0, 1) for dz in (0, 1, 2, 3) for dx in (0, 1) if (dy, dz, dx) != (0, 0, 0)]
    spot = lambda dy, dz, dx: (1 - y if dy else y, along(z, dz), 1 - x if dx else x)
    sibling = device(y, z, x, 1 - c)
    crossed = [device(y, along(z, step), x, 1 - c) for step in LINE]
    meet([device(*spot(*o), c) for o in others] + [sibling] + crossed)

    started = []

    def go(copy):
        copy.start()
        started.append(copy)

    for i, (step, core) in enumerate([(0, 1 - c)] + [(step, core) for step in LINE for core in (c, 1 - c)]):
        go(remote(cond.at[along(z, step)], c_buf.at[z, c], c_send.at[i], c_recv.at[z, c], device(y, along(z, step), x, core)))

    mine = pl.ds(pl.multiple_of(rows * c, 8), rows)
    square[...] = jnp.zeros_like(square)
    square[0 : w_router.shape[0], 0:rows] = wide_float(w_router[...])
    router = square[...].T[:rows]
    for i, (w, fold, stage) in enumerate(((w_ada, a_fold, a_stage), (w_qkv, q_fold, q_stage), (w_out, o_fold, o_stage))):
        cut = w.shape[1] // 2
        for h in (0, 1):
            fold[h, :, :cut] = wide_float(w[:, h * cut : (h + 1) * cut])
            if i == 2:
                fold[h, :, cut:] = router
        go(remote(fold.at[1 - c], stage.at[mine, :], pre_send.at[i], pre_recv.at[i], sibling))
        stage[mine, :] = fold[c]

    depth, width = e1.shape[1], w1.shape[2]
    cols = lambda n: pl.ds(pl.multiple_of(width * n, 128), width)
    strip = lambda n: pl.ds(pl.multiple_of(depth * n, 16), depth)
    load = pltpu.make_async_copy(e1.at[:, :, cols(k)], strip_own, l_sem.at[0])
    load.start()
    plane = [o for o in others if o[0] == 0]

    def send_experts(steps, aside):
        for i, o in enumerate(plane):
            if o[1] in steps and o[2] == aside:
                ty, tz, tx = spot(*o)
                go(remote(e1.at[:, :, cols(2 * tz + tx)], w1.at[:, strip(gy), :], a_send.at[i], a_recv.at[k], device(ty, tz, tx, c)))

    send_experts((1,), 0)

    def folded(i, stage):
        theirs = stage.at[pl.ds(pl.multiple_of(rows * (1 - c), 8), rows), :]
        remote(theirs, theirs, pre_send.at[i], pre_recv.at[i], sibling).wait_recv()
        return low(stage[...])

    block = folded(0, a_stage)
    width_a = a_full.shape[3]
    number = 2 * y + x
    to_y, to_x = device(1 - y, z, x, c), device(y, z, 1 - x, c)
    for i in (0, 1):
        a_full[i, number] = block[:, i * width_a : (i + 1) * width_a]

    def send_a(i, n, lane, to):
        go(remote(a_full.at[i, n], a_full.at[i, n], r_send.at[i, lane], r_recv.at[i, n], to))

    def wait_a(i, n):
        remote(a_full.at[i, n], a_full.at[i, n], r_send.at[0, 0], r_recv.at[i, n], sibling).wait_recv()

    for i in (0, 1):
        send_a(i, number, 0, to_x)
    for i in (0, 1):
        send_a(i, number, 1, to_y)
    q_block[...] = folded(1, q_stage)
    o_block[...] = folded(2, o_stage)
    gathers = []
    for i, (block, full, y_first) in enumerate(((q_block, q_full, False), (o_block, o_full, True))):
        slot = functools.partial(lambda full, n: full.at[c, pl.ds(pl.multiple_of(2 * rows * n, 16), 2 * rows), :], full)
        gathers.append(Gather(here, y_first, block, slot, g_send.at[i], g_recv.at[i], g_pair.at[i]))
        slot(me)[...] = block[...]
    gather_start(gathers)

    n_y, n_x = 2 * (1 - y) + x, 2 * y + 1 - x
    n_xy = 2 * (1 - y) + 1 - x
    for i in (0, 1):
        wait_a(i, n_x)
        send_a(i, n_x, 2, to_y)
    gather_second(gathers, 0)

    c_buf[z, c] = cond[z]
    for step, core in [(0, 1 - c)] + [(step, core) for step in LINE for core in (c, 1 - c)]:
        block = c_buf.at[along(z, step), core]
        remote(block, block, c_send.at[0], c_recv.at[along(z, step), core], sibling).wait_recv()
    lhs = low(jnp.concatenate([c_buf[i, 0] + c_buf[i, 1] for i in range(4)], axis=0))[:, : 8 * rows]
    for i in (0, 1):
        wait_a(i, n_y)
        wait_a(i, n_xy)
        term = nn(lhs, a_full[i].reshape(8 * rows, width_a))
        for line in range(4):
            z_part[line, 4 * i : 4 * (i + 1), :] = term[8 * line : 8 * line + 4]
    for step in LINE:
        at = along(z, step)
        go(remote(z_part.at[at], z_got.at[step - 1], m_send.at[step], m_recv.at[step], device(y, at, x, c)))
    send_experts((2, 3), 0)
    gather_line(gathers, 1)
    slim = w1s.shape[1]
    for n in range(16):
        block = wide_float(w_fc1[:, slim * n : slim * (n + 1)])
        f1[n] = low(jnp.concatenate([block, jnp.zeros((f1.shape[1] - rows, slim), jnp.float32)], axis=0))
    for i, o in enumerate(others):
        ty, tz, tx = spot(*o)
        go(remote(f1.at[chip(ty, tz, tx)], s_got.at[c, me], b_send.at[i], b_recv.at[me], device(ty, tz, tx, c)))
    s_got[c, me] = f1[me]
    gather_second(gathers, 1)
    gather_line(gathers, 2)
    send_experts((0, 1, 2, 3), 1)
    total = z_part[z]
    for step in LINE:
        remote(z_got.at[step - 1], z_got.at[step - 1], m_send.at[0], m_recv.at[step], sibling).wait_recv()
        total = total + z_got[step - 1]
    mod[c] = jnp.concatenate([total, pltpu.roll(total, 4, 0)], axis=1)
    go(remote(mod.at[c], mod.at[c], m_send.at[0], m_recv.at[0], sibling))
    gather_second(gathers, 2)
    gather_line(gathers, 3)
    gather_second(gathers, 3)
    remote(mod.at[1 - c], mod.at[1 - c], m_send.at[0], m_recv.at[0], sibling).wait_recv()

    item = item_mask(lengths, tokens.shape)
    residual = wide_float(tokens[...])
    normed, _ = norm(residual)
    attn_in[...] = low(normed * (1.0 + own_modulation(here, mod, item, 0, 1)) + own_modulation(here, mod, item, 0, 0))
    grad[...] = low(wide_float(cotangent[...]) * own_modulation(here, mod, item, 1, 2))
    for step in (0,) + LINE:
        gather_third(gathers, step)
    for gather in gathers:
        gather.finish()
    keep = []

    def leave(source, target):
        keep.append(pltpu.make_async_copy(source, target, o_sem.at[len(keep)]))
        keep[-1].start()

    leave(q_full, qkv_w)
    leave(o_full, out_w)

    cut = q_full.shape[2]
    for h in (0, 1):
        qkv[:, h * cut : (h + 1) * cut] = low(nn(attn_in[...], q_full[h]))

    side = wide_float(item[:, :128])
    same = side == side.T
    left, sides = head_lanes()
    for pair in range(model // 128):
        q, key, value = [qkv[:, base + 128 * pair : base + 128 * (pair + 1)] for base in (0, model, 2 * model)]
        outs = []
        for j, side in enumerate(sides):
            scores = jnp.where(same, nt(q * side, key) * 0.125, -1e30)
            weight = jnp.exp(scores - jnp.max(scores, axis=-1, keepdims=True))
            prob = weight / jnp.sum(weight, axis=-1, keepdims=True)
            probs[2 * pair + j] = prob
            outs.append(nn(low(prob), value))
        attn_low[:, 128 * pair : 128 * (pair + 1)] = low(jnp.where(left, outs[0], outs[1]))
    cut = model // 2
    for h in (0, 1):
        attn_proj[:, h * cut : (h + 1) * cut] = nn(attn_low[...], o_full[h, :, :cut])
    middle[...] = residual + own_modulation(here, mod, item, 0, 2) * attn_proj[...]
    normed, _ = norm(middle[...])
    mixed[...] = low(normed * (1.0 + own_modulation(here, mod, item, 1, 1)) + own_modulation(here, mod, item, 1, 0))
    lane = lax.broadcasted_iota(jnp.int32, (1, 128), 1)
    logits = jnp.where(lane < 8, nn(mixed[...], o_full[0, :, cut:]), -1e30)
    weight = jnp.exp(logits - jnp.max(logits, axis=-1, keepdims=True))
    chance[...] = weight / jnp.sum(weight, axis=-1, keepdims=True)
    turned = jnp.where(choices(routes, square), chance[...], 0.0).T[:8]
    high = low(turned)
    gates[...] = jnp.concatenate([high, low(turned - wide_float(high))], axis=0)
    for source, target in (
        (mixed, mixed_out), (grad, grad_out), (gates, gates_out), (mod, mod_out), (attn_in, attn_in_out), (qkv, qkv_out), (probs, probs_out),
        (attn_low, attn_low_out), (attn_proj, attn_proj_out), (middle, middle_out), (chance, chance_out),
    ):
        leave(source, target)

    load.wait()
    leave(strip_own, w1.at[:, strip(gy), :])
    for i, o in enumerate([(0, 0, 0)] + [o for step in (0, 1, 3, 2) for o in plane if o[1] == step]):
        _, sz, sx = spot(*o)
        source = 2 * sz + sx
        block = w1.at[:, strip(2 * source + c), :]
        if i:
            remote(block, block, a_send.at[0], a_recv.at[source], sibling).wait_recv()
        go(remote(block if i else strip_own, block, a_pair_send.at[i], a_pair.at[source], sibling))
    for o in others:
        n = chip(*spot(*o))
        remote(s_got.at[c, n], s_got.at[c, n], b_send.at[0], b_recv.at[n], sibling).wait_recv()
    go(remote(s_got.at[c], s_got.at[c], b_pair.at[0], b_pair.at[1], sibling))


    for copy in started:
        copy.wait_send()
    for source in range(8):
        block = w1.at[:, strip(2 * source + 1 - c), :]
        remote(block, block, a_send.at[0], a_pair.at[source], sibling).wait_recv()
    remote(s_got.at[1 - c], s_got.at[1 - c], b_pair.at[0], b_pair.at[1], sibling).wait_recv()
    for n in range(32):
        s_rows[n * rows : (n + 1) * rows, :] = wide_float(s_got[n % 2, n // 2])[:rows]
    w1s[...] = low(s_rows[...])
    leave(w1s, w1s_out)
    for copy in keep:
        copy.wait()


def front(lengths, tokens, cotangent, routes, condition, w_ada, w_qkv, w_out, w_router, w_fc1, e_fc1):
    rows, model = w_out.shape
    toks = tokens.shape[0]
    c = place()[3]
    cond = condition.astype(jnp.float32).reshape(2, 2, 4, 2, 2, rows).transpose(2, 0, 1, 3, 4, 5).reshape(4, 2, 8 * rows)
    spot = jnp.arange(8) == (2 * c + jnp.arange(2))[:, None]
    cond = jnp.einsum("zil,is->zsl", cond, spot.astype(jnp.float32), precision=precise)
    cond = jnp.pad(cond, ((0, 0), (0, 0), (0, -8 * rows % 128)))
    ff = w_fc1.shape[1]
    slim, wide = ff // 16, ff // 8
    experts = e_fc1.shape[0]
    bf, f32 = jnp.bfloat16, jnp.float32
    shape = jax.ShapeDtypeStruct
    q_half, o_half, a_half = w_qkv.shape[1] // 2, w_out.shape[1] // 2 + 128, w_ada.shape[1] // 2
    shapes = (
        shape((experts, model, wide), bf),
        shape((model, slim), bf),
        shape((2, model, q_half), bf),
        shape((2, model, o_half), bf),
        shape((2, 8, a_half), f32),
        shape((toks, model), bf),
        shape((toks, model), bf),
        shape((16, toks), bf),
        shape((toks, model), bf),
        shape((toks, 3 * model), bf),
        shape((HEADS, toks, toks), f32),
        shape((toks, model), bf),
        shape((toks, model), f32),
        shape((toks, model), f32),
        shape((toks, 128), f32),
    )
    result = pl.pallas_call(
        front_kernel,
        out_shape=shapes,
        in_specs=[pl.BlockSpec(memory_space=pltpu.SMEM)]
        + [pl.BlockSpec(memory_space=VMEM)] * 9
        + [pl.BlockSpec(memory_space=ANY)],
        out_specs=[pl.BlockSpec(memory_space=ANY)] * 15,
        scratch_shapes=[VMEM(a.shape, a.dtype) for a in (shapes[1], *shapes[4:])]
        + [
            VMEM((128, 128), f32), VMEM((experts, e_fc1.shape[1], wide), bf), VMEM((16, 32, slim), bf), VMEM((2, 16, 32, slim), bf), VMEM((model, slim), f32),
            VMEM((2, model, q_half), bf), VMEM((2, model, o_half), bf), VMEM((2, 4, 2 * rows, a_half // 2), bf),
            VMEM((2, rows, q_half), f32), VMEM((2, rows, o_half), f32), VMEM((2, rows, a_half), f32),
            VMEM((2 * rows, q_half), f32), VMEM((2 * rows, o_half), f32), VMEM((2 * rows, a_half), f32),
            VMEM((2 * rows, q_half), bf), VMEM((2 * rows, o_half), bf),
            VMEM((4, 2, 8, cond.shape[2]), f32), VMEM((4, 8, a_half // 2), f32), VMEM((3, 8, a_half // 2), f32),
            DMA((3,)), DMA((3,)), DMA((2, 31)), DMA((2, 16)), DMA((2, 16)), DMA((7,)), DMA((8,)), DMA((8,)), DMA((8,)),
            DMA((15,)), DMA((16,)), DMA((2,)), DMA((1,)), DMA((15,)), DMA((7,)), DMA((4, 2)), DMA((4,)), DMA((4,)), DMA((2, 3)), DMA((2, 4)),
        ],
        compiler_params=pltpu.CompilerParams(collective_id=1, has_side_effects=True, vmem_limit_bytes=62 << 20),
        name="front",
    )(lengths, tokens, cotangent, routes.T, cond, w_ada, w_qkv, w_out, w_router.T, w_fc1, e_fc1)
    return result


def gelu_both(h):
    root = math.sqrt(2.0 / math.pi)
    square = h * h
    t = jnp.tanh(h * (root + (root * 0.044715) * square))
    half = 0.5 * (1.0 + t)
    slope = half + (0.5 * h) * (1.0 - t * t) * (root + (3.0 * root * 0.044715) * square)
    return h * half, slope


def ffn_chunk(xt, gt, w1, w2, gate, row):
    a, d = gelu_both(nn(xt, w1))
    gi = nt(gt, w2)
    product = None
    if gate is not None:
        product = nt(row, (a * gi).astype(jnp.bfloat16))
        a, d = a * gate, d * gate
    a = a.astype(jnp.bfloat16)
    p = (gi * d).astype(jnp.bfloat16)
    return a, p, nn(a, w2), nt(p, w1), product


def ffn_shared(slots, X, G, w1s, w2s, act_s, pre_s, sums, sums_back):
    toks = X.shape[1]
    xt = jnp.concatenate([X[n] for n in slots], axis=0)
    gt = jnp.concatenate([G[n] for n in slots], axis=0)
    a, p, total, total_back, _ = ffn_chunk(xt, gt, w1s[...], w2s[...], None, None)
    for i, n in enumerate(slots):
        act_s[n] = a[i * toks : (i + 1) * toks]
        pre_s[n] = p[i * toks : (i + 1) * toks]
    sums[...] = total
    sums_back[...] = total_back


def ffn_experts(low, high, slots, X, G, gates, w1, w2, act, pre, sums, sums_back, gc):
    experts, toks, wide = w1.shape[0], X.shape[1], w1.shape[2]
    first = lax.axis_index("gx") * experts
    xt = jnp.concatenate([X[n] for n in slots], axis=0)
    gt = jnp.concatenate([G[n] for n in slots], axis=0)

    def expert(e, product):
        kind = lax.broadcasted_iota(jnp.int32, (16, 128), 0)
        spread = ((kind == first + e) | (kind == first + e + 8)).astype(jnp.bfloat16)
        gate = jnp.concatenate([tn(gates[n], spread) for n in slots], axis=0)
        gate = jnp.concatenate([gate] * (wide // 128), axis=1)
        row = (lax.broadcasted_iota(jnp.int32, (8, wide), 0) == first + e).astype(jnp.bfloat16)
        a, p, total, total_back, more = ffn_chunk(xt, gt, w1[e], w2[e], gate, row)
        for i, n in enumerate(slots):
            act[e, n] = a[i * toks : (i + 1) * toks]
            pre[e, n] = p[i * toks : (i + 1) * toks]
        sums[...] += total
        sums_back[...] += total_back
        return product + more

    product = lax.fori_loop(low, high, expert, jnp.zeros((8, len(slots) * toks), jnp.float32))
    for i, n in enumerate(slots):
        part = product[:, i * toks : (i + 1) * toks]
        gc[n] = part if low == 0 else gc[n] + part


def block_kernel(
    mixed, grad, gates, w1_in, w1s_in, w2_in, w2s_in,
    sum_branch, sum_back, sum_gc, out1, out1s, out2, out2s,
    own1, own1s, own2, own2s, X, G, gt, w1, w1s, w2, w2s, act, pre, act_s, pre_s, tile_sum, tile_back,
    p_branch, p_back, p_gc, r_branch, r_back, r_gc, d1, d1s, d2, d2s, from1, from1s, from2, from2s,
    l_sem, o_sem, g_send, g_recv, send, recv, t_send, t_recv, w_send, w_recv,
):
    here = y, z, x, c = place()
    me = chip(y, z, x)
    spot = lambda dy, dz, dx: (1 - y if dy else y, along(z, dz), 1 - x if dx else x)
    sibling = device(y, z, x, 1 - c)
    experts = w1.shape[0]
    meet(cross_partners(here) + [sibling])

    gathers, local = [], []
    for i, (block, full, y_first) in enumerate(((mixed, X, True), (grad, G, False), (gates, gt, True))):
        slot = functools.partial(lambda full, n: full.at[n], full)
        gathers.append(Gather(here, y_first, block, slot, g_send.at[i], g_recv.at[i]))
        local.append(pltpu.make_async_copy(block, slot(me), l_sem.at[i]))
    gather_start(gathers)
    half2, half2s = w2_in.shape[1], w2s_in.shape[0]
    own2_at = w2.at[:, pl.ds(pl.multiple_of(half2 * c, 16), half2), :]
    own2s_at = w2s.at[pl.ds(pl.multiple_of(half2s * c, 16), half2s), :]
    for i, (source, target) in enumerate(((w1_in, w1), (w1s_in, w1s), (w2_in, own2_at), (w2s_in, own2s_at))):
        local.append(pltpu.make_async_copy(source, target, l_sem.at[3 + i]))
    for i, (source, target) in enumerate(((w2_in, own2_at), (w2s_in, own2s_at))):
        local.append(remote(source, target, w_send.at[i], w_recv.at[i], sibling))
    for copy in local:
        copy.start()

    def tile(step, part):
        slots = [chip(*spot(dy, step, dx)) for dy in (0, 1) for dx in (0, 1)]
        if part == 0:
            ffn_shared(slots, X, G, w1s, w2s, act_s, pre_s, tile_sum, tile_back)
        low, high = (0, experts // 2) if part == 0 else (experts // 2, experts)
        ffn_experts(low, high, slots, X, G, gt, w1, w2, act, pre, tile_sum, tile_back, p_gc)
        if part == 1:
            toks = X.shape[1]
            for i, n in enumerate(slots):
                at = slice(i * toks, (i + 1) * toks)
                p_branch[n] = tile_sum[at, :].astype(jnp.bfloat16)
                p_back[n] = tile_back[at, :].astype(jnp.bfloat16)

    scatters = []
    for i, (part, got, y_first) in enumerate(((p_branch, r_branch, False), (p_back, r_back, True), (p_gc, r_gc, False))):
        take = functools.partial(lambda ref, n: ref.at[n], part)
        land = functools.partial(lambda ref, n: ref.at[n], got)
        scatters.append(Scatter(here, y_first, take, land, send.at[i], recv.at[i]))

    def back_first(step):
        for scatter in scatters:
            scatter.first(step)

    gather_second(gathers, 0)
    gather_line(gathers, 1)
    gather_second(gathers, 1)
    gather_third(gathers, 0)
    for copy in local:
        copy.wait()
    tile(0, 0)
    gather_line(gathers, 2)
    tile(0, 1)
    gather_third(gathers, 1)
    tile(1, 0)
    gather_second(gathers, 2)
    tile(1, 1)
    gather_line(gathers, 3)
    gather_third(gathers, 2)
    tile(2, 0)
    gather_second(gathers, 3)
    tile(2, 1)
    back_first(2)
    back_first(1)
    gather_third(gathers, 3)
    tile(3, 0)

    def back_one(step):
        for scatter in scatters:
            scatter.one(1, step)
        for scatter in scatters:
            scatter.one(0, step)

    def back_two(step):
        for scatter in scatters:
            scatter.two(step)

    flat = lambda value: value.reshape(value.shape[0] * value.shape[1], value.shape[2])
    twins = [None] * (2 * experts)
    leaving = []

    def leave(source, target):
        leaving.append(pltpu.make_async_copy(source, target, o_sem.at[len(leaving)]))
        leaving[-1].start()


    def weight(e):
        d1[e] = tn(flat(X[...]), flat(pre[e])).astype(jnp.bfloat16).reshape(d1.shape[1:])
        d2[e] = tn(flat(act[e]), flat(G[...])).astype(jnp.bfloat16).reshape(d2.shape[1:])
        for i, (part, got) in enumerate(((d1.at[e, :, 1 - c], from1.at[e]), (d2.at[e, 1 - c], from2.at[e]))):
            twins[2 * e + i] = remote(part, got, t_send.at[2 * e + i], t_recv.at[2 * e + i], sibling)
            twins[2 * e + i].start()

    def home(e):
        twins[2 * e].wait()
        own1[e] = (d1[e, :, c].astype(jnp.float32) + from1[e].astype(jnp.float32)).astype(jnp.bfloat16)
        twins[2 * e + 1].wait()
        own2[e] = d2[e, c].astype(jnp.float32) + from2[e].astype(jnp.float32)
        leave(own1.at[e], out1.at[e])
        leave(own2.at[e], out2.at[e])

    back_one(2)
    tile(3, 1)
    back_first(3)
    back_two(2)
    back_one(1)
    weight(0)
    back_two(1)
    home(0)
    back_first(0)
    weight(1)
    back_one(3)
    back_two(3)
    home(1)
    weight(2)
    home(2)
    weight(3)
    d1s[...] = tn(flat(X[...]), flat(pre_s[...])).reshape(d1s.shape)
    d2s[...] = tn(flat(act_s[...]), flat(G[...])).astype(jnp.bfloat16).reshape(d2s.shape)
    twin1s = remote(d1s.at[:, 1 - c], from1s, t_send.at[2 * experts], t_recv.at[2 * experts], sibling)
    twin2s = remote(d2s.at[1 - c], from2s, t_send.at[2 * experts + 1], t_recv.at[2 * experts + 1], sibling)
    twin1s.start()
    twin2s.start()
    home(3)
    back_one(0)
    twin1s.wait()
    total = d1s[:, c] + from1s[...]
    own1s[...] = low(jnp.concatenate([total, jnp.zeros((16, own1s.shape[1] - total.shape[1], total.shape[2]), jnp.float32)], axis=1))
    twin2s.wait()
    own2s[...] = d2s[c].astype(jnp.float32) + from2s[...].astype(jnp.float32)
    leave(own1s, out1s)
    leave(own2s, out2s)
    back_two(0)
    sum_branch[...] = scatters[0].total()
    sum_back[...] = scatters[1].total()
    sum_gc[...] = scatters[2].total()
    for copy in leaving:
        copy.wait()
    for gather in gathers:
        gather.finish()
    for scatter in scatters:
        scatter.finish()


def block(mixed, grad, gates, w1, w1s, e_fc2, w_fc2):
    bf, f32 = jnp.bfloat16, jnp.float32
    toks, model = mixed.shape
    experts, _, wide = w1.shape
    slim = w1s.shape[1]
    rows = model // 32
    shape = jax.ShapeDtypeStruct
    blocks = lambda *dims: VMEM((16, toks) + dims, bf)
    return pl.pallas_call(
        block_kernel,
        out_shape=[
            shape((toks, model), f32),
            shape((toks, model), f32),
            shape((8, 128), f32),
            shape((experts, 8, 2 * rows, wide), bf),
            shape((16, 32, slim), bf),
            shape((experts, wide // 2, model), f32),
            shape((slim // 2, model), f32),
        ],
        in_specs=[pl.BlockSpec(memory_space=VMEM)] * 3 + [pl.BlockSpec(memory_space=ANY)] * 4,
        out_specs=[pl.BlockSpec(memory_space=VMEM)] * 3 + [pl.BlockSpec(memory_space=ANY)] * 4,
        scratch_shapes=[
            VMEM((experts, 8, 2 * rows, wide), bf), VMEM((16, 32, slim), bf), VMEM((experts, wide // 2, model), f32), VMEM((slim // 2, model), f32),
            blocks(model), blocks(model), VMEM((16, 16, 128), bf),
            VMEM(w1.shape, bf), VMEM(w1s.shape, bf), VMEM((experts, wide, model), bf), VMEM((slim, model), bf),
            VMEM((experts, 16, toks, wide), bf), VMEM((experts, 16, toks, wide), bf), blocks(slim), blocks(slim),
            VMEM((4 * toks, model), f32), VMEM((4 * toks, model), f32),
            blocks(model), blocks(model), VMEM((16, 8, 128), f32),
            VMEM((15, toks, model), bf), VMEM((15, toks, model), bf), VMEM((15, 8, 128), f32),
            VMEM((experts, 8, 2, 2 * rows, wide), bf), VMEM((16, 2, rows, slim), f32),
            VMEM((experts, 2, wide // 2, model), bf), VMEM((2, slim // 2, model), bf),
            VMEM((experts, 8, 2 * rows, wide), bf), VMEM((16, rows, slim), f32),
            VMEM((experts, wide // 2, model), bf), VMEM((slim // 2, model), bf),
            DMA((7,)), DMA((2 * experts + 2,)), DMA((3, 15)), DMA((3, 16)), DMA((3, 15)), DMA((3, 15)), DMA((2 * experts + 2,)), DMA((2 * experts + 2,)),
            DMA((2,)), DMA((2,)),
        ],
        compiler_params=pltpu.CompilerParams(collective_id=2, has_side_effects=True, vmem_limit_bytes=62 << 20),
        name="block",
    )(mixed, grad, gates, w1, w1s, e_fc2, w_fc2)


def rear_kernel(lengths, *refs):
    incoming, refs = refs[:16], refs[16:]
    (qkv_in, out_in, part1, part1s, output, d_tokens, d_ada, d_qkv, d_out, d_router, own1, own1s), refs = refs[:12], refs[12:]
    (sum_branch, sum_back, sum_gc, tokens, cotangent, routes, condition, mod, mixed, attn_in, qkv, probs, attn_low, attn_proj, middle, chance), refs = refs[:16], refs[16:]
    (square, strip_own, slice_own, q_w, o_w, grad_attn, grad_qkv, grad_mid, o_mine, o_got, q_mine, q_got, part_o, part_a, part_b, got_o, got_a, got_b, fin, mod_tile, all_mod, l_sem, s_send, s_recv, send, recv, g_send, g_recv, g_pair, f_send, f_recv, a_send, a_recv, b_send, b_recv, i_sem) = refs
    here = y, z, x, c = place()
    me, k = chip(y, z, x), 2 * z + x
    sibling = device(y, z, x, 1 - c)
    others = [(dy, dz, dx) for dy in (0, 1) for dz in (0, 1, 2, 3) for dx in (0, 1) if (dy, dz, dx) != (0, 0, 0)]
    plane = [o for o in others if o[0] == 0]
    spot = lambda dy, dz, dx: (1 - y if dy else y, along(z, dz), 1 - x if dx else x)
    held = (sum_branch, sum_back, sum_gc, tokens, cotangent, routes, condition, mod, mixed, attn_in, qkv, probs, attn_low, attn_proj, middle, chance)
    loads = [pltpu.make_async_copy(a, b, i_sem.at[i]) for i, (a, b) in enumerate(zip(incoming, held))]
    local = [pltpu.make_async_copy(qkv_in, q_w, l_sem.at[0]), pltpu.make_async_copy(out_in, o_w, l_sem.at[1])]
    for copy in loads + local:
        copy.start()
    meet([device(*spot(*o), c) for o in others] + [sibling])
    started = []

    def go(copy):
        copy.start()
        started.append(copy)

    wide = part1.shape[3]
    columns = lambda n: own1.at[:, :, pl.ds(pl.multiple_of(wide * n, 128), wide)]
    home = [pltpu.make_async_copy(part1.at[:, k], strip_own, l_sem.at[2]), pltpu.make_async_copy(part1s.at[me], slice_own, l_sem.at[3])]
    for copy in home:
        copy.start()

    def send_experts(aside):
        for i, o in enumerate(plane):
            if o[2] == aside:
                ty, tz, tx = spot(*o)
                go(remote(part1.at[:, 2 * tz + tx], columns(k), a_send.at[i], a_recv.at[k], device(ty, tz, tx, c)))

    send_experts(0)
    for i, o in enumerate(others):
        go(remote(part1s.at[chip(*spot(*o))], own1s.at[me], b_send.at[i], b_recv.at[me], device(*spot(*o), c)))

    for copy in loads:
        copy.wait()
    item = item_mask(lengths, tokens.shape)
    first = ~item
    model = item.shape[1]
    cut = model // 2
    modulation = functools.partial(own_modulation, here, mod, item)
    rows16 = {}

    def per_item(part, value):
        for i, mask in enumerate((first, ~first)):
            rows16[2 * part + i] = jnp.sum(jnp.where(mask, value, 0.0), axis=0, keepdims=True)

    out_grad = wide_float(cotangent[...])
    branch = sum_branch[...]
    output[...] = low(middle[...] + modulation(1, 2) * branch)
    per_item(5, out_grad * branch)
    chosen = choices(routes, square)
    turned = jnp.concatenate([sum_gc[...], jnp.zeros((120, 128), jnp.float32)], axis=0).T
    grad_chance = jnp.where(chosen, turned, 0.0)
    share = chance[...]
    grad_logits = low(share * (grad_chance - jnp.sum(grad_chance * share, axis=-1, keepdims=True)))
    term_router = tn(mixed[...], grad_logits)
    for copy in local + home:
        copy.wait()
    home = [pltpu.make_async_copy(strip_own, columns(k), l_sem.at[2]), pltpu.make_async_copy(slice_own, own1s.at[me], l_sem.at[3])]
    for copy in home:
        copy.start()
    grad_mixed = sum_back[...] + nt(grad_logits, o_w[0, :, cut:])
    normed, scale = norm(middle[...])
    per_item(3, grad_mixed)
    per_item(4, grad_mixed * normed)
    grad_mid[...] = out_grad + norm_back(grad_mixed * (1.0 + modulation(1, 1)), normed, scale)
    per_item(2, grad_mid[...] * attn_proj[...])
    grad_proj = low(grad_mid[...] * modulation(0, 2))
    for h in (0, 1):
        term = jnp.concatenate([tn(attn_low[...], grad_proj[:, h * cut : (h + 1) * cut]), term_router], axis=1)
        o_mine[h] = low(term)
    swap_o = remote(o_mine.at[1 - c], o_got, s_send.at[0], s_recv.at[0], sibling)
    swap_o.start()
    grad_attn[...] = low(nt(grad_proj[:, :cut], o_w[0, :, :cut]) + nt(grad_proj[:, cut:], o_w[1, :, :cut]))

    rows = o_got.shape[0] // 16
    scatters = []
    for i, (part, got, y_first) in enumerate(((part_o, got_o, False), (part_a, got_a, True), (part_b, got_b, False))):
        take = functools.partial(lambda ref, n: ref.at[n], part)
        land = functools.partial(lambda ref, n: ref.at[n], got)
        scatters.append(Scatter(here, y_first, take, land, send.at[i], recv.at[i], relay=True))

    swap_o.wait()
    for n in range(16):
        at = slice(n * rows, (n + 1) * rows)
        part_o[n] = low(wide_float(o_mine[c, at, :]) + wide_float(o_got[at, :]))
    for step in (3, 2, 1, 0):
        scatters[0].first(step)

    left, sides = head_lanes()
    for pair in range(model // 128):
        at = slice(128 * pair, 128 * (pair + 1))
        q, key, value = [qkv[:, base + 128 * pair : base + 128 * (pair + 1)] for base in (0, model, 2 * model)]
        ga = grad_attn[:, at]
        outs = []
        for j, side in enumerate(sides):
            prob = probs[2 * pair + j]
            grad_probs = nt(ga * side, value)
            grad_scores = low(prob * (grad_probs - jnp.sum(grad_probs * prob, axis=-1, keepdims=True)))
            outs.append((nn(grad_scores, key) * 0.125, tn(grad_scores, q) * 0.125, tn(low(prob), ga)))
        for base, one, two in zip((0, model, 2 * model), *outs):
            grad_qkv[:, base + 128 * pair : base + 128 * (pair + 1)] = low(jnp.where(left, one, two))

    third = q_w.shape[2]
    for h in (0, 1):
        q_mine[h] = low(tn(attn_in[...], grad_qkv[:, h * third : (h + 1) * third]))
    swap_q = {}
    for step in (3, 2, 1, 0):
        for side in (0, 1):
            at = pl.ds(pl.multiple_of(2 * rows * (4 * side + along(z, step)), 16), 2 * rows)
            i = 1 + 2 * step + side
            swap_q[step, side] = remote(q_mine.at[1 - c, at, :], q_got.at[at, :], s_send.at[i], s_recv.at[i], sibling)
            swap_q[step, side].start()
    send_experts(1)
    grad_in = nt(grad_qkv[:, :third], q_w[0]) + nt(grad_qkv[:, third:], q_w[1])
    normed, scale = norm(wide_float(tokens[...]))
    per_item(0, grad_in)
    per_item(1, grad_in * normed)
    d_tokens[...] = grad_mid[...] + norm_back(grad_in * (1.0 + modulation(0, 1)), normed, scale)
    rows16[12] = wide_float(condition[...])
    rows16[13] = jnp.zeros((2, model), jnp.float32)
    mod_tile[...] = low(jnp.concatenate([rows16[i] for i in range(14)], axis=0))

    slot = lambda n: all_mod.at[n, c]
    spread = Gather(here, False, mod_tile, slot, g_send, g_recv, g_pair)
    all_mod[me, c] = mod_tile[...]
    gather_start([spread])
    edge = part_a.shape[2]

    def fold(step):
        for side in (0, 1):
            swap_q[step, side].wait()
            first_n = 8 * side + 2 * along(z, step)
            for n in (first_n, first_n + 1):
                at = pl.ds(pl.multiple_of(rows * n, 16), rows)
                total = low(wide_float(q_mine[c, at, :]) + wide_float(q_got[at, :]))
                part_a[n] = total[:, :edge]
                part_b[n] = total[:, edge:]
        for scatter in scatters[1:]:
            scatter.first(step)

    fold(3)
    fold(2)

    def turn(at):
        if at == 0:
            spread.second(0)
            for step in LINE:
                gather_line([spread], step)
        elif at == 1:
            for step in LINE:
                spread.second(step)
        elif at == 2:
            for step in (0,) + LINE:
                spread.third(step)
            spread.finish()
        else:
            flat = all_mod[...].reshape(32 * 16, model)
            share_rows = rows // 2
            own = (2 * me + c) * share_rows
            source = lax.broadcasted_iota(jnp.int32, (model, 128), 0)
            lane = lax.broadcasted_iota(jnp.int32, (model, 128), 1)
            own_columns = nn(flat, low(wide_float((source == own + lane) & (lane < share_rows))))
            row = lax.broadcasted_iota(jnp.int32, (512, 128), 0) % 16
            own_columns = jnp.where((row >= 12) & (row < 14), own_columns, 0.0)
            for part in range(6):
                lhs = low(pltpu.roll(own_columns, 512 + 2 * part - 12, 0))
                d_ada[:, part * model : (part + 1) * model] = tn(lhs, flat)[:share_rows]

    scatter_all(scatters, fold, turn)
    fin[c] = jnp.concatenate([scatters[1].total(), scatters[2].total(), scatters[0].total()], axis=1)
    half = rows // 2
    mine = pl.ds(pl.multiple_of(half * c, 8), half)
    theirs = pl.ds(pl.multiple_of(half * (1 - c), 8), half)
    swap = remote(fin.at[c, theirs, :], fin.at[c, theirs, :], f_send, f_recv, sibling)
    swap.start()

    for i, o in enumerate(plane):
        n = 2 * spot(*o)[1] + spot(*o)[2]
        remote(columns(n), columns(n), a_send.at[i], a_recv.at[n], sibling).wait_recv()
    for copy in home:
        copy.wait()
    for i, o in enumerate(others):
        n = chip(*spot(*o))
        remote(own1s.at[n], own1s.at[n], b_send.at[i], b_recv.at[n], sibling).wait_recv()
    for scatter in scatters:
        scatter.finish()
    for copy in started:
        copy.wait_send()
    swap.wait_send()
    remote(fin.at[1 - c, mine, :], fin.at[1 - c, mine, :], f_send, f_recv, sibling).wait_recv()
    for h in (0, 1):
        d_qkv[:, h * third : (h + 1) * third] = fin[h, mine, :third]
        d_out[:, h * cut : (h + 1) * cut] = fin[h, mine, third : third + cut]
    d_router[0:half, :] = fin[0, mine, third + cut :]
    d_router[half:, :] = jnp.zeros((128 - half, 128), jnp.float32)


def rear(lengths, sums, tokens, cotangent, routes, condition, saved, qkv_w, out_w, part1, part1s):
    bf, f32 = jnp.bfloat16, jnp.float32
    toks, model = tokens.shape
    rows = model // 16
    experts, _, depth, wide = part1.shape
    q_half, o_half = qkv_w.shape[2], out_w.shape[2]
    a_half = model
    incoming = (*sums, tokens, cotangent, routes.T, condition, *saved)
    shape = jax.ShapeDtypeStruct
    return pl.pallas_call(
        rear_kernel,
        out_shape=[
            shape((toks, model), bf),
            shape((toks, model), f32),
            shape((rows // 2, 6 * model), f32),
            shape((rows // 2, 2 * q_half), f32),
            shape((rows // 2, model), f32),
            shape((128, 128), f32),
            shape((experts, depth, 8 * wide), bf),
            shape(part1s.shape, bf),
        ],
        in_specs=[pl.BlockSpec(memory_space=pltpu.SMEM)] + [pl.BlockSpec(memory_space=ANY)] * 20,
        out_specs=[pl.BlockSpec(memory_space=VMEM)] * 6 + [pl.BlockSpec(memory_space=ANY)] * 2,
        scratch_shapes=[VMEM(a.shape, a.dtype) for a in incoming]
        + [
            VMEM((128, 128), f32), VMEM((experts, depth, wide), bf), VMEM(part1s.shape[1:], bf), VMEM(qkv_w.shape, bf), VMEM(out_w.shape, bf),
            VMEM((toks, model), bf), VMEM((toks, 3 * model), bf), VMEM((toks, model), f32),
            VMEM((2, model, o_half), bf), VMEM((model, o_half), bf),
            VMEM((2, model, q_half), bf), VMEM((model, q_half), bf),
            VMEM((16, rows, o_half), bf), VMEM((16, rows, a_half), bf), VMEM((16, rows, q_half - a_half), bf),
            VMEM((15, rows, o_half), bf), VMEM((15, rows, a_half), bf), VMEM((15, rows, q_half - a_half), bf),
            VMEM((2, rows, q_half + o_half), f32), VMEM((16, model), bf), VMEM((16, 2, 16, model), bf),
            DMA((4,)), DMA((9,)), DMA((9,)), DMA((3, 15)), DMA((3, 15)), DMA((31,)), DMA((16,)), DMA((16,)), DMA, DMA,
            DMA((7,)), DMA((8,)), DMA((15,)), DMA((16,)), DMA((16,)),
        ],
        compiler_params=pltpu.CompilerParams(collective_id=3, has_side_effects=True, vmem_limit_bytes=62 << 20),
        name="rear",
    )(lengths, *incoming, qkv_w, out_w, part1, part1s)


def finish_kernel(*refs):
    count = (len(refs) - 4) // 3
    inputs, outputs, staged = refs[:count], refs[count : 2 * count], refs[2 * count : 3 * count]
    e1, fc1, sem_in, sem = refs[3 * count :]
    loads = [pltpu.make_async_copy(a, b, sem_in.at[i]) for i, (a, b) in enumerate(zip(inputs, staged))]
    stores = []

    def store(source, target):
        stores.append(pltpu.make_async_copy(source, target, sem.at[len(stores)]))
        stores[-1].start()

    for copy in loads:
        copy.start()
    low_e1, slices, router = staged[:3]
    loads[0].wait()
    for e in range(low_e1.shape[0]):
        e1[e] = wide_float(low_e1[e])
        store(e1.at[e], outputs[0].at[e])
    for load, source, target in zip(loads[3:], staged[3:], outputs[3:]):
        load.wait()
        store(source, target)
    loads[1].wait()
    loads[2].wait()
    slim = slices.shape[2]
    for n in range(slices.shape[0] // 2):
        pair = [wide_float(slices[2 * n + i])[: fc1.shape[0]] for i in (0, 1)]
        fc1[:, 2 * n * slim : 2 * (n + 1) * slim] = jnp.concatenate(pair, axis=1)
    store(fc1, outputs[1])
    outputs[2][...] = router[...].T[: outputs[2].shape[0], : outputs[2].shape[1]]
    for copy in stores:
        copy.wait()


def finish(own1, own1s, d_router, *others):
    f32 = jnp.float32
    rows = own1.shape[1] // 2
    wide = (rows, own1s.shape[0] * own1s.shape[2])
    shape = jax.ShapeDtypeStruct
    result = pl.pallas_call(
        finish_kernel,
        out_shape=[shape(own1.shape, f32), shape(wide, f32), shape((8, rows), f32)] + [shape(a.shape, a.dtype) for a in others],
        in_specs=[pl.BlockSpec(memory_space=ANY)] * (3 + len(others)),
        out_specs=[pl.BlockSpec(memory_space=ANY)] * 2
        + [pl.BlockSpec(memory_space=VMEM)]
        + [pl.BlockSpec(memory_space=ANY)] * len(others),
        scratch_shapes=[VMEM(a.shape, a.dtype) for a in (own1, own1s, d_router, *others)]
        + [VMEM(own1.shape, f32), VMEM(wide, f32), DMA((3 + len(others),)), DMA((8 + len(others),))],
        compiler_params=pltpu.CompilerParams(vmem_limit_bytes=62 << 20),
        name="finish",
    )(own1, own1s, d_router, *others)
    return result[0], result[1], result[2].T, *result[3:]


def layer_norm(values):
    average = jnp.mean(values, axis=-1, keepdims=True)
    centred = values - average
    return centred * lax.rsqrt(jnp.mean(centred * centred, axis=-1, keepdims=True) + layer_epsilon)


def modulate(values, shift_by, scale_by):
    return layer_norm(values) * (1.0 + scale_by) + shift_by


def sinusoid(timesteps, model_width):
    half_width = model_width // 2
    frequency = jnp.exp(-math.log(10000.0) * jnp.arange(half_width, dtype=jnp.float32) / half_width)
    angles = timesteps.astype(jnp.float32)[:, None] * frequency[None, :]
    return jnp.concatenate([jnp.cos(angles), jnp.sin(angles)], axis=1)


def membership(lengths, tok_count):
    bounds = jnp.cumsum(lengths)[:-1]
    position = jnp.arange(tok_count, dtype=jnp.int32)
    item_of = jnp.sum((position[:, None] >= bounds[None, :]).astype(jnp.int32), axis=1)
    item_ids = jnp.arange(lengths.shape[0], dtype=jnp.int32)
    return ((item_of[:, None] == item_ids[None, :]).astype(jnp.float32), item_of)


def slot_index(routes, expert_count, capacity):
    flat_routes = routes.reshape(-1)
    expert_hot = (
        flat_routes[:, None] == jnp.arange(expert_count, dtype=jnp.int32)[None, :]
    ).astype(jnp.int32)
    before = jnp.cumsum(expert_hot, axis=0) - expert_hot
    rank_in = jnp.sum(before * expert_hot, axis=1)
    return (flat_routes * capacity + rank_in).reshape(routes.shape)


def dot_float(left_side, right_side):
    return jnp.dot(left_side, right_side, preferred_element_type=jnp.float32)


def dot_rows(left_side, right_side):
    return jnp.einsum("td,tf->df", left_side, right_side, preferred_element_type=jnp.float32)


def dot_cols(left_side, right_side):
    return jnp.einsum("tf,df->td", left_side, right_side, preferred_element_type=jnp.float32)


def dot_halves(left_side, halves):
    return jnp.concatenate([dot_float(left_side, halves[0]), dot_float(left_side, halves[1])], axis=1)


def by_slices(
    tokens, timesteps, lengths, routes, cotangent, w_ada, w_qkv, w_out, w_fc1, w_fc2, w_router, e_fc1, e_fc2
):
    model_width = tokens.shape[1]
    condition = jax.nn.silu(sinusoid(timesteps, model_width)).astype(jnp.bfloat16)
    (w1, w1s, qkv_w, out_w, mod, mixed, grad, gates, attn_in, qkv, probs, attn_low, attn_proj, middle,
     chance) = front(
        lengths, tokens, cotangent, routes, condition, w_ada, w_qkv, w_out, w_router, w_fc1, e_fc1
    )
    *sums, part1, part1s, d_e2, d_fc2 = block(mixed, grad, gates, w1, w1s, e_fc2, w_fc2)
    saved = (mod, mixed, attn_in, qkv, probs, attn_low, attn_proj, middle, chance)
    output, d_tokens, d_ada, d_qkv, d_out, d_router, own1, own1s = rear(
        lengths, sums, tokens, cotangent, routes, condition, saved, qkv_w, out_w, part1, part1s
    )
    d_e1, d_fc1, d_router, output, d_tokens, d_ada, d_qkv, d_out, d_fc2, d_e2 = finish(
        own1, own1s, d_router, output, d_tokens, d_ada, d_qkv, d_out, d_fc2, d_e2
    )
    return (output, d_tokens, d_ada, d_qkv, d_out, d_fc1, d_fc2, d_router, d_e1, d_e2)


def by_weights(
    tokens,
    timesteps,
    lengths,
    routes,
    cotangent,
    w_ada,
    w_qkv,
    w_out,
    w_fc1,
    w_fc2,
    w_router,
    e_fc1,
    e_fc2,
):
    tok_count, model_width = tokens.shape
    head_count = HEADS
    head_size = model_width // head_count
    expert_count = w_router.shape[1]
    capacity = CAP
    score_scale = head_size ** (-0.5)
    residual = tokens.astype(jnp.float32)
    member, item_of = membership(lengths[0], tok_count)
    ada_full, qkv_full, out_full = (
        lax.all_gather(w_ada, ("gx", "gy"), axis=0, tiled=True),
        lax.all_gather(w_qkv, ("gx", "gy"), axis=0, tiled=True),
        lax.all_gather(w_out, ("gx", "gy"), axis=0, tiled=True),
    )
    condition = jax.nn.silu(sinusoid(timesteps, model_width)).astype(jnp.bfloat16)
    modulation = dot_float(condition, ada_full)
    token_mod = jnp.dot(member, modulation, precision=precise)
    shift_attn, scale_attn, gate_attn, shift_mlp, scale_mlp, gate_mlp = jnp.split(
        token_mod, 6, axis=1
    )
    attn_in = modulate(residual, shift_attn, scale_attn).astype(jnp.bfloat16)
    qkv_low = dot_float(attn_in, qkv_full).astype(jnp.bfloat16)
    queries, key_rows, value_rows = [
        portion.reshape(tok_count, head_count, head_size)
        for portion in jnp.split(qkv_low, 3, axis=1)
    ]
    same_item = item_of[:, None] == item_of[None, :]
    scores = (
        jnp.einsum("qhd,khd->hqk", queries, key_rows, preferred_element_type=jnp.float32)
        * score_scale
    )
    scores = jnp.where(same_item[None], scores, -1e30)
    attn_probs = jax.nn.softmax(scores, axis=-1)
    probs_low = attn_probs.astype(jnp.bfloat16)
    attn_low = jnp.einsum("hqk,khd->qhd", probs_low, value_rows, preferred_element_type=jnp.float32)
    attn_low = attn_low.reshape(tok_count, model_width).astype(jnp.bfloat16)
    attn_proj = dot_float(attn_low, out_full)
    middle = residual + gate_attn * attn_proj
    mixed_in = modulate(middle, shift_mlp, scale_mlp).astype(jnp.bfloat16)
    fc1_full, fc2_full, router_full = (
        lax.all_gather(w_fc1, ("gx", "gy"), axis=0, tiled=True),
        lax.all_gather(w_fc2, ("gx", "gy"), axis=0, tiled=True),
        lax.all_gather(w_router, ("gx", "gy"), axis=0, tiled=True),
    )
    hidden_pre = dot_float(mixed_in, fc1_full)
    hidden = jax.nn.gelu(hidden_pre).astype(jnp.bfloat16)
    shared = dot_float(hidden, fc2_full)
    chance = jax.nn.softmax(dot_float(mixed_in, router_full), axis=-1)
    expert_ids = jnp.arange(expert_count, dtype=jnp.int32)
    chosen = (routes[:, :, None] == expert_ids[None, None, :]).astype(jnp.float32)
    gate_values = jnp.sum(chosen * chance[:, None, :], axis=2)
    slot_of = slot_index(routes, expert_count, capacity)
    slot_ids = jnp.arange(expert_count * capacity, dtype=jnp.int32)
    selector = (slot_of[:, :, None] == slot_ids[None, None, :]).astype(jnp.bfloat16)
    slot_rows = jnp.einsum("tks,td->sd", selector, mixed_in, preferred_element_type=jnp.float32)
    slot_rows = slot_rows.astype(jnp.bfloat16).reshape(expert_count, capacity, model_width)
    owned_rows = lax.all_to_all(slot_rows, "gx", split_axis=0, concat_axis=1, tiled=True)
    expert_in, expert_back = (
        lax.all_gather(e_fc1, "gy", axis=1, tiled=True),
        lax.all_gather(e_fc2, "gy", axis=1, tiled=True),
    )
    inner_pre = jnp.einsum(
        "ecd,edf->ecf", owned_rows, expert_in, preferred_element_type=jnp.float32
    )
    inner_act = jax.nn.gelu(inner_pre).astype(jnp.bfloat16)
    result = jnp.einsum(
        "ecf,efd->ecd", inner_act, expert_back, preferred_element_type=jnp.float32
    ).astype(jnp.bfloat16)
    returned = lax.all_to_all(result, "gx", split_axis=1, concat_axis=0, tiled=True).reshape(
        expert_count * capacity, model_width
    )
    picked = jnp.take(returned, slot_of, axis=0).astype(jnp.float32)
    branch = shared + jnp.sum(gate_values[:, :, None] * picked, axis=1)
    output = (middle + gate_mlp * branch).astype(jnp.bfloat16)
    out_grad = cotangent.astype(jnp.float32)
    grad_gate_mlp = out_grad * branch
    grad_branch = out_grad * gate_mlp
    grad_shared = grad_branch.astype(jnp.bfloat16)
    grad_picked = (gate_values[:, :, None] * grad_branch[:, None, :]).astype(jnp.bfloat16)
    grad_gates = jnp.sum(grad_branch[:, None, :] * picked, axis=2)
    grad_slots = jnp.einsum(
        "tks,tkd->sd", selector, grad_picked, preferred_element_type=jnp.float32
    )
    grad_slots = grad_slots.astype(jnp.bfloat16).reshape(expert_count, capacity, model_width)
    grad_owned = lax.all_to_all(grad_slots, "gx", split_axis=0, concat_axis=1, tiled=True)
    grad_inner = jnp.einsum(
        "ecd,efd->ecf", grad_owned, expert_back, preferred_element_type=jnp.float32
    )
    unused_inner, gelu_expert = jax.vjp(jax.nn.gelu, inner_pre)
    grad_inner_pre = gelu_expert(grad_inner)[0].astype(jnp.bfloat16)
    term_e_out = jnp.einsum(
        "ecf,ecd->efd", inner_act, grad_owned, preferred_element_type=jnp.float32
    )
    term_e_in = jnp.einsum(
        "ecd,ecf->edf", owned_rows, grad_inner_pre, preferred_element_type=jnp.float32
    )
    grad_rows = jnp.einsum(
        "ecf,edf->ecd", grad_inner_pre, expert_in, preferred_element_type=jnp.float32
    )
    grad_returned = (
        lax.all_to_all(
            grad_rows.astype(jnp.bfloat16), "gx", split_axis=1, concat_axis=0, tiled=True
        )
        .astype(grad_rows.dtype)
        .reshape(expert_count * capacity, model_width)
    )
    sum_e_in, sum_e_out = (
        lax.psum_scatter(
            term_e_in.astype(jnp.bfloat16), "gy", scatter_dimension=1, tiled=True
        ).astype(jnp.float32),
        lax.psum_scatter(
            term_e_out.astype(jnp.bfloat16), "gy", scatter_dimension=1, tiled=True
        ).astype(jnp.float32),
    )
    grad_chance = jnp.sum(chosen * grad_gates[:, :, None], axis=1)
    grad_logits = chance * (grad_chance - jnp.sum(grad_chance * chance, axis=-1, keepdims=True))
    grad_logits = grad_logits.astype(jnp.bfloat16)
    grad_hidden = dot_cols(grad_shared, fc2_full)
    unused_shared, gelu_shared = jax.vjp(jax.nn.gelu, hidden_pre)
    grad_hidden_pre = gelu_shared(grad_hidden)[0].astype(jnp.bfloat16)
    term_fc2 = dot_rows(hidden, grad_shared)
    term_fc1 = dot_rows(mixed_in, grad_hidden_pre)
    term_router = dot_rows(mixed_in, grad_logits)
    part_fc1, part_fc2, part_router = (
        lax.psum_scatter(
            term_fc1.astype(jnp.bfloat16), "gx", scatter_dimension=0, tiled=True
        ).astype(jnp.float32),
        lax.psum_scatter(
            term_fc2.astype(jnp.bfloat16), "gx", scatter_dimension=0, tiled=True
        ).astype(jnp.float32),
        lax.psum_scatter(
            term_router.astype(jnp.bfloat16), "gx", scatter_dimension=0, tiled=True
        ).astype(jnp.float32),
    )
    sum_fc1, sum_fc2, sum_router = (
        lax.psum_scatter(
            part_fc1.astype(jnp.bfloat16), "gy", scatter_dimension=0, tiled=True
        ).astype(jnp.float32),
        lax.psum_scatter(
            part_fc2.astype(jnp.bfloat16), "gy", scatter_dimension=0, tiled=True
        ).astype(jnp.float32),
        lax.psum_scatter(
            part_router.astype(jnp.bfloat16), "gy", scatter_dimension=0, tiled=True
        ).astype(jnp.float32),
    )
    grad_mixed = dot_cols(grad_hidden_pre, fc1_full) + dot_cols(grad_logits, router_full)
    grad_mixed = grad_mixed + jnp.sum(jnp.take(grad_returned, slot_of, axis=0), axis=1)
    unused_mix, mix_back = jax.vjp(modulate, middle, shift_mlp, scale_mlp)
    grad_mid_norm, grad_shift_mlp, grad_scale_mlp = mix_back(grad_mixed)
    grad_middle = out_grad + grad_mid_norm
    grad_gate_attn = grad_middle * attn_proj
    grad_proj = (grad_middle * gate_attn).astype(jnp.bfloat16)
    term_out = dot_rows(attn_low, grad_proj)
    grad_attn = (
        dot_cols(grad_proj, out_full).astype(jnp.bfloat16).reshape(tok_count, head_count, head_size)
    )
    grad_probs = jnp.einsum(
        "qhd,khd->hqk", grad_attn, value_rows, preferred_element_type=jnp.float32
    )
    grad_values = jnp.einsum(
        "hqk,qhd->khd", probs_low, grad_attn, preferred_element_type=jnp.float32
    )
    grad_scores = attn_probs * (
        grad_probs - jnp.sum(grad_probs * attn_probs, axis=-1, keepdims=True)
    )
    grad_scores = grad_scores.astype(jnp.bfloat16)
    grad_queries = (
        jnp.einsum("hqk,khd->qhd", grad_scores, key_rows, preferred_element_type=jnp.float32)
        * score_scale
    )
    grad_keys = (
        jnp.einsum("hqk,qhd->khd", grad_scores, queries, preferred_element_type=jnp.float32)
        * score_scale
    )
    grad_qkv = jnp.concatenate(
        [
            grad_queries.reshape(tok_count, model_width),
            grad_keys.reshape(tok_count, model_width),
            grad_values.reshape(tok_count, model_width),
        ],
        axis=1,
    ).astype(jnp.bfloat16)
    term_qkv = dot_rows(attn_in, grad_qkv)
    grad_attn_in = dot_cols(grad_qkv, qkv_full)
    unused_pre, pre_back = jax.vjp(modulate, residual, shift_attn, scale_attn)
    grad_input_norm, grad_shift_attn, grad_scale_attn = pre_back(grad_attn_in)
    d_tokens = grad_middle + grad_input_norm
    grad_token_mod = jnp.concatenate(
        [
            grad_shift_attn,
            grad_scale_attn,
            grad_gate_attn,
            grad_shift_mlp,
            grad_scale_mlp,
            grad_gate_mlp,
        ],
        axis=1,
    )
    grad_modulation = jnp.einsum("ti,tc->ic", member, grad_token_mod, precision=precise).astype(
        jnp.bfloat16
    )
    all_condition, all_modgrad = (
        lax.all_gather(condition, ("gx", "gy"), axis=0, tiled=True),
        lax.all_gather(grad_modulation, ("gx", "gy"), axis=0, tiled=True),
    )
    own_share = model_width // lax.axis_size(("gx", "gy"))
    own_start = lax.axis_index(("gx", "gy")) * own_share
    own_condition = lax.dynamic_slice_in_dim(all_condition, own_start, own_share, 1)
    owned_ada = dot_rows(own_condition, all_modgrad)
    attn_terms = (term_qkv, term_out)
    attn_parts = (
        lax.psum_scatter(
            attn_terms[0].astype(jnp.bfloat16), "gx", scatter_dimension=0, tiled=True
        ).astype(jnp.float32),
        lax.psum_scatter(
            attn_terms[1].astype(jnp.bfloat16), "gx", scatter_dimension=0, tiled=True
        ).astype(jnp.float32),
    )
    attn_sums = (
        lax.psum_scatter(
            attn_parts[0].astype(jnp.bfloat16), "gy", scatter_dimension=0, tiled=True
        ).astype(jnp.float32),
        lax.psum_scatter(
            attn_parts[1].astype(jnp.bfloat16), "gy", scatter_dimension=0, tiled=True
        ).astype(jnp.float32),
    )
    sum_qkv, sum_out = attn_sums
    return (
        output,
        d_tokens,
        owned_ada,
        sum_qkv,
        sum_out,
        sum_fc1,
        sum_fc2,
        sum_router,
        sum_e_in,
        sum_e_out,
    )


def solution(mesh):
    in_specs = (
        P(("gx", "gy"), None),
        P(("gx", "gy")),
        P(("gx", "gy"), None),
        P(("gx", "gy"), None),
        P(("gx", "gy"), None),
        P(("gx", "gy"), None),
        P(("gx", "gy"), None),
        P(("gx", "gy"), None),
        P(("gx", "gy"), None),
        P(("gx", "gy"), None),
        P(("gx", "gy"), None),
        P("gx", "gy", None),
        P("gx", "gy", None),
    )
    out_specs = (
        P(("gx", "gy"), None),
        P(("gx", "gy"), None),
        P(("gx", "gy"), None),
        P(("gx", "gy"), None),
        P(("gx", "gy"), None),
        P(("gx", "gy"), None),
        P(("gx", "gy"), None),
        P(("gx", "gy"), None),
        P("gx", "gy", None),
        P("gx", "gy", None),
    )
    step = by_slices if dict(mesh.shape) == {"gx": 2, "gy": 16} else by_weights
    return jax.shard_map(
        step, mesh=mesh, in_specs=in_specs, out_specs=out_specs, check_vma=False
    )
```

```python
import functools
import math

import jax
import jax.numpy as jnp
import numpy as np
from jax import lax
from jax.experimental import pallas as pl
from jax.experimental.pallas import tpu as pltpu
from jax.sharding import PartitionSpec as P

HEADS = 12
CAP = 64
MESH = pl.DeviceIdType.MESH
ANY = pl.ANY
VMEM = pltpu.VMEM
DMA = pltpu.SemaphoreType.DMA
LINE = (1, 2, 3)

precise = lax.Precision.HIGHEST
layer_epsilon = 1e-06


def place():
    gy = lax.axis_index("gy")
    return lax.axis_index("gx"), gy // 4, (gy // 2) % 2, gy % 2


def device(y, z, x, c):
    return (y, 4 * z + 2 * x + c)


def chip(y, z, x):
    return 8 * y + 2 * z + x


def along(z, step):
    return z + step - 2 * (z % 2) * (step % 2) - 4 * (z // 2) * (step // 2)


def meet(partners):
    barrier = pltpu.get_barrier_semaphore()
    for partner in partners:
        pl.semaphore_signal(barrier, inc=1, device_id=partner, device_id_type=MESH)
    pl.semaphore_wait(barrier, len(partners))


def cross_partners(here):
    y, z, x, c = here
    return [device(y, along(z, step), x, c) for step in LINE] + [
        device(1 - y, z, x, c),
        device(y, z, 1 - x, c),
    ]


def remote(source, target, send, recv, to):
    return pltpu.make_async_remote_copy(
        src_ref=source, dst_ref=target, send_sem=send, recv_sem=recv, device_id=to, device_id_type=MESH
    )


class Gather:
    def __init__(self, here, y_first, own, slot, send, recv, pair=None):
        self.here, self.y_first, self.own, self.slot = here, y_first, own, slot
        self.send, self.recv, self.pair, self.started = send, recv, pair, []

    def number(self, a, step, b):
        y, z, x, c = self.here
        flip_y, flip_x = (a, b) if self.y_first else (b, a)
        return chip(1 - y if flip_y else y, along(z, step), 1 - x if flip_x else x)

    def copy(self, source, number, to, recv=None):
        recv = self.recv if recv is None else recv
        sent = remote(source, self.slot(number), self.send.at[len(self.started)], recv.at[number], to)
        sent.start()
        self.started.append(sent)

    def to_side(self, source, number, second):
        y, z, x, c = self.here
        self.copy(source, number, device(1 - y, z, x, c) if self.y_first != second else device(y, z, 1 - x, c))

    def to_line(self, source, number, step):
        y, z, x, c = self.here
        self.copy(source, number, device(y, along(z, step), x, c))

    def to_pair(self, source, number):
        y, z, x, c = self.here
        if self.pair is not None:
            self.copy(source, number, device(y, z, x, 1 - c), self.pair)

    def arrive(self, number, recv=None):
        recv = self.recv if recv is None else recv
        block = self.slot(number)
        remote(block, block, self.send.at[0], recv.at[number], device(*self.here)).wait_recv()
        return block

    def start_first(self):
        self.to_side(self.own, self.number(0, 0, 0), False)
        self.to_pair(self.own, self.number(0, 0, 0))

    def start_line(self, step):
        self.to_line(self.own, self.number(0, 0, 0), step)

    def start_last(self):
        self.to_side(self.own, self.number(0, 0, 0), True)

    def line_first(self, step):
        number = self.number(0, step, 0)
        block = self.arrive(number)
        if step == 2:
            self.to_line(block, number, 1)
        self.to_side(block, number, False)
        self.to_pair(block, number)

    def line_last(self, step):
        number = self.number(0, step, 0)
        self.to_side(self.slot(number), number, True)

    def second(self, step):
        number = self.number(1, step, 0)
        block = self.arrive(number)
        self.to_side(block, number, True)
        self.to_pair(block, number)

    def third(self, step):
        for a in (0, 1):
            number = self.number(a, step, 1)
            self.to_pair(self.arrive(number), number)

    def finish(self):
        for sent in self.started:
            sent.wait_send()
        if self.pair is not None:
            for number in range(16):
                self.arrive(number, self.pair)


def gather_start(gathers):
    for gather in gathers:
        gather.start_first()
    for step in (1, 2):
        for gather in gathers:
            gather.start_line(step)
    for gather in gathers:
        gather.start_last()


def gather_line(gathers, step):
    for gather in gathers:
        gather.line_first(step)
    for gather in gathers:
        gather.line_last(step)


def gather_second(gathers, step):
    for gather in gathers:
        gather.second(step)


def gather_third(gathers, step):
    for gather in gathers:
        gather.third(step)


def gather_all(gathers, between=None):
    gather_start(gathers)
    gather_second(gathers, 0)
    for step in LINE:
        gather_line(gathers, step)
        gather_second(gathers, step)
    if between is not None:
        between()
    for step in (0,) + LINE:
        gather_third(gathers, step)
    for gather in gathers:
        gather.finish()


class Scatter:
    def __init__(self, here, y_first, part, got, send, recv, relay=False):
        self.here, self.y_first, self.part, self.got, self.relay = here, y_first, part, got, relay
        self.send, self.recv, self.started = send, recv, []

    def number(self, a, b, step):
        y, z, x, c = self.here
        flip_y, flip_x = (a, b) if self.y_first else (b, a)
        return chip(1 - y if flip_y else y, along(z, step), 1 - x if flip_x else x)

    def toward(self, second):
        y, z, x, c = self.here
        return device(1 - y, z, x, c) if self.y_first != second else device(y, z, 1 - x, c)

    def copy(self, source, index, to):
        sent = remote(source, self.got(index), self.send.at[len(self.started)], self.recv.at[index], to)
        sent.start()
        self.started.append(sent)

    def arrive(self, index):
        block = self.got(index)
        remote(block, block, self.send.at[0], self.recv.at[index], device(*self.here)).wait_recv()
        return block

    def first(self, step):
        for b in (1, 0):
            self.copy(self.part(self.number(1, b, step)), 4 * b + step, self.toward(False))

    def add(self, number, index):
        block, mine = self.arrive(index), self.part(number)
        total = mine[...].astype(jnp.float32) + block[...].astype(jnp.float32)
        mine[...] = total.astype(mine.dtype)

    def one(self, b, step):
        number = self.number(0, b, step)
        self.add(number, 4 * b + step)
        if b == 1:
            self.copy(self.part(number), 8 + step, self.toward(True))

    def two(self, step):
        y, z, x, c = self.here
        number = self.number(0, 0, step)
        self.add(number, 8 + step)
        if self.relay and step == 2:
            self.add(number, 14)
        if step:
            self.copy(self.part(number), 11 + step, device(y, along(z, 1 if self.relay and step == 3 else step), x, c))

    def total(self):
        result = self.part(self.number(0, 0, 0))[...].astype(jnp.float32)
        for step in (1, 2) if self.relay else (1, 2, 3):
            result = result + self.arrive(11 + step)[...].astype(jnp.float32)
        return result

    def finish(self):
        for sent in self.started:
            sent.wait_send()


def scatter_all(scatters, more, between):
    order = (3, 2, 1, 0)
    for turn, step in enumerate(order):
        for b in (1, 0):
            for scatter in scatters:
                scatter.one(b, step)
        if turn + 2 < 4:
            more(order[turn + 2])
        if turn:
            for scatter in scatters:
                scatter.two(order[turn - 1])
        between(turn)
    for scatter in scatters:
        scatter.two(order[3])


def nt(a, b):
    return lax.dot_general(a, b, (((1,), (1,)), ((), ())), preferred_element_type=jnp.float32)


def tn(a, b):
    return lax.dot_general(a, b, (((0,), (0,)), ((), ())), preferred_element_type=jnp.float32)


def nn(a, b):
    return jnp.dot(a, b, preferred_element_type=jnp.float32)


def low(value):
    return value.astype(jnp.bfloat16)


def wide_float(value):
    return value.astype(jnp.float32)


def norm(values):
    centred = values - jnp.mean(values, axis=-1, keepdims=True)
    scale = lax.rsqrt(jnp.mean(centred * centred, axis=-1, keepdims=True) + layer_epsilon)
    return centred * scale, scale


def norm_back(grad, normed, scale):
    pulled = grad - jnp.mean(grad, axis=-1, keepdims=True) - normed * jnp.mean(grad * normed, axis=-1, keepdims=True)
    return scale * pulled


def item_mask(lengths, shape):
    return lax.broadcasted_iota(jnp.int32, shape, 0) >= lengths[0, 0]


def choices(routes, square):
    square[...] = jnp.zeros_like(square)
    square[0 : routes.shape[0], :] = wide_float(routes[...])
    named = square[...].T
    lane = wide_float(lax.broadcasted_iota(jnp.int32, (1, 128), 1))
    return (named[:, 0:1] == lane) | (named[:, 1:2] == lane)


def own_modulation(here, mod, item, half, part):
    first = 2 * here[3]
    model = item.shape[1]
    at = slice(part * model, (part + 1) * model)
    return jnp.where(item, mod[half, pl.ds(first + 1, 1), at], mod[half, pl.ds(first, 1), at])


def frequencies(model_width):
    half = model_width // 2
    return np.tile(np.exp(-math.log(10000.0) * np.arange(half) / half).astype(np.float32), 2)


def conditions(steps, shape, first, column, half, frequency):
    row = lax.broadcasted_iota(jnp.int32, shape, 0) - first
    angle = jnp.where(row == 0, wide_float(steps[0]), wide_float(steps[1])) * frequency
    wave = jnp.where(column < half, jnp.cos(angle), jnp.sin(angle))
    value = wave / (1.0 + jnp.exp(-wave))
    return wide_float(low(jnp.where((row == 0) | (row == 1), value, 0.0)))


def head_lanes():
    lane = lax.broadcasted_iota(jnp.int32, (1, 128), 1)
    return lane < 64, [low(wide_float(lane < 64)), low(wide_float(lane >= 64))]


def front_kernel(
    lengths, steps, tokens, cotangent, routes, waves, w_ada, w_qkv, w_out, w_router, w_fc1, e1,
    w1, w1s_out, qkv_w, out_w, mod_out, mixed_out, grad_out, gates_out, attn_in_out, qkv_out, probs_out, attn_low_out, attn_proj_out, middle_out, chance_out,
    w1s, mod, mixed, grad, gates, attn_in, qkv, probs, attn_low, attn_proj, middle, chance,
    square, cond, strip_own, f1, s_got, s_rows, q_full, o_full, a_full, q_fold, o_fold, a_fold, q_stage, o_stage, a_stage, q_block, o_block, c_buf, z_part, z_got,
    pre_send, pre_recv, g_send, g_recv, g_pair, a_send, a_recv, a_pair_send, a_pair, b_send, b_recv, b_pair, l_sem, o_sem,
    c_send, c_recv, m_send, m_recv, r_send, r_recv,
):
    here = y, z, x, c = place()
    me, k, gy = chip(y, z, x), 2 * z + x, 4 * z + 2 * x + c
    rows, model = w_out.shape
    others = [(dy, dz, dx) for dy in (0, 1) for dz in (0, 1, 2, 3) for dx in (0, 1) if (dy, dz, dx) != (0, 0, 0)]
    spot = lambda dy, dz, dx: (1 - y if dy else y, along(z, dz), 1 - x if dx else x)
    sibling = device(y, z, x, 1 - c)
    crossed = [device(y, along(z, step), x, 1 - c) for step in LINE]
    meet([device(*spot(*o), c) for o in others] + [sibling] + crossed)

    started = []

    def go(copy):
        copy.start()
        started.append(copy)

    lane = lax.broadcasted_iota(jnp.int32, cond.shape[1:], 1)
    for at in range(4):
        column = model // 2 * (lane // (4 * rows)) + 4 * rows * at + lane % (4 * rows)
        cond[at] = jnp.where(lane < 8 * rows, conditions(steps, cond.shape[1:], 2 * c, column, model // 2, waves[at : at + 1, :]), 0.0)
    for i, (step, core) in enumerate([(0, 1 - c)] + [(step, core) for step in LINE for core in (c, 1 - c)]):
        go(remote(cond.at[along(z, step)], c_buf.at[z, c], c_send.at[i], c_recv.at[z, c], device(y, along(z, step), x, core)))

    mine = pl.ds(pl.multiple_of(rows * c, 8), rows)
    square[...] = jnp.zeros_like(square)
    square[0 : w_router.shape[0], 0:rows] = wide_float(w_router[...])
    router = square[...].T[:rows]
    for i, (w, fold, stage) in enumerate(((w_ada, a_fold, a_stage), (w_qkv, q_fold, q_stage), (w_out, o_fold, o_stage))):
        cut = w.shape[1] // 2
        for h in (0, 1):
            fold[h, :, :cut] = wide_float(w[:, h * cut : (h + 1) * cut])
            if i == 2:
                fold[h, :, cut:] = router
        go(remote(fold.at[1 - c], stage.at[mine, :], pre_send.at[i], pre_recv.at[i], sibling))
        stage[mine, :] = fold[c]

    depth, width = e1.shape[1], w1.shape[2]
    cols = lambda n: pl.ds(pl.multiple_of(width * n, 128), width)
    strip = lambda n: pl.ds(pl.multiple_of(depth * n, 16), depth)
    load = pltpu.make_async_copy(e1.at[:, :, cols(k)], strip_own, l_sem.at[0])
    load.start()
    plane = [o for o in others if o[0] == 0]

    def send_experts(steps, aside):
        for i, o in enumerate(plane):
            if o[1] in steps and o[2] == aside:
                ty, tz, tx = spot(*o)
                go(remote(e1.at[:, :, cols(2 * tz + tx)], w1.at[:, strip(gy), :], a_send.at[i], a_recv.at[k], device(ty, tz, tx, c)))

    send_experts((1,), 0)

    def folded(i, stage):
        theirs = stage.at[pl.ds(pl.multiple_of(rows * (1 - c), 8), rows), :]
        remote(theirs, theirs, pre_send.at[i], pre_recv.at[i], sibling).wait_recv()
        return low(stage[...])

    block = folded(0, a_stage)
    width_a = a_full.shape[3]
    number = 2 * y + x
    to_y, to_x = device(1 - y, z, x, c), device(y, z, 1 - x, c)
    for i in (0, 1):
        a_full[i, number] = block[:, i * width_a : (i + 1) * width_a]

    def send_a(i, n, lane, to):
        go(remote(a_full.at[i, n], a_full.at[i, n], r_send.at[i, lane], r_recv.at[i, n], to))

    def wait_a(i, n):
        remote(a_full.at[i, n], a_full.at[i, n], r_send.at[0, 0], r_recv.at[i, n], sibling).wait_recv()

    send_a(0, number, 0, to_y)
    send_a(1, number, 0, to_x)
    send_a(0, number, 1, to_x)
    send_a(1, number, 1, to_y)
    q_block[...] = folded(1, q_stage)
    o_block[...] = folded(2, o_stage)
    gathers = []
    for i, (block, full, y_first) in enumerate(((q_block, q_full, False), (o_block, o_full, True))):
        slot = functools.partial(lambda full, n: full.at[c, pl.ds(pl.multiple_of(2 * rows * n, 16), 2 * rows), :], full)
        gathers.append(Gather(here, y_first, block, slot, g_send.at[i], g_recv.at[i], g_pair.at[i]))
        slot(me)[...] = block[...]
    gather_start(gathers)

    n_y, n_x = 2 * (1 - y) + x, 2 * y + 1 - x
    n_xy = 2 * (1 - y) + 1 - x
    wait_a(0, n_y)
    send_a(0, n_y, 2, to_x)
    wait_a(1, n_x)
    send_a(1, n_x, 2, to_y)
    gather_second(gathers, 0)

    c_buf[z, c] = cond[z]
    for step, core in [(0, 1 - c)] + [(step, core) for step in LINE for core in (c, 1 - c)]:
        block = c_buf.at[along(z, step), core]
        remote(block, block, c_send.at[0], c_recv.at[along(z, step), core], sibling).wait_recv()
    lhs = low(jnp.concatenate([c_buf[i, 0] + c_buf[i, 1] for i in range(4)], axis=0))[:, : 8 * rows]
    for i, n_last in enumerate((n_x, n_y)):
        wait_a(i, n_last)
        wait_a(i, n_xy)
        term = nn(lhs, a_full[i].reshape(8 * rows, width_a))
        for line in range(4):
            z_part[line, 4 * i : 4 * (i + 1), :] = term[8 * line : 8 * line + 4]
    for step in LINE:
        at = along(z, step)
        go(remote(z_part.at[at], z_got.at[step - 1], m_send.at[step], m_recv.at[step], device(y, at, x, c)))
    send_experts((2, 3), 0)
    gather_line(gathers, 1)
    slim = w1s.shape[1]
    for n in range(16):
        block = wide_float(w_fc1[:, slim * n : slim * (n + 1)])
        f1[n] = low(jnp.concatenate([block, jnp.zeros((f1.shape[1] - rows, slim), jnp.float32)], axis=0))
    for i, o in enumerate(others):
        ty, tz, tx = spot(*o)
        go(remote(f1.at[chip(ty, tz, tx)], s_got.at[c, me], b_send.at[i], b_recv.at[me], device(ty, tz, tx, c)))
    s_got[c, me] = f1[me]
    gather_second(gathers, 1)
    gather_line(gathers, 2)
    send_experts((0, 1, 2, 3), 1)
    gather_second(gathers, 2)
    gather_line(gathers, 3)
    gather_second(gathers, 3)
    total = z_part[z]
    for step in LINE:
        remote(z_got.at[step - 1], z_got.at[step - 1], m_send.at[0], m_recv.at[step], sibling).wait_recv()
        total = total + z_got[step - 1]
    mod[c] = jnp.concatenate([total, pltpu.roll(total, 4, 0)], axis=1)
    go(remote(mod.at[c], mod.at[c], m_send.at[0], m_recv.at[0], sibling))
    remote(mod.at[1 - c], mod.at[1 - c], m_send.at[0], m_recv.at[0], sibling).wait_recv()

    item = item_mask(lengths, tokens.shape)
    residual = wide_float(tokens[...])
    normed, _ = norm(residual)
    attn_in[...] = low(normed * (1.0 + own_modulation(here, mod, item, 0, 1)) + own_modulation(here, mod, item, 0, 0))
    grad[...] = low(wide_float(cotangent[...]) * own_modulation(here, mod, item, 1, 2))
    for step in (0,) + LINE:
        gather_third(gathers, step)
    for gather in gathers:
        gather.finish()
    keep = []

    def leave(source, target):
        keep.append(pltpu.make_async_copy(source, target, o_sem.at[len(keep)]))
        keep[-1].start()

    leave(q_full, qkv_w)
    leave(o_full, out_w)

    cut = q_full.shape[2]
    for h in (0, 1):
        qkv[:, h * cut : (h + 1) * cut] = low(nn(attn_in[...], q_full[h]))

    side = wide_float(item[:, :128])
    same = side == side.T
    left, sides = head_lanes()
    for pair in range(model // 128):
        q, key, value = [qkv[:, base + 128 * pair : base + 128 * (pair + 1)] for base in (0, model, 2 * model)]
        outs = []
        for j, side in enumerate(sides):
            scores = jnp.where(same, nt(q * side, key) * 0.125, -1e30)
            weight = jnp.exp(scores - jnp.max(scores, axis=-1, keepdims=True))
            prob = weight / jnp.sum(weight, axis=-1, keepdims=True)
            probs[2 * pair + j] = prob
            outs.append(nn(low(prob), value))
        attn_low[:, 128 * pair : 128 * (pair + 1)] = low(jnp.where(left, outs[0], outs[1]))
    cut = model // 2
    for h in (0, 1):
        attn_proj[:, h * cut : (h + 1) * cut] = nn(attn_low[...], o_full[h, :, :cut])
    middle[...] = residual + own_modulation(here, mod, item, 0, 2) * attn_proj[...]
    normed, _ = norm(middle[...])
    mixed[...] = low(normed * (1.0 + own_modulation(here, mod, item, 1, 1)) + own_modulation(here, mod, item, 1, 0))
    lane = lax.broadcasted_iota(jnp.int32, (1, 128), 1)
    logits = jnp.where(lane < 8, nn(mixed[...], o_full[0, :, cut:]), -1e30)
    weight = jnp.exp(logits - jnp.max(logits, axis=-1, keepdims=True))
    chance[...] = weight / jnp.sum(weight, axis=-1, keepdims=True)
    turned = jnp.where(choices(routes, square), chance[...], 0.0).T[:8]
    high = low(turned)
    gates[...] = jnp.concatenate([high, low(turned - wide_float(high))], axis=0)
    for source, target in (
        (mixed, mixed_out), (grad, grad_out), (gates, gates_out), (mod, mod_out), (attn_in, attn_in_out), (qkv, qkv_out), (probs, probs_out),
        (attn_low, attn_low_out), (attn_proj, attn_proj_out), (middle, middle_out), (chance, chance_out),
    ):
        leave(source, target)

    for o in others:
        n = chip(*spot(*o))
        remote(s_got.at[c, n], s_got.at[c, n], b_send.at[0], b_recv.at[n], sibling).wait_recv()
    go(remote(s_got.at[c], s_got.at[c], b_pair.at[0], b_pair.at[1], sibling))


    load.wait()
    leave(strip_own, w1.at[:, strip(gy), :])
    for i, o in enumerate([(0, 0, 0)] + [o for step in (0, 1, 3, 2) for o in plane if o[1] == step]):
        _, sz, sx = spot(*o)
        source = 2 * sz + sx
        block = w1.at[:, strip(2 * source + c), :]
        if i:
            remote(block, block, a_send.at[0], a_recv.at[source], sibling).wait_recv()
        go(remote(block if i else strip_own, block, a_pair_send.at[i], a_pair.at[source], sibling))
    remote(s_got.at[1 - c], s_got.at[1 - c], b_pair.at[0], b_pair.at[1], sibling).wait_recv()
    for n in range(32):
        s_rows[n * rows : (n + 1) * rows, :] = wide_float(s_got[n % 2, n // 2])[:rows]
    w1s[...] = low(s_rows[...])
    leave(w1s, w1s_out)
    for copy in started:
        copy.wait_send()
    for source in range(8):
        block = w1.at[:, strip(2 * source + 1 - c), :]
        remote(block, block, a_send.at[0], a_pair.at[source], sibling).wait_recv()
    for copy in keep:
        copy.wait()


def front(lengths, timesteps, tokens, cotangent, routes, w_ada, w_qkv, w_out, w_router, w_fc1, e_fc1):
    rows, model = w_out.shape
    toks = tokens.shape[0]
    waves = frequencies(model).reshape(2, 4, 4 * rows).transpose(1, 0, 2).reshape(4, 8 * rows)
    waves = np.pad(waves, ((0, 0), (0, -8 * rows % 128)))
    ff = w_fc1.shape[1]
    slim, wide = ff // 16, ff // 8
    experts = e_fc1.shape[0]
    bf, f32 = jnp.bfloat16, jnp.float32
    shape = jax.ShapeDtypeStruct
    q_half, o_half, a_half = w_qkv.shape[1] // 2, w_out.shape[1] // 2 + 128, w_ada.shape[1] // 2
    shapes = (
        shape((experts, model, wide), bf),
        shape((model, slim), bf),
        shape((2, model, q_half), bf),
        shape((2, model, o_half), bf),
        shape((2, 8, a_half), f32),
        shape((toks, model), bf),
        shape((toks, model), bf),
        shape((16, toks), bf),
        shape((toks, model), bf),
        shape((toks, 3 * model), bf),
        shape((HEADS, toks, toks), f32),
        shape((toks, model), bf),
        shape((toks, model), f32),
        shape((toks, model), f32),
        shape((toks, 128), f32),
    )
    result = pl.pallas_call(
        front_kernel,
        out_shape=shapes,
        in_specs=[pl.BlockSpec(memory_space=pltpu.SMEM)] * 2
        + [pl.BlockSpec(memory_space=VMEM)] * 9
        + [pl.BlockSpec(memory_space=ANY)],
        out_specs=[pl.BlockSpec(memory_space=ANY)] * 15,
        scratch_shapes=[VMEM(a.shape, a.dtype) for a in (shapes[1], *shapes[4:])]
        + [
            VMEM((128, 128), f32), VMEM((4, 8, 8 * rows + -8 * rows % 128), f32), VMEM((experts, e_fc1.shape[1], wide), bf), VMEM((16, 32, slim), bf), VMEM((2, 16, 32, slim), bf), VMEM((model, slim), f32),
            VMEM((2, model, q_half), bf), VMEM((2, model, o_half), bf), VMEM((2, 4, 2 * rows, a_half // 2), bf),
            VMEM((2, rows, q_half), f32), VMEM((2, rows, o_half), f32), VMEM((2, rows, a_half), f32),
            VMEM((2 * rows, q_half), f32), VMEM((2 * rows, o_half), f32), VMEM((2 * rows, a_half), f32),
            VMEM((2 * rows, q_half), bf), VMEM((2 * rows, o_half), bf),
            VMEM((4, 2, 8, 8 * rows + -8 * rows % 128), f32), VMEM((4, 8, a_half // 2), f32), VMEM((3, 8, a_half // 2), f32),
            DMA((3,)), DMA((3,)), DMA((2, 31)), DMA((2, 16)), DMA((2, 16)), DMA((7,)), DMA((8,)), DMA((8,)), DMA((8,)),
            DMA((15,)), DMA((16,)), DMA((2,)), DMA((1,)), DMA((15,)), DMA((7,)), DMA((4, 2)), DMA((4,)), DMA((4,)), DMA((2, 3)), DMA((2, 4)),
        ],
        compiler_params=pltpu.CompilerParams(collective_id=1, has_side_effects=True, vmem_limit_bytes=62 << 20),
        name="front",
    )(lengths, timesteps, tokens, cotangent, routes.T, waves, w_ada, w_qkv, w_out, w_router.T, w_fc1, e_fc1)
    return result


def gelu_both(h):
    root = math.sqrt(2.0 / math.pi)
    square = h * h
    t = jnp.tanh(h * (root + (root * 0.044715) * square))
    half = 0.5 * (1.0 + t)
    slope = half + (0.5 * h) * (1.0 - t * t) * (root + (3.0 * root * 0.044715) * square)
    return h * half, slope


def ffn_chunk(xt, gt, w1, w2, gate, row):
    a, d = gelu_both(nn(xt, w1))
    gi = nt(gt, w2)
    product = None
    if gate is not None:
        product = nt(row, (a * gi).astype(jnp.bfloat16))
        a, d = a * gate, d * gate
    a = a.astype(jnp.bfloat16)
    p = (gi * d).astype(jnp.bfloat16)
    return a, p, nn(a, w2), nt(p, w1), product


def ffn_shared(slots, X, G, w1s, w2s, act_s, pre_s, sums, sums_back):
    toks = X.shape[1]
    xt = jnp.concatenate([X[n] for n in slots], axis=0)
    gt = jnp.concatenate([G[n] for n in slots], axis=0)
    a, p, total, total_back, _ = ffn_chunk(xt, gt, w1s[...], w2s[...], None, None)
    for i, n in enumerate(slots):
        act_s[n] = a[i * toks : (i + 1) * toks]
        pre_s[n] = p[i * toks : (i + 1) * toks]
    sums[...] = total
    sums_back[...] = total_back


def ffn_experts(low, high, slots, X, G, gates, w1, w2, act, pre, sums, sums_back, gc):
    experts, toks, wide = w1.shape[0], X.shape[1], w1.shape[2]
    first = lax.axis_index("gx") * experts
    xt = jnp.concatenate([X[n] for n in slots], axis=0)
    gt = jnp.concatenate([G[n] for n in slots], axis=0)

    def expert(e, product):
        kind = lax.broadcasted_iota(jnp.int32, (16, 128), 0)
        spread = ((kind == first + e) | (kind == first + e + 8)).astype(jnp.bfloat16)
        gate = jnp.concatenate([tn(gates[n], spread) for n in slots], axis=0)
        gate = jnp.concatenate([gate] * (wide // 128), axis=1)
        row = (lax.broadcasted_iota(jnp.int32, (8, wide), 0) == first + e).astype(jnp.bfloat16)
        a, p, total, total_back, more = ffn_chunk(xt, gt, w1[e], w2[e], gate, row)
        for i, n in enumerate(slots):
            act[e, n] = a[i * toks : (i + 1) * toks]
            pre[e, n] = p[i * toks : (i + 1) * toks]
        sums[...] += total
        sums_back[...] += total_back
        return product + more

    product = lax.fori_loop(low, high, expert, jnp.zeros((8, len(slots) * toks), jnp.float32))
    for i, n in enumerate(slots):
        part = product[:, i * toks : (i + 1) * toks]
        gc[n] = part if low == 0 else gc[n] + part


def block_kernel(
    mixed, grad, gates, w1_in, w1s_in, w2_in, w2s_in,
    sum_branch, sum_back, sum_gc, near1, far1, out1s, out2, out2s,
    own1, own1s, own2, own2s, X, G, gt, w1, w1s, w2, w2s, act, pre, act_s, pre_s, tile_sum, tile_back,
    p_branch, p_back, p_gc, r_branch, r_back, r_gc, d1, d1s, d2, d2s, from1, from1s, from2, from2s,
    l_sem, o_sem, g_send, g_recv, send, recv, t_send, t_recv, w_send, w_recv, h_send, h_recv,
):
    here = y, z, x, c = place()
    me = chip(y, z, x)
    spot = lambda dy, dz, dx: (1 - y if dy else y, along(z, dz), 1 - x if dx else x)
    sibling = device(y, z, x, 1 - c)
    experts = w1.shape[0]
    meet(cross_partners(here) + [sibling])

    gathers, local = [], []
    for i, (block, full, y_first) in enumerate(((mixed, X, True), (grad, G, False), (gates, gt, True))):
        slot = functools.partial(lambda full, n: full.at[n], full)
        gathers.append(Gather(here, y_first, block, slot, g_send.at[i], g_recv.at[i]))
        local.append(pltpu.make_async_copy(block, slot(me), l_sem.at[i]))
    gather_start(gathers)
    half2, half2s = w2_in.shape[1], w2s_in.shape[0]
    own2_at = w2.at[:, pl.ds(pl.multiple_of(half2 * c, 16), half2), :]
    own2s_at = w2s.at[pl.ds(pl.multiple_of(half2s * c, 16), half2s), :]
    for i, (source, target) in enumerate(((w1_in, w1), (w1s_in, w1s), (w2_in, own2_at), (w2s_in, own2s_at))):
        local.append(pltpu.make_async_copy(source, target, l_sem.at[3 + i]))
    for i, (source, target) in enumerate(((w2_in, own2_at), (w2s_in, own2s_at))):
        local.append(remote(source, target, w_send.at[i], w_recv.at[i], sibling))
    for copy in local:
        copy.start()

    def tile(step, part):
        slots = [chip(*spot(dy, step, dx)) for dy in (0, 1) for dx in (0, 1)]
        if part == 0:
            ffn_shared(slots, X, G, w1s, w2s, act_s, pre_s, tile_sum, tile_back)
        low, high = (0, experts // 2) if part == 0 else (experts // 2, experts)
        ffn_experts(low, high, slots, X, G, gt, w1, w2, act, pre, tile_sum, tile_back, p_gc)
        if part == 1:
            toks = X.shape[1]
            for i, n in enumerate(slots):
                at = slice(i * toks, (i + 1) * toks)
                p_branch[n] = tile_sum[at, :].astype(jnp.bfloat16)
                p_back[n] = tile_back[at, :].astype(jnp.bfloat16)

    scatters = []
    for i, (part, got, y_first) in enumerate(((p_branch, r_branch, False), (p_back, r_back, True), (p_gc, r_gc, False))):
        take = functools.partial(lambda ref, n: ref.at[n], part)
        land = functools.partial(lambda ref, n: ref.at[n], got)
        scatters.append(Scatter(here, y_first, take, land, send.at[i], recv.at[i]))

    def back_first(step):
        for scatter in scatters:
            scatter.first(step)

    gather_second(gathers, 0)
    gather_line(gathers, 1)
    gather_second(gathers, 1)
    gather_third(gathers, 0)
    for copy in local:
        copy.wait()
    tile(0, 0)
    gather_line(gathers, 2)
    tile(0, 1)
    gather_third(gathers, 1)
    tile(1, 0)
    gather_second(gathers, 2)
    tile(1, 1)
    gather_line(gathers, 3)
    gather_third(gathers, 2)
    tile(2, 0)
    gather_second(gathers, 3)
    tile(2, 1)
    back_first(2)
    gather_third(gathers, 3)
    tile(3, 0)

    def back_one(b, step):
        for scatter in scatters:
            scatter.one(b, step)

    def back_two(step):
        for scatter in scatters:
            scatter.two(step)

    flat = lambda value: value.reshape(value.shape[0] * value.shape[1], value.shape[2])
    twins = [None] * (2 * experts)
    leaving, homeward = [], []

    def leave(source, target):
        leaving.append(pltpu.make_async_copy(source, target, o_sem.at[len(leaving)]))
        leaving[-1].start()


    def weight(e):
        d1[e] = tn(flat(X[...]), flat(pre[e])).astype(jnp.bfloat16).reshape(d1.shape[1:])
        d2[e] = tn(flat(act[e]), flat(G[...])).astype(jnp.bfloat16).reshape(d2.shape[1:])
        for i, (part, got) in enumerate(((d1.at[e, :, 1 - c], from1.at[e]), (d2.at[e, 1 - c], from2.at[e]))):
            twins[2 * e + i] = remote(part, got, t_send.at[2 * e + i], t_recv.at[2 * e + i], sibling)
            twins[2 * e + i].start()

    def home(e):
        twins[2 * e].wait()
        own1[e] = (d1[e, :, c].astype(jnp.float32) + from1[e].astype(jnp.float32)).astype(jnp.bfloat16)
        twins[2 * e + 1].wait()
        own2[e] = d2[e, c].astype(jnp.float32) + from2[e].astype(jnp.float32)
        leave(own2.at[e], out2.at[e])
        for i in range(4):
            leave(own1.at[e, 2 * i + 1 - x], far1.at[e, i])
        leave(own1.at[e, 2 * z + x], near1.at[e, z])

    def along_home(e):
        for step in LINE:
            at = along(z, step)
            sent = remote(own1.at[e, 2 * at + x], near1.at[e, z], h_send.at[e, step], h_recv.at[e, z], device(y, at, x, c))
            sent.start()
            homeward.append(sent)


    back_one(1, 2)
    tile(3, 1)
    back_first(3)
    back_one(0, 2)
    back_two(2)
    weight(0)
    back_one(1, 3)
    back_first(1)
    weight(1)
    home(0)
    back_one(0, 3)
    back_two(3)
    home(1)
    back_one(1, 1)
    back_first(0)
    weight(2)
    back_one(0, 1)
    along_home(0)
    along_home(1)
    back_two(1)
    home(2)
    back_one(1, 0)
    along_home(2)
    weight(3)
    d1s[...] = tn(flat(X[...]), flat(pre_s[...])).reshape(d1s.shape)
    d2s[...] = tn(flat(act_s[...]), flat(G[...])).astype(jnp.bfloat16).reshape(d2s.shape)
    twin1s = remote(d1s.at[:, 1 - c], from1s, t_send.at[2 * experts], t_recv.at[2 * experts], sibling)
    twin2s = remote(d2s.at[1 - c], from2s, t_send.at[2 * experts + 1], t_recv.at[2 * experts + 1], sibling)
    twin1s.start()
    twin2s.start()
    home(3)
    along_home(3)
    back_one(0, 0)
    twin1s.wait()
    total = d1s[:, c] + from1s[...]
    own1s[...] = low(jnp.concatenate([total, jnp.zeros((16, own1s.shape[1] - total.shape[1], total.shape[2]), jnp.float32)], axis=1))
    twin2s.wait()
    own2s[...] = d2s[c].astype(jnp.float32) + from2s[...].astype(jnp.float32)
    leave(own1s, out1s)
    leave(own2s, out2s)
    back_two(0)
    sum_branch[...] = scatters[0].total()
    sum_back[...] = scatters[1].total()
    sum_gc[...] = scatters[2].total()
    for copy in leaving:
        copy.wait()
    for sent in homeward:
        sent.wait_send()
    for e in range(experts):
        for step in LINE:
            block = near1.at[e, along(z, step)]
            remote(block, block, h_send.at[0, 0], h_recv.at[e, along(z, step)], sibling).wait_recv()
    for gather in gathers:
        gather.finish()
    for scatter in scatters:
        scatter.finish()


def block(mixed, grad, gates, w1, w1s, e_fc2, w_fc2):
    bf, f32 = jnp.bfloat16, jnp.float32
    toks, model = mixed.shape
    experts, _, wide = w1.shape
    slim = w1s.shape[1]
    rows = model // 32
    shape = jax.ShapeDtypeStruct
    blocks = lambda *dims: VMEM((16, toks) + dims, bf)
    return pl.pallas_call(
        block_kernel,
        out_shape=[
            shape((toks, model), f32),
            shape((toks, model), f32),
            shape((8, 128), f32),
            shape((experts, 4, 2 * rows, wide), bf),
            shape((experts, 4, 2 * rows, wide), bf),
            shape((16, 32, slim), bf),
            shape((experts, wide // 2, model), f32),
            shape((slim // 2, model), f32),
        ],
        in_specs=[pl.BlockSpec(memory_space=VMEM)] * 3 + [pl.BlockSpec(memory_space=ANY)] * 4,
        out_specs=[pl.BlockSpec(memory_space=VMEM)] * 3 + [pl.BlockSpec(memory_space=ANY)] * 5,
        scratch_shapes=[
            VMEM((experts, 8, 2 * rows, wide), bf), VMEM((16, 32, slim), bf), VMEM((experts, wide // 2, model), f32), VMEM((slim // 2, model), f32),
            blocks(model), blocks(model), VMEM((16, 16, 128), bf),
            VMEM(w1.shape, bf), VMEM(w1s.shape, bf), VMEM((experts, wide, model), bf), VMEM((slim, model), bf),
            VMEM((experts, 16, toks, wide), bf), VMEM((experts, 16, toks, wide), bf), blocks(slim), blocks(slim),
            VMEM((4 * toks, model), f32), VMEM((4 * toks, model), f32),
            blocks(model), blocks(model), VMEM((16, 8, 128), f32),
            VMEM((15, toks, model), bf), VMEM((15, toks, model), bf), VMEM((15, 8, 128), f32),
            VMEM((experts, 8, 2, 2 * rows, wide), bf), VMEM((16, 2, rows, slim), f32),
            VMEM((experts, 2, wide // 2, model), bf), VMEM((2, slim // 2, model), bf),
            VMEM((experts, 8, 2 * rows, wide), bf), VMEM((16, rows, slim), f32),
            VMEM((experts, wide // 2, model), bf), VMEM((slim // 2, model), bf),
            DMA((7,)), DMA((6 * experts + 2,)), DMA((3, 15)), DMA((3, 16)), DMA((3, 15)), DMA((3, 15)), DMA((2 * experts + 2,)), DMA((2 * experts + 2,)),
            DMA((2,)), DMA((2,)), DMA((experts, 4)), DMA((experts, 4)),
        ],
        compiler_params=pltpu.CompilerParams(collective_id=2, has_side_effects=True, vmem_limit_bytes=62 << 20),
        name="block",
    )(mixed, grad, gates, w1, w1s, e_fc2, w_fc2)


def rear_kernel(lengths, steps, waves, *refs):
    incoming, refs = refs[:15], refs[15:]
    (qkv_in, out_in, part1, part1s, output, d_tokens, d_ada, d_qkv, d_out, d_router, own1, own1s), refs = refs[:12], refs[12:]
    (sum_branch, sum_back, sum_gc, tokens, cotangent, routes, mod, mixed, attn_in, qkv, probs, attn_low, attn_proj, middle, chance), refs = refs[:15], refs[15:]
    (square, slice_own, q_w, o_w, grad_attn, grad_qkv, grad_mid, o_mine, o_got, q_mine, q_got, part_o, part_a, part_b, got_o, got_a, got_b, fin, mod_tile, all_mod, l_sem, s_send, s_recv, send, recv, g_send, g_recv, g_pair, f_send, f_recv, a_send, a_recv, b_send, b_recv, i_sem) = refs
    here = y, z, x, c = place()
    me = chip(y, z, x)
    sibling = device(y, z, x, 1 - c)
    others = [(dy, dz, dx) for dy in (0, 1) for dz in (0, 1, 2, 3) for dx in (0, 1) if (dy, dz, dx) != (0, 0, 0)]
    spot = lambda dy, dz, dx: (1 - y if dy else y, along(z, dz), 1 - x if dx else x)
    held = (sum_branch, sum_back, sum_gc, tokens, cotangent, routes, mod, mixed, attn_in, qkv, probs, attn_low, attn_proj, middle, chance)
    loads = [pltpu.make_async_copy(a, b, i_sem.at[i]) for i, (a, b) in enumerate(zip(incoming, held))]
    local = [pltpu.make_async_copy(qkv_in, q_w, l_sem.at[0]), pltpu.make_async_copy(out_in, o_w, l_sem.at[1])]
    for copy in loads + local:
        copy.start()
    meet([device(*spot(*o), c) for o in others] + [sibling])
    started = []

    def go(copy):
        copy.start()
        started.append(copy)

    home = [pltpu.make_async_copy(part1s.at[me], slice_own, l_sem.at[3])]
    home[0].start()
    for step in (0, 1, 2, 3):
        at = along(z, step)
        go(remote(part1.at[:, at], own1.at[:, z], a_send.at[step], a_recv.at[z], device(y, at, 1 - x, c)))
    for i, o in enumerate(others):
        go(remote(part1s.at[chip(*spot(*o))], own1s.at[me], b_send.at[i], b_recv.at[me], device(*spot(*o), c)))

    for copy in loads:
        copy.wait()
    item = item_mask(lengths, tokens.shape)
    first = ~item
    model = item.shape[1]
    cut = model // 2
    modulation = functools.partial(own_modulation, here, mod, item)
    rows16 = {}

    def per_item(part, value):
        for i, mask in enumerate((first, ~first)):
            rows16[2 * part + i] = jnp.sum(jnp.where(mask, value, 0.0), axis=0, keepdims=True)

    out_grad = wide_float(cotangent[...])
    branch = sum_branch[...]
    output[...] = low(middle[...] + modulation(1, 2) * branch)
    per_item(5, out_grad * branch)
    chosen = choices(routes, square)
    turned = jnp.concatenate([sum_gc[...], jnp.zeros((120, 128), jnp.float32)], axis=0).T
    grad_chance = jnp.where(chosen, turned, 0.0)
    share = chance[...]
    grad_logits = low(share * (grad_chance - jnp.sum(grad_chance * share, axis=-1, keepdims=True)))
    term_router = tn(mixed[...], grad_logits)
    for copy in local + home:
        copy.wait()
    home = [pltpu.make_async_copy(slice_own, own1s.at[me], l_sem.at[3])]
    home[0].start()
    grad_mixed = sum_back[...] + nt(grad_logits, o_w[0, :, cut:])
    normed, scale = norm(middle[...])
    per_item(3, grad_mixed)
    per_item(4, grad_mixed * normed)
    grad_mid[...] = out_grad + norm_back(grad_mixed * (1.0 + modulation(1, 1)), normed, scale)
    per_item(2, grad_mid[...] * attn_proj[...])
    grad_proj = low(grad_mid[...] * modulation(0, 2))
    for h in (0, 1):
        term = jnp.concatenate([tn(attn_low[...], grad_proj[:, h * cut : (h + 1) * cut]), term_router], axis=1)
        o_mine[h] = low(term)
    swap_o = remote(o_mine.at[1 - c], o_got, s_send.at[0], s_recv.at[0], sibling)
    swap_o.start()
    grad_attn[...] = low(nt(grad_proj[:, :cut], o_w[0, :, :cut]) + nt(grad_proj[:, cut:], o_w[1, :, :cut]))

    rows = o_got.shape[0] // 16
    scatters = []
    for i, (part, got, y_first) in enumerate(((part_o, got_o, False), (part_a, got_a, True), (part_b, got_b, False))):
        take = functools.partial(lambda ref, n: ref.at[n], part)
        land = functools.partial(lambda ref, n: ref.at[n], got)
        scatters.append(Scatter(here, y_first, take, land, send.at[i], recv.at[i], relay=True))

    swap_o.wait()
    for n in range(16):
        at = slice(n * rows, (n + 1) * rows)
        part_o[n] = low(wide_float(o_mine[c, at, :]) + wide_float(o_got[at, :]))
    for step in (3, 2, 1, 0):
        scatters[0].first(step)

    left, sides = head_lanes()
    for pair in range(model // 128):
        at = slice(128 * pair, 128 * (pair + 1))
        q, key, value = [qkv[:, base + 128 * pair : base + 128 * (pair + 1)] for base in (0, model, 2 * model)]
        ga = grad_attn[:, at]
        outs = []
        for j, side in enumerate(sides):
            prob = probs[2 * pair + j]
            grad_probs = nt(ga * side, value)
            grad_scores = low(prob * (grad_probs - jnp.sum(grad_probs * prob, axis=-1, keepdims=True)))
            outs.append((nn(grad_scores, key) * 0.125, tn(grad_scores, q) * 0.125, tn(low(prob), ga)))
        for base, one, two in zip((0, model, 2 * model), *outs):
            grad_qkv[:, base + 128 * pair : base + 128 * (pair + 1)] = low(jnp.where(left, one, two))

    third = q_w.shape[2]
    for h in (0, 1):
        q_mine[h] = low(tn(attn_in[...], grad_qkv[:, h * third : (h + 1) * third]))
    swap_q = {}
    for step in (3, 2, 1, 0):
        for side in (0, 1):
            at = pl.ds(pl.multiple_of(2 * rows * (4 * side + along(z, step)), 16), 2 * rows)
            i = 1 + 2 * step + side
            swap_q[step, side] = remote(q_mine.at[1 - c, at, :], q_got.at[at, :], s_send.at[i], s_recv.at[i], sibling)
            swap_q[step, side].start()
    grad_in = nt(grad_qkv[:, :third], q_w[0]) + nt(grad_qkv[:, third:], q_w[1])
    normed, scale = norm(wide_float(tokens[...]))
    per_item(0, grad_in)
    per_item(1, grad_in * normed)
    d_tokens[...] = grad_mid[...] + norm_back(grad_in * (1.0 + modulation(0, 1)), normed, scale)
    column = lax.broadcasted_iota(jnp.int32, (8, model), 1)
    last = jnp.concatenate([rows16[8 + i] for i in range(4)] + [jnp.zeros((4, model), jnp.float32)], axis=0)
    last = last + conditions(steps, (8, model), 4, column, model // 2, waves[...])
    mod_tile[...] = low(jnp.concatenate([rows16[i] for i in range(8)] + [last], axis=0))

    slot = lambda n: all_mod.at[n, c]
    spread = Gather(here, False, mod_tile, slot, g_send, g_recv, g_pair)
    all_mod[me, c] = mod_tile[...]
    gather_start([spread])
    edge = part_a.shape[2]

    def fold(step):
        for side in (0, 1):
            swap_q[step, side].wait()
            first_n = 8 * side + 2 * along(z, step)
            for n in (first_n, first_n + 1):
                at = pl.ds(pl.multiple_of(rows * n, 16), rows)
                total = low(wide_float(q_mine[c, at, :]) + wide_float(q_got[at, :]))
                part_a[n] = total[:, :edge]
                part_b[n] = total[:, edge:]
        for scatter in scatters[1:]:
            scatter.first(step)

    fold(3)
    fold(2)

    def turn(at):
        if at == 1:
            spread.second(0)
            for step in LINE:
                gather_line([spread], step)
        elif at == 2:
            for step in LINE:
                spread.second(step)
        elif at == 3:
            for step in (0,) + LINE:
                spread.third(step)
            spread.finish()
            flat = all_mod[...].reshape(32 * 16, model)
            share_rows = rows // 2
            own = (2 * me + c) * share_rows
            source = lax.broadcasted_iota(jnp.int32, (model, 128), 0)
            lane = lax.broadcasted_iota(jnp.int32, (model, 128), 1)
            own_columns = nn(flat, low(wide_float((source == own + lane) & (lane < share_rows))))
            row = lax.broadcasted_iota(jnp.int32, (512, 128), 0) % 16
            own_columns = jnp.where((row >= 12) & (row < 14), own_columns, 0.0)
            for part in range(6):
                lhs = low(pltpu.roll(own_columns, 512 + 2 * part - 12, 0))
                d_ada[:, part * model : (part + 1) * model] = tn(lhs, flat)[:share_rows]

    scatter_all(scatters, fold, turn)
    fin[c] = jnp.concatenate([scatters[1].total(), scatters[2].total(), scatters[0].total()], axis=1)
    half = rows // 2
    mine = pl.ds(pl.multiple_of(half * c, 8), half)
    theirs = pl.ds(pl.multiple_of(half * (1 - c), 8), half)
    swap = remote(fin.at[c, theirs, :], fin.at[c, theirs, :], f_send, f_recv, sibling)
    swap.start()

    for at in range(4):
        remote(own1.at[:, at], own1.at[:, at], a_send.at[0], a_recv.at[at], sibling).wait_recv()
    for copy in home:
        copy.wait()
    for i, o in enumerate(others):
        n = chip(*spot(*o))
        remote(own1s.at[n], own1s.at[n], b_send.at[i], b_recv.at[n], sibling).wait_recv()
    for scatter in scatters:
        scatter.finish()
    for copy in started:
        copy.wait_send()
    swap.wait_send()
    remote(fin.at[1 - c, mine, :], fin.at[1 - c, mine, :], f_send, f_recv, sibling).wait_recv()
    for h in (0, 1):
        d_qkv[:, h * third : (h + 1) * third] = fin[h, mine, :third]
        d_out[:, h * cut : (h + 1) * cut] = fin[h, mine, third : third + cut]
    d_router[0:half, :] = fin[0, mine, third + cut :]
    d_router[half:, :] = jnp.zeros((128 - half, 128), jnp.float32)


def rear(lengths, timesteps, sums, tokens, cotangent, routes, saved, qkv_w, out_w, part1, part1s):
    bf, f32 = jnp.bfloat16, jnp.float32
    toks, model = tokens.shape
    rows = model // 16
    q_half, o_half = qkv_w.shape[2], out_w.shape[2]
    a_half = model
    incoming = (*sums, tokens, cotangent, routes.T, *saved)
    shape = jax.ShapeDtypeStruct
    return pl.pallas_call(
        rear_kernel,
        out_shape=[
            shape((toks, model), bf),
            shape((toks, model), f32),
            shape((rows // 2, 6 * model), f32),
            shape((rows // 2, 2 * q_half), f32),
            shape((rows // 2, model), f32),
            shape((128, 128), f32),
            shape(part1.shape, bf),
            shape(part1s.shape, bf),
        ],
        in_specs=[pl.BlockSpec(memory_space=pltpu.SMEM)] * 2
        + [pl.BlockSpec(memory_space=VMEM)]
        + [pl.BlockSpec(memory_space=ANY)] * 19,
        out_specs=[pl.BlockSpec(memory_space=VMEM)] * 6 + [pl.BlockSpec(memory_space=ANY)] * 2,
        scratch_shapes=[VMEM(a.shape, a.dtype) for a in incoming]
        + [
            VMEM((128, 128), f32), VMEM(part1s.shape[1:], bf), VMEM(qkv_w.shape, bf), VMEM(out_w.shape, bf),
            VMEM((toks, model), bf), VMEM((toks, 3 * model), bf), VMEM((toks, model), f32),
            VMEM((2, model, o_half), bf), VMEM((model, o_half), bf),
            VMEM((2, model, q_half), bf), VMEM((model, q_half), bf),
            VMEM((16, rows, o_half), bf), VMEM((16, rows, a_half), bf), VMEM((16, rows, q_half - a_half), bf),
            VMEM((15, rows, o_half), bf), VMEM((15, rows, a_half), bf), VMEM((15, rows, q_half - a_half), bf),
            VMEM((2, rows, q_half + o_half), f32), VMEM((16, model), bf), VMEM((16, 2, 16, model), bf),
            DMA((4,)), DMA((9,)), DMA((9,)), DMA((3, 15)), DMA((3, 15)), DMA((31,)), DMA((16,)), DMA((16,)), DMA, DMA,
            DMA((4,)), DMA((4,)), DMA((15,)), DMA((16,)), DMA((16,)),
        ],
        compiler_params=pltpu.CompilerParams(collective_id=3, has_side_effects=True, vmem_limit_bytes=62 << 20),
        name="rear",
    )(lengths, timesteps, frequencies(model)[None], *incoming, qkv_w, out_w, part1, part1s)


def finish_kernel(*refs):
    count = (len(refs) - 3) // 3
    inputs, outputs, staged = refs[:count], refs[count : 2 * count - 1], refs[2 * count - 1 : 3 * count - 1]
    e1, fc1, sem_in, sem = refs[3 * count - 1 :]
    loads = [pltpu.make_async_copy(a, b, sem_in.at[i]) for i, (a, b) in enumerate(zip(inputs, staged))]
    stores = []

    def store(source, target):
        stores.append(pltpu.make_async_copy(source, target, sem.at[len(stores)]))
        stores[-1].start()

    for copy in loads:
        copy.start()
    near, far, slices, router = staged[:4]
    x = place()[2]
    wide = near.shape[3]
    loads[0].wait()
    loads[1].wait()
    for e in range(near.shape[0]):
        for at in range(near.shape[1]):
            e1[e, :, pl.ds(pl.multiple_of(wide * (2 * at + x), 128), wide)] = wide_float(near[e, at])
            e1[e, :, pl.ds(pl.multiple_of(wide * (2 * at + 1 - x), 128), wide)] = wide_float(far[e, at])
        store(e1.at[e], outputs[0].at[e])
    for load, source, target in zip(loads[4:], staged[4:], outputs[3:]):
        load.wait()
        store(source, target)
    loads[2].wait()
    loads[3].wait()
    rows, slim = fc1.shape[0], slices.shape[2]
    for n in range(slices.shape[0] // 2):
        pair = [wide_float(slices[2 * n + i])[:rows] for i in (0, 1)]
        fc1[:, 2 * n * slim : 2 * (n + 1) * slim] = jnp.concatenate(pair, axis=1)
    store(fc1, outputs[1])
    outputs[2][...] = router[...].T[: outputs[2].shape[0], : outputs[2].shape[1]]
    for copy in stores:
        copy.wait()


def finish(near1, far1, own1s, d_router, *others):
    f32 = jnp.float32
    experts, _, depth, wide = near1.shape
    rows = depth // 2
    e1, fc1 = (experts, depth, 8 * wide), (rows, own1s.shape[0] * own1s.shape[2])
    shape = jax.ShapeDtypeStruct
    inputs = (near1, far1, own1s, d_router, *others)
    result = pl.pallas_call(
        finish_kernel,
        out_shape=[shape(e1, f32), shape(fc1, f32), shape((8, rows), f32)] + [shape(a.shape, a.dtype) for a in others],
        in_specs=[pl.BlockSpec(memory_space=ANY)] * len(inputs),
        out_specs=[pl.BlockSpec(memory_space=ANY)] * 2
        + [pl.BlockSpec(memory_space=VMEM)]
        + [pl.BlockSpec(memory_space=ANY)] * len(others),
        scratch_shapes=[VMEM(a.shape, a.dtype) for a in inputs]
        + [VMEM(e1, f32), VMEM(fc1, f32), DMA((len(inputs),)), DMA((8 + len(others),))],
        compiler_params=pltpu.CompilerParams(vmem_limit_bytes=62 << 20),
        name="finish",
    )(*inputs)
    return result[0], result[1], result[2].T, *result[3:]


def layer_norm(values):
    average = jnp.mean(values, axis=-1, keepdims=True)
    centred = values - average
    return centred * lax.rsqrt(jnp.mean(centred * centred, axis=-1, keepdims=True) + layer_epsilon)


def modulate(values, shift_by, scale_by):
    return layer_norm(values) * (1.0 + scale_by) + shift_by


def sinusoid(timesteps, model_width):
    half_width = model_width // 2
    frequency = jnp.exp(-math.log(10000.0) * jnp.arange(half_width, dtype=jnp.float32) / half_width)
    angles = timesteps.astype(jnp.float32)[:, None] * frequency[None, :]
    return jnp.concatenate([jnp.cos(angles), jnp.sin(angles)], axis=1)


def membership(lengths, tok_count):
    bounds = jnp.cumsum(lengths)[:-1]
    position = jnp.arange(tok_count, dtype=jnp.int32)
    item_of = jnp.sum((position[:, None] >= bounds[None, :]).astype(jnp.int32), axis=1)
    item_ids = jnp.arange(lengths.shape[0], dtype=jnp.int32)
    return ((item_of[:, None] == item_ids[None, :]).astype(jnp.float32), item_of)


def slot_index(routes, expert_count, capacity):
    flat_routes = routes.reshape(-1)
    expert_hot = (
        flat_routes[:, None] == jnp.arange(expert_count, dtype=jnp.int32)[None, :]
    ).astype(jnp.int32)
    before = jnp.cumsum(expert_hot, axis=0) - expert_hot
    rank_in = jnp.sum(before * expert_hot, axis=1)
    return (flat_routes * capacity + rank_in).reshape(routes.shape)


def dot_float(left_side, right_side):
    return jnp.dot(left_side, right_side, preferred_element_type=jnp.float32)


def dot_rows(left_side, right_side):
    return jnp.einsum("td,tf->df", left_side, right_side, preferred_element_type=jnp.float32)


def dot_cols(left_side, right_side):
    return jnp.einsum("tf,df->td", left_side, right_side, preferred_element_type=jnp.float32)


def dot_halves(left_side, halves):
    return jnp.concatenate([dot_float(left_side, halves[0]), dot_float(left_side, halves[1])], axis=1)


def by_slices(
    tokens, timesteps, lengths, routes, cotangent, w_ada, w_qkv, w_out, w_fc1, w_fc2, w_router, e_fc1, e_fc2
):
    (w1, w1s, qkv_w, out_w, mod, mixed, grad, gates, attn_in, qkv, probs, attn_low, attn_proj, middle,
     chance) = front(
        lengths, timesteps, tokens, cotangent, routes, w_ada, w_qkv, w_out, w_router, w_fc1, e_fc1
    )
    *sums, near1, far1, part1s, d_e2, d_fc2 = block(mixed, grad, gates, w1, w1s, e_fc2, w_fc2)
    saved = (mod, mixed, attn_in, qkv, probs, attn_low, attn_proj, middle, chance)
    output, d_tokens, d_ada, d_qkv, d_out, d_router, own1, own1s = rear(
        lengths, timesteps, sums, tokens, cotangent, routes, saved, qkv_w, out_w, far1, part1s
    )
    d_e1, d_fc1, d_router, output, d_tokens, d_ada, d_qkv, d_out, d_fc2, d_e2 = finish(
        near1, own1, own1s, d_router, output, d_tokens, d_ada, d_qkv, d_out, d_fc2, d_e2
    )
    return (output, d_tokens, d_ada, d_qkv, d_out, d_fc1, d_fc2, d_router, d_e1, d_e2)


def by_weights(
    tokens,
    timesteps,
    lengths,
    routes,
    cotangent,
    w_ada,
    w_qkv,
    w_out,
    w_fc1,
    w_fc2,
    w_router,
    e_fc1,
    e_fc2,
):
    tok_count, model_width = tokens.shape
    head_count = HEADS
    head_size = model_width // head_count
    expert_count = w_router.shape[1]
    capacity = CAP
    score_scale = head_size ** (-0.5)
    residual = tokens.astype(jnp.float32)
    member, item_of = membership(lengths[0], tok_count)
    ada_full, qkv_full, out_full = (
        lax.all_gather(w_ada, ("gx", "gy"), axis=0, tiled=True),
        lax.all_gather(w_qkv, ("gx", "gy"), axis=0, tiled=True),
        lax.all_gather(w_out, ("gx", "gy"), axis=0, tiled=True),
    )
    condition = jax.nn.silu(sinusoid(timesteps, model_width)).astype(jnp.bfloat16)
    modulation = dot_float(condition, ada_full)
    token_mod = jnp.dot(member, modulation, precision=precise)
    shift_attn, scale_attn, gate_attn, shift_mlp, scale_mlp, gate_mlp = jnp.split(
        token_mod, 6, axis=1
    )
    attn_in = modulate(residual, shift_attn, scale_attn).astype(jnp.bfloat16)
    qkv_low = dot_float(attn_in, qkv_full).astype(jnp.bfloat16)
    queries, key_rows, value_rows = [
        portion.reshape(tok_count, head_count, head_size)
        for portion in jnp.split(qkv_low, 3, axis=1)
    ]
    same_item = item_of[:, None] == item_of[None, :]
    scores = (
        jnp.einsum("qhd,khd->hqk", queries, key_rows, preferred_element_type=jnp.float32)
        * score_scale
    )
    scores = jnp.where(same_item[None], scores, -1e30)
    attn_probs = jax.nn.softmax(scores, axis=-1)
    probs_low = attn_probs.astype(jnp.bfloat16)
    attn_low = jnp.einsum("hqk,khd->qhd", probs_low, value_rows, preferred_element_type=jnp.float32)
    attn_low = attn_low.reshape(tok_count, model_width).astype(jnp.bfloat16)
    attn_proj = dot_float(attn_low, out_full)
    middle = residual + gate_attn * attn_proj
    mixed_in = modulate(middle, shift_mlp, scale_mlp).astype(jnp.bfloat16)
    fc1_full, fc2_full, router_full = (
        lax.all_gather(w_fc1, ("gx", "gy"), axis=0, tiled=True),
        lax.all_gather(w_fc2, ("gx", "gy"), axis=0, tiled=True),
        lax.all_gather(w_router, ("gx", "gy"), axis=0, tiled=True),
    )
    hidden_pre = dot_float(mixed_in, fc1_full)
    hidden = jax.nn.gelu(hidden_pre).astype(jnp.bfloat16)
    shared = dot_float(hidden, fc2_full)
    chance = jax.nn.softmax(dot_float(mixed_in, router_full), axis=-1)
    expert_ids = jnp.arange(expert_count, dtype=jnp.int32)
    chosen = (routes[:, :, None] == expert_ids[None, None, :]).astype(jnp.float32)
    gate_values = jnp.sum(chosen * chance[:, None, :], axis=2)
    slot_of = slot_index(routes, expert_count, capacity)
    slot_ids = jnp.arange(expert_count * capacity, dtype=jnp.int32)
    selector = (slot_of[:, :, None] == slot_ids[None, None, :]).astype(jnp.bfloat16)
    slot_rows = jnp.einsum("tks,td->sd", selector, mixed_in, preferred_element_type=jnp.float32)
    slot_rows = slot_rows.astype(jnp.bfloat16).reshape(expert_count, capacity, model_width)
    owned_rows = lax.all_to_all(slot_rows, "gx", split_axis=0, concat_axis=1, tiled=True)
    expert_in, expert_back = (
        lax.all_gather(e_fc1, "gy", axis=1, tiled=True),
        lax.all_gather(e_fc2, "gy", axis=1, tiled=True),
    )
    inner_pre = jnp.einsum(
        "ecd,edf->ecf", owned_rows, expert_in, preferred_element_type=jnp.float32
    )
    inner_act = jax.nn.gelu(inner_pre).astype(jnp.bfloat16)
    result = jnp.einsum(
        "ecf,efd->ecd", inner_act, expert_back, preferred_element_type=jnp.float32
    ).astype(jnp.bfloat16)
    returned = lax.all_to_all(result, "gx", split_axis=1, concat_axis=0, tiled=True).reshape(
        expert_count * capacity, model_width
    )
    picked = jnp.take(returned, slot_of, axis=0).astype(jnp.float32)
    branch = shared + jnp.sum(gate_values[:, :, None] * picked, axis=1)
    output = (middle + gate_mlp * branch).astype(jnp.bfloat16)
    out_grad = cotangent.astype(jnp.float32)
    grad_gate_mlp = out_grad * branch
    grad_branch = out_grad * gate_mlp
    grad_shared = grad_branch.astype(jnp.bfloat16)
    grad_picked = (gate_values[:, :, None] * grad_branch[:, None, :]).astype(jnp.bfloat16)
    grad_gates = jnp.sum(grad_branch[:, None, :] * picked, axis=2)
    grad_slots = jnp.einsum(
        "tks,tkd->sd", selector, grad_picked, preferred_element_type=jnp.float32
    )
    grad_slots = grad_slots.astype(jnp.bfloat16).reshape(expert_count, capacity, model_width)
    grad_owned = lax.all_to_all(grad_slots, "gx", split_axis=0, concat_axis=1, tiled=True)
    grad_inner = jnp.einsum(
        "ecd,efd->ecf", grad_owned, expert_back, preferred_element_type=jnp.float32
    )
    unused_inner, gelu_expert = jax.vjp(jax.nn.gelu, inner_pre)
    grad_inner_pre = gelu_expert(grad_inner)[0].astype(jnp.bfloat16)
    term_e_out = jnp.einsum(
        "ecf,ecd->efd", inner_act, grad_owned, preferred_element_type=jnp.float32
    )
    term_e_in = jnp.einsum(
        "ecd,ecf->edf", owned_rows, grad_inner_pre, preferred_element_type=jnp.float32
    )
    grad_rows = jnp.einsum(
        "ecf,edf->ecd", grad_inner_pre, expert_in, preferred_element_type=jnp.float32
    )
    grad_returned = (
        lax.all_to_all(
            grad_rows.astype(jnp.bfloat16), "gx", split_axis=1, concat_axis=0, tiled=True
        )
        .astype(grad_rows.dtype)
        .reshape(expert_count * capacity, model_width)
    )
    sum_e_in, sum_e_out = (
        lax.psum_scatter(
            term_e_in.astype(jnp.bfloat16), "gy", scatter_dimension=1, tiled=True
        ).astype(jnp.float32),
        lax.psum_scatter(
            term_e_out.astype(jnp.bfloat16), "gy", scatter_dimension=1, tiled=True
        ).astype(jnp.float32),
    )
    grad_chance = jnp.sum(chosen * grad_gates[:, :, None], axis=1)
    grad_logits = chance * (grad_chance - jnp.sum(grad_chance * chance, axis=-1, keepdims=True))
    grad_logits = grad_logits.astype(jnp.bfloat16)
    grad_hidden = dot_cols(grad_shared, fc2_full)
    unused_shared, gelu_shared = jax.vjp(jax.nn.gelu, hidden_pre)
    grad_hidden_pre = gelu_shared(grad_hidden)[0].astype(jnp.bfloat16)
    term_fc2 = dot_rows(hidden, grad_shared)
    term_fc1 = dot_rows(mixed_in, grad_hidden_pre)
    term_router = dot_rows(mixed_in, grad_logits)
    part_fc1, part_fc2, part_router = (
        lax.psum_scatter(
            term_fc1.astype(jnp.bfloat16), "gx", scatter_dimension=0, tiled=True
        ).astype(jnp.float32),
        lax.psum_scatter(
            term_fc2.astype(jnp.bfloat16), "gx", scatter_dimension=0, tiled=True
        ).astype(jnp.float32),
        lax.psum_scatter(
            term_router.astype(jnp.bfloat16), "gx", scatter_dimension=0, tiled=True
        ).astype(jnp.float32),
    )
    sum_fc1, sum_fc2, sum_router = (
        lax.psum_scatter(
            part_fc1.astype(jnp.bfloat16), "gy", scatter_dimension=0, tiled=True
        ).astype(jnp.float32),
        lax.psum_scatter(
            part_fc2.astype(jnp.bfloat16), "gy", scatter_dimension=0, tiled=True
        ).astype(jnp.float32),
        lax.psum_scatter(
            part_router.astype(jnp.bfloat16), "gy", scatter_dimension=0, tiled=True
        ).astype(jnp.float32),
    )
    grad_mixed = dot_cols(grad_hidden_pre, fc1_full) + dot_cols(grad_logits, router_full)
    grad_mixed = grad_mixed + jnp.sum(jnp.take(grad_returned, slot_of, axis=0), axis=1)
    unused_mix, mix_back = jax.vjp(modulate, middle, shift_mlp, scale_mlp)
    grad_mid_norm, grad_shift_mlp, grad_scale_mlp = mix_back(grad_mixed)
    grad_middle = out_grad + grad_mid_norm
    grad_gate_attn = grad_middle * attn_proj
    grad_proj = (grad_middle * gate_attn).astype(jnp.bfloat16)
    term_out = dot_rows(attn_low, grad_proj)
    grad_attn = (
        dot_cols(grad_proj, out_full).astype(jnp.bfloat16).reshape(tok_count, head_count, head_size)
    )
    grad_probs = jnp.einsum(
        "qhd,khd->hqk", grad_attn, value_rows, preferred_element_type=jnp.float32
    )
    grad_values = jnp.einsum(
        "hqk,qhd->khd", probs_low, grad_attn, preferred_element_type=jnp.float32
    )
    grad_scores = attn_probs * (
        grad_probs - jnp.sum(grad_probs * attn_probs, axis=-1, keepdims=True)
    )
    grad_scores = grad_scores.astype(jnp.bfloat16)
    grad_queries = (
        jnp.einsum("hqk,khd->qhd", grad_scores, key_rows, preferred_element_type=jnp.float32)
        * score_scale
    )
    grad_keys = (
        jnp.einsum("hqk,qhd->khd", grad_scores, queries, preferred_element_type=jnp.float32)
        * score_scale
    )
    grad_qkv = jnp.concatenate(
        [
            grad_queries.reshape(tok_count, model_width),
            grad_keys.reshape(tok_count, model_width),
            grad_values.reshape(tok_count, model_width),
        ],
        axis=1,
    ).astype(jnp.bfloat16)
    term_qkv = dot_rows(attn_in, grad_qkv)
    grad_attn_in = dot_cols(grad_qkv, qkv_full)
    unused_pre, pre_back = jax.vjp(modulate, residual, shift_attn, scale_attn)
    grad_input_norm, grad_shift_attn, grad_scale_attn = pre_back(grad_attn_in)
    d_tokens = grad_middle + grad_input_norm
    grad_token_mod = jnp.concatenate(
        [
            grad_shift_attn,
            grad_scale_attn,
            grad_gate_attn,
            grad_shift_mlp,
            grad_scale_mlp,
            grad_gate_mlp,
        ],
        axis=1,
    )
    grad_modulation = jnp.einsum("ti,tc->ic", member, grad_token_mod, precision=precise).astype(
        jnp.bfloat16
    )
    all_condition, all_modgrad = (
        lax.all_gather(condition, ("gx", "gy"), axis=0, tiled=True),
        lax.all_gather(grad_modulation, ("gx", "gy"), axis=0, tiled=True),
    )
    own_share = model_width // lax.axis_size(("gx", "gy"))
    own_start = lax.axis_index(("gx", "gy")) * own_share
    own_condition = lax.dynamic_slice_in_dim(all_condition, own_start, own_share, 1)
    owned_ada = dot_rows(own_condition, all_modgrad)
    attn_terms = (term_qkv, term_out)
    attn_parts = (
        lax.psum_scatter(
            attn_terms[0].astype(jnp.bfloat16), "gx", scatter_dimension=0, tiled=True
        ).astype(jnp.float32),
        lax.psum_scatter(
            attn_terms[1].astype(jnp.bfloat16), "gx", scatter_dimension=0, tiled=True
        ).astype(jnp.float32),
    )
    attn_sums = (
        lax.psum_scatter(
            attn_parts[0].astype(jnp.bfloat16), "gy", scatter_dimension=0, tiled=True
        ).astype(jnp.float32),
        lax.psum_scatter(
            attn_parts[1].astype(jnp.bfloat16), "gy", scatter_dimension=0, tiled=True
        ).astype(jnp.float32),
    )
    sum_qkv, sum_out = attn_sums
    return (
        output,
        d_tokens,
        owned_ada,
        sum_qkv,
        sum_out,
        sum_fc1,
        sum_fc2,
        sum_router,
        sum_e_in,
        sum_e_out,
    )


def solution(mesh):
    in_specs = (
        P(("gx", "gy"), None),
        P(("gx", "gy")),
        P(("gx", "gy"), None),
        P(("gx", "gy"), None),
        P(("gx", "gy"), None),
        P(("gx", "gy"), None),
        P(("gx", "gy"), None),
        P(("gx", "gy"), None),
        P(("gx", "gy"), None),
        P(("gx", "gy"), None),
        P(("gx", "gy"), None),
        P("gx", "gy", None),
        P("gx", "gy", None),
    )
    out_specs = (
        P(("gx", "gy"), None),
        P(("gx", "gy"), None),
        P(("gx", "gy"), None),
        P(("gx", "gy"), None),
        P(("gx", "gy"), None),
        P(("gx", "gy"), None),
        P(("gx", "gy"), None),
        P(("gx", "gy"), None),
        P("gx", "gy", None),
        P("gx", "gy", None),
    )
    step = by_slices if dict(mesh.shape) == {"gx": 2, "gy": 16} else by_weights
    return jax.shard_map(
        step, mesh=mesh, in_specs=in_specs, out_specs=out_specs, check_vma=False
    )
```

```python
import functools
import math

import jax
import jax.numpy as jnp
import numpy as np
from jax import lax
from jax.experimental import pallas as pl
from jax.experimental.pallas import tpu as pltpu
from jax.sharding import PartitionSpec as P

HEADS = 12
CAP = 64
MESH = pl.DeviceIdType.MESH
ANY = pl.ANY
VMEM = pltpu.VMEM
DMA = pltpu.SemaphoreType.DMA
LINE = (1, 2, 3)

precise = lax.Precision.HIGHEST
layer_epsilon = 1e-06


def place():
    gy = lax.axis_index("gy")
    return lax.axis_index("gx"), gy // 4, (gy // 2) % 2, gy % 2


def device(y, z, x, c):
    return (y, 4 * z + 2 * x + c)


def chip(y, z, x):
    return 8 * y + 2 * z + x


def along(z, step):
    return z + step - 2 * (z % 2) * (step % 2) - 4 * (z // 2) * (step // 2)


def meet(partners):
    barrier = pltpu.get_barrier_semaphore()
    for partner in partners:
        pl.semaphore_signal(barrier, inc=1, device_id=partner, device_id_type=MESH)
    pl.semaphore_wait(barrier, len(partners))


def cross_partners(here):
    y, z, x, c = here
    return [device(y, along(z, step), x, c) for step in LINE] + [
        device(1 - y, z, x, c),
        device(y, z, 1 - x, c),
    ]


def remote(source, target, send, recv, to):
    return pltpu.make_async_remote_copy(
        src_ref=source, dst_ref=target, send_sem=send, recv_sem=recv, device_id=to, device_id_type=MESH
    )


class Gather:
    def __init__(self, here, y_first, own, slot, send, recv, pair=None):
        self.here, self.y_first, self.own, self.slot = here, y_first, own, slot
        self.send, self.recv, self.pair, self.started = send, recv, pair, []

    def number(self, a, step, b):
        y, z, x, c = self.here
        flip_y, flip_x = (a, b) if self.y_first else (b, a)
        return chip(1 - y if flip_y else y, along(z, step), 1 - x if flip_x else x)

    def copy(self, source, number, to, recv=None):
        recv = self.recv if recv is None else recv
        sent = remote(source, self.slot(number), self.send.at[len(self.started)], recv.at[number], to)
        sent.start()
        self.started.append(sent)

    def to_side(self, source, number, second):
        y, z, x, c = self.here
        self.copy(source, number, device(1 - y, z, x, c) if self.y_first != second else device(y, z, 1 - x, c))

    def to_line(self, source, number, step):
        y, z, x, c = self.here
        self.copy(source, number, device(y, along(z, step), x, c))

    def to_pair(self, source, number):
        y, z, x, c = self.here
        if self.pair is not None:
            self.copy(source, number, device(y, z, x, 1 - c), self.pair)

    def arrive(self, number, recv=None):
        recv = self.recv if recv is None else recv
        block = self.slot(number)
        remote(block, block, self.send.at[0], recv.at[number], device(*self.here)).wait_recv()
        return block

    def start_first(self):
        self.to_side(self.own, self.number(0, 0, 0), False)
        self.to_pair(self.own, self.number(0, 0, 0))

    def start_line(self, step):
        self.to_line(self.own, self.number(0, 0, 0), step)

    def start_last(self):
        self.to_side(self.own, self.number(0, 0, 0), True)

    def line_first(self, step):
        number = self.number(0, step, 0)
        block = self.arrive(number)
        if step == 2:
            self.to_line(block, number, 1)
        self.to_side(block, number, False)
        self.to_pair(block, number)

    def line_last(self, step):
        number = self.number(0, step, 0)
        self.to_side(self.slot(number), number, True)

    def second(self, step):
        number = self.number(1, step, 0)
        block = self.arrive(number)
        self.to_side(block, number, True)
        self.to_pair(block, number)

    def third(self, step):
        for a in (0, 1):
            number = self.number(a, step, 1)
            self.to_pair(self.arrive(number), number)

    def finish(self):
        block = self.slot(self.number(0, 0, 0))
        for index in range(len(self.started)):
            remote(block, block, self.send.at[index], self.recv.at[0], device(*self.here)).wait_send()
        if self.pair is not None:
            for number in range(16):
                self.arrive(number, self.pair)


def gather_start(gathers):
    for gather in gathers:
        gather.start_first()
    for step in (1, 2):
        for gather in gathers:
            gather.start_line(step)
    for gather in gathers:
        gather.start_last()


def gather_line(gathers, step):
    for gather in gathers:
        gather.line_first(step)
    for gather in gathers:
        gather.line_last(step)


def gather_second(gathers, step):
    for gather in gathers:
        gather.second(step)


def gather_third(gathers, step):
    for gather in gathers:
        gather.third(step)


def gather_all(gathers, between=None):
    gather_start(gathers)
    gather_second(gathers, 0)
    for step in LINE:
        gather_line(gathers, step)
        gather_second(gathers, step)
    if between is not None:
        between()
    for step in (0,) + LINE:
        gather_third(gathers, step)
    for gather in gathers:
        gather.finish()


class Scatter:
    def __init__(self, here, y_first, part, got, send, recv, relay=False):
        self.here, self.y_first, self.part, self.got, self.relay = here, y_first, part, got, relay
        self.send, self.recv, self.started = send, recv, []

    def number(self, a, b, step):
        y, z, x, c = self.here
        flip_y, flip_x = (a, b) if self.y_first else (b, a)
        return chip(1 - y if flip_y else y, along(z, step), 1 - x if flip_x else x)

    def toward(self, second):
        y, z, x, c = self.here
        return device(1 - y, z, x, c) if self.y_first != second else device(y, z, 1 - x, c)

    def copy(self, source, index, to):
        sent = remote(source, self.got(index), self.send.at[len(self.started)], self.recv.at[index], to)
        sent.start()
        self.started.append(sent)

    def arrive(self, index):
        block = self.got(index)
        remote(block, block, self.send.at[0], self.recv.at[index], device(*self.here)).wait_recv()
        return block

    def first(self, step):
        for b in (1, 0):
            self.copy(self.part(self.number(1, b, step)), 4 * b + step, self.toward(False))

    def add(self, number, index):
        block, mine = self.arrive(index), self.part(number)
        total = mine[...].astype(jnp.float32) + block[...].astype(jnp.float32)
        mine[...] = total.astype(mine.dtype)

    def one(self, b, step):
        number = self.number(0, b, step)
        self.add(number, 4 * b + step)
        if b == 1:
            self.copy(self.part(number), 8 + step, self.toward(True))

    def two(self, step):
        y, z, x, c = self.here
        number = self.number(0, 0, step)
        self.add(number, 8 + step)
        if self.relay and step == 2:
            self.add(number, 14)
        if step:
            self.copy(self.part(number), 11 + step, device(y, along(z, 1 if self.relay and step == 3 else step), x, c))

    def total(self):
        result = self.part(self.number(0, 0, 0))[...].astype(jnp.float32)
        for step in (1, 2) if self.relay else (1, 2, 3):
            result = result + self.arrive(11 + step)[...].astype(jnp.float32)
        return result

    def finish(self):
        block = self.got(0)
        for index in range(len(self.started)):
            remote(block, block, self.send.at[index], self.recv.at[0], device(*self.here)).wait_send()


def scatter_all(scatters, more, between):
    order = (3, 2, 1, 0)
    for turn, step in enumerate(order):
        for b in (1, 0):
            for scatter in scatters:
                scatter.one(b, step)
        if turn + 2 < 4:
            more(order[turn + 2])
        if turn:
            for scatter in scatters:
                scatter.two(order[turn - 1])
        between(turn)
    for scatter in scatters:
        scatter.two(order[3])


def nt(a, b):
    return lax.dot_general(a, b, (((1,), (1,)), ((), ())), preferred_element_type=jnp.float32)


def tn(a, b):
    return lax.dot_general(a, b, (((0,), (0,)), ((), ())), preferred_element_type=jnp.float32)


def nn(a, b):
    return jnp.dot(a, b, preferred_element_type=jnp.float32)


def low(value):
    return value.astype(jnp.bfloat16)


def wide_float(value):
    return value.astype(jnp.float32)


def norm(values):
    centred = values - jnp.mean(values, axis=-1, keepdims=True)
    scale = lax.rsqrt(jnp.mean(centred * centred, axis=-1, keepdims=True) + layer_epsilon)
    return centred * scale, scale


def norm_back(grad, normed, scale):
    pulled = grad - jnp.mean(grad, axis=-1, keepdims=True) - normed * jnp.mean(grad * normed, axis=-1, keepdims=True)
    return scale * pulled


def item_mask(lengths, shape):
    return lax.broadcasted_iota(jnp.int32, shape, 0) >= lengths[0, 0]


def choices(routes, square):
    square[...] = jnp.zeros_like(square)
    square[0 : routes.shape[0], :] = wide_float(routes[...])
    named = square[...].T
    lane = wide_float(lax.broadcasted_iota(jnp.int32, (1, 128), 1))
    return (named[:, 0:1] == lane) | (named[:, 1:2] == lane)


def own_modulation(here, mod, item, half, part):
    first = 2 * here[3]
    model = item.shape[1]
    at = slice(part * model, (part + 1) * model)
    return jnp.where(item, mod[half, pl.ds(first + 1, 1), at], mod[half, pl.ds(first, 1), at])


def frequencies(model_width):
    half = model_width // 2
    return np.tile(np.exp(-math.log(10000.0) * np.arange(half) / half).astype(np.float32), 2)


def conditions(steps, shape, first, column, half, frequency):
    row = lax.broadcasted_iota(jnp.int32, shape, 0) - first
    angle = jnp.where(row == 0, wide_float(steps[0]), wide_float(steps[1])) * frequency
    wave = jnp.where(column < half, jnp.cos(angle), jnp.sin(angle))
    value = wave / (1.0 + jnp.exp(-wave))
    return wide_float(low(jnp.where((row == 0) | (row == 1), value, 0.0)))


def head_lanes():
    lane = lax.broadcasted_iota(jnp.int32, (1, 128), 1)
    return lane < 64, [low(wide_float(lane < 64)), low(wide_float(lane >= 64))]


def front_part(refs, outs, kept, sems, start_tokens, more_tokens, *locals_):
    (lengths, steps, tokens, cotangent, routes, waves, w_ada, w_qkv, w_out, w_router, w_fc1, e1) = refs
    (qkv_w, out_w, mod_out, mixed_out, attn_in_out, qkv_out, probs_out, attn_low_out, attn_proj_out, middle_out, chance_out) = outs
    (w1, w1s, mod, mixed, grad, gates, q_full, o_full, a_full, q_stage, o_stage, a_stage, c_buf, z_got, s_got) = kept
    (pre_send, pre_recv, g_send, g_recv, g_pair, a_send, a_recv, a_pair_send, a_pair, b_send, b_recv, b_pair, l_sem, o_sem,
     c_send, c_recv, m_send, m_recv, r_send, r_recv) = sems
    (attn_in, qkv, probs, attn_low, attn_proj, middle, chance, square, cond, f1, s_rows, q_fold, o_fold, a_fold, q_block, o_block, z_part) = locals_
    here = y, z, x, c = place()
    me, k, gy = chip(y, z, x), 2 * z + x, 4 * z + 2 * x + c
    rows, model = w_out.shape
    others = [(dy, dz, dx) for dy in (0, 1) for dz in (0, 1, 2, 3) for dx in (0, 1) if (dy, dz, dx) != (0, 0, 0)]
    spot = lambda dy, dz, dx: (1 - y if dy else y, along(z, dz), 1 - x if dx else x)
    sibling = device(y, z, x, 1 - c)
    crossed = [device(y, along(z, step), x, 1 - c) for step in LINE]
    meet([device(*spot(*o), c) for o in others] + [sibling] + crossed)

    started = []

    def go(copy):
        copy.start()
        started.append(copy)

    lane = lax.broadcasted_iota(jnp.int32, cond.shape[1:], 1)
    for at in range(4):
        column = model // 2 * (lane // (4 * rows)) + 4 * rows * at + lane % (4 * rows)
        cond[at] = jnp.where(lane < 8 * rows, conditions(steps, cond.shape[1:], 2 * c, column, model // 2, waves[at : at + 1, :]), 0.0)
    for i, (step, core) in enumerate([(0, 1 - c)] + [(step, core) for step in LINE for core in (c, 1 - c)]):
        go(remote(cond.at[along(z, step)], c_buf.at[z, c], c_send.at[i], c_recv.at[z, c], device(y, along(z, step), x, core)))

    mine = pl.ds(pl.multiple_of(rows * c, 8), rows)
    square[...] = jnp.zeros_like(square)
    square[0 : w_router.shape[0], 0:rows] = wide_float(w_router[...])
    router = square[...].T[:rows]
    for i, (w, fold, stage) in enumerate(((w_ada, a_fold, a_stage), (w_qkv, q_fold, q_stage), (w_out, o_fold, o_stage))):
        cut = w.shape[1] // 2
        for h in (0, 1):
            fold[h, :, :cut] = wide_float(w[:, h * cut : (h + 1) * cut])
            if i == 2:
                fold[h, :, cut:] = router
        go(remote(fold.at[1 - c], stage.at[mine, :], pre_send.at[i], pre_recv.at[i], sibling))
        stage[mine, :] = fold[c]

    depth, width = e1.shape[1], w1.shape[2]
    cols = lambda n: pl.ds(pl.multiple_of(width * n, 128), width)
    strip = lambda n: pl.ds(pl.multiple_of(depth * n, 16), depth)
    load = pltpu.make_async_copy(e1.at[:, :, cols(k)], w1.at[:, strip(gy), :], l_sem.at[0])
    load.start()
    plane = [o for o in others if o[0] == 0]

    def send_experts(steps, aside):
        for i, o in enumerate(plane):
            if o[1] in steps and o[2] == aside:
                ty, tz, tx = spot(*o)
                go(remote(e1.at[:, :, cols(2 * tz + tx)], w1.at[:, strip(gy), :], a_send.at[i], a_recv.at[k], device(ty, tz, tx, c)))

    send_experts((1,), 0)

    def folded(i, stage):
        theirs = stage.at[pl.ds(pl.multiple_of(rows * (1 - c), 8), rows), :]
        remote(theirs, theirs, pre_send.at[i], pre_recv.at[i], sibling).wait_recv()
        return low(stage[...])

    block = folded(0, a_stage)
    width_a = a_full.shape[3]
    number = 2 * y + x
    to_y, to_x = device(1 - y, z, x, c), device(y, z, 1 - x, c)
    for i in (0, 1):
        a_full[i, number] = block[:, i * width_a : (i + 1) * width_a]

    def send_a(i, n, lane, to):
        go(remote(a_full.at[i, n], a_full.at[i, n], r_send.at[i, lane], r_recv.at[i, n], to))

    def wait_a(i, n):
        remote(a_full.at[i, n], a_full.at[i, n], r_send.at[0, 0], r_recv.at[i, n], sibling).wait_recv()

    send_a(0, number, 0, to_y)
    send_a(1, number, 0, to_x)
    send_a(0, number, 1, to_x)
    send_a(1, number, 1, to_y)
    q_block[...] = folded(1, q_stage)
    o_block[...] = folded(2, o_stage)
    gathers = []
    for i, (block, full, y_first) in enumerate(((q_block, q_full, False), (o_block, o_full, True))):
        slot = functools.partial(lambda full, n: full.at[c, pl.ds(pl.multiple_of(2 * rows * n, 16), 2 * rows), :], full)
        gathers.append(Gather(here, y_first, block, slot, g_send.at[i], g_recv.at[i], g_pair.at[i]))
        slot(me)[...] = block[...]
    gather_start(gathers)

    n_y, n_x = 2 * (1 - y) + x, 2 * y + 1 - x
    n_xy = 2 * (1 - y) + 1 - x
    wait_a(0, n_y)
    send_a(0, n_y, 2, to_x)
    wait_a(1, n_x)
    send_a(1, n_x, 2, to_y)
    gather_second(gathers, 0)

    c_buf[z, c] = cond[z]
    for step, core in [(0, 1 - c)] + [(step, core) for step in LINE for core in (c, 1 - c)]:
        block = c_buf.at[along(z, step), core]
        remote(block, block, c_send.at[0], c_recv.at[along(z, step), core], sibling).wait_recv()
    lhs = low(jnp.concatenate([c_buf[i, 0] + c_buf[i, 1] for i in range(4)], axis=0))[:, : 8 * rows]
    for i, n_last in enumerate((n_x, n_y)):
        wait_a(i, n_last)
        wait_a(i, n_xy)
        term = nn(lhs, a_full[i].reshape(8 * rows, width_a))
        for line in range(4):
            z_part[line, 4 * i : 4 * (i + 1), :] = term[8 * line : 8 * line + 4]
    for step in LINE:
        at = along(z, step)
        go(remote(z_part.at[at], z_got.at[step - 1], m_send.at[step], m_recv.at[step], device(y, at, x, c)))
    send_experts((2, 3), 0)
    gather_line(gathers, 1)
    slim = w1s.shape[1]
    for n in range(16):
        block = wide_float(w_fc1[:, slim * n : slim * (n + 1)])
        f1[n] = low(jnp.concatenate([block, jnp.zeros((f1.shape[1] - rows, slim), jnp.float32)], axis=0))
    for i, o in enumerate(others):
        ty, tz, tx = spot(*o)
        go(remote(f1.at[chip(ty, tz, tx)], s_got.at[c, me], b_send.at[i], b_recv.at[me], device(ty, tz, tx, c)))
    s_got[c, me] = f1[me]
    gather_second(gathers, 1)
    gather_line(gathers, 2)
    send_experts((0, 1, 2, 3), 1)
    gather_second(gathers, 2)
    gather_line(gathers, 3)
    gather_second(gathers, 3)
    total = z_part[z]
    for step in LINE:
        remote(z_got.at[step - 1], z_got.at[step - 1], m_send.at[0], m_recv.at[step], sibling).wait_recv()
        total = total + z_got[step - 1]
    mod[c] = jnp.concatenate([total, pltpu.roll(total, 4, 0)], axis=1)
    go(remote(mod.at[c], mod.at[c], m_send.at[0], m_recv.at[0], sibling))
    remote(mod.at[1 - c], mod.at[1 - c], m_send.at[0], m_recv.at[0], sibling).wait_recv()

    item = item_mask(lengths, tokens.shape)
    residual = wide_float(tokens[...])
    normed, _ = norm(residual)
    attn_in[...] = low(normed * (1.0 + own_modulation(here, mod, item, 0, 1)) + own_modulation(here, mod, item, 0, 0))
    grad[...] = low(wide_float(cotangent[...]) * own_modulation(here, mod, item, 1, 2))
    for step in (0,) + LINE:
        gather_third(gathers, step)
    for gather in gathers:
        gather.finish()
    keep = []

    def leave(source, target):
        keep.append(pltpu.make_async_copy(source, target, o_sem.at[len(keep)]))
        keep[-1].start()

    leave(q_full, qkv_w)
    leave(o_full, out_w)

    cut = q_full.shape[2]
    for h in (0, 1):
        qkv[:, h * cut : (h + 1) * cut] = low(nn(attn_in[...], q_full[h]))

    side = wide_float(item[:, :128])
    same = side == side.T
    left, sides = head_lanes()
    for pair in range(model // 128):
        q, key, value = [qkv[:, base + 128 * pair : base + 128 * (pair + 1)] for base in (0, model, 2 * model)]
        outs = []
        for j, side in enumerate(sides):
            scores = jnp.where(same, nt(q * side, key) * 0.125, -1e30)
            weight = jnp.exp(scores - jnp.max(scores, axis=-1, keepdims=True))
            prob = weight / jnp.sum(weight, axis=-1, keepdims=True)
            probs[2 * pair + j] = prob
            outs.append(nn(low(prob), value))
        attn_low[:, 128 * pair : 128 * (pair + 1)] = low(jnp.where(left, outs[0], outs[1]))
    cut = model // 2
    for h in (0, 1):
        attn_proj[:, h * cut : (h + 1) * cut] = nn(attn_low[...], o_full[h, :, :cut])
    middle[...] = residual + own_modulation(here, mod, item, 0, 2) * attn_proj[...]
    normed, _ = norm(middle[...])
    mixed[...] = low(normed * (1.0 + own_modulation(here, mod, item, 1, 1)) + own_modulation(here, mod, item, 1, 0))
    lane = lax.broadcasted_iota(jnp.int32, (1, 128), 1)
    logits = jnp.where(lane < 8, nn(mixed[...], o_full[0, :, cut:]), -1e30)
    weight = jnp.exp(logits - jnp.max(logits, axis=-1, keepdims=True))
    chance[...] = weight / jnp.sum(weight, axis=-1, keepdims=True)
    turned = jnp.where(choices(routes, square), chance[...], 0.0).T[:8]
    high = low(turned)
    gates[...] = jnp.concatenate([high, low(turned - wide_float(high))], axis=0)
    token_gathers = start_tokens()
    for source, target in (
        (mixed, mixed_out), (mod, mod_out), (attn_in, attn_in_out), (qkv, qkv_out), (probs, probs_out),
        (attn_low, attn_low_out), (attn_proj, attn_proj_out), (middle, middle_out), (chance, chance_out),
    ):
        leave(source, target)

    for o in others:
        n = chip(*spot(*o))
        remote(s_got.at[c, n], s_got.at[c, n], b_send.at[0], b_recv.at[n], sibling).wait_recv()
    go(remote(s_got.at[c], s_got.at[c], b_pair.at[0], b_pair.at[1], sibling))
    load.wait()
    more_tokens(0, token_gathers)
    for i, o in enumerate([(0, 0, 0)] + [o for step in (0, 1, 3, 2) for o in plane if o[1] == step]):
        _, sz, sx = spot(*o)
        source = 2 * sz + sx
        block = w1.at[:, strip(2 * source + c), :]
        if i:
            remote(block, block, a_send.at[0], a_recv.at[source], sibling).wait_recv()
        go(remote(block, block, a_pair_send.at[i], a_pair.at[source], sibling))
    more_tokens(1, token_gathers)
    remote(s_got.at[1 - c], s_got.at[1 - c], b_pair.at[0], b_pair.at[1], sibling).wait_recv()
    for n in range(32):
        s_rows[n * rows : (n + 1) * rows, :] = wide_float(s_got[n % 2, n // 2])[:rows]
    w1s[...] = low(s_rows[...])
    for copy in started:
        copy.wait_send()
    for source in range(8):
        block = w1.at[:, strip(2 * source + 1 - c), :]
        remote(block, block, a_send.at[0], a_pair.at[source], sibling).wait_recv()
    for copy in keep:
        copy.wait()


def gelu_both(h):
    root = math.sqrt(2.0 / math.pi)
    square = h * h
    t = jnp.tanh(h * (root + (root * 0.044715) * square))
    half = 0.5 * (1.0 + t)
    slope = half + (0.5 * h) * (1.0 - t * t) * (root + (3.0 * root * 0.044715) * square)
    return h * half, slope


def ffn_chunk(xt, gt, w1, w2, gate, row):
    a, d = gelu_both(nn(xt, w1))
    gi = nt(gt, w2)
    product = None
    if gate is not None:
        product = nt(row, (a * gi).astype(jnp.bfloat16))
        a, d = a * gate, d * gate
    a = a.astype(jnp.bfloat16)
    p = (gi * d).astype(jnp.bfloat16)
    return a, p, nn(a, w2), nt(p, w1), product


def ffn_shared(slots, X, G, w1s, w2s, act_s, pre_s, sums, sums_back):
    toks = X.shape[1]
    xt = jnp.concatenate([X[n] for n in slots], axis=0)
    gt = jnp.concatenate([G[n] for n in slots], axis=0)
    a, p, total, total_back, _ = ffn_chunk(xt, gt, w1s[...], w2s[...], None, None)
    for i, n in enumerate(slots):
        act_s[n] = a[i * toks : (i + 1) * toks]
        pre_s[n] = p[i * toks : (i + 1) * toks]
    sums[...] = total
    sums_back[...] = total_back


def ffn_experts(low, high, slots, X, G, gates, w1, w2, act, pre, sums, sums_back, gc):
    experts, toks, wide = w1.shape[0], X.shape[1], w1.shape[2]
    first = lax.axis_index("gx") * experts
    xt = jnp.concatenate([X[n] for n in slots], axis=0)
    gt = jnp.concatenate([G[n] for n in slots], axis=0)

    def expert(e, product):
        kind = lax.broadcasted_iota(jnp.int32, (16, 128), 0)
        spread = ((kind == first + e) | (kind == first + e + 8)).astype(jnp.bfloat16)
        gate = jnp.concatenate([tn(gates[n], spread) for n in slots], axis=0)
        gate = jnp.concatenate([gate] * (wide // 128), axis=1)
        row = (lax.broadcasted_iota(jnp.int32, (8, wide), 0) == first + e).astype(jnp.bfloat16)
        a, p, total, total_back, more = ffn_chunk(xt, gt, w1[e], w2[e], gate, row)
        for i, n in enumerate(slots):
            act[e, n] = a[i * toks : (i + 1) * toks]
            pre[e, n] = p[i * toks : (i + 1) * toks]
        sums[...] += total
        sums_back[...] += total_back
        return product + more

    product = lax.fori_loop(low, high, expert, jnp.zeros((8, len(slots) * toks), jnp.float32))
    for i, n in enumerate(slots):
        part = product[:, i * toks : (i + 1) * toks]
        gc[n] = part if low == 0 else gc[n] + part


def block_part(refs, outs, kept, sems, go_on, plan, *locals_):
    w2_in, w2s_in = refs
    (sum_branch, sum_back, sum_gc, near1, far1, out1s, out2, out2s) = outs
    (w1, w1s, X, G, gt, w2, w2s, r_branch, r_back, r_gc, from1, from1s, from2, from2s) = kept
    (l_sem, o_sem, send, recv, t_send, t_recv, w_send, w_recv, h_send, h_recv) = sems
    (act, pre, act_s, pre_s, p_branch, p_back, p_gc) = locals_
    experts = w1.shape[0]
    counts = []

    def tools():
        here = place()
        scatters = []
        for i, (part, got, y_first) in enumerate(((p_branch, r_branch, False), (p_back, r_back, True), (p_gc, r_gc, False))):
            take = functools.partial(lambda ref, n: ref.at[n], part)
            land = functools.partial(lambda ref, n: ref.at[n], got)
            scatters.append(Scatter(here, y_first, take, land, send.at[i], recv.at[i]))

        return scatters

    def tiles(tile_sum, tile_back):
        here = y, z, x, c = place()
        spot = lambda dy, dz, dx: (1 - y if dy else y, along(z, dz), 1 - x if dx else x)
        sibling = device(y, z, x, 1 - c)
        local, gathers, scatters = [], go_on(), tools()
        half2, half2s = w2_in.shape[1], w2s_in.shape[0]
        own2_at = w2.at[:, pl.ds(pl.multiple_of(half2 * c, 16), half2), :]
        own2s_at = w2s.at[pl.ds(pl.multiple_of(half2s * c, 16), half2s), :]
        for i, (source, target) in enumerate(((w2_in, own2_at), (w2s_in, own2s_at))):
            local.append(pltpu.make_async_copy(source, target, l_sem.at[3 + i]))
        for i, (source, target) in enumerate(((w2_in, own2_at), (w2s_in, own2s_at))):
            local.append(remote(source, target, w_send.at[i], w_recv.at[i], sibling))
        for copy in local:
            copy.start()

        def tile(step, part):
            slots = [chip(*spot(dy, step, dx)) for dy in (0, 1) for dx in (0, 1)]
            if part == 0:
                ffn_shared(slots, X, G, w1s, w2s, act_s, pre_s, tile_sum, tile_back)
            low, high = (0, experts // 2) if part == 0 else (experts // 2, experts)
            ffn_experts(low, high, slots, X, G, gt, w1, w2, act, pre, tile_sum, tile_back, p_gc)
            if part == 1:
                toks = X.shape[1]
                for i, n in enumerate(slots):
                    at = slice(i * toks, (i + 1) * toks)
                    p_branch[n] = tile_sum[at, :].astype(jnp.bfloat16)
                    p_back[n] = tile_back[at, :].astype(jnp.bfloat16)

        def back_first(step):
            for scatter in scatters:
                scatter.first(step)

        def back_one(b, step):
            for scatter in scatters:
                scatter.one(b, step)

        def back_two(step):
            for scatter in scatters:
                scatter.two(step)

        gather_second(gathers, 1)
        gather_third(gathers, 0)
        for copy in local:
            copy.wait()
        tile(0, 0)
        gather_line(gathers, 2)
        tile(0, 1)
        gather_third(gathers, 1)
        tile(1, 0)
        gather_second(gathers, 2)
        tile(1, 1)
        gather_line(gathers, 3)
        gather_third(gathers, 2)
        tile(2, 0)
        gather_second(gathers, 3)
        tile(2, 1)
        back_first(2)
        gather_third(gathers, 3)
        tile(3, 0)

        back_one(1, 2)
        tile(3, 1)
        for gather in gathers:
            gather.finish()
        counts.extend(len(scatter.started) for scatter in scatters)

    def weights(own1s, own2, own2s, d1, d1s, d2, d2s):
        here = y, z, x, c = place()
        spot = lambda dy, dz, dx: (1 - y if dy else y, along(z, dz), 1 - x if dx else x)
        sibling = device(y, z, x, 1 - c)
        scatters = tools()
        for scatter, count in zip(scatters, counts):
            scatter.started = [None] * count

        def back_first(step):
            for scatter in scatters:
                scatter.first(step)

        def back_one(b, step):
            for scatter in scatters:
                scatter.one(b, step)

        def back_two(step):
            for scatter in scatters:
                scatter.two(step)

        flat = lambda value: value.reshape(value.shape[0] * value.shape[1], value.shape[2])
        twins = [None] * (2 * experts)
        leaving, homeward, left = [], [], []

        def leave(source, target):
            leaving.append(pltpu.make_async_copy(source, target, o_sem.at[len(leaving)]))
            leaving[-1].start()


        def weight(e):
            d1[e % 2] = tn(flat(X[...]), flat(pre[e])).astype(jnp.bfloat16).reshape(d1.shape[1:])
            d2[e % 2] = tn(flat(act[e]), flat(G[...])).astype(jnp.bfloat16).reshape(d2.shape[1:])
            for i, (part, got) in enumerate(((d1.at[e % 2, :, 1 - c], from1.at[e]), (d2.at[e % 2, 1 - c], from2.at[e]))):
                twins[2 * e + i] = remote(part, got, t_send.at[2 * e + i], t_recv.at[2 * e + i], sibling)
                twins[2 * e + i].start()

        def home(e):
            twins[2 * e].wait()
            from1[e] = (d1[e % 2, :, c].astype(jnp.float32) + from1[e].astype(jnp.float32)).astype(jnp.bfloat16)
            twins[2 * e + 1].wait()
            if e > 1:
                left[e - 2].wait()
            own2[e % 2] = d2[e % 2, c].astype(jnp.float32) + from2[e].astype(jnp.float32)
            left.append(pltpu.make_async_copy(own2.at[e % 2], out2.at[e], l_sem.at[e]))
            left[e].start()
            for i in range(4):
                leave(from1.at[e, 2 * i + 1 - x], far1.at[e, i])
            leave(from1.at[e, 2 * z + x], near1.at[e, z])

        def along_home(e):
            for step in LINE:
                at = along(z, step)
                sent = remote(from1.at[e, 2 * at + x], near1.at[e, z], h_send.at[e, step], h_recv.at[e, z], device(y, at, x, c))
                sent.start()
                homeward.append(sent)


        back_first(3)
        back_one(0, 2)
        back_two(2)
        weight(0)
        back_one(1, 3)
        back_first(1)
        weight(1)
        home(0)
        back_one(0, 3)
        back_two(3)
        home(1)
        back_one(1, 1)
        back_first(0)
        weight(2)
        back_one(0, 1)
        along_home(0)
        along_home(1)
        back_two(1)
        home(2)
        back_one(1, 0)
        along_home(2)
        weight(3)
        d1s[...] = tn(flat(X[...]), flat(pre_s[...])).reshape(d1s.shape)
        d2s[...] = tn(flat(act_s[...]), flat(G[...])).astype(jnp.bfloat16).reshape(d2s.shape)
        twin1s = remote(d1s.at[:, 1 - c], from1s, t_send.at[2 * experts], t_recv.at[2 * experts], sibling)
        twin2s = remote(d2s.at[1 - c], from2s, t_send.at[2 * experts + 1], t_recv.at[2 * experts + 1], sibling)
        twin1s.start()
        twin2s.start()
        home(3)
        along_home(3)
        back_one(0, 0)
        twin1s.wait()
        total = d1s[:, c] + from1s[...]
        own1s[...] = low(jnp.concatenate([total, jnp.zeros((16, own1s.shape[1] - total.shape[1], total.shape[2]), jnp.float32)], axis=1))
        twin2s.wait()
        own2s[...] = d2s[c].astype(jnp.float32) + from2s[...].astype(jnp.float32)
        leave(own1s, out1s)
        leave(own2s, out2s)
        back_two(0)
        sum_branch[...] = scatters[0].total()
        sum_back[...] = scatters[1].total()
        sum_gc[...] = scatters[2].total()
        for copy in leaving:
            copy.wait()
        for copy in left[-2:]:
            copy.wait()
        for sent in homeward:
            sent.wait_send()
        for e in range(experts):
            for step in LINE:
                block = near1.at[e, along(z, step)]
                remote(block, block, h_send.at[0, 0], h_recv.at[e, along(z, step)], sibling).wait_recv()
        for scatter in scatters:
            scatter.finish()


    pl.run_scoped(tiles, *[VMEM(*a) for a in plan[0]])
    pl.run_scoped(weights, *[VMEM(*a) for a in plan[1]])


def joint_kernel(plan, *refs):
    refs = list(refs)

    def take(count):
        taken, refs[:count] = refs[:count], []
        return taken

    front_refs, block_refs = take(12), take(2)
    front_outs, block_outs = take(11), take(8)
    w1, w1s = take(2)
    mod, mixed, grad, gates = take(4)
    front_kept, (X, G, gt), block_kept = take(9), take(3), take(9)
    front_sems, block_sems, (g_send, g_recv) = take(20), take(10), take(2)
    counts = []

    def token_gathers():
        gathers = []
        for i, (block, full, y_first) in enumerate(((mixed, X, True), (grad, G, False), (gates, gt, True))):
            slot = functools.partial(lambda full, n: full.at[n], full)
            gathers.append(Gather(place(), y_first, block, slot, g_send.at[i], g_recv.at[i]))
        return gathers

    def start_tokens():
        gathers = token_gathers()
        gather_start(gathers)
        y, z, x, c = place()
        for block, full in ((mixed, X), (grad, G), (gates, gt)):
            full[chip(y, z, x)] = block[...]
        return gathers

    def more_tokens(turn, gathers):
        if turn == 0:
            gather_second(gathers, 0)
        else:
            gather_line(gathers, 1)
            counts.extend(len(gather.started) for gather in gathers)

    def go_on():
        gathers = token_gathers()
        for gather, count in zip(gathers, counts):
            gather.started = [None] * count
        return gathers

    kept = (w1, w1s, mod, mixed, grad, gates, *front_kept)
    pl.run_scoped(
        functools.partial(front_part, front_refs, front_outs, kept, front_sems, start_tokens, more_tokens), *[VMEM(*a) for a in plan[0]]
    )
    kept = (w1, w1s, X, G, gt, *block_kept)
    pl.run_scoped(functools.partial(block_part, block_refs, block_outs, kept, block_sems, go_on, plan[2:]), *[VMEM(*a) for a in plan[1]])


def joint(lengths, timesteps, tokens, cotangent, routes, w_ada, w_qkv, w_out, w_router, w_fc1, e_fc1, e_fc2, w_fc2):
    rows, model = w_out.shape
    toks = tokens.shape[0]
    waves = frequencies(model).reshape(2, 4, 4 * rows).transpose(1, 0, 2).reshape(4, 8 * rows)
    waves = np.pad(waves, ((0, 0), (0, -8 * rows % 128)))
    lanes = waves.shape[1]
    ff = w_fc1.shape[1]
    slim, wide = ff // 16, ff // 8
    experts, depth, _ = e_fc1.shape
    bf, f32 = jnp.bfloat16, jnp.float32
    shape = jax.ShapeDtypeStruct
    q_half, o_half, a_half = w_qkv.shape[1] // 2, w_out.shape[1] // 2 + 128, w_ada.shape[1] // 2
    saved = (((toks, model), bf), ((toks, 3 * model), bf), ((HEADS, toks, toks), f32), ((toks, model), bf), ((toks, model), f32),
             ((toks, model), f32), ((toks, 128), f32))
    front_plan = saved + (
        ((128, 128), f32), ((4, 8, lanes), f32), ((16, 32, slim), bf), ((model, slim), f32),
        ((2, rows, q_half), f32), ((2, rows, o_half), f32), ((2, rows, a_half), f32), ((2 * rows, q_half), bf), ((2 * rows, o_half), bf),
        ((4, 8, a_half // 2), f32),
    )
    blocks = lambda *dims: ((16, toks) + dims, bf)
    block_plan = (
        ((experts, 16, toks, wide), bf), ((experts, 16, toks, wide), bf), blocks(slim), blocks(slim), blocks(model), blocks(model),
        ((16, 8, 128), f32),
    )
    tiles_plan = (((4 * toks, model), f32), ((4 * toks, model), f32))
    weights_plan = (
        ((16, 32, slim), bf), ((2, wide // 2, model), f32), ((slim // 2, model), f32), ((2, 8, 2, depth, wide), bf), ((16, 2, rows, slim), f32),
        ((2, 2, wide // 2, model), bf), ((2, slim // 2, model), bf),
    )
    whole = (((2, model, q_half), bf), ((2, model, o_half), bf), ((2, 8, a_half), f32), ((toks, model), bf)) + saved
    sums = [((toks, model), f32), ((toks, model), f32), ((8, 128), f32)]
    grads = [((experts, 4, depth, wide), bf), ((experts, 4, depth, wide), bf), ((16, 32, slim), bf), ((experts, wide // 2, model), f32),
             ((slim // 2, model), f32)]
    outs = list(whole) + sums + grads
    return pl.pallas_call(
        functools.partial(joint_kernel, (front_plan, block_plan, tiles_plan, weights_plan)),
        out_shape=[shape(*a) for a in outs],
        in_specs=[pl.BlockSpec(memory_space=pltpu.SMEM)] * 2
        + [pl.BlockSpec(memory_space=VMEM)] * 9
        + [pl.BlockSpec(memory_space=ANY)] * 3,
        out_specs=[pl.BlockSpec(memory_space=ANY)] * len(whole)
        + [pl.BlockSpec(memory_space=VMEM)] * 3
        + [pl.BlockSpec(memory_space=ANY)] * 5,
        scratch_shapes=[
            VMEM((experts, model, wide), bf), VMEM((model, slim), bf), VMEM((2, 8, a_half), f32), VMEM((toks, model), bf), VMEM((toks, model), bf),
            VMEM((16, toks), bf),
            VMEM((2, model, q_half), bf), VMEM((2, model, o_half), bf), VMEM((2, 4, 2 * rows, a_half // 2), bf),
            VMEM((2 * rows, q_half), f32), VMEM((2 * rows, o_half), f32), VMEM((2 * rows, a_half), f32),
            VMEM((4, 2, 8, lanes), f32), VMEM((3, 8, a_half // 2), f32), VMEM((2, 16, 32, slim), bf),
            VMEM((16, toks, model), bf), VMEM((16, toks, model), bf), VMEM((16, 16, 128), bf),
            VMEM((experts, wide, model), bf), VMEM((slim, model), bf),
            VMEM((15, toks, model), bf), VMEM((15, toks, model), bf), VMEM((15, 8, 128), f32),
            VMEM((experts, 8, depth, wide), bf), VMEM((16, rows, slim), f32), VMEM((experts, wide // 2, model), bf), VMEM((slim // 2, model), bf),
            DMA((3,)), DMA((3,)), DMA((2, 31)), DMA((2, 16)), DMA((2, 16)), DMA((7,)), DMA((8,)), DMA((8,)), DMA((8,)),
            DMA((15,)), DMA((16,)), DMA((2,)), DMA((1,)), DMA((15,)), DMA((7,)), DMA((4, 2)), DMA((4,)), DMA((4,)), DMA((2, 3)), DMA((2, 4)),
            DMA((7,)), DMA((6 * experts + 2,)), DMA((3, 15)), DMA((3, 15)), DMA((2 * experts + 2,)), DMA((2 * experts + 2,)),
            DMA((2,)), DMA((2,)), DMA((experts, 4)), DMA((experts, 4)),
            DMA((3, 15)), DMA((3, 16)),
        ],
        compiler_params=pltpu.CompilerParams(collective_id=1, has_side_effects=True, vmem_limit_bytes=62 << 20),
        name="joint",
    )(lengths, timesteps, tokens, cotangent, routes.T, waves, w_ada, w_qkv, w_out, w_router.T, w_fc1, e_fc1, e_fc2, w_fc2)


def rear_kernel(lengths, steps, waves, *refs):
    incoming, refs = refs[:15], refs[15:]
    (qkv_in, out_in, part1, part1s, output, d_tokens, d_ada, d_qkv, d_out, d_router, own1, own1s), refs = refs[:12], refs[12:]
    (sum_branch, sum_back, sum_gc, tokens, cotangent, routes, mod, mixed, attn_in, qkv, probs, attn_low, attn_proj, middle, chance), refs = refs[:15], refs[15:]
    (square, slice_own, q_w, o_w, grad_attn, grad_qkv, grad_mid, o_mine, o_got, q_mine, q_got, part_o, part_a, part_b, got_o, got_a, got_b, fin, mod_tile, all_mod, l_sem, s_send, s_recv, send, recv, g_send, g_recv, g_pair, f_send, f_recv, a_send, a_recv, b_send, b_recv, i_sem) = refs
    here = y, z, x, c = place()
    me = chip(y, z, x)
    sibling = device(y, z, x, 1 - c)
    others = [(dy, dz, dx) for dy in (0, 1) for dz in (0, 1, 2, 3) for dx in (0, 1) if (dy, dz, dx) != (0, 0, 0)]
    spot = lambda dy, dz, dx: (1 - y if dy else y, along(z, dz), 1 - x if dx else x)
    held = (sum_branch, sum_back, sum_gc, tokens, cotangent, routes, mod, mixed, attn_in, qkv, probs, attn_low, attn_proj, middle, chance)
    loads = [pltpu.make_async_copy(a, b, i_sem.at[i]) for i, (a, b) in enumerate(zip(incoming, held))]
    local = [pltpu.make_async_copy(qkv_in, q_w, l_sem.at[0]), pltpu.make_async_copy(out_in, o_w, l_sem.at[1])]
    for copy in loads + local:
        copy.start()
    meet([device(*spot(*o), c) for o in others] + [sibling])
    started = []

    def go(copy):
        copy.start()
        started.append(copy)

    home = [pltpu.make_async_copy(part1s.at[me], slice_own, l_sem.at[3])]
    home[0].start()
    for step in (0, 1, 2, 3):
        at = along(z, step)
        go(remote(part1.at[:, at], own1.at[:, z], a_send.at[step], a_recv.at[z], device(y, at, 1 - x, c)))
    for i, o in enumerate(others):
        go(remote(part1s.at[chip(*spot(*o))], own1s.at[me], b_send.at[i], b_recv.at[me], device(*spot(*o), c)))

    for copy in loads:
        copy.wait()
    item = item_mask(lengths, tokens.shape)
    first = ~item
    model = item.shape[1]
    cut = model // 2
    modulation = functools.partial(own_modulation, here, mod, item)
    rows16 = {}

    def per_item(part, value):
        for i, mask in enumerate((first, ~first)):
            rows16[2 * part + i] = jnp.sum(jnp.where(mask, value, 0.0), axis=0, keepdims=True)

    out_grad = wide_float(cotangent[...])
    branch = sum_branch[...]
    output[...] = low(middle[...] + modulation(1, 2) * branch)
    per_item(5, out_grad * branch)
    chosen = choices(routes, square)
    turned = jnp.concatenate([sum_gc[...], jnp.zeros((120, 128), jnp.float32)], axis=0).T
    grad_chance = jnp.where(chosen, turned, 0.0)
    share = chance[...]
    grad_logits = low(share * (grad_chance - jnp.sum(grad_chance * share, axis=-1, keepdims=True)))
    term_router = tn(mixed[...], grad_logits)
    for copy in local + home:
        copy.wait()
    home = [pltpu.make_async_copy(slice_own, own1s.at[me], l_sem.at[3])]
    home[0].start()
    grad_mixed = sum_back[...] + nt(grad_logits, o_w[0, :, cut:])
    normed, scale = norm(middle[...])
    per_item(3, grad_mixed)
    per_item(4, grad_mixed * normed)
    grad_mid[...] = out_grad + norm_back(grad_mixed * (1.0 + modulation(1, 1)), normed, scale)
    per_item(2, grad_mid[...] * attn_proj[...])
    grad_proj = low(grad_mid[...] * modulation(0, 2))
    for h in (0, 1):
        term = jnp.concatenate([tn(attn_low[...], grad_proj[:, h * cut : (h + 1) * cut]), term_router], axis=1)
        o_mine[h] = low(term)
    swap_o = remote(o_mine.at[1 - c], o_got, s_send.at[0], s_recv.at[0], sibling)
    swap_o.start()
    grad_attn[...] = low(nt(grad_proj[:, :cut], o_w[0, :, :cut]) + nt(grad_proj[:, cut:], o_w[1, :, :cut]))

    rows = o_got.shape[0] // 16
    scatters = []
    for i, (part, got, y_first) in enumerate(((part_o, got_o, False), (part_a, got_a, True), (part_b, got_b, False))):
        take = functools.partial(lambda ref, n: ref.at[n], part)
        land = functools.partial(lambda ref, n: ref.at[n], got)
        scatters.append(Scatter(here, y_first, take, land, send.at[i], recv.at[i], relay=True))

    swap_o.wait()
    for n in range(16):
        at = slice(n * rows, (n + 1) * rows)
        part_o[n] = low(wide_float(o_mine[c, at, :]) + wide_float(o_got[at, :]))
    for step in (3, 2, 1, 0):
        scatters[0].first(step)

    left, sides = head_lanes()
    for pair in range(model // 128):
        at = slice(128 * pair, 128 * (pair + 1))
        q, key, value = [qkv[:, base + 128 * pair : base + 128 * (pair + 1)] for base in (0, model, 2 * model)]
        ga = grad_attn[:, at]
        outs = []
        for j, side in enumerate(sides):
            prob = probs[2 * pair + j]
            grad_probs = nt(ga * side, value)
            grad_scores = low(prob * (grad_probs - jnp.sum(grad_probs * prob, axis=-1, keepdims=True)))
            outs.append((nn(grad_scores, key) * 0.125, tn(grad_scores, q) * 0.125, tn(low(prob), ga)))
        for base, one, two in zip((0, model, 2 * model), *outs):
            grad_qkv[:, base + 128 * pair : base + 128 * (pair + 1)] = low(jnp.where(left, one, two))

    third = q_w.shape[2]
    for h in (0, 1):
        q_mine[h] = low(tn(attn_in[...], grad_qkv[:, h * third : (h + 1) * third]))
    swap_q = {}
    for step in (3, 2, 1, 0):
        for side in (0, 1):
            at = pl.ds(pl.multiple_of(2 * rows * (4 * side + along(z, step)), 16), 2 * rows)
            i = 1 + 2 * step + side
            swap_q[step, side] = remote(q_mine.at[1 - c, at, :], q_got.at[at, :], s_send.at[i], s_recv.at[i], sibling)
            swap_q[step, side].start()
    grad_in = nt(grad_qkv[:, :third], q_w[0]) + nt(grad_qkv[:, third:], q_w[1])
    normed, scale = norm(wide_float(tokens[...]))
    per_item(0, grad_in)
    per_item(1, grad_in * normed)
    d_tokens[...] = grad_mid[...] + norm_back(grad_in * (1.0 + modulation(0, 1)), normed, scale)
    column = lax.broadcasted_iota(jnp.int32, (8, model), 1)
    last = jnp.concatenate([rows16[8 + i] for i in range(4)] + [jnp.zeros((4, model), jnp.float32)], axis=0)
    last = last + conditions(steps, (8, model), 4, column, model // 2, waves[...])
    mod_tile[...] = low(jnp.concatenate([rows16[i] for i in range(8)] + [last], axis=0))

    slot = lambda n: all_mod.at[n, c]
    spread = Gather(here, False, mod_tile, slot, g_send, g_recv, g_pair)
    all_mod[me, c] = mod_tile[...]
    gather_start([spread])
    edge = part_a.shape[2]

    def fold(step):
        for side in (0, 1):
            swap_q[step, side].wait()
            first_n = 8 * side + 2 * along(z, step)
            for n in (first_n, first_n + 1):
                at = pl.ds(pl.multiple_of(rows * n, 16), rows)
                total = low(wide_float(q_mine[c, at, :]) + wide_float(q_got[at, :]))
                part_a[n] = total[:, :edge]
                part_b[n] = total[:, edge:]
        for scatter in scatters[1:]:
            scatter.first(step)

    fold(3)
    fold(2)

    def turn(at):
        if at == 1:
            spread.second(0)
            for step in LINE:
                gather_line([spread], step)
        elif at == 2:
            for step in LINE:
                spread.second(step)
        elif at == 3:
            for step in (0,) + LINE:
                spread.third(step)
            spread.finish()
            flat = all_mod[...].reshape(32 * 16, model)
            share_rows = rows // 2
            own = (2 * me + c) * share_rows
            source = lax.broadcasted_iota(jnp.int32, (model, 128), 0)
            lane = lax.broadcasted_iota(jnp.int32, (model, 128), 1)
            own_columns = nn(flat, low(wide_float((source == own + lane) & (lane < share_rows))))
            row = lax.broadcasted_iota(jnp.int32, (512, 128), 0) % 16
            own_columns = jnp.where((row >= 12) & (row < 14), own_columns, 0.0)
            for part in range(6):
                lhs = low(pltpu.roll(own_columns, 512 + 2 * part - 12, 0))
                d_ada[:, part * model : (part + 1) * model] = tn(lhs, flat)[:share_rows]

    scatter_all(scatters, fold, turn)
    fin[c] = jnp.concatenate([scatters[1].total(), scatters[2].total(), scatters[0].total()], axis=1)
    half = rows // 2
    mine = pl.ds(pl.multiple_of(half * c, 8), half)
    theirs = pl.ds(pl.multiple_of(half * (1 - c), 8), half)
    swap = remote(fin.at[c, theirs, :], fin.at[c, theirs, :], f_send, f_recv, sibling)
    swap.start()

    for at in range(4):
        remote(own1.at[:, at], own1.at[:, at], a_send.at[0], a_recv.at[at], sibling).wait_recv()
    for copy in home:
        copy.wait()
    for i, o in enumerate(others):
        n = chip(*spot(*o))
        remote(own1s.at[n], own1s.at[n], b_send.at[i], b_recv.at[n], sibling).wait_recv()
    for scatter in scatters:
        scatter.finish()
    for copy in started:
        copy.wait_send()
    swap.wait_send()
    remote(fin.at[1 - c, mine, :], fin.at[1 - c, mine, :], f_send, f_recv, sibling).wait_recv()
    for h in (0, 1):
        d_qkv[:, h * third : (h + 1) * third] = fin[h, mine, :third]
        d_out[:, h * cut : (h + 1) * cut] = fin[h, mine, third : third + cut]
    d_router[0:half, :] = fin[0, mine, third + cut :]
    d_router[half:, :] = jnp.zeros((128 - half, 128), jnp.float32)


def rear(lengths, timesteps, sums, tokens, cotangent, routes, saved, qkv_w, out_w, part1, part1s):
    bf, f32 = jnp.bfloat16, jnp.float32
    toks, model = tokens.shape
    rows = model // 16
    q_half, o_half = qkv_w.shape[2], out_w.shape[2]
    a_half = model
    incoming = (*sums, tokens, cotangent, routes.T, *saved)
    shape = jax.ShapeDtypeStruct
    return pl.pallas_call(
        rear_kernel,
        out_shape=[
            shape((toks, model), bf),
            shape((toks, model), f32),
            shape((rows // 2, 6 * model), f32),
            shape((rows // 2, 2 * q_half), f32),
            shape((rows // 2, model), f32),
            shape((128, 128), f32),
            shape(part1.shape, bf),
            shape(part1s.shape, bf),
        ],
        in_specs=[pl.BlockSpec(memory_space=pltpu.SMEM)] * 2
        + [pl.BlockSpec(memory_space=VMEM)]
        + [pl.BlockSpec(memory_space=ANY)] * 19,
        out_specs=[pl.BlockSpec(memory_space=VMEM)] * 6 + [pl.BlockSpec(memory_space=ANY)] * 2,
        scratch_shapes=[VMEM(a.shape, a.dtype) for a in incoming]
        + [
            VMEM((128, 128), f32), VMEM(part1s.shape[1:], bf), VMEM(qkv_w.shape, bf), VMEM(out_w.shape, bf),
            VMEM((toks, model), bf), VMEM((toks, 3 * model), bf), VMEM((toks, model), f32),
            VMEM((2, model, o_half), bf), VMEM((model, o_half), bf),
            VMEM((2, model, q_half), bf), VMEM((model, q_half), bf),
            VMEM((16, rows, o_half), bf), VMEM((16, rows, a_half), bf), VMEM((16, rows, q_half - a_half), bf),
            VMEM((15, rows, o_half), bf), VMEM((15, rows, a_half), bf), VMEM((15, rows, q_half - a_half), bf),
            VMEM((2, rows, q_half + o_half), f32), VMEM((16, model), bf), VMEM((16, 2, 16, model), bf),
            DMA((4,)), DMA((9,)), DMA((9,)), DMA((3, 15)), DMA((3, 15)), DMA((31,)), DMA((16,)), DMA((16,)), DMA, DMA,
            DMA((4,)), DMA((4,)), DMA((15,)), DMA((16,)), DMA((16,)),
        ],
        compiler_params=pltpu.CompilerParams(collective_id=3, has_side_effects=True, vmem_limit_bytes=62 << 20),
        name="rear",
    )(lengths, timesteps, frequencies(model)[None], *incoming, qkv_w, out_w, part1, part1s)


def finish_kernel(*refs):
    count = (len(refs) - 3) // 3
    inputs, outputs, staged = refs[:count], refs[count : 2 * count - 1], refs[2 * count - 1 : 3 * count - 1]
    e1, fc1, sem_in, sem = refs[3 * count - 1 :]
    loads = [pltpu.make_async_copy(a, b, sem_in.at[i]) for i, (a, b) in enumerate(zip(inputs, staged))]
    stores = []

    def store(source, target):
        stores.append(pltpu.make_async_copy(source, target, sem.at[len(stores)]))
        stores[-1].start()

    for copy in loads:
        copy.start()
    near, far, slices, router = staged[:4]
    x = place()[2]
    wide = near.shape[3]
    loads[0].wait()
    loads[1].wait()
    for e in range(near.shape[0]):
        for at in range(near.shape[1]):
            e1[e, :, pl.ds(pl.multiple_of(wide * (2 * at + x), 128), wide)] = wide_float(near[e, at])
            e1[e, :, pl.ds(pl.multiple_of(wide * (2 * at + 1 - x), 128), wide)] = wide_float(far[e, at])
        store(e1.at[e], outputs[0].at[e])
    for load, source, target in zip(loads[4:], staged[4:], outputs[3:]):
        load.wait()
        store(source, target)
    loads[2].wait()
    loads[3].wait()
    rows, slim = fc1.shape[0], slices.shape[2]
    for n in range(slices.shape[0] // 2):
        pair = [wide_float(slices[2 * n + i])[:rows] for i in (0, 1)]
        fc1[:, 2 * n * slim : 2 * (n + 1) * slim] = jnp.concatenate(pair, axis=1)
    store(fc1, outputs[1])
    outputs[2][...] = router[...].T[: outputs[2].shape[0], : outputs[2].shape[1]]
    for copy in stores:
        copy.wait()


def finish(near1, far1, own1s, d_router, *others):
    f32 = jnp.float32
    experts, _, depth, wide = near1.shape
    rows = depth // 2
    e1, fc1 = (experts, depth, 8 * wide), (rows, own1s.shape[0] * own1s.shape[2])
    shape = jax.ShapeDtypeStruct
    inputs = (near1, far1, own1s, d_router, *others)
    result = pl.pallas_call(
        finish_kernel,
        out_shape=[shape(e1, f32), shape(fc1, f32), shape((8, rows), f32)] + [shape(a.shape, a.dtype) for a in others],
        in_specs=[pl.BlockSpec(memory_space=ANY)] * len(inputs),
        out_specs=[pl.BlockSpec(memory_space=ANY)] * 2
        + [pl.BlockSpec(memory_space=VMEM)]
        + [pl.BlockSpec(memory_space=ANY)] * len(others),
        scratch_shapes=[VMEM(a.shape, a.dtype) for a in inputs]
        + [VMEM(e1, f32), VMEM(fc1, f32), DMA((len(inputs),)), DMA((8 + len(others),))],
        compiler_params=pltpu.CompilerParams(vmem_limit_bytes=62 << 20),
        name="finish",
    )(*inputs)
    return result[0], result[1], result[2].T, *result[3:]


def layer_norm(values):
    average = jnp.mean(values, axis=-1, keepdims=True)
    centred = values - average
    return centred * lax.rsqrt(jnp.mean(centred * centred, axis=-1, keepdims=True) + layer_epsilon)


def modulate(values, shift_by, scale_by):
    return layer_norm(values) * (1.0 + scale_by) + shift_by


def sinusoid(timesteps, model_width):
    half_width = model_width // 2
    frequency = jnp.exp(-math.log(10000.0) * jnp.arange(half_width, dtype=jnp.float32) / half_width)
    angles = timesteps.astype(jnp.float32)[:, None] * frequency[None, :]
    return jnp.concatenate([jnp.cos(angles), jnp.sin(angles)], axis=1)


def membership(lengths, tok_count):
    bounds = jnp.cumsum(lengths)[:-1]
    position = jnp.arange(tok_count, dtype=jnp.int32)
    item_of = jnp.sum((position[:, None] >= bounds[None, :]).astype(jnp.int32), axis=1)
    item_ids = jnp.arange(lengths.shape[0], dtype=jnp.int32)
    return ((item_of[:, None] == item_ids[None, :]).astype(jnp.float32), item_of)


def slot_index(routes, expert_count, capacity):
    flat_routes = routes.reshape(-1)
    expert_hot = (
        flat_routes[:, None] == jnp.arange(expert_count, dtype=jnp.int32)[None, :]
    ).astype(jnp.int32)
    before = jnp.cumsum(expert_hot, axis=0) - expert_hot
    rank_in = jnp.sum(before * expert_hot, axis=1)
    return (flat_routes * capacity + rank_in).reshape(routes.shape)


def dot_float(left_side, right_side):
    return jnp.dot(left_side, right_side, preferred_element_type=jnp.float32)


def dot_rows(left_side, right_side):
    return jnp.einsum("td,tf->df", left_side, right_side, preferred_element_type=jnp.float32)


def dot_cols(left_side, right_side):
    return jnp.einsum("tf,df->td", left_side, right_side, preferred_element_type=jnp.float32)


def dot_halves(left_side, halves):
    return jnp.concatenate([dot_float(left_side, halves[0]), dot_float(left_side, halves[1])], axis=1)


def by_slices(
    tokens, timesteps, lengths, routes, cotangent, w_ada, w_qkv, w_out, w_fc1, w_fc2, w_router, e_fc1, e_fc2
):
    (qkv_w, out_w, mod, mixed, attn_in, qkv, probs, attn_low, attn_proj, middle, chance, *sums, near1, far1, part1s, d_e2,
     d_fc2) = joint(
        lengths, timesteps, tokens, cotangent, routes, w_ada, w_qkv, w_out, w_router, w_fc1, e_fc1, e_fc2, w_fc2
    )
    saved = (mod, mixed, attn_in, qkv, probs, attn_low, attn_proj, middle, chance)
    output, d_tokens, d_ada, d_qkv, d_out, d_router, own1, own1s = rear(
        lengths, timesteps, sums, tokens, cotangent, routes, saved, qkv_w, out_w, far1, part1s
    )
    d_e1, d_fc1, d_router, output, d_tokens, d_ada, d_qkv, d_out, d_fc2, d_e2 = finish(
        near1, own1, own1s, d_router, output, d_tokens, d_ada, d_qkv, d_out, d_fc2, d_e2
    )
    return (output, d_tokens, d_ada, d_qkv, d_out, d_fc1, d_fc2, d_router, d_e1, d_e2)


def by_weights(
    tokens,
    timesteps,
    lengths,
    routes,
    cotangent,
    w_ada,
    w_qkv,
    w_out,
    w_fc1,
    w_fc2,
    w_router,
    e_fc1,
    e_fc2,
):
    tok_count, model_width = tokens.shape
    head_count = HEADS
    head_size = model_width // head_count
    expert_count = w_router.shape[1]
    capacity = CAP
    score_scale = head_size ** (-0.5)
    residual = tokens.astype(jnp.float32)
    member, item_of = membership(lengths[0], tok_count)
    ada_full, qkv_full, out_full = (
        lax.all_gather(w_ada, ("gx", "gy"), axis=0, tiled=True),
        lax.all_gather(w_qkv, ("gx", "gy"), axis=0, tiled=True),
        lax.all_gather(w_out, ("gx", "gy"), axis=0, tiled=True),
    )
    condition = jax.nn.silu(sinusoid(timesteps, model_width)).astype(jnp.bfloat16)
    modulation = dot_float(condition, ada_full)
    token_mod = jnp.dot(member, modulation, precision=precise)
    shift_attn, scale_attn, gate_attn, shift_mlp, scale_mlp, gate_mlp = jnp.split(
        token_mod, 6, axis=1
    )
    attn_in = modulate(residual, shift_attn, scale_attn).astype(jnp.bfloat16)
    qkv_low = dot_float(attn_in, qkv_full).astype(jnp.bfloat16)
    queries, key_rows, value_rows = [
        portion.reshape(tok_count, head_count, head_size)
        for portion in jnp.split(qkv_low, 3, axis=1)
    ]
    same_item = item_of[:, None] == item_of[None, :]
    scores = (
        jnp.einsum("qhd,khd->hqk", queries, key_rows, preferred_element_type=jnp.float32)
        * score_scale
    )
    scores = jnp.where(same_item[None], scores, -1e30)
    attn_probs = jax.nn.softmax(scores, axis=-1)
    probs_low = attn_probs.astype(jnp.bfloat16)
    attn_low = jnp.einsum("hqk,khd->qhd", probs_low, value_rows, preferred_element_type=jnp.float32)
    attn_low = attn_low.reshape(tok_count, model_width).astype(jnp.bfloat16)
    attn_proj = dot_float(attn_low, out_full)
    middle = residual + gate_attn * attn_proj
    mixed_in = modulate(middle, shift_mlp, scale_mlp).astype(jnp.bfloat16)
    fc1_full, fc2_full, router_full = (
        lax.all_gather(w_fc1, ("gx", "gy"), axis=0, tiled=True),
        lax.all_gather(w_fc2, ("gx", "gy"), axis=0, tiled=True),
        lax.all_gather(w_router, ("gx", "gy"), axis=0, tiled=True),
    )
    hidden_pre = dot_float(mixed_in, fc1_full)
    hidden = jax.nn.gelu(hidden_pre).astype(jnp.bfloat16)
    shared = dot_float(hidden, fc2_full)
    chance = jax.nn.softmax(dot_float(mixed_in, router_full), axis=-1)
    expert_ids = jnp.arange(expert_count, dtype=jnp.int32)
    chosen = (routes[:, :, None] == expert_ids[None, None, :]).astype(jnp.float32)
    gate_values = jnp.sum(chosen * chance[:, None, :], axis=2)
    slot_of = slot_index(routes, expert_count, capacity)
    slot_ids = jnp.arange(expert_count * capacity, dtype=jnp.int32)
    selector = (slot_of[:, :, None] == slot_ids[None, None, :]).astype(jnp.bfloat16)
    slot_rows = jnp.einsum("tks,td->sd", selector, mixed_in, preferred_element_type=jnp.float32)
    slot_rows = slot_rows.astype(jnp.bfloat16).reshape(expert_count, capacity, model_width)
    owned_rows = lax.all_to_all(slot_rows, "gx", split_axis=0, concat_axis=1, tiled=True)
    expert_in, expert_back = (
        lax.all_gather(e_fc1, "gy", axis=1, tiled=True),
        lax.all_gather(e_fc2, "gy", axis=1, tiled=True),
    )
    inner_pre = jnp.einsum(
        "ecd,edf->ecf", owned_rows, expert_in, preferred_element_type=jnp.float32
    )
    inner_act = jax.nn.gelu(inner_pre).astype(jnp.bfloat16)
    result = jnp.einsum(
        "ecf,efd->ecd", inner_act, expert_back, preferred_element_type=jnp.float32
    ).astype(jnp.bfloat16)
    returned = lax.all_to_all(result, "gx", split_axis=1, concat_axis=0, tiled=True).reshape(
        expert_count * capacity, model_width
    )
    picked = jnp.take(returned, slot_of, axis=0).astype(jnp.float32)
    branch = shared + jnp.sum(gate_values[:, :, None] * picked, axis=1)
    output = (middle + gate_mlp * branch).astype(jnp.bfloat16)
    out_grad = cotangent.astype(jnp.float32)
    grad_gate_mlp = out_grad * branch
    grad_branch = out_grad * gate_mlp
    grad_shared = grad_branch.astype(jnp.bfloat16)
    grad_picked = (gate_values[:, :, None] * grad_branch[:, None, :]).astype(jnp.bfloat16)
    grad_gates = jnp.sum(grad_branch[:, None, :] * picked, axis=2)
    grad_slots = jnp.einsum(
        "tks,tkd->sd", selector, grad_picked, preferred_element_type=jnp.float32
    )
    grad_slots = grad_slots.astype(jnp.bfloat16).reshape(expert_count, capacity, model_width)
    grad_owned = lax.all_to_all(grad_slots, "gx", split_axis=0, concat_axis=1, tiled=True)
    grad_inner = jnp.einsum(
        "ecd,efd->ecf", grad_owned, expert_back, preferred_element_type=jnp.float32
    )
    unused_inner, gelu_expert = jax.vjp(jax.nn.gelu, inner_pre)
    grad_inner_pre = gelu_expert(grad_inner)[0].astype(jnp.bfloat16)
    term_e_out = jnp.einsum(
        "ecf,ecd->efd", inner_act, grad_owned, preferred_element_type=jnp.float32
    )
    term_e_in = jnp.einsum(
        "ecd,ecf->edf", owned_rows, grad_inner_pre, preferred_element_type=jnp.float32
    )
    grad_rows = jnp.einsum(
        "ecf,edf->ecd", grad_inner_pre, expert_in, preferred_element_type=jnp.float32
    )
    grad_returned = (
        lax.all_to_all(
            grad_rows.astype(jnp.bfloat16), "gx", split_axis=1, concat_axis=0, tiled=True
        )
        .astype(grad_rows.dtype)
        .reshape(expert_count * capacity, model_width)
    )
    sum_e_in, sum_e_out = (
        lax.psum_scatter(
            term_e_in.astype(jnp.bfloat16), "gy", scatter_dimension=1, tiled=True
        ).astype(jnp.float32),
        lax.psum_scatter(
            term_e_out.astype(jnp.bfloat16), "gy", scatter_dimension=1, tiled=True
        ).astype(jnp.float32),
    )
    grad_chance = jnp.sum(chosen * grad_gates[:, :, None], axis=1)
    grad_logits = chance * (grad_chance - jnp.sum(grad_chance * chance, axis=-1, keepdims=True))
    grad_logits = grad_logits.astype(jnp.bfloat16)
    grad_hidden = dot_cols(grad_shared, fc2_full)
    unused_shared, gelu_shared = jax.vjp(jax.nn.gelu, hidden_pre)
    grad_hidden_pre = gelu_shared(grad_hidden)[0].astype(jnp.bfloat16)
    term_fc2 = dot_rows(hidden, grad_shared)
    term_fc1 = dot_rows(mixed_in, grad_hidden_pre)
    term_router = dot_rows(mixed_in, grad_logits)
    part_fc1, part_fc2, part_router = (
        lax.psum_scatter(
            term_fc1.astype(jnp.bfloat16), "gx", scatter_dimension=0, tiled=True
        ).astype(jnp.float32),
        lax.psum_scatter(
            term_fc2.astype(jnp.bfloat16), "gx", scatter_dimension=0, tiled=True
        ).astype(jnp.float32),
        lax.psum_scatter(
            term_router.astype(jnp.bfloat16), "gx", scatter_dimension=0, tiled=True
        ).astype(jnp.float32),
    )
    sum_fc1, sum_fc2, sum_router = (
        lax.psum_scatter(
            part_fc1.astype(jnp.bfloat16), "gy", scatter_dimension=0, tiled=True
        ).astype(jnp.float32),
        lax.psum_scatter(
            part_fc2.astype(jnp.bfloat16), "gy", scatter_dimension=0, tiled=True
        ).astype(jnp.float32),
        lax.psum_scatter(
            part_router.astype(jnp.bfloat16), "gy", scatter_dimension=0, tiled=True
        ).astype(jnp.float32),
    )
    grad_mixed = dot_cols(grad_hidden_pre, fc1_full) + dot_cols(grad_logits, router_full)
    grad_mixed = grad_mixed + jnp.sum(jnp.take(grad_returned, slot_of, axis=0), axis=1)
    unused_mix, mix_back = jax.vjp(modulate, middle, shift_mlp, scale_mlp)
    grad_mid_norm, grad_shift_mlp, grad_scale_mlp = mix_back(grad_mixed)
    grad_middle = out_grad + grad_mid_norm
    grad_gate_attn = grad_middle * attn_proj
    grad_proj = (grad_middle * gate_attn).astype(jnp.bfloat16)
    term_out = dot_rows(attn_low, grad_proj)
    grad_attn = (
        dot_cols(grad_proj, out_full).astype(jnp.bfloat16).reshape(tok_count, head_count, head_size)
    )
    grad_probs = jnp.einsum(
        "qhd,khd->hqk", grad_attn, value_rows, preferred_element_type=jnp.float32
    )
    grad_values = jnp.einsum(
        "hqk,qhd->khd", probs_low, grad_attn, preferred_element_type=jnp.float32
    )
    grad_scores = attn_probs * (
        grad_probs - jnp.sum(grad_probs * attn_probs, axis=-1, keepdims=True)
    )
    grad_scores = grad_scores.astype(jnp.bfloat16)
    grad_queries = (
        jnp.einsum("hqk,khd->qhd", grad_scores, key_rows, preferred_element_type=jnp.float32)
        * score_scale
    )
    grad_keys = (
        jnp.einsum("hqk,qhd->khd", grad_scores, queries, preferred_element_type=jnp.float32)
        * score_scale
    )
    grad_qkv = jnp.concatenate(
        [
            grad_queries.reshape(tok_count, model_width),
            grad_keys.reshape(tok_count, model_width),
            grad_values.reshape(tok_count, model_width),
        ],
        axis=1,
    ).astype(jnp.bfloat16)
    term_qkv = dot_rows(attn_in, grad_qkv)
    grad_attn_in = dot_cols(grad_qkv, qkv_full)
    unused_pre, pre_back = jax.vjp(modulate, residual, shift_attn, scale_attn)
    grad_input_norm, grad_shift_attn, grad_scale_attn = pre_back(grad_attn_in)
    d_tokens = grad_middle + grad_input_norm
    grad_token_mod = jnp.concatenate(
        [
            grad_shift_attn,
            grad_scale_attn,
            grad_gate_attn,
            grad_shift_mlp,
            grad_scale_mlp,
            grad_gate_mlp,
        ],
        axis=1,
    )
    grad_modulation = jnp.einsum("ti,tc->ic", member, grad_token_mod, precision=precise).astype(
        jnp.bfloat16
    )
    all_condition, all_modgrad = (
        lax.all_gather(condition, ("gx", "gy"), axis=0, tiled=True),
        lax.all_gather(grad_modulation, ("gx", "gy"), axis=0, tiled=True),
    )
    own_share = model_width // lax.axis_size(("gx", "gy"))
    own_start = lax.axis_index(("gx", "gy")) * own_share
    own_condition = lax.dynamic_slice_in_dim(all_condition, own_start, own_share, 1)
    owned_ada = dot_rows(own_condition, all_modgrad)
    attn_terms = (term_qkv, term_out)
    attn_parts = (
        lax.psum_scatter(
            attn_terms[0].astype(jnp.bfloat16), "gx", scatter_dimension=0, tiled=True
        ).astype(jnp.float32),
        lax.psum_scatter(
            attn_terms[1].astype(jnp.bfloat16), "gx", scatter_dimension=0, tiled=True
        ).astype(jnp.float32),
    )
    attn_sums = (
        lax.psum_scatter(
            attn_parts[0].astype(jnp.bfloat16), "gy", scatter_dimension=0, tiled=True
        ).astype(jnp.float32),
        lax.psum_scatter(
            attn_parts[1].astype(jnp.bfloat16), "gy", scatter_dimension=0, tiled=True
        ).astype(jnp.float32),
    )
    sum_qkv, sum_out = attn_sums
    return (
        output,
        d_tokens,
        owned_ada,
        sum_qkv,
        sum_out,
        sum_fc1,
        sum_fc2,
        sum_router,
        sum_e_in,
        sum_e_out,
    )


def solution(mesh):
    in_specs = (
        P(("gx", "gy"), None),
        P(("gx", "gy")),
        P(("gx", "gy"), None),
        P(("gx", "gy"), None),
        P(("gx", "gy"), None),
        P(("gx", "gy"), None),
        P(("gx", "gy"), None),
        P(("gx", "gy"), None),
        P(("gx", "gy"), None),
        P(("gx", "gy"), None),
        P(("gx", "gy"), None),
        P("gx", "gy", None),
        P("gx", "gy", None),
    )
    out_specs = (
        P(("gx", "gy"), None),
        P(("gx", "gy"), None),
        P(("gx", "gy"), None),
        P(("gx", "gy"), None),
        P(("gx", "gy"), None),
        P(("gx", "gy"), None),
        P(("gx", "gy"), None),
        P(("gx", "gy"), None),
        P("gx", "gy", None),
        P("gx", "gy", None),
    )
    step = by_slices if dict(mesh.shape) == {"gx": 2, "gy": 16} else by_weights
    return jax.shard_map(
        step, mesh=mesh, in_specs=in_specs, out_specs=out_specs, check_vma=False
    )
```

```python
import functools
import math

import jax
import jax.numpy as jnp
import numpy as np
from jax import lax
from jax.experimental import pallas as pl
from jax.experimental.pallas import tpu as pltpu
from jax.sharding import PartitionSpec as P

HEADS = 12
CAP = 64
MESH = pl.DeviceIdType.MESH
ANY = pl.ANY
VMEM = pltpu.VMEM
DMA = pltpu.SemaphoreType.DMA
LINE = (1, 2, 3)

precise = lax.Precision.HIGHEST
layer_epsilon = 1e-06


def place():
    gy = lax.axis_index("gy")
    return lax.axis_index("gx"), gy // 4, (gy // 2) % 2, gy % 2


def device(y, z, x, c):
    return (y, 4 * z + 2 * x + c)


def chip(y, z, x):
    return 8 * y + 2 * z + x


def along(z, step):
    return z + step - 2 * (z % 2) * (step % 2) - 4 * (z // 2) * (step // 2)


def meet(partners):
    barrier = pltpu.get_barrier_semaphore()
    for partner in partners:
        pl.semaphore_signal(barrier, inc=1, device_id=partner, device_id_type=MESH)
    pl.semaphore_wait(barrier, len(partners))


def cross_partners(here):
    y, z, x, c = here
    return [device(y, along(z, step), x, c) for step in LINE] + [
        device(1 - y, z, x, c),
        device(y, z, 1 - x, c),
    ]


def remote(source, target, send, recv, to):
    return pltpu.make_async_remote_copy(
        src_ref=source, dst_ref=target, send_sem=send, recv_sem=recv, device_id=to, device_id_type=MESH
    )


class Gather:
    def __init__(self, here, y_first, own, slot, send, recv, pair=None):
        self.here, self.y_first, self.own, self.slot = here, y_first, own, slot
        self.send, self.recv, self.pair, self.started = send, recv, pair, []

    def number(self, a, step, b):
        y, z, x, c = self.here
        flip_y, flip_x = (a, b) if self.y_first else (b, a)
        return chip(1 - y if flip_y else y, along(z, step), 1 - x if flip_x else x)

    def copy(self, source, number, to, recv=None):
        recv = self.recv if recv is None else recv
        sent = remote(source, self.slot(number), self.send.at[len(self.started)], recv.at[number], to)
        sent.start()
        self.started.append(sent)

    def to_side(self, source, number, second):
        y, z, x, c = self.here
        self.copy(source, number, device(1 - y, z, x, c) if self.y_first != second else device(y, z, 1 - x, c))

    def to_line(self, source, number, step):
        y, z, x, c = self.here
        self.copy(source, number, device(y, along(z, step), x, c))

    def to_pair(self, source, number):
        y, z, x, c = self.here
        if self.pair is not None:
            self.copy(source, number, device(y, z, x, 1 - c), self.pair)

    def arrive(self, number, recv=None):
        recv = self.recv if recv is None else recv
        block = self.slot(number)
        remote(block, block, self.send.at[0], recv.at[number], device(*self.here)).wait_recv()
        return block

    def start_first(self):
        self.to_side(self.own, self.number(0, 0, 0), False)
        self.to_pair(self.own, self.number(0, 0, 0))

    def start_line(self, step):
        self.to_line(self.own, self.number(0, 0, 0), step)

    def start_last(self):
        self.to_side(self.own, self.number(0, 0, 0), True)

    def line_first(self, step):
        number = self.number(0, step, 0)
        block = self.arrive(number)
        if step == 2:
            self.to_line(block, number, 1)
        self.to_side(block, number, False)
        self.to_pair(block, number)

    def line_last(self, step):
        number = self.number(0, step, 0)
        self.to_side(self.slot(number), number, True)

    def second(self, step):
        number = self.number(1, step, 0)
        block = self.arrive(number)
        self.to_side(block, number, True)
        self.to_pair(block, number)

    def third(self, step):
        for a in (0, 1):
            number = self.number(a, step, 1)
            self.to_pair(self.arrive(number), number)

    def finish(self):
        block = self.slot(self.number(0, 0, 0))
        for index in range(len(self.started)):
            remote(block, block, self.send.at[index], self.recv.at[0], device(*self.here)).wait_send()
        if self.pair is not None:
            for number in range(16):
                self.arrive(number, self.pair)


def gather_start(gathers):
    for gather in gathers:
        gather.start_first()
    for step in (1, 2):
        for gather in gathers:
            gather.start_line(step)
    for gather in gathers:
        gather.start_last()


def gather_line(gathers, step):
    for gather in gathers:
        gather.line_first(step)
    for gather in gathers:
        gather.line_last(step)


def gather_second(gathers, step):
    for gather in gathers:
        gather.second(step)


def gather_third(gathers, step):
    for gather in gathers:
        gather.third(step)


def gather_all(gathers, between=None):
    gather_start(gathers)
    gather_second(gathers, 0)
    for step in LINE:
        gather_line(gathers, step)
        gather_second(gathers, step)
    if between is not None:
        between()
    for step in (0,) + LINE:
        gather_third(gathers, step)
    for gather in gathers:
        gather.finish()


class Scatter:
    def __init__(self, here, y_first, part, got, send, recv, relay=False):
        self.here, self.y_first, self.part, self.got, self.relay = here, y_first, part, got, relay
        self.send, self.recv, self.started = send, recv, []

    def number(self, a, b, step):
        y, z, x, c = self.here
        flip_y, flip_x = (a, b) if self.y_first else (b, a)
        return chip(1 - y if flip_y else y, along(z, step), 1 - x if flip_x else x)

    def toward(self, second):
        y, z, x, c = self.here
        return device(1 - y, z, x, c) if self.y_first != second else device(y, z, 1 - x, c)

    def copy(self, source, index, to):
        sent = remote(source, self.got(index), self.send.at[len(self.started)], self.recv.at[index], to)
        sent.start()
        self.started.append(sent)

    def arrive(self, index):
        block = self.got(index)
        remote(block, block, self.send.at[0], self.recv.at[index], device(*self.here)).wait_recv()
        return block

    def first(self, step):
        for b in (1, 0):
            self.copy(self.part(self.number(1, b, step)), 4 * b + step, self.toward(False))

    def add(self, number, index):
        block, mine = self.arrive(index), self.part(number)
        total = mine[...].astype(jnp.float32) + block[...].astype(jnp.float32)
        mine[...] = total.astype(mine.dtype)

    def one(self, b, step):
        number = self.number(0, b, step)
        self.add(number, 4 * b + step)
        if b == 1:
            self.copy(self.part(number), 8 + step, self.toward(True))

    def two(self, step):
        y, z, x, c = self.here
        number = self.number(0, 0, step)
        self.add(number, 8 + step)
        if self.relay and step == 2:
            self.add(number, 14)
        if step:
            self.copy(self.part(number), 11 + step, device(y, along(z, 1 if self.relay and step == 3 else step), x, c))

    def total(self):
        result = self.part(self.number(0, 0, 0))[...].astype(jnp.float32)
        for step in (1, 2) if self.relay else (1, 2, 3):
            result = result + self.arrive(11 + step)[...].astype(jnp.float32)
        return result

    def finish(self):
        block = self.got(0)
        for index in range(len(self.started)):
            remote(block, block, self.send.at[index], self.recv.at[0], device(*self.here)).wait_send()


def scatter_all(scatters, more, between):
    order = (3, 2, 1, 0)
    for turn, step in enumerate(order):
        for b in (1, 0):
            for scatter in scatters:
                scatter.one(b, step)
        if turn + 2 < 4:
            more(order[turn + 2])
        if turn:
            for scatter in scatters:
                scatter.two(order[turn - 1])
        between(turn)
    for scatter in scatters:
        scatter.two(order[3])


def nt(a, b):
    return lax.dot_general(a, b, (((1,), (1,)), ((), ())), preferred_element_type=jnp.float32)


def tn(a, b):
    return lax.dot_general(a, b, (((0,), (0,)), ((), ())), preferred_element_type=jnp.float32)


def nn(a, b):
    return jnp.dot(a, b, preferred_element_type=jnp.float32)


def low(value):
    return value.astype(jnp.bfloat16)


def wide_float(value):
    return value.astype(jnp.float32)


def norm(values):
    centred = values - jnp.mean(values, axis=-1, keepdims=True)
    scale = lax.rsqrt(jnp.mean(centred * centred, axis=-1, keepdims=True) + layer_epsilon)
    return centred * scale, scale


def norm_back(grad, normed, scale):
    pulled = grad - jnp.mean(grad, axis=-1, keepdims=True) - normed * jnp.mean(grad * normed, axis=-1, keepdims=True)
    return scale * pulled


def item_mask(lengths, shape):
    return lax.broadcasted_iota(jnp.int32, shape, 0) >= lengths[0, 0]


def choices(routes, square):
    square[...] = jnp.zeros_like(square)
    square[0 : routes.shape[0], :] = wide_float(routes[...])
    named = square[...].T
    lane = wide_float(lax.broadcasted_iota(jnp.int32, (1, 128), 1))
    return (named[:, 0:1] == lane) | (named[:, 1:2] == lane)


def own_modulation(here, mod, item, half, part):
    first = 2 * here[3]
    model = item.shape[1]
    at = slice(part * model, (part + 1) * model)
    return jnp.where(item, mod[half, pl.ds(first + 1, 1), at], mod[half, pl.ds(first, 1), at])


def frequencies(model_width):
    half = model_width // 2
    return np.tile(np.exp(-math.log(10000.0) * np.arange(half) / half).astype(np.float32), 2)


def conditions(steps, shape, first, column, half, frequency):
    row = lax.broadcasted_iota(jnp.int32, shape, 0) - first
    angle = jnp.where(row == 0, wide_float(steps[0]), wide_float(steps[1])) * frequency
    wave = jnp.where(column < half, jnp.cos(angle), jnp.sin(angle))
    value = wave / (1.0 + jnp.exp(-wave))
    return wide_float(low(jnp.where((row == 0) | (row == 1), value, 0.0)))


def head_lanes():
    lane = lax.broadcasted_iota(jnp.int32, (1, 128), 1)
    return lane < 64, [low(wide_float(lane < 64)), low(wide_float(lane >= 64))]


def front_part(refs, outs, kept, sems, start_tokens, more_tokens, *locals_):
    (lengths, steps, tokens, cotangent, routes, waves, w_ada, w_qkv, w_out, w_router, w_fc1, e1) = refs
    (qkv_w, out_w, mod_out, mixed_out, attn_in_out, qkv_out, probs_out, attn_low_out, attn_proj_out, middle_out, chance_out) = outs
    (w1, w1s, mod, mixed, grad, gates, q_full, o_full, a_full, q_stage, o_stage, a_stage, c_buf, z_got, s_got) = kept
    (pre_send, pre_recv, g_send, g_recv, g_pair, a_send, a_recv, a_pair_send, a_pair, b_send, b_recv, b_pair, l_sem, o_sem,
     c_send, c_recv, m_send, m_recv, r_send, r_recv) = sems
    (attn_in, qkv, probs, attn_low, attn_proj, middle, chance, square, cond, f1, s_rows, q_fold, o_fold, a_fold, q_block, o_block, z_part) = locals_
    here = y, z, x, c = place()
    me, k, gy = chip(y, z, x), 2 * z + x, 4 * z + 2 * x + c
    rows, model = w_out.shape
    others = [(dy, dz, dx) for dy in (0, 1) for dz in (0, 1, 2, 3) for dx in (0, 1) if (dy, dz, dx) != (0, 0, 0)]
    spot = lambda dy, dz, dx: (1 - y if dy else y, along(z, dz), 1 - x if dx else x)
    sibling = device(y, z, x, 1 - c)
    crossed = [device(y, along(z, step), x, 1 - c) for step in LINE]
    meet([device(*spot(*o), c) for o in others] + [sibling] + crossed)

    started = []

    def go(copy):
        copy.start()
        started.append(copy)

    lane = lax.broadcasted_iota(jnp.int32, cond.shape[1:], 1)
    for at in range(4):
        column = model // 2 * (lane // (4 * rows)) + 4 * rows * at + lane % (4 * rows)
        cond[at] = jnp.where(lane < 8 * rows, conditions(steps, cond.shape[1:], 2 * c, column, model // 2, waves[at : at + 1, :]), 0.0)
    for i, (step, core) in enumerate([(0, 1 - c)] + [(step, core) for step in LINE for core in (c, 1 - c)]):
        go(remote(cond.at[along(z, step)], c_buf.at[z, c], c_send.at[i], c_recv.at[z, c], device(y, along(z, step), x, core)))

    mine = pl.ds(pl.multiple_of(rows * c, 8), rows)
    square[...] = jnp.zeros_like(square)
    square[0 : w_router.shape[0], 0:rows] = wide_float(w_router[...])
    router = square[...].T[:rows]
    for i, (w, fold, stage) in enumerate(((w_ada, a_fold, a_stage), (w_qkv, q_fold, q_stage), (w_out, o_fold, o_stage))):
        cut = w.shape[1] // 2
        for h in (0, 1):
            fold[h, :, :cut] = wide_float(w[:, h * cut : (h + 1) * cut])
            if i == 2:
                fold[h, :, cut:] = router
        go(remote(fold.at[1 - c], stage.at[mine, :], pre_send.at[i], pre_recv.at[i], sibling))
        stage[mine, :] = fold[c]

    depth, width = e1.shape[1], w1.shape[2]
    cols = lambda n: pl.ds(pl.multiple_of(width * n, 128), width)
    strip = lambda n: pl.ds(pl.multiple_of(depth * n, 16), depth)
    load = pltpu.make_async_copy(e1.at[:, :, cols(k)], w1.at[:, strip(gy), :], l_sem.at[0])
    load.start()
    plane = [o for o in others if o[0] == 0]

    def send_experts(steps, aside):
        for i, o in enumerate(plane):
            if o[1] in steps and o[2] == aside:
                ty, tz, tx = spot(*o)
                go(remote(e1.at[:, :, cols(2 * tz + tx)], w1.at[:, strip(gy), :], a_send.at[i], a_recv.at[k], device(ty, tz, tx, c)))


    def folded(i, stage):
        theirs = stage.at[pl.ds(pl.multiple_of(rows * (1 - c), 8), rows), :]
        remote(theirs, theirs, pre_send.at[i], pre_recv.at[i], sibling).wait_recv()
        return low(stage[...])

    block = folded(0, a_stage)
    width_a = a_full.shape[3]
    number = 2 * y + x
    to_y, to_x = device(1 - y, z, x, c), device(y, z, 1 - x, c)
    for i in (0, 1):
        a_full[i, number] = block[:, i * width_a : (i + 1) * width_a]

    def send_a(i, n, lane, to):
        go(remote(a_full.at[i, n], a_full.at[i, n], r_send.at[i, lane], r_recv.at[i, n], to))

    def wait_a(i, n):
        remote(a_full.at[i, n], a_full.at[i, n], r_send.at[0, 0], r_recv.at[i, n], sibling).wait_recv()

    send_a(0, number, 0, to_y)
    send_a(1, number, 0, to_x)
    send_a(0, number, 1, to_x)
    send_a(1, number, 1, to_y)
    q_block[...] = folded(1, q_stage)
    o_block[...] = folded(2, o_stage)
    gathers = []
    for i, (block, full, y_first) in enumerate(((q_block, q_full, False), (o_block, o_full, True))):
        slot = functools.partial(lambda full, n: full.at[c, pl.ds(pl.multiple_of(2 * rows * n, 16), 2 * rows), :], full)
        gathers.append(Gather(here, y_first, block, slot, g_send.at[i], g_recv.at[i], g_pair.at[i]))
        slot(me)[...] = block[...]
    gather_start(gathers)

    n_y, n_x = 2 * (1 - y) + x, 2 * y + 1 - x
    n_xy = 2 * (1 - y) + 1 - x
    wait_a(0, n_y)
    send_a(0, n_y, 2, to_x)
    wait_a(1, n_x)
    send_a(1, n_x, 2, to_y)
    gather_second(gathers, 0)

    c_buf[z, c] = cond[z]
    for step, core in [(0, 1 - c)] + [(step, core) for step in LINE for core in (c, 1 - c)]:
        block = c_buf.at[along(z, step), core]
        remote(block, block, c_send.at[0], c_recv.at[along(z, step), core], sibling).wait_recv()
    lhs = low(jnp.concatenate([c_buf[i, 0] + c_buf[i, 1] for i in range(4)], axis=0))[:, : 8 * rows]
    for i, n_last in enumerate((n_x, n_y)):
        wait_a(i, n_last)
        wait_a(i, n_xy)
        term = nn(lhs, a_full[i].reshape(8 * rows, width_a))
        for line in range(4):
            z_part[line, 4 * i : 4 * (i + 1), :] = term[8 * line : 8 * line + 4]
    for step in LINE:
        at = along(z, step)
        go(remote(z_part.at[at], z_got.at[step - 1], m_send.at[step], m_recv.at[step], device(y, at, x, c)))
    gather_line(gathers, 1)
    slim = w1s.shape[1]
    for n in range(16):
        block = wide_float(w_fc1[:, slim * n : slim * (n + 1)])
        f1[n] = low(jnp.concatenate([block, jnp.zeros((f1.shape[1] - rows, slim), jnp.float32)], axis=0))
    for i, o in enumerate(others):
        ty, tz, tx = spot(*o)
        go(remote(f1.at[chip(ty, tz, tx)], s_got.at[c, me], b_send.at[i], b_recv.at[me], device(ty, tz, tx, c)))
    s_got[c, me] = f1[me]
    gather_second(gathers, 1)
    gather_line(gathers, 2)
    send_experts((2, 3, 1), 0)
    gather_second(gathers, 2)
    gather_line(gathers, 3)
    gather_second(gathers, 3)
    send_experts((0, 1, 2, 3), 1)
    total = z_part[z]
    for step in LINE:
        remote(z_got.at[step - 1], z_got.at[step - 1], m_send.at[0], m_recv.at[step], sibling).wait_recv()
        total = total + z_got[step - 1]
    mod[c] = jnp.concatenate([total, pltpu.roll(total, 4, 0)], axis=1)
    go(remote(mod.at[c], mod.at[c], m_send.at[0], m_recv.at[0], sibling))
    remote(mod.at[1 - c], mod.at[1 - c], m_send.at[0], m_recv.at[0], sibling).wait_recv()

    item = item_mask(lengths, tokens.shape)
    residual = wide_float(tokens[...])
    normed, _ = norm(residual)
    attn_in[...] = low(normed * (1.0 + own_modulation(here, mod, item, 0, 1)) + own_modulation(here, mod, item, 0, 0))
    grad[...] = low(wide_float(cotangent[...]) * own_modulation(here, mod, item, 1, 2))
    token_gathers = start_tokens(None, (1,))
    for step in (0,) + LINE:
        gather_third(gathers, step)
    for gather in gathers:
        gather.finish()
    keep = []

    def leave(source, target):
        keep.append(pltpu.make_async_copy(source, target, o_sem.at[len(keep)]))
        keep[-1].start()

    leave(q_full, qkv_w)
    leave(o_full, out_w)

    cut = q_full.shape[2]
    for h in (0, 1):
        qkv[:, h * cut : (h + 1) * cut] = low(nn(attn_in[...], q_full[h]))

    side = wide_float(item[:, :128])
    same = side == side.T
    left, sides = head_lanes()
    for pair in range(model // 128):
        q, key, value = [qkv[:, base + 128 * pair : base + 128 * (pair + 1)] for base in (0, model, 2 * model)]
        outs = []
        for j, side in enumerate(sides):
            scores = jnp.where(same, nt(q * side, key) * 0.125, -1e30)
            weight = jnp.exp(scores - jnp.max(scores, axis=-1, keepdims=True))
            prob = weight / jnp.sum(weight, axis=-1, keepdims=True)
            probs[2 * pair + j] = prob
            outs.append(nn(low(prob), value))
        attn_low[:, 128 * pair : 128 * (pair + 1)] = low(jnp.where(left, outs[0], outs[1]))
    cut = model // 2
    for h in (0, 1):
        attn_proj[:, h * cut : (h + 1) * cut] = nn(attn_low[...], o_full[h, :, :cut])
    middle[...] = residual + own_modulation(here, mod, item, 0, 2) * attn_proj[...]
    normed, _ = norm(middle[...])
    mixed[...] = low(normed * (1.0 + own_modulation(here, mod, item, 1, 1)) + own_modulation(here, mod, item, 1, 0))
    lane = lax.broadcasted_iota(jnp.int32, (1, 128), 1)
    logits = jnp.where(lane < 8, nn(mixed[...], o_full[0, :, cut:]), -1e30)
    weight = jnp.exp(logits - jnp.max(logits, axis=-1, keepdims=True))
    chance[...] = weight / jnp.sum(weight, axis=-1, keepdims=True)
    turned = jnp.where(choices(routes, square), chance[...], 0.0).T[:8]
    high = low(turned)
    gates[...] = jnp.concatenate([high, low(turned - wide_float(high))], axis=0)
    start_tokens(token_gathers, (0, 2))
    for source, target in (
        (mixed, mixed_out), (mod, mod_out), (attn_in, attn_in_out), (qkv, qkv_out), (probs, probs_out),
        (attn_low, attn_low_out), (attn_proj, attn_proj_out), (middle, middle_out), (chance, chance_out),
    ):
        leave(source, target)

    for o in others:
        n = chip(*spot(*o))
        remote(s_got.at[c, n], s_got.at[c, n], b_send.at[0], b_recv.at[n], sibling).wait_recv()
    go(remote(s_got.at[c], s_got.at[c], b_pair.at[0], b_pair.at[1], sibling))
    load.wait()
    more_tokens(0, token_gathers)
    for i, o in enumerate([(0, 0, 0)] + [o for step in (0, 1, 3, 2) for o in plane if o[1] == step]):
        _, sz, sx = spot(*o)
        source = 2 * sz + sx
        block = w1.at[:, strip(2 * source + c), :]
        if i:
            remote(block, block, a_send.at[0], a_recv.at[source], sibling).wait_recv()
        go(remote(block, block, a_pair_send.at[i], a_pair.at[source], sibling))
    more_tokens(1, token_gathers)
    remote(s_got.at[1 - c], s_got.at[1 - c], b_pair.at[0], b_pair.at[1], sibling).wait_recv()
    for n in range(32):
        s_rows[n * rows : (n + 1) * rows, :] = wide_float(s_got[n % 2, n // 2])[:rows]
    w1s[...] = low(s_rows[...])
    for copy in started:
        copy.wait_send()
    for source in range(8):
        block = w1.at[:, strip(2 * source + 1 - c), :]
        remote(block, block, a_send.at[0], a_pair.at[source], sibling).wait_recv()
    for copy in keep:
        copy.wait()


def gelu_both(h):
    root = math.sqrt(2.0 / math.pi)
    square = h * h
    t = jnp.tanh(h * (root + (root * 0.044715) * square))
    half = 0.5 * (1.0 + t)
    slope = half + (0.5 * h) * (1.0 - t * t) * (root + (3.0 * root * 0.044715) * square)
    return h * half, slope


def ffn_chunk(xt, gt, w1, w2, gate, row):
    a, d = gelu_both(nn(xt, w1))
    gi = nt(gt, w2)
    product = None
    if gate is not None:
        product = nt(row, (a * gi).astype(jnp.bfloat16))
        a, d = a * gate, d * gate
    a = a.astype(jnp.bfloat16)
    p = (gi * d).astype(jnp.bfloat16)
    return a, p, nn(a, w2), nt(p, w1), product


def ffn_shared(slots, X, G, w1s, w2s, act_s, pre_s, sums, sums_back):
    toks = X.shape[1]
    xt = jnp.concatenate([X[n] for n in slots], axis=0)
    gt = jnp.concatenate([G[n] for n in slots], axis=0)
    a, p, total, total_back, _ = ffn_chunk(xt, gt, w1s[...], w2s[...], None, None)
    for i, n in enumerate(slots):
        act_s[n] = a[i * toks : (i + 1) * toks]
        pre_s[n] = p[i * toks : (i + 1) * toks]
    sums[...] = total
    sums_back[...] = total_back


def ffn_experts(low, high, slots, X, G, gates, w1, w2, act, pre, sums, sums_back, gc):
    experts, toks, wide = w1.shape[0], X.shape[1], w1.shape[2]
    first = lax.axis_index("gx") * experts
    xt = jnp.concatenate([X[n] for n in slots], axis=0)
    gt = jnp.concatenate([G[n] for n in slots], axis=0)

    def expert(e, product):
        kind = lax.broadcasted_iota(jnp.int32, (16, 128), 0)
        spread = ((kind == first + e) | (kind == first + e + 8)).astype(jnp.bfloat16)
        gate = jnp.concatenate([tn(gates[n], spread) for n in slots], axis=0)
        gate = jnp.concatenate([gate] * (wide // 128), axis=1)
        row = (lax.broadcasted_iota(jnp.int32, (8, wide), 0) == first + e).astype(jnp.bfloat16)
        a, p, total, total_back, more = ffn_chunk(xt, gt, w1[e], w2[e], gate, row)
        for i, n in enumerate(slots):
            act[e, n] = a[i * toks : (i + 1) * toks]
            pre[e, n] = p[i * toks : (i + 1) * toks]
        sums[...] += total
        sums_back[...] += total_back
        return product + more

    product = lax.fori_loop(low, high, expert, jnp.zeros((8, len(slots) * toks), jnp.float32))
    for i, n in enumerate(slots):
        part = product[:, i * toks : (i + 1) * toks]
        gc[n] = part if low == 0 else gc[n] + part


def block_part(refs, outs, kept, sems, go_on, plan, *locals_):
    w2_in, w2s_in = refs
    (sum_branch, sum_back, sum_gc, near1, far1, out1s, out2, out2s) = outs
    (w1, w1s, X, G, gt, w2, w2s, r_branch, r_back, r_gc, from1, from1s, from2, from2s) = kept
    (l_sem, o_sem, send, recv, t_send, t_recv, w_send, w_recv, h_send, h_recv) = sems
    (act, pre, act_s, pre_s, p_branch, p_back, p_gc) = locals_
    experts = w1.shape[0]
    counts = []

    def tools():
        here = place()
        scatters = []
        for i, (part, got, y_first) in enumerate(((p_branch, r_branch, False), (p_back, r_back, True), (p_gc, r_gc, False))):
            take = functools.partial(lambda ref, n: ref.at[n], part)
            land = functools.partial(lambda ref, n: ref.at[n], got)
            scatters.append(Scatter(here, y_first, take, land, send.at[i], recv.at[i]))

        return scatters

    def tiles(tile_sum, tile_back):
        here = y, z, x, c = place()
        spot = lambda dy, dz, dx: (1 - y if dy else y, along(z, dz), 1 - x if dx else x)
        sibling = device(y, z, x, 1 - c)
        local, gathers, scatters = [], go_on(), tools()
        half2, half2s = w2_in.shape[1], w2s_in.shape[0]
        own2_at = w2.at[:, pl.ds(pl.multiple_of(half2 * c, 16), half2), :]
        own2s_at = w2s.at[pl.ds(pl.multiple_of(half2s * c, 16), half2s), :]
        for i, (source, target) in enumerate(((w2_in, own2_at), (w2s_in, own2s_at))):
            local.append(pltpu.make_async_copy(source, target, l_sem.at[3 + i]))
        for i, (source, target) in enumerate(((w2_in, own2_at), (w2s_in, own2s_at))):
            local.append(remote(source, target, w_send.at[i], w_recv.at[i], sibling))
        for copy in local:
            copy.start()

        def tile(step, part):
            slots = [chip(*spot(dy, step, dx)) for dy in (0, 1) for dx in (0, 1)]
            if part == 0:
                ffn_shared(slots, X, G, w1s, w2s, act_s, pre_s, tile_sum, tile_back)
            low, high = (0, experts // 2) if part == 0 else (experts // 2, experts)
            ffn_experts(low, high, slots, X, G, gt, w1, w2, act, pre, tile_sum, tile_back, p_gc)
            if part == 1:
                toks = X.shape[1]
                for i, n in enumerate(slots):
                    at = slice(i * toks, (i + 1) * toks)
                    p_branch[n] = tile_sum[at, :].astype(jnp.bfloat16)
                    p_back[n] = tile_back[at, :].astype(jnp.bfloat16)

        def back_first(step):
            for scatter in scatters:
                scatter.first(step)

        def back_one(b, step):
            for scatter in scatters:
                scatter.one(b, step)

        def back_two(step):
            for scatter in scatters:
                scatter.two(step)

        gather_second(gathers, 1)
        gather_third(gathers, 0)
        for copy in local:
            copy.wait()
        tile(0, 0)
        gather_line(gathers, 2)
        tile(0, 1)
        gather_third(gathers, 1)
        tile(1, 0)
        gather_second(gathers, 2)
        tile(1, 1)
        gather_line(gathers, 3)
        gather_third(gathers, 2)
        tile(2, 0)
        gather_second(gathers, 3)
        tile(2, 1)
        back_first(2)
        gather_third(gathers, 3)
        tile(3, 0)

        back_one(1, 2)
        tile(3, 1)
        for gather in gathers:
            gather.finish()
        counts.extend(len(scatter.started) for scatter in scatters)

    def weights(own1s, own2, own2s, d1, d1s, d2, d2s):
        here = y, z, x, c = place()
        spot = lambda dy, dz, dx: (1 - y if dy else y, along(z, dz), 1 - x if dx else x)
        sibling = device(y, z, x, 1 - c)
        scatters = tools()
        for scatter, count in zip(scatters, counts):
            scatter.started = [None] * count

        def back_first(step):
            for scatter in scatters:
                scatter.first(step)

        def back_one(b, step):
            for scatter in scatters:
                scatter.one(b, step)

        def back_two(step):
            for scatter in scatters:
                scatter.two(step)

        flat = lambda value: value.reshape(value.shape[0] * value.shape[1], value.shape[2])
        twins = [None] * (2 * experts)
        leaving, homeward, left = [], [], []

        def leave(source, target):
            leaving.append(pltpu.make_async_copy(source, target, o_sem.at[len(leaving)]))
            leaving[-1].start()


        def weight(e):
            d1[e % 2] = tn(flat(X[...]), flat(pre[e])).astype(jnp.bfloat16).reshape(d1.shape[1:])
            d2[e % 2] = tn(flat(act[e]), flat(G[...])).astype(jnp.bfloat16).reshape(d2.shape[1:])
            for i, (part, got) in enumerate(((d1.at[e % 2, :, 1 - c], from1.at[e]), (d2.at[e % 2, 1 - c], from2.at[e]))):
                twins[2 * e + i] = remote(part, got, t_send.at[2 * e + i], t_recv.at[2 * e + i], sibling)
                twins[2 * e + i].start()

        def home(e):
            twins[2 * e].wait()
            from1[e] = (d1[e % 2, :, c].astype(jnp.float32) + from1[e].astype(jnp.float32)).astype(jnp.bfloat16)
            twins[2 * e + 1].wait()
            if e > 1:
                left[e - 2].wait()
            own2[e % 2] = d2[e % 2, c].astype(jnp.float32) + from2[e].astype(jnp.float32)
            left.append(pltpu.make_async_copy(own2.at[e % 2], out2.at[e], l_sem.at[e]))
            left[e].start()
            for i in range(4):
                leave(from1.at[e, 2 * i + 1 - x], far1.at[e, i])
            leave(from1.at[e, 2 * z + x], near1.at[e, z])

        def along_home(e):
            for step in LINE:
                at = along(z, step)
                sent = remote(from1.at[e, 2 * at + x], near1.at[e, z], h_send.at[e, step], h_recv.at[e, z], device(y, at, x, c))
                sent.start()
                homeward.append(sent)


        back_first(3)
        back_one(0, 2)
        back_two(2)
        weight(0)
        back_one(1, 3)
        back_first(1)
        weight(1)
        home(0)
        back_one(0, 3)
        back_two(3)
        home(1)
        back_one(1, 1)
        back_first(0)
        weight(2)
        back_one(0, 1)
        along_home(0)
        along_home(1)
        back_two(1)
        home(2)
        back_one(1, 0)
        along_home(2)
        weight(3)
        d1s[...] = tn(flat(X[...]), flat(pre_s[...])).reshape(d1s.shape)
        d2s[...] = tn(flat(act_s[...]), flat(G[...])).astype(jnp.bfloat16).reshape(d2s.shape)
        twin1s = remote(d1s.at[:, 1 - c], from1s, t_send.at[2 * experts], t_recv.at[2 * experts], sibling)
        twin2s = remote(d2s.at[1 - c], from2s, t_send.at[2 * experts + 1], t_recv.at[2 * experts + 1], sibling)
        twin1s.start()
        twin2s.start()
        home(3)
        along_home(3)
        back_one(0, 0)
        twin1s.wait()
        total = d1s[:, c] + from1s[...]
        own1s[...] = low(jnp.concatenate([total, jnp.zeros((16, own1s.shape[1] - total.shape[1], total.shape[2]), jnp.float32)], axis=1))
        twin2s.wait()
        own2s[...] = d2s[c].astype(jnp.float32) + from2s[...].astype(jnp.float32)
        leave(own1s, out1s)
        leave(own2s, out2s)
        back_two(0)
        sum_branch[...] = scatters[0].total()
        sum_back[...] = scatters[1].total()
        sum_gc[...] = scatters[2].total()
        for copy in leaving:
            copy.wait()
        for copy in left[-2:]:
            copy.wait()
        for sent in homeward:
            sent.wait_send()
        for e in range(experts):
            for step in LINE:
                block = near1.at[e, along(z, step)]
                remote(block, block, h_send.at[0, 0], h_recv.at[e, along(z, step)], sibling).wait_recv()
        for scatter in scatters:
            scatter.finish()


    pl.run_scoped(tiles, *[VMEM(*a) for a in plan[0]])
    pl.run_scoped(weights, *[VMEM(*a) for a in plan[1]])


def joint_kernel(plan, *refs):
    refs = list(refs)

    def take(count):
        taken, refs[:count] = refs[:count], []
        return taken

    front_refs, block_refs = take(12), take(2)
    front_outs, block_outs = take(11), take(8)
    w1, w1s = take(2)
    mod, mixed, grad, gates = take(4)
    front_kept, (X, G, gt), block_kept = take(9), take(3), take(9)
    front_sems, block_sems, (g_send, g_recv) = take(20), take(10), take(2)
    counts = []

    def token_gathers():
        gathers = []
        for i, (block, full, y_first) in enumerate(((mixed, X, True), (grad, G, False), (gates, gt, True))):
            slot = functools.partial(lambda full, n: full.at[n], full)
            gathers.append(Gather(place(), y_first, block, slot, g_send.at[i], g_recv.at[i]))
        return gathers

    def start_tokens(gathers, which):
        gathers = token_gathers() if gathers is None else gathers
        gather_start([gathers[i] for i in which])
        y, z, x, c = place()
        for i in which:
            block, full = ((mixed, X), (grad, G), (gates, gt))[i]
            full[chip(y, z, x)] = block[...]
        return gathers

    def more_tokens(turn, gathers):
        if turn == 0:
            gather_second(gathers, 0)
        else:
            gather_line(gathers, 1)
            counts.extend(len(gather.started) for gather in gathers)

    def go_on():
        gathers = token_gathers()
        for gather, count in zip(gathers, counts):
            gather.started = [None] * count
        return gathers

    kept = (w1, w1s, mod, mixed, grad, gates, *front_kept)
    pl.run_scoped(
        functools.partial(front_part, front_refs, front_outs, kept, front_sems, start_tokens, more_tokens), *[VMEM(*a) for a in plan[0]]
    )
    kept = (w1, w1s, X, G, gt, *block_kept)
    pl.run_scoped(functools.partial(block_part, block_refs, block_outs, kept, block_sems, go_on, plan[2:]), *[VMEM(*a) for a in plan[1]])


def joint(lengths, timesteps, tokens, cotangent, routes, w_ada, w_qkv, w_out, w_router, w_fc1, e_fc1, e_fc2, w_fc2):
    rows, model = w_out.shape
    toks = tokens.shape[0]
    waves = frequencies(model).reshape(2, 4, 4 * rows).transpose(1, 0, 2).reshape(4, 8 * rows)
    waves = np.pad(waves, ((0, 0), (0, -8 * rows % 128)))
    lanes = waves.shape[1]
    ff = w_fc1.shape[1]
    slim, wide = ff // 16, ff // 8
    experts, depth, _ = e_fc1.shape
    bf, f32 = jnp.bfloat16, jnp.float32
    shape = jax.ShapeDtypeStruct
    q_half, o_half, a_half = w_qkv.shape[1] // 2, w_out.shape[1] // 2 + 128, w_ada.shape[1] // 2
    saved = (((toks, model), bf), ((toks, 3 * model), bf), ((HEADS, toks, toks), f32), ((toks, model), bf), ((toks, model), f32),
             ((toks, model), f32), ((toks, 128), f32))
    front_plan = saved + (
        ((128, 128), f32), ((4, 8, lanes), f32), ((16, 32, slim), bf), ((model, slim), f32),
        ((2, rows, q_half), f32), ((2, rows, o_half), f32), ((2, rows, a_half), f32), ((2 * rows, q_half), bf), ((2 * rows, o_half), bf),
        ((4, 8, a_half // 2), f32),
    )
    blocks = lambda *dims: ((16, toks) + dims, bf)
    block_plan = (
        ((experts, 16, toks, wide), bf), ((experts, 16, toks, wide), bf), blocks(slim), blocks(slim), blocks(model), blocks(model),
        ((16, 8, 128), f32),
    )
    tiles_plan = (((4 * toks, model), f32), ((4 * toks, model), f32))
    weights_plan = (
        ((16, 32, slim), bf), ((2, wide // 2, model), f32), ((slim // 2, model), f32), ((2, 8, 2, depth, wide), bf), ((16, 2, rows, slim), f32),
        ((2, 2, wide // 2, model), bf), ((2, slim // 2, model), bf),
    )
    whole = (((2, model, q_half), bf), ((2, model, o_half), bf), ((2, 8, a_half), f32), ((toks, model), bf)) + saved
    sums = [((toks, model), f32), ((toks, model), f32), ((8, 128), f32)]
    grads = [((experts, 4, depth, wide), bf), ((experts, 4, depth, wide), bf), ((16, 32, slim), bf), ((experts, wide // 2, model), f32),
             ((slim // 2, model), f32)]
    outs = list(whole) + sums + grads
    return pl.pallas_call(
        functools.partial(joint_kernel, (front_plan, block_plan, tiles_plan, weights_plan)),
        out_shape=[shape(*a) for a in outs],
        in_specs=[pl.BlockSpec(memory_space=pltpu.SMEM)] * 2
        + [pl.BlockSpec(memory_space=VMEM)] * 9
        + [pl.BlockSpec(memory_space=ANY)] * 3,
        out_specs=[pl.BlockSpec(memory_space=ANY)] * len(whole)
        + [pl.BlockSpec(memory_space=VMEM)] * 3
        + [pl.BlockSpec(memory_space=ANY)] * 5,
        scratch_shapes=[
            VMEM((experts, model, wide), bf), VMEM((model, slim), bf), VMEM((2, 8, a_half), f32), VMEM((toks, model), bf), VMEM((toks, model), bf),
            VMEM((16, toks), bf),
            VMEM((2, model, q_half), bf), VMEM((2, model, o_half), bf), VMEM((2, 4, 2 * rows, a_half // 2), bf),
            VMEM((2 * rows, q_half), f32), VMEM((2 * rows, o_half), f32), VMEM((2 * rows, a_half), f32),
            VMEM((4, 2, 8, lanes), f32), VMEM((3, 8, a_half // 2), f32), VMEM((2, 16, 32, slim), bf),
            VMEM((16, toks, model), bf), VMEM((16, toks, model), bf), VMEM((16, 16, 128), bf),
            VMEM((experts, wide, model), bf), VMEM((slim, model), bf),
            VMEM((15, toks, model), bf), VMEM((15, toks, model), bf), VMEM((15, 8, 128), f32),
            VMEM((experts, 8, depth, wide), bf), VMEM((16, rows, slim), f32), VMEM((experts, wide // 2, model), bf), VMEM((slim // 2, model), bf),
            DMA((3,)), DMA((3,)), DMA((2, 31)), DMA((2, 16)), DMA((2, 16)), DMA((7,)), DMA((8,)), DMA((8,)), DMA((8,)),
            DMA((15,)), DMA((16,)), DMA((2,)), DMA((1,)), DMA((15,)), DMA((7,)), DMA((4, 2)), DMA((4,)), DMA((4,)), DMA((2, 3)), DMA((2, 4)),
            DMA((7,)), DMA((6 * experts + 2,)), DMA((3, 15)), DMA((3, 15)), DMA((2 * experts + 2,)), DMA((2 * experts + 2,)),
            DMA((2,)), DMA((2,)), DMA((experts, 4)), DMA((experts, 4)),
            DMA((3, 15)), DMA((3, 16)),
        ],
        compiler_params=pltpu.CompilerParams(collective_id=1, has_side_effects=True, vmem_limit_bytes=62 << 20),
        name="joint",
    )(lengths, timesteps, tokens, cotangent, routes.T, waves, w_ada, w_qkv, w_out, w_router.T, w_fc1, e_fc1, e_fc2, w_fc2)


def rear_kernel(lengths, steps, waves, *refs):
    incoming, refs = refs[:15], refs[15:]
    (qkv_in, out_in, part1, part1s, output, d_tokens, d_ada, d_qkv, d_out, d_router, own1, own1s), refs = refs[:12], refs[12:]
    (sum_branch, sum_back, sum_gc, tokens, cotangent, routes, mod, mixed, attn_in, qkv, probs, attn_low, attn_proj, middle, chance), refs = refs[:15], refs[15:]
    (square, slice_own, q_w, o_w, grad_attn, grad_qkv, grad_mid, o_mine, o_got, q_mine, q_got, part_o, part_a, part_b, got_o, got_a, got_b, fin, mod_tile, all_mod, l_sem, s_send, s_recv, send, recv, g_send, g_recv, g_pair, f_send, f_recv, a_send, a_recv, b_send, b_recv, i_sem) = refs
    here = y, z, x, c = place()
    me = chip(y, z, x)
    sibling = device(y, z, x, 1 - c)
    others = [(dy, dz, dx) for dy in (0, 1) for dz in (0, 1, 2, 3) for dx in (0, 1) if (dy, dz, dx) != (0, 0, 0)]
    spot = lambda dy, dz, dx: (1 - y if dy else y, along(z, dz), 1 - x if dx else x)
    held = (sum_branch, sum_back, sum_gc, tokens, cotangent, routes, mod, mixed, attn_in, qkv, probs, attn_low, attn_proj, middle, chance)
    loads = [pltpu.make_async_copy(a, b, i_sem.at[i]) for i, (a, b) in enumerate(zip(incoming, held))]
    local = [pltpu.make_async_copy(qkv_in, q_w, l_sem.at[0]), pltpu.make_async_copy(out_in, o_w, l_sem.at[1])]
    for copy in loads + local:
        copy.start()
    meet([device(*spot(*o), c) for o in others] + [sibling])
    started = []

    def go(copy):
        copy.start()
        started.append(copy)

    home = [pltpu.make_async_copy(part1s.at[me], slice_own, l_sem.at[3])]
    home[0].start()
    for step in (0, 1, 2, 3):
        at = along(z, step)
        go(remote(part1.at[:, at], own1.at[:, z], a_send.at[step], a_recv.at[z], device(y, at, 1 - x, c)))
    for i, o in enumerate(others):
        go(remote(part1s.at[chip(*spot(*o))], own1s.at[me], b_send.at[i], b_recv.at[me], device(*spot(*o), c)))

    for copy in loads:
        copy.wait()
    item = item_mask(lengths, tokens.shape)
    first = ~item
    model = item.shape[1]
    cut = model // 2
    modulation = functools.partial(own_modulation, here, mod, item)
    rows16 = {}

    def per_item(part, value):
        for i, mask in enumerate((first, ~first)):
            rows16[2 * part + i] = jnp.sum(jnp.where(mask, value, 0.0), axis=0, keepdims=True)

    out_grad = wide_float(cotangent[...])
    branch = sum_branch[...]
    output[...] = low(middle[...] + modulation(1, 2) * branch)
    per_item(5, out_grad * branch)
    chosen = choices(routes, square)
    turned = jnp.concatenate([sum_gc[...], jnp.zeros((120, 128), jnp.float32)], axis=0).T
    grad_chance = jnp.where(chosen, turned, 0.0)
    share = chance[...]
    grad_logits = low(share * (grad_chance - jnp.sum(grad_chance * share, axis=-1, keepdims=True)))
    term_router = tn(mixed[...], grad_logits)
    for copy in local + home:
        copy.wait()
    home = [pltpu.make_async_copy(slice_own, own1s.at[me], l_sem.at[3])]
    home[0].start()
    grad_mixed = sum_back[...] + nt(grad_logits, o_w[0, :, cut:])
    normed, scale = norm(middle[...])
    per_item(3, grad_mixed)
    per_item(4, grad_mixed * normed)
    grad_mid[...] = out_grad + norm_back(grad_mixed * (1.0 + modulation(1, 1)), normed, scale)
    per_item(2, grad_mid[...] * attn_proj[...])
    grad_proj = low(grad_mid[...] * modulation(0, 2))
    for h in (0, 1):
        term = jnp.concatenate([tn(attn_low[...], grad_proj[:, h * cut : (h + 1) * cut]), term_router], axis=1)
        o_mine[h] = low(term)
    swap_o = remote(o_mine.at[1 - c], o_got, s_send.at[0], s_recv.at[0], sibling)
    swap_o.start()
    grad_attn[...] = low(nt(grad_proj[:, :cut], o_w[0, :, :cut]) + nt(grad_proj[:, cut:], o_w[1, :, :cut]))

    rows = o_got.shape[0] // 16
    scatters = []
    for i, (part, got, y_first) in enumerate(((part_o, got_o, False), (part_a, got_a, True), (part_b, got_b, False))):
        take = functools.partial(lambda ref, n: ref.at[n], part)
        land = functools.partial(lambda ref, n: ref.at[n], got)
        scatters.append(Scatter(here, y_first, take, land, send.at[i], recv.at[i], relay=True))

    swap_o.wait()
    for n in range(16):
        at = slice(n * rows, (n + 1) * rows)
        part_o[n] = low(wide_float(o_mine[c, at, :]) + wide_float(o_got[at, :]))
    for step in (3, 2, 1, 0):
        scatters[0].first(step)

    left, sides = head_lanes()
    for pair in range(model // 128):
        at = slice(128 * pair, 128 * (pair + 1))
        q, key, value = [qkv[:, base + 128 * pair : base + 128 * (pair + 1)] for base in (0, model, 2 * model)]
        ga = grad_attn[:, at]
        outs = []
        for j, side in enumerate(sides):
            prob = probs[2 * pair + j]
            grad_probs = nt(ga * side, value)
            grad_scores = low(prob * (grad_probs - jnp.sum(grad_probs * prob, axis=-1, keepdims=True)))
            outs.append((nn(grad_scores, key) * 0.125, tn(grad_scores, q) * 0.125, tn(low(prob), ga)))
        for base, one, two in zip((0, model, 2 * model), *outs):
            grad_qkv[:, base + 128 * pair : base + 128 * (pair + 1)] = low(jnp.where(left, one, two))

    third = q_w.shape[2]
    for h in (0, 1):
        q_mine[h] = low(tn(attn_in[...], grad_qkv[:, h * third : (h + 1) * third]))
    swap_q = {}
    for step in (3, 2, 1, 0):
        for side in (0, 1):
            at = pl.ds(pl.multiple_of(2 * rows * (4 * side + along(z, step)), 16), 2 * rows)
            i = 1 + 2 * step + side
            swap_q[step, side] = remote(q_mine.at[1 - c, at, :], q_got.at[at, :], s_send.at[i], s_recv.at[i], sibling)
            swap_q[step, side].start()
    grad_in = nt(grad_qkv[:, :third], q_w[0]) + nt(grad_qkv[:, third:], q_w[1])
    normed, scale = norm(wide_float(tokens[...]))
    per_item(0, grad_in)
    per_item(1, grad_in * normed)
    d_tokens[...] = grad_mid[...] + norm_back(grad_in * (1.0 + modulation(0, 1)), normed, scale)
    column = lax.broadcasted_iota(jnp.int32, (8, model), 1)
    last = jnp.concatenate([rows16[8 + i] for i in range(4)] + [jnp.zeros((4, model), jnp.float32)], axis=0)
    last = last + conditions(steps, (8, model), 4, column, model // 2, waves[...])
    mod_tile[...] = low(jnp.concatenate([rows16[i] for i in range(8)] + [last], axis=0))

    slot = lambda n: all_mod.at[n, c]
    spread = Gather(here, False, mod_tile, slot, g_send, g_recv, g_pair)
    all_mod[me, c] = mod_tile[...]
    gather_start([spread])
    edge = part_a.shape[2]

    def fold(step):
        for side in (0, 1):
            swap_q[step, side].wait()
            first_n = 8 * side + 2 * along(z, step)
            for n in (first_n, first_n + 1):
                at = pl.ds(pl.multiple_of(rows * n, 16), rows)
                total = low(wide_float(q_mine[c, at, :]) + wide_float(q_got[at, :]))
                part_a[n] = total[:, :edge]
                part_b[n] = total[:, edge:]
        for scatter in scatters[1:]:
            scatter.first(step)

    fold(3)
    fold(2)

    def turn(at):
        if at == 1:
            spread.second(0)
            for step in LINE:
                gather_line([spread], step)
        elif at == 2:
            for step in LINE:
                spread.second(step)
        elif at == 3:
            for step in (0,) + LINE:
                spread.third(step)
            spread.finish()
            flat = all_mod[...].reshape(32 * 16, model)
            share_rows = rows // 2
            own = (2 * me + c) * share_rows
            source = lax.broadcasted_iota(jnp.int32, (model, 128), 0)
            lane = lax.broadcasted_iota(jnp.int32, (model, 128), 1)
            own_columns = nn(flat, low(wide_float((source == own + lane) & (lane < share_rows))))
            row = lax.broadcasted_iota(jnp.int32, (512, 128), 0) % 16
            own_columns = jnp.where((row >= 12) & (row < 14), own_columns, 0.0)
            for part in range(6):
                lhs = low(pltpu.roll(own_columns, 512 + 2 * part - 12, 0))
                d_ada[:, part * model : (part + 1) * model] = tn(lhs, flat)[:share_rows]

    scatter_all(scatters, fold, turn)
    fin[c] = jnp.concatenate([scatters[1].total(), scatters[2].total(), scatters[0].total()], axis=1)
    half = rows // 2
    mine = pl.ds(pl.multiple_of(half * c, 8), half)
    theirs = pl.ds(pl.multiple_of(half * (1 - c), 8), half)
    swap = remote(fin.at[c, theirs, :], fin.at[c, theirs, :], f_send, f_recv, sibling)
    swap.start()

    for at in range(4):
        remote(own1.at[:, at], own1.at[:, at], a_send.at[0], a_recv.at[at], sibling).wait_recv()
    for copy in home:
        copy.wait()
    for i, o in enumerate(others):
        n = chip(*spot(*o))
        remote(own1s.at[n], own1s.at[n], b_send.at[i], b_recv.at[n], sibling).wait_recv()
    for scatter in scatters:
        scatter.finish()
    for copy in started:
        copy.wait_send()
    swap.wait_send()
    remote(fin.at[1 - c, mine, :], fin.at[1 - c, mine, :], f_send, f_recv, sibling).wait_recv()
    for h in (0, 1):
        d_qkv[:, h * third : (h + 1) * third] = fin[h, mine, :third]
        d_out[:, h * cut : (h + 1) * cut] = fin[h, mine, third : third + cut]
    d_router[0:half, :] = fin[0, mine, third + cut :]
    d_router[half:, :] = jnp.zeros((128 - half, 128), jnp.float32)


def rear(lengths, timesteps, sums, tokens, cotangent, routes, saved, qkv_w, out_w, part1, part1s):
    bf, f32 = jnp.bfloat16, jnp.float32
    toks, model = tokens.shape
    rows = model // 16
    q_half, o_half = qkv_w.shape[2], out_w.shape[2]
    a_half = model
    incoming = (*sums, tokens, cotangent, routes.T, *saved)
    shape = jax.ShapeDtypeStruct
    return pl.pallas_call(
        rear_kernel,
        out_shape=[
            shape((toks, model), bf),
            shape((toks, model), f32),
            shape((rows // 2, 6 * model), f32),
            shape((rows // 2, 2 * q_half), f32),
            shape((rows // 2, model), f32),
            shape((128, 128), f32),
            shape(part1.shape, bf),
            shape(part1s.shape, bf),
        ],
        in_specs=[pl.BlockSpec(memory_space=pltpu.SMEM)] * 2
        + [pl.BlockSpec(memory_space=VMEM)]
        + [pl.BlockSpec(memory_space=ANY)] * 19,
        out_specs=[pl.BlockSpec(memory_space=VMEM)] * 6 + [pl.BlockSpec(memory_space=ANY)] * 2,
        scratch_shapes=[VMEM(a.shape, a.dtype) for a in incoming]
        + [
            VMEM((128, 128), f32), VMEM(part1s.shape[1:], bf), VMEM(qkv_w.shape, bf), VMEM(out_w.shape, bf),
            VMEM((toks, model), bf), VMEM((toks, 3 * model), bf), VMEM((toks, model), f32),
            VMEM((2, model, o_half), bf), VMEM((model, o_half), bf),
            VMEM((2, model, q_half), bf), VMEM((model, q_half), bf),
            VMEM((16, rows, o_half), bf), VMEM((16, rows, a_half), bf), VMEM((16, rows, q_half - a_half), bf),
            VMEM((15, rows, o_half), bf), VMEM((15, rows, a_half), bf), VMEM((15, rows, q_half - a_half), bf),
            VMEM((2, rows, q_half + o_half), f32), VMEM((16, model), bf), VMEM((16, 2, 16, model), bf),
            DMA((4,)), DMA((9,)), DMA((9,)), DMA((3, 15)), DMA((3, 15)), DMA((31,)), DMA((16,)), DMA((16,)), DMA, DMA,
            DMA((4,)), DMA((4,)), DMA((15,)), DMA((16,)), DMA((16,)),
        ],
        compiler_params=pltpu.CompilerParams(collective_id=3, has_side_effects=True, vmem_limit_bytes=62 << 20),
        name="rear",
    )(lengths, timesteps, frequencies(model)[None], *incoming, qkv_w, out_w, part1, part1s)


def finish_kernel(*refs):
    count = (len(refs) - 3) // 3
    inputs, outputs, staged = refs[:count], refs[count : 2 * count - 1], refs[2 * count - 1 : 3 * count - 1]
    e1, fc1, sem_in, sem = refs[3 * count - 1 :]
    loads = [pltpu.make_async_copy(a, b, sem_in.at[i]) for i, (a, b) in enumerate(zip(inputs, staged))]
    stores = []

    def store(source, target):
        stores.append(pltpu.make_async_copy(source, target, sem.at[len(stores)]))
        stores[-1].start()

    for copy in loads:
        copy.start()
    near, far, slices, router = staged[:4]
    x = place()[2]
    wide = near.shape[3]
    loads[0].wait()
    loads[1].wait()
    for e in range(near.shape[0]):
        for at in range(near.shape[1]):
            e1[e, :, pl.ds(pl.multiple_of(wide * (2 * at + x), 128), wide)] = wide_float(near[e, at])
            e1[e, :, pl.ds(pl.multiple_of(wide * (2 * at + 1 - x), 128), wide)] = wide_float(far[e, at])
        store(e1.at[e], outputs[0].at[e])
    for load, source, target in zip(loads[4:], staged[4:], outputs[3:]):
        load.wait()
        store(source, target)
    loads[2].wait()
    loads[3].wait()
    rows, slim = fc1.shape[0], slices.shape[2]
    for n in range(slices.shape[0] // 2):
        pair = [wide_float(slices[2 * n + i])[:rows] for i in (0, 1)]
        fc1[:, 2 * n * slim : 2 * (n + 1) * slim] = jnp.concatenate(pair, axis=1)
    store(fc1, outputs[1])
    outputs[2][...] = router[...].T[: outputs[2].shape[0], : outputs[2].shape[1]]
    for copy in stores:
        copy.wait()


def finish(near1, far1, own1s, d_router, *others):
    f32 = jnp.float32
    experts, _, depth, wide = near1.shape
    rows = depth // 2
    e1, fc1 = (experts, depth, 8 * wide), (rows, own1s.shape[0] * own1s.shape[2])
    shape = jax.ShapeDtypeStruct
    inputs = (near1, far1, own1s, d_router, *others)
    result = pl.pallas_call(
        finish_kernel,
        out_shape=[shape(e1, f32), shape(fc1, f32), shape((8, rows), f32)] + [shape(a.shape, a.dtype) for a in others],
        in_specs=[pl.BlockSpec(memory_space=ANY)] * len(inputs),
        out_specs=[pl.BlockSpec(memory_space=ANY)] * 2
        + [pl.BlockSpec(memory_space=VMEM)]
        + [pl.BlockSpec(memory_space=ANY)] * len(others),
        scratch_shapes=[VMEM(a.shape, a.dtype) for a in inputs]
        + [VMEM(e1, f32), VMEM(fc1, f32), DMA((len(inputs),)), DMA((8 + len(others),))],
        compiler_params=pltpu.CompilerParams(vmem_limit_bytes=62 << 20),
        name="finish",
    )(*inputs)
    return result[0], result[1], result[2].T, *result[3:]


def layer_norm(values):
    average = jnp.mean(values, axis=-1, keepdims=True)
    centred = values - average
    return centred * lax.rsqrt(jnp.mean(centred * centred, axis=-1, keepdims=True) + layer_epsilon)


def modulate(values, shift_by, scale_by):
    return layer_norm(values) * (1.0 + scale_by) + shift_by


def sinusoid(timesteps, model_width):
    half_width = model_width // 2
    frequency = jnp.exp(-math.log(10000.0) * jnp.arange(half_width, dtype=jnp.float32) / half_width)
    angles = timesteps.astype(jnp.float32)[:, None] * frequency[None, :]
    return jnp.concatenate([jnp.cos(angles), jnp.sin(angles)], axis=1)


def membership(lengths, tok_count):
    bounds = jnp.cumsum(lengths)[:-1]
    position = jnp.arange(tok_count, dtype=jnp.int32)
    item_of = jnp.sum((position[:, None] >= bounds[None, :]).astype(jnp.int32), axis=1)
    item_ids = jnp.arange(lengths.shape[0], dtype=jnp.int32)
    return ((item_of[:, None] == item_ids[None, :]).astype(jnp.float32), item_of)


def slot_index(routes, expert_count, capacity):
    flat_routes = routes.reshape(-1)
    expert_hot = (
        flat_routes[:, None] == jnp.arange(expert_count, dtype=jnp.int32)[None, :]
    ).astype(jnp.int32)
    before = jnp.cumsum(expert_hot, axis=0) - expert_hot
    rank_in = jnp.sum(before * expert_hot, axis=1)
    return (flat_routes * capacity + rank_in).reshape(routes.shape)


def dot_float(left_side, right_side):
    return jnp.dot(left_side, right_side, preferred_element_type=jnp.float32)


def dot_rows(left_side, right_side):
    return jnp.einsum("td,tf->df", left_side, right_side, preferred_element_type=jnp.float32)


def dot_cols(left_side, right_side):
    return jnp.einsum("tf,df->td", left_side, right_side, preferred_element_type=jnp.float32)


def dot_halves(left_side, halves):
    return jnp.concatenate([dot_float(left_side, halves[0]), dot_float(left_side, halves[1])], axis=1)


def by_slices(
    tokens, timesteps, lengths, routes, cotangent, w_ada, w_qkv, w_out, w_fc1, w_fc2, w_router, e_fc1, e_fc2
):
    (qkv_w, out_w, mod, mixed, attn_in, qkv, probs, attn_low, attn_proj, middle, chance, *sums, near1, far1, part1s, d_e2,
     d_fc2) = joint(
        lengths, timesteps, tokens, cotangent, routes, w_ada, w_qkv, w_out, w_router, w_fc1, e_fc1, e_fc2, w_fc2
    )
    saved = (mod, mixed, attn_in, qkv, probs, attn_low, attn_proj, middle, chance)
    output, d_tokens, d_ada, d_qkv, d_out, d_router, own1, own1s = rear(
        lengths, timesteps, sums, tokens, cotangent, routes, saved, qkv_w, out_w, far1, part1s
    )
    d_e1, d_fc1, d_router, output, d_tokens, d_ada, d_qkv, d_out, d_fc2, d_e2 = finish(
        near1, own1, own1s, d_router, output, d_tokens, d_ada, d_qkv, d_out, d_fc2, d_e2
    )
    return (output, d_tokens, d_ada, d_qkv, d_out, d_fc1, d_fc2, d_router, d_e1, d_e2)


def by_weights(
    tokens,
    timesteps,
    lengths,
    routes,
    cotangent,
    w_ada,
    w_qkv,
    w_out,
    w_fc1,
    w_fc2,
    w_router,
    e_fc1,
    e_fc2,
):
    tok_count, model_width = tokens.shape
    head_count = HEADS
    head_size = model_width // head_count
    expert_count = w_router.shape[1]
    capacity = CAP
    score_scale = head_size ** (-0.5)
    residual = tokens.astype(jnp.float32)
    member, item_of = membership(lengths[0], tok_count)
    ada_full, qkv_full, out_full = (
        lax.all_gather(w_ada, ("gx", "gy"), axis=0, tiled=True),
        lax.all_gather(w_qkv, ("gx", "gy"), axis=0, tiled=True),
        lax.all_gather(w_out, ("gx", "gy"), axis=0, tiled=True),
    )
    condition = jax.nn.silu(sinusoid(timesteps, model_width)).astype(jnp.bfloat16)
    modulation = dot_float(condition, ada_full)
    token_mod = jnp.dot(member, modulation, precision=precise)
    shift_attn, scale_attn, gate_attn, shift_mlp, scale_mlp, gate_mlp = jnp.split(
        token_mod, 6, axis=1
    )
    attn_in = modulate(residual, shift_attn, scale_attn).astype(jnp.bfloat16)
    qkv_low = dot_float(attn_in, qkv_full).astype(jnp.bfloat16)
    queries, key_rows, value_rows = [
        portion.reshape(tok_count, head_count, head_size)
        for portion in jnp.split(qkv_low, 3, axis=1)
    ]
    same_item = item_of[:, None] == item_of[None, :]
    scores = (
        jnp.einsum("qhd,khd->hqk", queries, key_rows, preferred_element_type=jnp.float32)
        * score_scale
    )
    scores = jnp.where(same_item[None], scores, -1e30)
    attn_probs = jax.nn.softmax(scores, axis=-1)
    probs_low = attn_probs.astype(jnp.bfloat16)
    attn_low = jnp.einsum("hqk,khd->qhd", probs_low, value_rows, preferred_element_type=jnp.float32)
    attn_low = attn_low.reshape(tok_count, model_width).astype(jnp.bfloat16)
    attn_proj = dot_float(attn_low, out_full)
    middle = residual + gate_attn * attn_proj
    mixed_in = modulate(middle, shift_mlp, scale_mlp).astype(jnp.bfloat16)
    fc1_full, fc2_full, router_full = (
        lax.all_gather(w_fc1, ("gx", "gy"), axis=0, tiled=True),
        lax.all_gather(w_fc2, ("gx", "gy"), axis=0, tiled=True),
        lax.all_gather(w_router, ("gx", "gy"), axis=0, tiled=True),
    )
    hidden_pre = dot_float(mixed_in, fc1_full)
    hidden = jax.nn.gelu(hidden_pre).astype(jnp.bfloat16)
    shared = dot_float(hidden, fc2_full)
    chance = jax.nn.softmax(dot_float(mixed_in, router_full), axis=-1)
    expert_ids = jnp.arange(expert_count, dtype=jnp.int32)
    chosen = (routes[:, :, None] == expert_ids[None, None, :]).astype(jnp.float32)
    gate_values = jnp.sum(chosen * chance[:, None, :], axis=2)
    slot_of = slot_index(routes, expert_count, capacity)
    slot_ids = jnp.arange(expert_count * capacity, dtype=jnp.int32)
    selector = (slot_of[:, :, None] == slot_ids[None, None, :]).astype(jnp.bfloat16)
    slot_rows = jnp.einsum("tks,td->sd", selector, mixed_in, preferred_element_type=jnp.float32)
    slot_rows = slot_rows.astype(jnp.bfloat16).reshape(expert_count, capacity, model_width)
    owned_rows = lax.all_to_all(slot_rows, "gx", split_axis=0, concat_axis=1, tiled=True)
    expert_in, expert_back = (
        lax.all_gather(e_fc1, "gy", axis=1, tiled=True),
        lax.all_gather(e_fc2, "gy", axis=1, tiled=True),
    )
    inner_pre = jnp.einsum(
        "ecd,edf->ecf", owned_rows, expert_in, preferred_element_type=jnp.float32
    )
    inner_act = jax.nn.gelu(inner_pre).astype(jnp.bfloat16)
    result = jnp.einsum(
        "ecf,efd->ecd", inner_act, expert_back, preferred_element_type=jnp.float32
    ).astype(jnp.bfloat16)
    returned = lax.all_to_all(result, "gx", split_axis=1, concat_axis=0, tiled=True).reshape(
        expert_count * capacity, model_width
    )
    picked = jnp.take(returned, slot_of, axis=0).astype(jnp.float32)
    branch = shared + jnp.sum(gate_values[:, :, None] * picked, axis=1)
    output = (middle + gate_mlp * branch).astype(jnp.bfloat16)
    out_grad = cotangent.astype(jnp.float32)
    grad_gate_mlp = out_grad * branch
    grad_branch = out_grad * gate_mlp
    grad_shared = grad_branch.astype(jnp.bfloat16)
    grad_picked = (gate_values[:, :, None] * grad_branch[:, None, :]).astype(jnp.bfloat16)
    grad_gates = jnp.sum(grad_branch[:, None, :] * picked, axis=2)
    grad_slots = jnp.einsum(
        "tks,tkd->sd", selector, grad_picked, preferred_element_type=jnp.float32
    )
    grad_slots = grad_slots.astype(jnp.bfloat16).reshape(expert_count, capacity, model_width)
    grad_owned = lax.all_to_all(grad_slots, "gx", split_axis=0, concat_axis=1, tiled=True)
    grad_inner = jnp.einsum(
        "ecd,efd->ecf", grad_owned, expert_back, preferred_element_type=jnp.float32
    )
    unused_inner, gelu_expert = jax.vjp(jax.nn.gelu, inner_pre)
    grad_inner_pre = gelu_expert(grad_inner)[0].astype(jnp.bfloat16)
    term_e_out = jnp.einsum(
        "ecf,ecd->efd", inner_act, grad_owned, preferred_element_type=jnp.float32
    )
    term_e_in = jnp.einsum(
        "ecd,ecf->edf", owned_rows, grad_inner_pre, preferred_element_type=jnp.float32
    )
    grad_rows = jnp.einsum(
        "ecf,edf->ecd", grad_inner_pre, expert_in, preferred_element_type=jnp.float32
    )
    grad_returned = (
        lax.all_to_all(
            grad_rows.astype(jnp.bfloat16), "gx", split_axis=1, concat_axis=0, tiled=True
        )
        .astype(grad_rows.dtype)
        .reshape(expert_count * capacity, model_width)
    )
    sum_e_in, sum_e_out = (
        lax.psum_scatter(
            term_e_in.astype(jnp.bfloat16), "gy", scatter_dimension=1, tiled=True
        ).astype(jnp.float32),
        lax.psum_scatter(
            term_e_out.astype(jnp.bfloat16), "gy", scatter_dimension=1, tiled=True
        ).astype(jnp.float32),
    )
    grad_chance = jnp.sum(chosen * grad_gates[:, :, None], axis=1)
    grad_logits = chance * (grad_chance - jnp.sum(grad_chance * chance, axis=-1, keepdims=True))
    grad_logits = grad_logits.astype(jnp.bfloat16)
    grad_hidden = dot_cols(grad_shared, fc2_full)
    unused_shared, gelu_shared = jax.vjp(jax.nn.gelu, hidden_pre)
    grad_hidden_pre = gelu_shared(grad_hidden)[0].astype(jnp.bfloat16)
    term_fc2 = dot_rows(hidden, grad_shared)
    term_fc1 = dot_rows(mixed_in, grad_hidden_pre)
    term_router = dot_rows(mixed_in, grad_logits)
    part_fc1, part_fc2, part_router = (
        lax.psum_scatter(
            term_fc1.astype(jnp.bfloat16), "gx", scatter_dimension=0, tiled=True
        ).astype(jnp.float32),
        lax.psum_scatter(
            term_fc2.astype(jnp.bfloat16), "gx", scatter_dimension=0, tiled=True
        ).astype(jnp.float32),
        lax.psum_scatter(
            term_router.astype(jnp.bfloat16), "gx", scatter_dimension=0, tiled=True
        ).astype(jnp.float32),
    )
    sum_fc1, sum_fc2, sum_router = (
        lax.psum_scatter(
            part_fc1.astype(jnp.bfloat16), "gy", scatter_dimension=0, tiled=True
        ).astype(jnp.float32),
        lax.psum_scatter(
            part_fc2.astype(jnp.bfloat16), "gy", scatter_dimension=0, tiled=True
        ).astype(jnp.float32),
        lax.psum_scatter(
            part_router.astype(jnp.bfloat16), "gy", scatter_dimension=0, tiled=True
        ).astype(jnp.float32),
    )
    grad_mixed = dot_cols(grad_hidden_pre, fc1_full) + dot_cols(grad_logits, router_full)
    grad_mixed = grad_mixed + jnp.sum(jnp.take(grad_returned, slot_of, axis=0), axis=1)
    unused_mix, mix_back = jax.vjp(modulate, middle, shift_mlp, scale_mlp)
    grad_mid_norm, grad_shift_mlp, grad_scale_mlp = mix_back(grad_mixed)
    grad_middle = out_grad + grad_mid_norm
    grad_gate_attn = grad_middle * attn_proj
    grad_proj = (grad_middle * gate_attn).astype(jnp.bfloat16)
    term_out = dot_rows(attn_low, grad_proj)
    grad_attn = (
        dot_cols(grad_proj, out_full).astype(jnp.bfloat16).reshape(tok_count, head_count, head_size)
    )
    grad_probs = jnp.einsum(
        "qhd,khd->hqk", grad_attn, value_rows, preferred_element_type=jnp.float32
    )
    grad_values = jnp.einsum(
        "hqk,qhd->khd", probs_low, grad_attn, preferred_element_type=jnp.float32
    )
    grad_scores = attn_probs * (
        grad_probs - jnp.sum(grad_probs * attn_probs, axis=-1, keepdims=True)
    )
    grad_scores = grad_scores.astype(jnp.bfloat16)
    grad_queries = (
        jnp.einsum("hqk,khd->qhd", grad_scores, key_rows, preferred_element_type=jnp.float32)
        * score_scale
    )
    grad_keys = (
        jnp.einsum("hqk,qhd->khd", grad_scores, queries, preferred_element_type=jnp.float32)
        * score_scale
    )
    grad_qkv = jnp.concatenate(
        [
            grad_queries.reshape(tok_count, model_width),
            grad_keys.reshape(tok_count, model_width),
            grad_values.reshape(tok_count, model_width),
        ],
        axis=1,
    ).astype(jnp.bfloat16)
    term_qkv = dot_rows(attn_in, grad_qkv)
    grad_attn_in = dot_cols(grad_qkv, qkv_full)
    unused_pre, pre_back = jax.vjp(modulate, residual, shift_attn, scale_attn)
    grad_input_norm, grad_shift_attn, grad_scale_attn = pre_back(grad_attn_in)
    d_tokens = grad_middle + grad_input_norm
    grad_token_mod = jnp.concatenate(
        [
            grad_shift_attn,
            grad_scale_attn,
            grad_gate_attn,
            grad_shift_mlp,
            grad_scale_mlp,
            grad_gate_mlp,
        ],
        axis=1,
    )
    grad_modulation = jnp.einsum("ti,tc->ic", member, grad_token_mod, precision=precise).astype(
        jnp.bfloat16
    )
    all_condition, all_modgrad = (
        lax.all_gather(condition, ("gx", "gy"), axis=0, tiled=True),
        lax.all_gather(grad_modulation, ("gx", "gy"), axis=0, tiled=True),
    )
    own_share = model_width // lax.axis_size(("gx", "gy"))
    own_start = lax.axis_index(("gx", "gy")) * own_share
    own_condition = lax.dynamic_slice_in_dim(all_condition, own_start, own_share, 1)
    owned_ada = dot_rows(own_condition, all_modgrad)
    attn_terms = (term_qkv, term_out)
    attn_parts = (
        lax.psum_scatter(
            attn_terms[0].astype(jnp.bfloat16), "gx", scatter_dimension=0, tiled=True
        ).astype(jnp.float32),
        lax.psum_scatter(
            attn_terms[1].astype(jnp.bfloat16), "gx", scatter_dimension=0, tiled=True
        ).astype(jnp.float32),
    )
    attn_sums = (
        lax.psum_scatter(
            attn_parts[0].astype(jnp.bfloat16), "gy", scatter_dimension=0, tiled=True
        ).astype(jnp.float32),
        lax.psum_scatter(
            attn_parts[1].astype(jnp.bfloat16), "gy", scatter_dimension=0, tiled=True
        ).astype(jnp.float32),
    )
    sum_qkv, sum_out = attn_sums
    return (
        output,
        d_tokens,
        owned_ada,
        sum_qkv,
        sum_out,
        sum_fc1,
        sum_fc2,
        sum_router,
        sum_e_in,
        sum_e_out,
    )


def solution(mesh):
    in_specs = (
        P(("gx", "gy"), None),
        P(("gx", "gy")),
        P(("gx", "gy"), None),
        P(("gx", "gy"), None),
        P(("gx", "gy"), None),
        P(("gx", "gy"), None),
        P(("gx", "gy"), None),
        P(("gx", "gy"), None),
        P(("gx", "gy"), None),
        P(("gx", "gy"), None),
        P(("gx", "gy"), None),
        P("gx", "gy", None),
        P("gx", "gy", None),
    )
    out_specs = (
        P(("gx", "gy"), None),
        P(("gx", "gy"), None),
        P(("gx", "gy"), None),
        P(("gx", "gy"), None),
        P(("gx", "gy"), None),
        P(("gx", "gy"), None),
        P(("gx", "gy"), None),
        P(("gx", "gy"), None),
        P("gx", "gy", None),
        P("gx", "gy", None),
    )
    step = by_slices if dict(mesh.shape) == {"gx": 2, "gy": 16} else by_weights
    return jax.shard_map(
        step, mesh=mesh, in_specs=in_specs, out_specs=out_specs, check_vma=False
    )
```

```python
import functools
import math

import jax
import jax.numpy as jnp
import numpy as np
from jax import lax
from jax.experimental import pallas as pl
from jax.experimental.pallas import tpu as pltpu
from jax.sharding import PartitionSpec as P

HEADS = 12
CAP = 64
MESH = pl.DeviceIdType.MESH
ANY = pl.ANY
VMEM = pltpu.VMEM
DMA = pltpu.SemaphoreType.DMA
LINE = (1, 2, 3)

precise = lax.Precision.HIGHEST
layer_epsilon = 1e-06


def place():
    gy = lax.axis_index("gy")
    return lax.axis_index("gx"), gy // 4, (gy // 2) % 2, gy % 2


def device(y, z, x, c):
    return (y, 4 * z + 2 * x + c)


def chip(y, z, x):
    return 8 * y + 2 * z + x


def along(z, step):
    return z + step - 2 * (z % 2) * (step % 2) - 4 * (z // 2) * (step // 2)


def meet(partners):
    barrier = pltpu.get_barrier_semaphore()
    for partner in partners:
        pl.semaphore_signal(barrier, inc=1, device_id=partner, device_id_type=MESH)
    pl.semaphore_wait(barrier, len(partners))


def cross_partners(here):
    y, z, x, c = here
    return [device(y, along(z, step), x, c) for step in LINE] + [
        device(1 - y, z, x, c),
        device(y, z, 1 - x, c),
    ]


def remote(source, target, send, recv, to):
    return pltpu.make_async_remote_copy(
        src_ref=source, dst_ref=target, send_sem=send, recv_sem=recv, device_id=to, device_id_type=MESH
    )


class Gather:
    def __init__(self, here, y_first, own, slot, send, recv, pair=None):
        self.here, self.y_first, self.own, self.slot = here, y_first, own, slot
        self.send, self.recv, self.pair, self.started = send, recv, pair, []

    def number(self, a, step, b):
        y, z, x, c = self.here
        flip_y, flip_x = (a, b) if self.y_first else (b, a)
        return chip(1 - y if flip_y else y, along(z, step), 1 - x if flip_x else x)

    def copy(self, source, number, to, recv=None):
        recv = self.recv if recv is None else recv
        sent = remote(source, self.slot(number), self.send.at[len(self.started)], recv.at[number], to)
        sent.start()
        self.started.append(sent)

    def to_side(self, source, number, second):
        y, z, x, c = self.here
        self.copy(source, number, device(1 - y, z, x, c) if self.y_first != second else device(y, z, 1 - x, c))

    def to_line(self, source, number, step):
        y, z, x, c = self.here
        self.copy(source, number, device(y, along(z, step), x, c))

    def to_pair(self, source, number):
        y, z, x, c = self.here
        if self.pair is not None:
            self.copy(source, number, device(y, z, x, 1 - c), self.pair)

    def arrive(self, number, recv=None):
        recv = self.recv if recv is None else recv
        block = self.slot(number)
        remote(block, block, self.send.at[0], recv.at[number], device(*self.here)).wait_recv()
        return block

    def start_first(self):
        self.to_side(self.own, self.number(0, 0, 0), False)
        self.to_pair(self.own, self.number(0, 0, 0))

    def start_line(self, step):
        self.to_line(self.own, self.number(0, 0, 0), step)

    def start_last(self):
        self.to_side(self.own, self.number(0, 0, 0), True)

    def line_first(self, step):
        number = self.number(0, step, 0)
        block = self.arrive(number)
        if step == 2:
            self.to_line(block, number, 1)
        self.to_side(block, number, False)
        self.to_pair(block, number)

    def line_last(self, step):
        number = self.number(0, step, 0)
        self.to_side(self.slot(number), number, True)

    def second(self, step):
        number = self.number(1, step, 0)
        block = self.arrive(number)
        self.to_side(block, number, True)
        self.to_pair(block, number)

    def third(self, step):
        for a in (0, 1):
            number = self.number(a, step, 1)
            self.to_pair(self.arrive(number), number)

    def finish(self):
        block = self.slot(self.number(0, 0, 0))
        for index in range(len(self.started)):
            remote(block, block, self.send.at[index], self.recv.at[0], device(*self.here)).wait_send()
        if self.pair is not None:
            for number in range(16):
                self.arrive(number, self.pair)


def gather_start(gathers):
    for gather in gathers:
        gather.start_first()
    for step in (1, 2):
        for gather in gathers:
            gather.start_line(step)
    for gather in gathers:
        gather.start_last()


def gather_line(gathers, step):
    for gather in gathers:
        gather.line_first(step)
    for gather in gathers:
        gather.line_last(step)


def gather_second(gathers, step):
    for gather in gathers:
        gather.second(step)


def gather_third(gathers, step):
    for gather in gathers:
        gather.third(step)


def gather_all(gathers, between=None):
    gather_start(gathers)
    gather_second(gathers, 0)
    for step in LINE:
        gather_line(gathers, step)
        gather_second(gathers, step)
    if between is not None:
        between()
    for step in (0,) + LINE:
        gather_third(gathers, step)
    for gather in gathers:
        gather.finish()


class Scatter:
    def __init__(self, here, y_first, part, got, send, recv, relay=False):
        self.here, self.y_first, self.part, self.got, self.relay = here, y_first, part, got, relay
        self.send, self.recv, self.started = send, recv, []

    def number(self, a, b, step):
        y, z, x, c = self.here
        flip_y, flip_x = (a, b) if self.y_first else (b, a)
        return chip(1 - y if flip_y else y, along(z, step), 1 - x if flip_x else x)

    def toward(self, second):
        y, z, x, c = self.here
        return device(1 - y, z, x, c) if self.y_first != second else device(y, z, 1 - x, c)

    def copy(self, source, index, to):
        sent = remote(source, self.got(index), self.send.at[len(self.started)], self.recv.at[index], to)
        sent.start()
        self.started.append(sent)

    def arrive(self, index):
        block = self.got(index)
        remote(block, block, self.send.at[0], self.recv.at[index], device(*self.here)).wait_recv()
        return block

    def first(self, step):
        for b in (1, 0):
            self.copy(self.part(self.number(1, b, step)), 4 * b + step, self.toward(False))

    def add(self, number, index):
        block, mine = self.arrive(index), self.part(number)
        total = mine[...].astype(jnp.float32) + block[...].astype(jnp.float32)
        mine[...] = total.astype(mine.dtype)

    def one(self, b, step):
        number = self.number(0, b, step)
        self.add(number, 4 * b + step)
        if b == 1:
            self.copy(self.part(number), 8 + step, self.toward(True))

    def two(self, step):
        y, z, x, c = self.here
        number = self.number(0, 0, step)
        self.add(number, 8 + step)
        if self.relay and step == 2:
            self.add(number, 14)
        if step:
            self.copy(self.part(number), 11 + step, device(y, along(z, 1 if self.relay and step == 3 else step), x, c))

    def total(self):
        result = self.part(self.number(0, 0, 0))[...].astype(jnp.float32)
        for step in (1, 2) if self.relay else (1, 2, 3):
            result = result + self.arrive(11 + step)[...].astype(jnp.float32)
        return result

    def finish(self):
        block = self.got(0)
        for index in range(len(self.started)):
            remote(block, block, self.send.at[index], self.recv.at[0], device(*self.here)).wait_send()


def scatter_all(scatters, more, between):
    order = (3, 2, 1, 0)
    for turn, step in enumerate(order):
        for b in (1, 0):
            for scatter in scatters:
                scatter.one(b, step)
        if turn + 2 < 4:
            more(order[turn + 2])
        if turn:
            for scatter in scatters:
                scatter.two(order[turn - 1])
        between(turn)
    for scatter in scatters:
        scatter.two(order[3])


def nt(a, b):
    return lax.dot_general(a, b, (((1,), (1,)), ((), ())), preferred_element_type=jnp.float32)


def tn(a, b):
    return lax.dot_general(a, b, (((0,), (0,)), ((), ())), preferred_element_type=jnp.float32)


def nn(a, b):
    return jnp.dot(a, b, preferred_element_type=jnp.float32)


def low(value):
    return value.astype(jnp.bfloat16)


def wide_float(value):
    return value.astype(jnp.float32)


def norm(values):
    centred = values - jnp.mean(values, axis=-1, keepdims=True)
    scale = lax.rsqrt(jnp.mean(centred * centred, axis=-1, keepdims=True) + layer_epsilon)
    return centred * scale, scale


def norm_back(grad, normed, scale):
    pulled = grad - jnp.mean(grad, axis=-1, keepdims=True) - normed * jnp.mean(grad * normed, axis=-1, keepdims=True)
    return scale * pulled


def item_mask(lengths, shape):
    return lax.broadcasted_iota(jnp.int32, shape, 0) >= lengths[0, 0]


def choices(routes, square):
    square[...] = jnp.zeros_like(square)
    square[0 : routes.shape[0], :] = wide_float(routes[...])
    named = square[...].T
    lane = wide_float(lax.broadcasted_iota(jnp.int32, (1, 128), 1))
    return (named[:, 0:1] == lane) | (named[:, 1:2] == lane)


def own_modulation(here, mod, item, half, part):
    first = 2 * here[3]
    model = item.shape[1]
    at = slice(part * model, (part + 1) * model)
    return jnp.where(item, mod[half, pl.ds(first + 1, 1), at], mod[half, pl.ds(first, 1), at])


def frequencies(model_width):
    half = model_width // 2
    return np.tile(np.exp(-math.log(10000.0) * np.arange(half) / half).astype(np.float32), 2)


def conditions(steps, shape, first, column, half, frequency):
    row = lax.broadcasted_iota(jnp.int32, shape, 0) - first
    angle = jnp.where(row == 0, wide_float(steps[0]), wide_float(steps[1])) * frequency
    wave = jnp.where(column < half, jnp.cos(angle), jnp.sin(angle))
    value = wave / (1.0 + jnp.exp(-wave))
    return wide_float(low(jnp.where((row == 0) | (row == 1), value, 0.0)))


def head_lanes():
    lane = lax.broadcasted_iota(jnp.int32, (1, 128), 1)
    return lane < 64, [low(wide_float(lane < 64)), low(wide_float(lane >= 64))]


def front_part(refs, outs, kept, sems, start_tokens, more_tokens, *locals_):
    (lengths, steps, tokens, cotangent, routes, waves, w_ada, w_qkv, w_out, w_router, w_fc1, e1) = refs
    (qkv_w, out_w, mod_out, mixed_out, attn_in_out, qkv_out, probs_out, attn_low_out, attn_proj_out, middle_out, chance_out) = outs
    (w1, w1s, mod, mixed, grad, gates, q_full, o_full, a_full, q_stage, o_stage, a_stage, c_buf, z_got, s_got) = kept
    (pre_send, pre_recv, g_send, g_recv, g_pair, a_send, a_recv, a_pair_send, a_pair, b_send, b_recv, b_pair, l_sem, o_sem,
     c_send, c_recv, m_send, m_recv, r_send, r_recv) = sems
    (attn_in, qkv, probs, attn_low, attn_proj, middle, chance, square, cond, f1, s_rows, q_fold, o_fold, a_fold, q_block, o_block, z_part) = locals_
    here = y, z, x, c = place()
    me, k, gy = chip(y, z, x), 2 * z + x, 4 * z + 2 * x + c
    rows, model = w_out.shape
    others = [(dy, dz, dx) for dy in (0, 1) for dz in (0, 1, 2, 3) for dx in (0, 1) if (dy, dz, dx) != (0, 0, 0)]
    spot = lambda dy, dz, dx: (1 - y if dy else y, along(z, dz), 1 - x if dx else x)
    sibling = device(y, z, x, 1 - c)
    crossed = [device(y, along(z, step), x, 1 - c) for step in LINE]
    meet([device(*spot(*o), c) for o in others] + [sibling] + crossed)

    started = []

    def go(copy):
        copy.start()
        started.append(copy)

    lane = lax.broadcasted_iota(jnp.int32, cond.shape[1:], 1)
    for at in range(4):
        column = model // 2 * (lane // (4 * rows)) + 4 * rows * at + lane % (4 * rows)
        cond[at] = jnp.where(lane < 8 * rows, conditions(steps, cond.shape[1:], 2 * c, column, model // 2, waves[at : at + 1, :]), 0.0)
    for i, (step, core) in enumerate([(0, 1 - c)] + [(step, core) for step in LINE for core in (c, 1 - c)]):
        go(remote(cond.at[along(z, step)], c_buf.at[z, c], c_send.at[i], c_recv.at[z, c], device(y, along(z, step), x, core)))

    mine = pl.ds(pl.multiple_of(rows * c, 8), rows)
    square[...] = jnp.zeros_like(square)
    square[0 : w_router.shape[0], 0:rows] = wide_float(w_router[...])
    router = square[...].T[:rows]
    for i, (w, fold, stage) in enumerate(((w_ada, a_fold, a_stage), (w_qkv, q_fold, q_stage), (w_out, o_fold, o_stage))):
        cut = w.shape[1] // 2
        for h in (0, 1):
            fold[h, :, :cut] = wide_float(w[:, h * cut : (h + 1) * cut])
            if i == 2:
                fold[h, :, cut:] = router
        go(remote(fold.at[1 - c], stage.at[mine, :], pre_send.at[i], pre_recv.at[i], sibling))
        stage[mine, :] = fold[c]

    depth, width = e1.shape[1], w1.shape[2]
    cols = lambda n: pl.ds(pl.multiple_of(width * n, 128), width)
    strip = lambda n: pl.ds(pl.multiple_of(depth * n, 16), depth)
    load = pltpu.make_async_copy(e1.at[:, :, cols(k)], w1.at[:, strip(gy), :], l_sem.at[0])
    load.start()
    plane = [o for o in others if o[0] == 0]

    def send_experts(steps, aside):
        for i, o in enumerate(plane):
            if o[1] in steps and o[2] == aside:
                ty, tz, tx = spot(*o)
                go(remote(e1.at[:, :, cols(2 * tz + tx)], w1.at[:, strip(gy), :], a_send.at[i], a_recv.at[k], device(ty, tz, tx, c)))


    def folded(i, stage):
        theirs = stage.at[pl.ds(pl.multiple_of(rows * (1 - c), 8), rows), :]
        remote(theirs, theirs, pre_send.at[i], pre_recv.at[i], sibling).wait_recv()
        return low(stage[...])

    block = folded(0, a_stage)
    width_a = a_full.shape[3]
    number = 2 * y + x
    to_y, to_x = device(1 - y, z, x, c), device(y, z, 1 - x, c)
    for i in (0, 1):
        a_full[i, number] = block[:, i * width_a : (i + 1) * width_a]

    def send_a(i, n, lane, to):
        go(remote(a_full.at[i, n], a_full.at[i, n], r_send.at[i, lane], r_recv.at[i, n], to))

    def wait_a(i, n):
        remote(a_full.at[i, n], a_full.at[i, n], r_send.at[0, 0], r_recv.at[i, n], sibling).wait_recv()

    send_a(0, number, 0, to_y)
    send_a(1, number, 0, to_x)
    send_a(0, number, 1, to_x)
    send_a(1, number, 1, to_y)
    q_block[...] = folded(1, q_stage)
    o_block[...] = folded(2, o_stage)
    gathers = []
    for i, (block, full, y_first) in enumerate(((q_block, q_full, False), (o_block, o_full, True))):
        slot = functools.partial(lambda full, n: full.at[c, pl.ds(pl.multiple_of(2 * rows * n, 16), 2 * rows), :], full)
        gathers.append(Gather(here, y_first, block, slot, g_send.at[i], g_recv.at[i], g_pair.at[i]))
        slot(me)[...] = block[...]
    gather_start(gathers)

    n_y, n_x = 2 * (1 - y) + x, 2 * y + 1 - x
    n_xy = 2 * (1 - y) + 1 - x
    wait_a(0, n_y)
    send_a(0, n_y, 2, to_x)
    wait_a(1, n_x)
    send_a(1, n_x, 2, to_y)
    gather_second(gathers, 0)

    c_buf[z, c] = cond[z]
    for step, core in [(0, 1 - c)] + [(step, core) for step in LINE for core in (c, 1 - c)]:
        block = c_buf.at[along(z, step), core]
        remote(block, block, c_send.at[0], c_recv.at[along(z, step), core], sibling).wait_recv()
    lhs = low(jnp.concatenate([c_buf[i, 0] + c_buf[i, 1] for i in range(4)], axis=0))[:, : 8 * rows]
    for i, n_last in enumerate((n_x, n_y)):
        wait_a(i, n_last)
        wait_a(i, n_xy)
        term = nn(lhs, a_full[i].reshape(8 * rows, width_a))
        for line in range(4):
            z_part[line, 4 * i : 4 * (i + 1), :] = term[8 * line : 8 * line + 4]
    for step in LINE:
        at = along(z, step)
        go(remote(z_part.at[at], z_got.at[step - 1], m_send.at[step], m_recv.at[step], device(y, at, x, c)))
    gather_line(gathers, 1)
    gather_second(gathers, 1)
    gather_line(gathers, 2)
    send_experts((2, 3, 1), 0)
    slim = w1s.shape[1]
    for n in range(16):
        block = wide_float(w_fc1[:, slim * n : slim * (n + 1)])
        f1[n] = low(jnp.concatenate([block, jnp.zeros((f1.shape[1] - rows, slim), jnp.float32)], axis=0))
    for i, o in enumerate(others):
        ty, tz, tx = spot(*o)
        go(remote(f1.at[chip(ty, tz, tx)], s_got.at[c, me], b_send.at[i], b_recv.at[me], device(ty, tz, tx, c)))
    s_got[c, me] = f1[me]
    gather_second(gathers, 2)
    gather_line(gathers, 3)
    gather_second(gathers, 3)
    send_experts((0, 1, 2, 3), 1)
    total = z_part[z]
    for step in LINE:
        remote(z_got.at[step - 1], z_got.at[step - 1], m_send.at[0], m_recv.at[step], sibling).wait_recv()
        total = total + z_got[step - 1]
    mod[c] = jnp.concatenate([total, pltpu.roll(total, 4, 0)], axis=1)
    go(remote(mod.at[c], mod.at[c], m_send.at[0], m_recv.at[0], sibling))
    remote(mod.at[1 - c], mod.at[1 - c], m_send.at[0], m_recv.at[0], sibling).wait_recv()

    item = item_mask(lengths, tokens.shape)
    residual = wide_float(tokens[...])
    normed, _ = norm(residual)
    attn_in[...] = low(normed * (1.0 + own_modulation(here, mod, item, 0, 1)) + own_modulation(here, mod, item, 0, 0))
    grad[...] = low(wide_float(cotangent[...]) * own_modulation(here, mod, item, 1, 2))
    token_gathers = start_tokens(None, (1,))
    for step in (0,) + LINE:
        gather_third(gathers, step)
    for gather in gathers:
        gather.finish()
    keep = []

    def leave(source, target):
        keep.append(pltpu.make_async_copy(source, target, o_sem.at[len(keep)]))
        keep[-1].start()

    leave(q_full, qkv_w)
    leave(o_full, out_w)

    cut = q_full.shape[2]
    for h in (0, 1):
        qkv[:, h * cut : (h + 1) * cut] = low(nn(attn_in[...], q_full[h]))

    side = wide_float(item[:, :128])
    same = side == side.T
    left, sides = head_lanes()
    for pair in range(model // 128):
        q, key, value = [qkv[:, base + 128 * pair : base + 128 * (pair + 1)] for base in (0, model, 2 * model)]
        outs = []
        for j, side in enumerate(sides):
            scores = jnp.where(same, nt(q * side, key) * 0.125, -1e30)
            weight = jnp.exp(scores - jnp.max(scores, axis=-1, keepdims=True))
            prob = weight / jnp.sum(weight, axis=-1, keepdims=True)
            probs[2 * pair + j] = prob
            outs.append(nn(low(prob), value))
        attn_low[:, 128 * pair : 128 * (pair + 1)] = low(jnp.where(left, outs[0], outs[1]))
    cut = model // 2
    for h in (0, 1):
        attn_proj[:, h * cut : (h + 1) * cut] = nn(attn_low[...], o_full[h, :, :cut])
    middle[...] = residual + own_modulation(here, mod, item, 0, 2) * attn_proj[...]
    normed, _ = norm(middle[...])
    mixed[...] = low(normed * (1.0 + own_modulation(here, mod, item, 1, 1)) + own_modulation(here, mod, item, 1, 0))
    lane = lax.broadcasted_iota(jnp.int32, (1, 128), 1)
    logits = jnp.where(lane < 8, nn(mixed[...], o_full[0, :, cut:]), -1e30)
    weight = jnp.exp(logits - jnp.max(logits, axis=-1, keepdims=True))
    chance[...] = weight / jnp.sum(weight, axis=-1, keepdims=True)
    turned = jnp.where(choices(routes, square), chance[...], 0.0).T[:8]
    high = low(turned)
    gates[...] = jnp.concatenate([high, low(turned - wide_float(high))], axis=0)
    start_tokens(token_gathers, (0, 2))
    for source, target in (
        (mixed, mixed_out), (mod, mod_out), (attn_in, attn_in_out), (qkv, qkv_out), (probs, probs_out),
        (attn_low, attn_low_out), (attn_proj, attn_proj_out), (middle, middle_out), (chance, chance_out),
    ):
        leave(source, target)

    for o in others:
        n = chip(*spot(*o))
        remote(s_got.at[c, n], s_got.at[c, n], b_send.at[0], b_recv.at[n], sibling).wait_recv()
    go(remote(s_got.at[c], s_got.at[c], b_pair.at[0], b_pair.at[1], sibling))
    load.wait()
    more_tokens(0, token_gathers)
    for i, o in enumerate([(0, 0, 0)] + [o for step in (0, 1, 3, 2) for o in plane if o[1] == step]):
        _, sz, sx = spot(*o)
        source = 2 * sz + sx
        block = w1.at[:, strip(2 * source + c), :]
        if i:
            remote(block, block, a_send.at[0], a_recv.at[source], sibling).wait_recv()
        go(remote(block, block, a_pair_send.at[i], a_pair.at[source], sibling))
    more_tokens(1, token_gathers)
    remote(s_got.at[1 - c], s_got.at[1 - c], b_pair.at[0], b_pair.at[1], sibling).wait_recv()
    for n in range(32):
        s_rows[n * rows : (n + 1) * rows, :] = wide_float(s_got[n % 2, n // 2])[:rows]
    w1s[...] = low(s_rows[...])
    for copy in started:
        copy.wait_send()
    for source in range(8):
        block = w1.at[:, strip(2 * source + 1 - c), :]
        remote(block, block, a_send.at[0], a_pair.at[source], sibling).wait_recv()
    for copy in keep:
        copy.wait()


def gelu_both(h):
    root = math.sqrt(2.0 / math.pi)
    square = h * h
    t = jnp.tanh(h * (root + (root * 0.044715) * square))
    half = 0.5 * (1.0 + t)
    slope = half + (0.5 * h) * (1.0 - t * t) * (root + (3.0 * root * 0.044715) * square)
    return h * half, slope


def ffn_chunk(xt, gt, w1, w2, gate, row):
    a, d = gelu_both(nn(xt, w1))
    gi = nt(gt, w2)
    product = None
    if gate is not None:
        product = nt(row, (a * gi).astype(jnp.bfloat16))
        a, d = a * gate, d * gate
    a = a.astype(jnp.bfloat16)
    p = (gi * d).astype(jnp.bfloat16)
    return a, p, nn(a, w2), nt(p, w1), product


def ffn_shared(slots, X, G, w1s, w2s, act_s, pre_s, sums, sums_back):
    toks = X.shape[1]
    xt = jnp.concatenate([X[n] for n in slots], axis=0)
    gt = jnp.concatenate([G[n] for n in slots], axis=0)
    a, p, total, total_back, _ = ffn_chunk(xt, gt, w1s[...], w2s[...], None, None)
    for i, n in enumerate(slots):
        act_s[n] = a[i * toks : (i + 1) * toks]
        pre_s[n] = p[i * toks : (i + 1) * toks]
    sums[...] = total
    sums_back[...] = total_back


def ffn_experts(low, high, slots, X, G, gates, w1, w2, act, pre, sums, sums_back, gc):
    experts, toks, wide = w1.shape[0], X.shape[1], w1.shape[2]
    first = lax.axis_index("gx") * experts
    xt = jnp.concatenate([X[n] for n in slots], axis=0)
    gt = jnp.concatenate([G[n] for n in slots], axis=0)

    def expert(e, product):
        kind = lax.broadcasted_iota(jnp.int32, (16, 128), 0)
        spread = ((kind == first + e) | (kind == first + e + 8)).astype(jnp.bfloat16)
        gate = jnp.concatenate([tn(gates[n], spread) for n in slots], axis=0)
        gate = jnp.concatenate([gate] * (wide // 128), axis=1)
        row = (lax.broadcasted_iota(jnp.int32, (8, wide), 0) == first + e).astype(jnp.bfloat16)
        a, p, total, total_back, more = ffn_chunk(xt, gt, w1[e], w2[e], gate, row)
        for i, n in enumerate(slots):
            act[e, n] = a[i * toks : (i + 1) * toks]
            pre[e, n] = p[i * toks : (i + 1) * toks]
        sums[...] += total
        sums_back[...] += total_back
        return product + more

    product = lax.fori_loop(low, high, expert, jnp.zeros((8, len(slots) * toks), jnp.float32))
    for i, n in enumerate(slots):
        part = product[:, i * toks : (i + 1) * toks]
        gc[n] = part if low == 0 else gc[n] + part


def block_part(refs, outs, kept, sems, go_on, plan, *locals_):
    w2_in, w2s_in = refs
    (sum_branch, sum_back, sum_gc, near1, far1, out1s, out2, out2s) = outs
    (w1, w1s, X, G, gt, w2, w2s, r_branch, r_back, r_gc, from1, from1s, from2, from2s) = kept
    (l_sem, o_sem, send, recv, t_send, t_recv, w_send, w_recv, h_send, h_recv) = sems
    (act, pre, act_s, pre_s, p_branch, p_back, p_gc) = locals_
    experts = w1.shape[0]
    counts = []

    def tools():
        here = place()
        scatters = []
        for i, (part, got, y_first) in enumerate(((p_branch, r_branch, False), (p_back, r_back, True), (p_gc, r_gc, False))):
            take = functools.partial(lambda ref, n: ref.at[n], part)
            land = functools.partial(lambda ref, n: ref.at[n], got)
            scatters.append(Scatter(here, y_first, take, land, send.at[i], recv.at[i]))

        return scatters

    def tiles(tile_sum, tile_back):
        here = y, z, x, c = place()
        spot = lambda dy, dz, dx: (1 - y if dy else y, along(z, dz), 1 - x if dx else x)
        sibling = device(y, z, x, 1 - c)
        local, gathers, scatters = [], go_on(), tools()
        half2, half2s = w2_in.shape[1], w2s_in.shape[0]
        own2_at = w2.at[:, pl.ds(pl.multiple_of(half2 * c, 16), half2), :]
        own2s_at = w2s.at[pl.ds(pl.multiple_of(half2s * c, 16), half2s), :]
        for i, (source, target) in enumerate(((w2_in, own2_at), (w2s_in, own2s_at))):
            local.append(pltpu.make_async_copy(source, target, l_sem.at[3 + i]))
        for i, (source, target) in enumerate(((w2_in, own2_at), (w2s_in, own2s_at))):
            local.append(remote(source, target, w_send.at[i], w_recv.at[i], sibling))
        for copy in local:
            copy.start()

        def tile(step, part):
            slots = [chip(*spot(dy, step, dx)) for dy in (0, 1) for dx in (0, 1)]
            if part == 0:
                ffn_shared(slots, X, G, w1s, w2s, act_s, pre_s, tile_sum, tile_back)
            low, high = (0, experts // 2) if part == 0 else (experts // 2, experts)
            ffn_experts(low, high, slots, X, G, gt, w1, w2, act, pre, tile_sum, tile_back, p_gc)
            if part == 1:
                toks = X.shape[1]
                for i, n in enumerate(slots):
                    at = slice(i * toks, (i + 1) * toks)
                    p_branch[n] = tile_sum[at, :].astype(jnp.bfloat16)
                    p_back[n] = tile_back[at, :].astype(jnp.bfloat16)

        def back_first(step):
            for scatter in scatters:
                scatter.first(step)

        def back_one(b, step):
            for scatter in scatters:
                scatter.one(b, step)

        def back_two(step):
            for scatter in scatters:
                scatter.two(step)

        gather_second(gathers, 1)
        gather_third(gathers, 0)
        for copy in local:
            copy.wait()
        tile(0, 0)
        gather_line(gathers, 2)
        tile(0, 1)
        gather_third(gathers, 1)
        tile(1, 0)
        gather_second(gathers, 2)
        tile(1, 1)
        gather_line(gathers, 3)
        gather_third(gathers, 2)
        tile(2, 0)
        gather_second(gathers, 3)
        tile(2, 1)
        back_first(2)
        gather_third(gathers, 3)
        tile(3, 0)

        back_one(1, 2)
        tile(3, 1)
        for gather in gathers:
            gather.finish()
        counts.extend(len(scatter.started) for scatter in scatters)

    def weights(own1s, own2, own2s, d1, d1s, d2, d2s):
        here = y, z, x, c = place()
        spot = lambda dy, dz, dx: (1 - y if dy else y, along(z, dz), 1 - x if dx else x)
        sibling = device(y, z, x, 1 - c)
        scatters = tools()
        for scatter, count in zip(scatters, counts):
            scatter.started = [None] * count

        def back_first(step):
            for scatter in scatters:
                scatter.first(step)

        def back_one(b, step):
            for scatter in scatters:
                scatter.one(b, step)

        def back_two(step):
            for scatter in scatters:
                scatter.two(step)

        flat = lambda value: value.reshape(value.shape[0] * value.shape[1], value.shape[2])
        twins = [None] * (2 * experts)
        leaving, homeward, left = [], [], []

        def leave(source, target):
            leaving.append(pltpu.make_async_copy(source, target, o_sem.at[len(leaving)]))
            leaving[-1].start()


        def weight(e):
            d1[e % 2] = tn(flat(X[...]), flat(pre[e])).astype(jnp.bfloat16).reshape(d1.shape[1:])
            d2[e % 2] = tn(flat(act[e]), flat(G[...])).astype(jnp.bfloat16).reshape(d2.shape[1:])
            for i, (part, got) in enumerate(((d1.at[e % 2, :, 1 - c], from1.at[e]), (d2.at[e % 2, 1 - c], from2.at[e]))):
                twins[2 * e + i] = remote(part, got, t_send.at[2 * e + i], t_recv.at[2 * e + i], sibling)
                twins[2 * e + i].start()

        def home(e):
            twins[2 * e].wait()
            from1[e] = (d1[e % 2, :, c].astype(jnp.float32) + from1[e].astype(jnp.float32)).astype(jnp.bfloat16)
            twins[2 * e + 1].wait()
            if e > 1:
                left[e - 2].wait()
            own2[e % 2] = d2[e % 2, c].astype(jnp.float32) + from2[e].astype(jnp.float32)
            left.append(pltpu.make_async_copy(own2.at[e % 2], out2.at[e], l_sem.at[e]))
            left[e].start()
            for i in range(4):
                leave(from1.at[e, 2 * i + 1 - x], far1.at[e, i])
            leave(from1.at[e, 2 * z + x], near1.at[e, z])

        def along_home(e):
            for step in LINE:
                at = along(z, step)
                sent = remote(from1.at[e, 2 * at + x], near1.at[e, z], h_send.at[e, step], h_recv.at[e, z], device(y, at, x, c))
                sent.start()
                homeward.append(sent)


        back_first(3)
        back_one(0, 2)
        back_two(2)
        weight(0)
        back_one(1, 3)
        back_first(1)
        weight(1)
        home(0)
        back_one(0, 3)
        back_two(3)
        home(1)
        back_one(1, 1)
        back_first(0)
        weight(2)
        back_one(0, 1)
        along_home(0)
        along_home(1)
        back_two(1)
        home(2)
        back_one(1, 0)
        along_home(2)
        weight(3)
        d1s[...] = tn(flat(X[...]), flat(pre_s[...])).reshape(d1s.shape)
        d2s[...] = tn(flat(act_s[...]), flat(G[...])).astype(jnp.bfloat16).reshape(d2s.shape)
        twin1s = remote(d1s.at[:, 1 - c], from1s, t_send.at[2 * experts], t_recv.at[2 * experts], sibling)
        twin2s = remote(d2s.at[1 - c], from2s, t_send.at[2 * experts + 1], t_recv.at[2 * experts + 1], sibling)
        twin1s.start()
        twin2s.start()
        home(3)
        along_home(3)
        back_one(0, 0)
        twin1s.wait()
        total = d1s[:, c] + from1s[...]
        own1s[...] = low(jnp.concatenate([total, jnp.zeros((16, own1s.shape[1] - total.shape[1], total.shape[2]), jnp.float32)], axis=1))
        twin2s.wait()
        own2s[...] = d2s[c].astype(jnp.float32) + from2s[...].astype(jnp.float32)
        leave(own1s, out1s)
        leave(own2s, out2s)
        back_two(0)
        sum_branch[...] = scatters[0].total()
        sum_back[...] = scatters[1].total()
        sum_gc[...] = scatters[2].total()
        for copy in leaving:
            copy.wait()
        for copy in left[-2:]:
            copy.wait()
        for sent in homeward:
            sent.wait_send()
        for e in range(experts):
            for step in LINE:
                block = near1.at[e, along(z, step)]
                remote(block, block, h_send.at[0, 0], h_recv.at[e, along(z, step)], sibling).wait_recv()
        for scatter in scatters:
            scatter.finish()


    pl.run_scoped(tiles, *[VMEM(*a) for a in plan[0]])
    pl.run_scoped(weights, *[VMEM(*a) for a in plan[1]])


def joint_kernel(plan, *refs):
    refs = list(refs)

    def take(count):
        taken, refs[:count] = refs[:count], []
        return taken

    front_refs, block_refs = take(12), take(2)
    front_outs, block_outs = take(11), take(8)
    w1, w1s = take(2)
    mod, mixed, grad, gates = take(4)
    front_kept, (X, G, gt), block_kept = take(9), take(3), take(9)
    front_sems, block_sems, (g_send, g_recv) = take(20), take(10), take(2)
    counts = []

    def token_gathers():
        gathers = []
        for i, (block, full, y_first) in enumerate(((mixed, X, True), (grad, G, False), (gates, gt, True))):
            slot = functools.partial(lambda full, n: full.at[n], full)
            gathers.append(Gather(place(), y_first, block, slot, g_send.at[i], g_recv.at[i]))
        return gathers

    def start_tokens(gathers, which):
        gathers = token_gathers() if gathers is None else gathers
        gather_start([gathers[i] for i in which])
        y, z, x, c = place()
        for i in which:
            block, full = ((mixed, X), (grad, G), (gates, gt))[i]
            full[chip(y, z, x)] = block[...]
        return gathers

    def more_tokens(turn, gathers):
        if turn == 0:
            gather_second(gathers, 0)
        else:
            gather_line(gathers, 1)
            counts.extend(len(gather.started) for gather in gathers)

    def go_on():
        gathers = token_gathers()
        for gather, count in zip(gathers, counts):
            gather.started = [None] * count
        return gathers

    kept = (w1, w1s, mod, mixed, grad, gates, *front_kept)
    pl.run_scoped(
        functools.partial(front_part, front_refs, front_outs, kept, front_sems, start_tokens, more_tokens), *[VMEM(*a) for a in plan[0]]
    )
    kept = (w1, w1s, X, G, gt, *block_kept)
    pl.run_scoped(functools.partial(block_part, block_refs, block_outs, kept, block_sems, go_on, plan[2:]), *[VMEM(*a) for a in plan[1]])


def joint(lengths, timesteps, tokens, cotangent, routes, w_ada, w_qkv, w_out, w_router, w_fc1, e_fc1, e_fc2, w_fc2):
    rows, model = w_out.shape
    toks = tokens.shape[0]
    waves = frequencies(model).reshape(2, 4, 4 * rows).transpose(1, 0, 2).reshape(4, 8 * rows)
    waves = np.pad(waves, ((0, 0), (0, -8 * rows % 128)))
    lanes = waves.shape[1]
    ff = w_fc1.shape[1]
    slim, wide = ff // 16, ff // 8
    experts, depth, _ = e_fc1.shape
    bf, f32 = jnp.bfloat16, jnp.float32
    shape = jax.ShapeDtypeStruct
    q_half, o_half, a_half = w_qkv.shape[1] // 2, w_out.shape[1] // 2 + 128, w_ada.shape[1] // 2
    saved = (((toks, model), bf), ((toks, 3 * model), bf), ((HEADS, toks, toks), f32), ((toks, model), bf), ((toks, model), f32),
             ((toks, model), f32), ((toks, 128), f32))
    front_plan = saved + (
        ((128, 128), f32), ((4, 8, lanes), f32), ((16, 32, slim), bf), ((model, slim), f32),
        ((2, rows, q_half), f32), ((2, rows, o_half), f32), ((2, rows, a_half), f32), ((2 * rows, q_half), bf), ((2 * rows, o_half), bf),
        ((4, 8, a_half // 2), f32),
    )
    blocks = lambda *dims: ((16, toks) + dims, bf)
    block_plan = (
        ((experts, 16, toks, wide), bf), ((experts, 16, toks, wide), bf), blocks(slim), blocks(slim), blocks(model), blocks(model),
        ((16, 8, 128), f32),
    )
    tiles_plan = (((4 * toks, model), f32), ((4 * toks, model), f32))
    weights_plan = (
        ((16, 32, slim), bf), ((2, wide // 2, model), f32), ((slim // 2, model), f32), ((2, 8, 2, depth, wide), bf), ((16, 2, rows, slim), f32),
        ((2, 2, wide // 2, model), bf), ((2, slim // 2, model), bf),
    )
    whole = (((2, model, q_half), bf), ((2, model, o_half), bf), ((2, 8, a_half), f32), ((toks, model), bf)) + saved
    sums = [((toks, model), f32), ((toks, model), f32), ((8, 128), f32)]
    grads = [((experts, 4, depth, wide), bf), ((experts, 4, depth, wide), bf), ((16, 32, slim), bf), ((experts, wide // 2, model), f32),
             ((slim // 2, model), f32)]
    outs = list(whole) + sums + grads
    return pl.pallas_call(
        functools.partial(joint_kernel, (front_plan, block_plan, tiles_plan, weights_plan)),
        out_shape=[shape(*a) for a in outs],
        in_specs=[pl.BlockSpec(memory_space=pltpu.SMEM)] * 2
        + [pl.BlockSpec(memory_space=VMEM)] * 9
        + [pl.BlockSpec(memory_space=ANY)] * 3,
        out_specs=[pl.BlockSpec(memory_space=ANY)] * len(whole)
        + [pl.BlockSpec(memory_space=VMEM)] * 3
        + [pl.BlockSpec(memory_space=ANY)] * 5,
        scratch_shapes=[
            VMEM((experts, model, wide), bf), VMEM((model, slim), bf), VMEM((2, 8, a_half), f32), VMEM((toks, model), bf), VMEM((toks, model), bf),
            VMEM((16, toks), bf),
            VMEM((2, model, q_half), bf), VMEM((2, model, o_half), bf), VMEM((2, 4, 2 * rows, a_half // 2), bf),
            VMEM((2 * rows, q_half), f32), VMEM((2 * rows, o_half), f32), VMEM((2 * rows, a_half), f32),
            VMEM((4, 2, 8, lanes), f32), VMEM((3, 8, a_half // 2), f32), VMEM((2, 16, 32, slim), bf),
            VMEM((16, toks, model), bf), VMEM((16, toks, model), bf), VMEM((16, 16, 128), bf),
            VMEM((experts, wide, model), bf), VMEM((slim, model), bf),
            VMEM((15, toks, model), bf), VMEM((15, toks, model), bf), VMEM((15, 8, 128), f32),
            VMEM((experts, 8, depth, wide), bf), VMEM((16, rows, slim), f32), VMEM((experts, wide // 2, model), bf), VMEM((slim // 2, model), bf),
            DMA((3,)), DMA((3,)), DMA((2, 31)), DMA((2, 16)), DMA((2, 16)), DMA((7,)), DMA((8,)), DMA((8,)), DMA((8,)),
            DMA((15,)), DMA((16,)), DMA((2,)), DMA((1,)), DMA((15,)), DMA((7,)), DMA((4, 2)), DMA((4,)), DMA((4,)), DMA((2, 3)), DMA((2, 4)),
            DMA((7,)), DMA((6 * experts + 2,)), DMA((3, 15)), DMA((3, 15)), DMA((2 * experts + 2,)), DMA((2 * experts + 2,)),
            DMA((2,)), DMA((2,)), DMA((experts, 4)), DMA((experts, 4)),
            DMA((3, 15)), DMA((3, 16)),
        ],
        compiler_params=pltpu.CompilerParams(collective_id=1, has_side_effects=True, vmem_limit_bytes=62 << 20),
        name="joint",
    )(lengths, timesteps, tokens, cotangent, routes.T, waves, w_ada, w_qkv, w_out, w_router.T, w_fc1, e_fc1, e_fc2, w_fc2)


def rear_kernel(lengths, steps, waves, *refs):
    incoming, refs = refs[:15], refs[15:]
    (qkv_in, out_in, part1, part1s, output, d_tokens, d_ada, d_qkv, d_out, d_router, own1, own1s), refs = refs[:12], refs[12:]
    (sum_branch, sum_back, sum_gc, tokens, cotangent, routes, mod, mixed, attn_in, qkv, probs, attn_low, attn_proj, middle, chance), refs = refs[:15], refs[15:]
    (square, slice_own, q_w, o_w, grad_attn, grad_qkv, grad_mid, o_mine, o_got, q_mine, q_got, part_o, part_a, part_b, got_o, got_a, got_b, fin, mod_tile, all_mod, l_sem, s_send, s_recv, send, recv, g_send, g_recv, g_pair, f_send, f_recv, a_send, a_recv, b_send, b_recv, i_sem) = refs
    here = y, z, x, c = place()
    me = chip(y, z, x)
    sibling = device(y, z, x, 1 - c)
    others = [(dy, dz, dx) for dy in (0, 1) for dz in (0, 1, 2, 3) for dx in (0, 1) if (dy, dz, dx) != (0, 0, 0)]
    spot = lambda dy, dz, dx: (1 - y if dy else y, along(z, dz), 1 - x if dx else x)
    held = (sum_branch, sum_back, sum_gc, tokens, cotangent, routes, mod, mixed, attn_in, qkv, probs, attn_low, attn_proj, middle, chance)
    loads = [pltpu.make_async_copy(a, b, i_sem.at[i]) for i, (a, b) in enumerate(zip(incoming, held))]
    local = [pltpu.make_async_copy(qkv_in, q_w, l_sem.at[0]), pltpu.make_async_copy(out_in, o_w, l_sem.at[1])]
    for copy in loads + local:
        copy.start()
    meet([device(*spot(*o), c) for o in others] + [sibling])
    started = []

    def go(copy):
        copy.start()
        started.append(copy)

    home = [pltpu.make_async_copy(part1s.at[me], slice_own, l_sem.at[3])]
    home[0].start()
    for step in (0, 1, 2, 3):
        at = along(z, step)
        go(remote(part1.at[:, at], own1.at[:, z], a_send.at[step], a_recv.at[z], device(y, at, 1 - x, c)))
    for i, o in enumerate(others):
        go(remote(part1s.at[chip(*spot(*o))], own1s.at[me], b_send.at[i], b_recv.at[me], device(*spot(*o), c)))

    for copy in loads:
        copy.wait()
    item = item_mask(lengths, tokens.shape)
    first = ~item
    model = item.shape[1]
    cut = model // 2
    modulation = functools.partial(own_modulation, here, mod, item)
    rows16 = {}

    def per_item(part, value):
        for i, mask in enumerate((first, ~first)):
            rows16[2 * part + i] = jnp.sum(jnp.where(mask, value, 0.0), axis=0, keepdims=True)

    out_grad = wide_float(cotangent[...])
    branch = sum_branch[...]
    output[...] = low(middle[...] + modulation(1, 2) * branch)
    per_item(5, out_grad * branch)
    chosen = choices(routes, square)
    turned = jnp.concatenate([sum_gc[...], jnp.zeros((120, 128), jnp.float32)], axis=0).T
    grad_chance = jnp.where(chosen, turned, 0.0)
    share = chance[...]
    grad_logits = low(share * (grad_chance - jnp.sum(grad_chance * share, axis=-1, keepdims=True)))
    term_router = tn(mixed[...], grad_logits)
    for copy in local + home:
        copy.wait()
    home = [pltpu.make_async_copy(slice_own, own1s.at[me], l_sem.at[3])]
    home[0].start()
    grad_mixed = sum_back[...] + nt(grad_logits, o_w[0, :, cut:])
    normed, scale = norm(middle[...])
    per_item(3, grad_mixed)
    per_item(4, grad_mixed * normed)
    grad_mid[...] = out_grad + norm_back(grad_mixed * (1.0 + modulation(1, 1)), normed, scale)
    per_item(2, grad_mid[...] * attn_proj[...])
    grad_proj = low(grad_mid[...] * modulation(0, 2))
    for h in (0, 1):
        term = jnp.concatenate([tn(attn_low[...], grad_proj[:, h * cut : (h + 1) * cut]), term_router], axis=1)
        o_mine[h] = low(term)
    swap_o = remote(o_mine.at[1 - c], o_got, s_send.at[0], s_recv.at[0], sibling)
    swap_o.start()
    grad_attn[...] = low(nt(grad_proj[:, :cut], o_w[0, :, :cut]) + nt(grad_proj[:, cut:], o_w[1, :, :cut]))

    rows = o_got.shape[0] // 16
    scatters = []
    for i, (part, got, y_first) in enumerate(((part_o, got_o, False), (part_a, got_a, True), (part_b, got_b, False))):
        take = functools.partial(lambda ref, n: ref.at[n], part)
        land = functools.partial(lambda ref, n: ref.at[n], got)
        scatters.append(Scatter(here, y_first, take, land, send.at[i], recv.at[i], relay=True))

    swap_o.wait()
    for n in range(16):
        at = slice(n * rows, (n + 1) * rows)
        part_o[n] = low(wide_float(o_mine[c, at, :]) + wide_float(o_got[at, :]))
    for step in (3, 2, 1, 0):
        scatters[0].first(step)

    left, sides = head_lanes()
    for pair in range(model // 128):
        at = slice(128 * pair, 128 * (pair + 1))
        q, key, value = [qkv[:, base + 128 * pair : base + 128 * (pair + 1)] for base in (0, model, 2 * model)]
        ga = grad_attn[:, at]
        outs = []
        for j, side in enumerate(sides):
            prob = probs[2 * pair + j]
            grad_probs = nt(ga * side, value)
            grad_scores = low(prob * (grad_probs - jnp.sum(grad_probs * prob, axis=-1, keepdims=True)))
            outs.append((nn(grad_scores, key) * 0.125, tn(grad_scores, q) * 0.125, tn(low(prob), ga)))
        for base, one, two in zip((0, model, 2 * model), *outs):
            grad_qkv[:, base + 128 * pair : base + 128 * (pair + 1)] = low(jnp.where(left, one, two))

    third = q_w.shape[2]
    for h in (0, 1):
        q_mine[h] = low(tn(attn_in[...], grad_qkv[:, h * third : (h + 1) * third]))
    swap_q = {}
    for step in (3, 2, 1, 0):
        for side in (0, 1):
            at = pl.ds(pl.multiple_of(2 * rows * (4 * side + along(z, step)), 16), 2 * rows)
            i = 1 + 2 * step + side
            swap_q[step, side] = remote(q_mine.at[1 - c, at, :], q_got.at[at, :], s_send.at[i], s_recv.at[i], sibling)
            swap_q[step, side].start()
    grad_in = nt(grad_qkv[:, :third], q_w[0]) + nt(grad_qkv[:, third:], q_w[1])
    normed, scale = norm(wide_float(tokens[...]))
    per_item(0, grad_in)
    per_item(1, grad_in * normed)
    d_tokens[...] = grad_mid[...] + norm_back(grad_in * (1.0 + modulation(0, 1)), normed, scale)
    column = lax.broadcasted_iota(jnp.int32, (8, model), 1)
    last = jnp.concatenate([rows16[8 + i] for i in range(4)] + [jnp.zeros((4, model), jnp.float32)], axis=0)
    last = last + conditions(steps, (8, model), 4, column, model // 2, waves[...])
    mod_tile[...] = low(jnp.concatenate([rows16[i] for i in range(8)] + [last], axis=0))

    slot = lambda n: all_mod.at[n, c]
    spread = Gather(here, False, mod_tile, slot, g_send, g_recv, g_pair)
    all_mod[me, c] = mod_tile[...]
    gather_start([spread])
    edge = part_a.shape[2]

    def fold(step):
        for side in (0, 1):
            swap_q[step, side].wait()
            first_n = 8 * side + 2 * along(z, step)
            for n in (first_n, first_n + 1):
                at = pl.ds(pl.multiple_of(rows * n, 16), rows)
                total = low(wide_float(q_mine[c, at, :]) + wide_float(q_got[at, :]))
                part_a[n] = total[:, :edge]
                part_b[n] = total[:, edge:]
        for scatter in scatters[1:]:
            scatter.first(step)

    fold(3)
    fold(2)

    def turn(at):
        if at == 1:
            spread.second(0)
            for step in LINE:
                gather_line([spread], step)
        elif at == 2:
            for step in LINE:
                spread.second(step)
        elif at == 3:
            for step in (0,) + LINE:
                spread.third(step)
            spread.finish()
            flat = all_mod[...].reshape(32 * 16, model)
            share_rows = rows // 2
            own = (2 * me + c) * share_rows
            source = lax.broadcasted_iota(jnp.int32, (model, 128), 0)
            lane = lax.broadcasted_iota(jnp.int32, (model, 128), 1)
            own_columns = nn(flat, low(wide_float((source == own + lane) & (lane < share_rows))))
            row = lax.broadcasted_iota(jnp.int32, (512, 128), 0) % 16
            own_columns = jnp.where((row >= 12) & (row < 14), own_columns, 0.0)
            for part in range(6):
                lhs = low(pltpu.roll(own_columns, 512 + 2 * part - 12, 0))
                d_ada[:, part * model : (part + 1) * model] = tn(lhs, flat)[:share_rows]

    scatter_all(scatters, fold, turn)
    fin[c] = jnp.concatenate([scatters[1].total(), scatters[2].total(), scatters[0].total()], axis=1)
    half = rows // 2
    mine = pl.ds(pl.multiple_of(half * c, 8), half)
    theirs = pl.ds(pl.multiple_of(half * (1 - c), 8), half)
    swap = remote(fin.at[c, theirs, :], fin.at[c, theirs, :], f_send, f_recv, sibling)
    swap.start()

    for at in range(4):
        remote(own1.at[:, at], own1.at[:, at], a_send.at[0], a_recv.at[at], sibling).wait_recv()
    for copy in home:
        copy.wait()
    for i, o in enumerate(others):
        n = chip(*spot(*o))
        remote(own1s.at[n], own1s.at[n], b_send.at[i], b_recv.at[n], sibling).wait_recv()
    for scatter in scatters:
        scatter.finish()
    for copy in started:
        copy.wait_send()
    swap.wait_send()
    remote(fin.at[1 - c, mine, :], fin.at[1 - c, mine, :], f_send, f_recv, sibling).wait_recv()
    for h in (0, 1):
        d_qkv[:, h * third : (h + 1) * third] = fin[h, mine, :third]
        d_out[:, h * cut : (h + 1) * cut] = fin[h, mine, third : third + cut]
    d_router[0:half, :] = fin[0, mine, third + cut :]
    d_router[half:, :] = jnp.zeros((128 - half, 128), jnp.float32)


def rear(lengths, timesteps, sums, tokens, cotangent, routes, saved, qkv_w, out_w, part1, part1s):
    bf, f32 = jnp.bfloat16, jnp.float32
    toks, model = tokens.shape
    rows = model // 16
    q_half, o_half = qkv_w.shape[2], out_w.shape[2]
    a_half = model
    incoming = (*sums, tokens, cotangent, routes.T, *saved)
    shape = jax.ShapeDtypeStruct
    return pl.pallas_call(
        rear_kernel,
        out_shape=[
            shape((toks, model), bf),
            shape((toks, model), f32),
            shape((rows // 2, 6 * model), f32),
            shape((rows // 2, 2 * q_half), f32),
            shape((rows // 2, model), f32),
            shape((128, 128), f32),
            shape(part1.shape, bf),
            shape(part1s.shape, bf),
        ],
        in_specs=[pl.BlockSpec(memory_space=pltpu.SMEM)] * 2
        + [pl.BlockSpec(memory_space=VMEM)]
        + [pl.BlockSpec(memory_space=ANY)] * 19,
        out_specs=[pl.BlockSpec(memory_space=VMEM)] * 6 + [pl.BlockSpec(memory_space=ANY)] * 2,
        scratch_shapes=[VMEM(a.shape, a.dtype) for a in incoming]
        + [
            VMEM((128, 128), f32), VMEM(part1s.shape[1:], bf), VMEM(qkv_w.shape, bf), VMEM(out_w.shape, bf),
            VMEM((toks, model), bf), VMEM((toks, 3 * model), bf), VMEM((toks, model), f32),
            VMEM((2, model, o_half), bf), VMEM((model, o_half), bf),
            VMEM((2, model, q_half), bf), VMEM((model, q_half), bf),
            VMEM((16, rows, o_half), bf), VMEM((16, rows, a_half), bf), VMEM((16, rows, q_half - a_half), bf),
            VMEM((15, rows, o_half), bf), VMEM((15, rows, a_half), bf), VMEM((15, rows, q_half - a_half), bf),
            VMEM((2, rows, q_half + o_half), f32), VMEM((16, model), bf), VMEM((16, 2, 16, model), bf),
            DMA((4,)), DMA((9,)), DMA((9,)), DMA((3, 15)), DMA((3, 15)), DMA((31,)), DMA((16,)), DMA((16,)), DMA, DMA,
            DMA((4,)), DMA((4,)), DMA((15,)), DMA((16,)), DMA((16,)),
        ],
        compiler_params=pltpu.CompilerParams(collective_id=3, has_side_effects=True, vmem_limit_bytes=62 << 20),
        name="rear",
    )(lengths, timesteps, frequencies(model)[None], *incoming, qkv_w, out_w, part1, part1s)


def finish_kernel(*refs):
    count = (len(refs) - 3) // 3
    inputs, outputs, staged = refs[:count], refs[count : 2 * count - 1], refs[2 * count - 1 : 3 * count - 1]
    e1, fc1, sem_in, sem = refs[3 * count - 1 :]
    loads = [pltpu.make_async_copy(a, b, sem_in.at[i]) for i, (a, b) in enumerate(zip(inputs, staged))]
    stores = []

    def store(source, target):
        stores.append(pltpu.make_async_copy(source, target, sem.at[len(stores)]))
        stores[-1].start()

    for copy in loads:
        copy.start()
    near, far, slices, router = staged[:4]
    x = place()[2]
    wide = near.shape[3]
    loads[0].wait()
    loads[1].wait()
    for e in range(near.shape[0]):
        for at in range(near.shape[1]):
            e1[e, :, pl.ds(pl.multiple_of(wide * (2 * at + x), 128), wide)] = wide_float(near[e, at])
            e1[e, :, pl.ds(pl.multiple_of(wide * (2 * at + 1 - x), 128), wide)] = wide_float(far[e, at])
        store(e1.at[e], outputs[0].at[e])
    for load, source, target in zip(loads[4:], staged[4:], outputs[3:]):
        load.wait()
        store(source, target)
    loads[2].wait()
    loads[3].wait()
    rows, slim = fc1.shape[0], slices.shape[2]
    for n in range(slices.shape[0] // 2):
        pair = [wide_float(slices[2 * n + i])[:rows] for i in (0, 1)]
        fc1[:, 2 * n * slim : 2 * (n + 1) * slim] = jnp.concatenate(pair, axis=1)
    store(fc1, outputs[1])
    outputs[2][...] = router[...].T[: outputs[2].shape[0], : outputs[2].shape[1]]
    for copy in stores:
        copy.wait()


def finish(near1, far1, own1s, d_router, *others):
    f32 = jnp.float32
    experts, _, depth, wide = near1.shape
    rows = depth // 2
    e1, fc1 = (experts, depth, 8 * wide), (rows, own1s.shape[0] * own1s.shape[2])
    shape = jax.ShapeDtypeStruct
    inputs = (near1, far1, own1s, d_router, *others)
    result = pl.pallas_call(
        finish_kernel,
        out_shape=[shape(e1, f32), shape(fc1, f32), shape((8, rows), f32)] + [shape(a.shape, a.dtype) for a in others],
        in_specs=[pl.BlockSpec(memory_space=ANY)] * len(inputs),
        out_specs=[pl.BlockSpec(memory_space=ANY)] * 2
        + [pl.BlockSpec(memory_space=VMEM)]
        + [pl.BlockSpec(memory_space=ANY)] * len(others),
        scratch_shapes=[VMEM(a.shape, a.dtype) for a in inputs]
        + [VMEM(e1, f32), VMEM(fc1, f32), DMA((len(inputs),)), DMA((8 + len(others),))],
        compiler_params=pltpu.CompilerParams(vmem_limit_bytes=62 << 20),
        name="finish",
    )(*inputs)
    return result[0], result[1], result[2].T, *result[3:]


def layer_norm(values):
    average = jnp.mean(values, axis=-1, keepdims=True)
    centred = values - average
    return centred * lax.rsqrt(jnp.mean(centred * centred, axis=-1, keepdims=True) + layer_epsilon)


def modulate(values, shift_by, scale_by):
    return layer_norm(values) * (1.0 + scale_by) + shift_by


def sinusoid(timesteps, model_width):
    half_width = model_width // 2
    frequency = jnp.exp(-math.log(10000.0) * jnp.arange(half_width, dtype=jnp.float32) / half_width)
    angles = timesteps.astype(jnp.float32)[:, None] * frequency[None, :]
    return jnp.concatenate([jnp.cos(angles), jnp.sin(angles)], axis=1)


def membership(lengths, tok_count):
    bounds = jnp.cumsum(lengths)[:-1]
    position = jnp.arange(tok_count, dtype=jnp.int32)
    item_of = jnp.sum((position[:, None] >= bounds[None, :]).astype(jnp.int32), axis=1)
    item_ids = jnp.arange(lengths.shape[0], dtype=jnp.int32)
    return ((item_of[:, None] == item_ids[None, :]).astype(jnp.float32), item_of)


def slot_index(routes, expert_count, capacity):
    flat_routes = routes.reshape(-1)
    expert_hot = (
        flat_routes[:, None] == jnp.arange(expert_count, dtype=jnp.int32)[None, :]
    ).astype(jnp.int32)
    before = jnp.cumsum(expert_hot, axis=0) - expert_hot
    rank_in = jnp.sum(before * expert_hot, axis=1)
    return (flat_routes * capacity + rank_in).reshape(routes.shape)


def dot_float(left_side, right_side):
    return jnp.dot(left_side, right_side, preferred_element_type=jnp.float32)


def dot_rows(left_side, right_side):
    return jnp.einsum("td,tf->df", left_side, right_side, preferred_element_type=jnp.float32)


def dot_cols(left_side, right_side):
    return jnp.einsum("tf,df->td", left_side, right_side, preferred_element_type=jnp.float32)


def dot_halves(left_side, halves):
    return jnp.concatenate([dot_float(left_side, halves[0]), dot_float(left_side, halves[1])], axis=1)


def by_slices(
    tokens, timesteps, lengths, routes, cotangent, w_ada, w_qkv, w_out, w_fc1, w_fc2, w_router, e_fc1, e_fc2
):
    (qkv_w, out_w, mod, mixed, attn_in, qkv, probs, attn_low, attn_proj, middle, chance, *sums, near1, far1, part1s, d_e2,
     d_fc2) = joint(
        lengths, timesteps, tokens, cotangent, routes, w_ada, w_qkv, w_out, w_router, w_fc1, e_fc1, e_fc2, w_fc2
    )
    saved = (mod, mixed, attn_in, qkv, probs, attn_low, attn_proj, middle, chance)
    output, d_tokens, d_ada, d_qkv, d_out, d_router, own1, own1s = rear(
        lengths, timesteps, sums, tokens, cotangent, routes, saved, qkv_w, out_w, far1, part1s
    )
    d_e1, d_fc1, d_router, output, d_tokens, d_ada, d_qkv, d_out, d_fc2, d_e2 = finish(
        near1, own1, own1s, d_router, output, d_tokens, d_ada, d_qkv, d_out, d_fc2, d_e2
    )
    return (output, d_tokens, d_ada, d_qkv, d_out, d_fc1, d_fc2, d_router, d_e1, d_e2)


def by_weights(
    tokens,
    timesteps,
    lengths,
    routes,
    cotangent,
    w_ada,
    w_qkv,
    w_out,
    w_fc1,
    w_fc2,
    w_router,
    e_fc1,
    e_fc2,
):
    tok_count, model_width = tokens.shape
    head_count = HEADS
    head_size = model_width // head_count
    expert_count = w_router.shape[1]
    capacity = CAP
    score_scale = head_size ** (-0.5)
    residual = tokens.astype(jnp.float32)
    member, item_of = membership(lengths[0], tok_count)
    ada_full, qkv_full, out_full = (
        lax.all_gather(w_ada, ("gx", "gy"), axis=0, tiled=True),
        lax.all_gather(w_qkv, ("gx", "gy"), axis=0, tiled=True),
        lax.all_gather(w_out, ("gx", "gy"), axis=0, tiled=True),
    )
    condition = jax.nn.silu(sinusoid(timesteps, model_width)).astype(jnp.bfloat16)
    modulation = dot_float(condition, ada_full)
    token_mod = jnp.dot(member, modulation, precision=precise)
    shift_attn, scale_attn, gate_attn, shift_mlp, scale_mlp, gate_mlp = jnp.split(
        token_mod, 6, axis=1
    )
    attn_in = modulate(residual, shift_attn, scale_attn).astype(jnp.bfloat16)
    qkv_low = dot_float(attn_in, qkv_full).astype(jnp.bfloat16)
    queries, key_rows, value_rows = [
        portion.reshape(tok_count, head_count, head_size)
        for portion in jnp.split(qkv_low, 3, axis=1)
    ]
    same_item = item_of[:, None] == item_of[None, :]
    scores = (
        jnp.einsum("qhd,khd->hqk", queries, key_rows, preferred_element_type=jnp.float32)
        * score_scale
    )
    scores = jnp.where(same_item[None], scores, -1e30)
    attn_probs = jax.nn.softmax(scores, axis=-1)
    probs_low = attn_probs.astype(jnp.bfloat16)
    attn_low = jnp.einsum("hqk,khd->qhd", probs_low, value_rows, preferred_element_type=jnp.float32)
    attn_low = attn_low.reshape(tok_count, model_width).astype(jnp.bfloat16)
    attn_proj = dot_float(attn_low, out_full)
    middle = residual + gate_attn * attn_proj
    mixed_in = modulate(middle, shift_mlp, scale_mlp).astype(jnp.bfloat16)
    fc1_full, fc2_full, router_full = (
        lax.all_gather(w_fc1, ("gx", "gy"), axis=0, tiled=True),
        lax.all_gather(w_fc2, ("gx", "gy"), axis=0, tiled=True),
        lax.all_gather(w_router, ("gx", "gy"), axis=0, tiled=True),
    )
    hidden_pre = dot_float(mixed_in, fc1_full)
    hidden = jax.nn.gelu(hidden_pre).astype(jnp.bfloat16)
    shared = dot_float(hidden, fc2_full)
    chance = jax.nn.softmax(dot_float(mixed_in, router_full), axis=-1)
    expert_ids = jnp.arange(expert_count, dtype=jnp.int32)
    chosen = (routes[:, :, None] == expert_ids[None, None, :]).astype(jnp.float32)
    gate_values = jnp.sum(chosen * chance[:, None, :], axis=2)
    slot_of = slot_index(routes, expert_count, capacity)
    slot_ids = jnp.arange(expert_count * capacity, dtype=jnp.int32)
    selector = (slot_of[:, :, None] == slot_ids[None, None, :]).astype(jnp.bfloat16)
    slot_rows = jnp.einsum("tks,td->sd", selector, mixed_in, preferred_element_type=jnp.float32)
    slot_rows = slot_rows.astype(jnp.bfloat16).reshape(expert_count, capacity, model_width)
    owned_rows = lax.all_to_all(slot_rows, "gx", split_axis=0, concat_axis=1, tiled=True)
    expert_in, expert_back = (
        lax.all_gather(e_fc1, "gy", axis=1, tiled=True),
        lax.all_gather(e_fc2, "gy", axis=1, tiled=True),
    )
    inner_pre = jnp.einsum(
        "ecd,edf->ecf", owned_rows, expert_in, preferred_element_type=jnp.float32
    )
    inner_act = jax.nn.gelu(inner_pre).astype(jnp.bfloat16)
    result = jnp.einsum(
        "ecf,efd->ecd", inner_act, expert_back, preferred_element_type=jnp.float32
    ).astype(jnp.bfloat16)
    returned = lax.all_to_all(result, "gx", split_axis=1, concat_axis=0, tiled=True).reshape(
        expert_count * capacity, model_width
    )
    picked = jnp.take(returned, slot_of, axis=0).astype(jnp.float32)
    branch = shared + jnp.sum(gate_values[:, :, None] * picked, axis=1)
    output = (middle + gate_mlp * branch).astype(jnp.bfloat16)
    out_grad = cotangent.astype(jnp.float32)
    grad_gate_mlp = out_grad * branch
    grad_branch = out_grad * gate_mlp
    grad_shared = grad_branch.astype(jnp.bfloat16)
    grad_picked = (gate_values[:, :, None] * grad_branch[:, None, :]).astype(jnp.bfloat16)
    grad_gates = jnp.sum(grad_branch[:, None, :] * picked, axis=2)
    grad_slots = jnp.einsum(
        "tks,tkd->sd", selector, grad_picked, preferred_element_type=jnp.float32
    )
    grad_slots = grad_slots.astype(jnp.bfloat16).reshape(expert_count, capacity, model_width)
    grad_owned = lax.all_to_all(grad_slots, "gx", split_axis=0, concat_axis=1, tiled=True)
    grad_inner = jnp.einsum(
        "ecd,efd->ecf", grad_owned, expert_back, preferred_element_type=jnp.float32
    )
    unused_inner, gelu_expert = jax.vjp(jax.nn.gelu, inner_pre)
    grad_inner_pre = gelu_expert(grad_inner)[0].astype(jnp.bfloat16)
    term_e_out = jnp.einsum(
        "ecf,ecd->efd", inner_act, grad_owned, preferred_element_type=jnp.float32
    )
    term_e_in = jnp.einsum(
        "ecd,ecf->edf", owned_rows, grad_inner_pre, preferred_element_type=jnp.float32
    )
    grad_rows = jnp.einsum(
        "ecf,edf->ecd", grad_inner_pre, expert_in, preferred_element_type=jnp.float32
    )
    grad_returned = (
        lax.all_to_all(
            grad_rows.astype(jnp.bfloat16), "gx", split_axis=1, concat_axis=0, tiled=True
        )
        .astype(grad_rows.dtype)
        .reshape(expert_count * capacity, model_width)
    )
    sum_e_in, sum_e_out = (
        lax.psum_scatter(
            term_e_in.astype(jnp.bfloat16), "gy", scatter_dimension=1, tiled=True
        ).astype(jnp.float32),
        lax.psum_scatter(
            term_e_out.astype(jnp.bfloat16), "gy", scatter_dimension=1, tiled=True
        ).astype(jnp.float32),
    )
    grad_chance = jnp.sum(chosen * grad_gates[:, :, None], axis=1)
    grad_logits = chance * (grad_chance - jnp.sum(grad_chance * chance, axis=-1, keepdims=True))
    grad_logits = grad_logits.astype(jnp.bfloat16)
    grad_hidden = dot_cols(grad_shared, fc2_full)
    unused_shared, gelu_shared = jax.vjp(jax.nn.gelu, hidden_pre)
    grad_hidden_pre = gelu_shared(grad_hidden)[0].astype(jnp.bfloat16)
    term_fc2 = dot_rows(hidden, grad_shared)
    term_fc1 = dot_rows(mixed_in, grad_hidden_pre)
    term_router = dot_rows(mixed_in, grad_logits)
    part_fc1, part_fc2, part_router = (
        lax.psum_scatter(
            term_fc1.astype(jnp.bfloat16), "gx", scatter_dimension=0, tiled=True
        ).astype(jnp.float32),
        lax.psum_scatter(
            term_fc2.astype(jnp.bfloat16), "gx", scatter_dimension=0, tiled=True
        ).astype(jnp.float32),
        lax.psum_scatter(
            term_router.astype(jnp.bfloat16), "gx", scatter_dimension=0, tiled=True
        ).astype(jnp.float32),
    )
    sum_fc1, sum_fc2, sum_router = (
        lax.psum_scatter(
            part_fc1.astype(jnp.bfloat16), "gy", scatter_dimension=0, tiled=True
        ).astype(jnp.float32),
        lax.psum_scatter(
            part_fc2.astype(jnp.bfloat16), "gy", scatter_dimension=0, tiled=True
        ).astype(jnp.float32),
        lax.psum_scatter(
            part_router.astype(jnp.bfloat16), "gy", scatter_dimension=0, tiled=True
        ).astype(jnp.float32),
    )
    grad_mixed = dot_cols(grad_hidden_pre, fc1_full) + dot_cols(grad_logits, router_full)
    grad_mixed = grad_mixed + jnp.sum(jnp.take(grad_returned, slot_of, axis=0), axis=1)
    unused_mix, mix_back = jax.vjp(modulate, middle, shift_mlp, scale_mlp)
    grad_mid_norm, grad_shift_mlp, grad_scale_mlp = mix_back(grad_mixed)
    grad_middle = out_grad + grad_mid_norm
    grad_gate_attn = grad_middle * attn_proj
    grad_proj = (grad_middle * gate_attn).astype(jnp.bfloat16)
    term_out = dot_rows(attn_low, grad_proj)
    grad_attn = (
        dot_cols(grad_proj, out_full).astype(jnp.bfloat16).reshape(tok_count, head_count, head_size)
    )
    grad_probs = jnp.einsum(
        "qhd,khd->hqk", grad_attn, value_rows, preferred_element_type=jnp.float32
    )
    grad_values = jnp.einsum(
        "hqk,qhd->khd", probs_low, grad_attn, preferred_element_type=jnp.float32
    )
    grad_scores = attn_probs * (
        grad_probs - jnp.sum(grad_probs * attn_probs, axis=-1, keepdims=True)
    )
    grad_scores = grad_scores.astype(jnp.bfloat16)
    grad_queries = (
        jnp.einsum("hqk,khd->qhd", grad_scores, key_rows, preferred_element_type=jnp.float32)
        * score_scale
    )
    grad_keys = (
        jnp.einsum("hqk,qhd->khd", grad_scores, queries, preferred_element_type=jnp.float32)
        * score_scale
    )
    grad_qkv = jnp.concatenate(
        [
            grad_queries.reshape(tok_count, model_width),
            grad_keys.reshape(tok_count, model_width),
            grad_values.reshape(tok_count, model_width),
        ],
        axis=1,
    ).astype(jnp.bfloat16)
    term_qkv = dot_rows(attn_in, grad_qkv)
    grad_attn_in = dot_cols(grad_qkv, qkv_full)
    unused_pre, pre_back = jax.vjp(modulate, residual, shift_attn, scale_attn)
    grad_input_norm, grad_shift_attn, grad_scale_attn = pre_back(grad_attn_in)
    d_tokens = grad_middle + grad_input_norm
    grad_token_mod = jnp.concatenate(
        [
            grad_shift_attn,
            grad_scale_attn,
            grad_gate_attn,
            grad_shift_mlp,
            grad_scale_mlp,
            grad_gate_mlp,
        ],
        axis=1,
    )
    grad_modulation = jnp.einsum("ti,tc->ic", member, grad_token_mod, precision=precise).astype(
        jnp.bfloat16
    )
    all_condition, all_modgrad = (
        lax.all_gather(condition, ("gx", "gy"), axis=0, tiled=True),
        lax.all_gather(grad_modulation, ("gx", "gy"), axis=0, tiled=True),
    )
    own_share = model_width // lax.axis_size(("gx", "gy"))
    own_start = lax.axis_index(("gx", "gy")) * own_share
    own_condition = lax.dynamic_slice_in_dim(all_condition, own_start, own_share, 1)
    owned_ada = dot_rows(own_condition, all_modgrad)
    attn_terms = (term_qkv, term_out)
    attn_parts = (
        lax.psum_scatter(
            attn_terms[0].astype(jnp.bfloat16), "gx", scatter_dimension=0, tiled=True
        ).astype(jnp.float32),
        lax.psum_scatter(
            attn_terms[1].astype(jnp.bfloat16), "gx", scatter_dimension=0, tiled=True
        ).astype(jnp.float32),
    )
    attn_sums = (
        lax.psum_scatter(
            attn_parts[0].astype(jnp.bfloat16), "gy", scatter_dimension=0, tiled=True
        ).astype(jnp.float32),
        lax.psum_scatter(
            attn_parts[1].astype(jnp.bfloat16), "gy", scatter_dimension=0, tiled=True
        ).astype(jnp.float32),
    )
    sum_qkv, sum_out = attn_sums
    return (
        output,
        d_tokens,
        owned_ada,
        sum_qkv,
        sum_out,
        sum_fc1,
        sum_fc2,
        sum_router,
        sum_e_in,
        sum_e_out,
    )


def solution(mesh):
    in_specs = (
        P(("gx", "gy"), None),
        P(("gx", "gy")),
        P(("gx", "gy"), None),
        P(("gx", "gy"), None),
        P(("gx", "gy"), None),
        P(("gx", "gy"), None),
        P(("gx", "gy"), None),
        P(("gx", "gy"), None),
        P(("gx", "gy"), None),
        P(("gx", "gy"), None),
        P(("gx", "gy"), None),
        P("gx", "gy", None),
        P("gx", "gy", None),
    )
    out_specs = (
        P(("gx", "gy"), None),
        P(("gx", "gy"), None),
        P(("gx", "gy"), None),
        P(("gx", "gy"), None),
        P(("gx", "gy"), None),
        P(("gx", "gy"), None),
        P(("gx", "gy"), None),
        P(("gx", "gy"), None),
        P("gx", "gy", None),
        P("gx", "gy", None),
    )
    step = by_slices if dict(mesh.shape) == {"gx": 2, "gy": 16} else by_weights
    return jax.shard_map(
        step, mesh=mesh, in_specs=in_specs, out_specs=out_specs, check_vma=False
    )
```
